32 devices in a mesh: grp: 2 (over x), wide: 4 (over y, core), head: 4 (over z).
Axes of the slice: x: 2, y: 2, z: 4, core: 2. Of those that a mesh axis runs over, the one named last changes fastest.
Arguments:
- tokens: bfloat16 [64, 8192], P('grp'), parts along dimension 0, may hold values from -30 to 30
- attn_gain: bfloat16 [8192], replicated, may hold values from 0.25 to 1.75
- ffn_gain: bfloat16 [8192], P('wide'), may hold values from 0.25 to 1.75
- w_query: bfloat16 [8192, 8192], P('wide', 'head'), may hold values from -0.0625 to 0.0625
- key_matrix: bfloat16 [8192, 1024], P('wide', 'head'), may hold values from -0.0625 to 0.0625
- value_matrix: bfloat16 [8192, 1024], P('wide', 'head'), may hold values from -0.0625 to 0.0625
- w_out: bfloat16 [8192, 8192], P('head', 'wide'), may hold values from -0.0625 to 0.0625
- w_gate: bfloat16 [8192, 14336], P('wide', 'head'), may hold values from -0.0625 to 0.0625
- w_up: bfloat16 [8192, 14336], P('wide', 'head'), may hold values from -0.0625 to 0.0625
- w_down: bfloat16 [14336, 8192], P('head', 'wide'), may hold values from -0.046875 to 0.046875
- kv_cache: bfloat16 [2, 16, 2048, 1024], P(None, 'grp', 'wide', 'head'), parts along dimension 1, may hold values from -250 to 250
- lengths: int32 [16], P('grp'), parts along dimension 0, may hold values from 1 to 2048, 8192 in all
- slots: int32 [16], P('grp'), parts along dimension 0, may hold values from 0 to 7, each once
Outputs:
- layer_out: bfloat16 [64, 8192], P(('grp', 'head'), 'wide'), parts along dimension 0
The draws below stay inside these ranges and needn't reach their ends.
There are 2 independent parts, one for each index of `grp`. The reference program is written for one: setup_inputs(seed, part) draws one part's arguments, and reference() takes and returns one part's arrays. A program takes and returns all parts, laid end to end along the dimension named above; an argument that names none is the same for every part. Nothing has to cross between parts.
Inputs may be any that keep to these rules, and one draw needn't show every extreme that they name: `lengths`: they sum to 8192, and the longest is exactly 2048. `slots`: each slot belongs to exactly one request.
All inputs are finite; a program needn't handle non-finite values.
Results may differ from the reference program's by a relative error of at most 0.0057.
Values may be sent and summed in bfloat16 or wider, within the bound.
No kernel may reach another device: no remote copies, remote signals or barrier semaphores. Data moves between devices by JAX's collectives and lax.ppermute only.
A program may use at most 128 MiB of HBM per device.

```python
import math
import jax
import jax.numpy as jnp
import numpy as np
from jax import lax

MODEL_WIDTH = 8192
QUERY_HEADS = 64
KEY_HEADS = 8
HEAD_WIDTH = 128
FFW = 14336
DRAFT_TOKENS = 4
GROUP_REQUESTS = 8
CACHE_SLOTS = 2048
TOKENS = 32


def draw_tokens(key, part):
    first_key, key_second_split, key_third_split = jax.random.split(jax.random.fold_in(key, 11), 3)
    column_scale = 10.0 ** (jnp.arange(MODEL_WIDTH, dtype=jnp.float32) / MODEL_WIDTH - 0.4) * jax.random.uniform(first_key, (MODEL_WIDTH,), jnp.float32, 0.8, 1.25)
    row_scale = 10.0 ** jax.random.uniform(key_second_split, (TOKENS, 1), jnp.float32, -0.2, 0.3)
    base = jnp.clip(jax.random.normal(key_third_split, (TOKENS, MODEL_WIDTH), jnp.float32), -3.0, 3.0)
    return (base * row_scale * column_scale[None, :]).astype(jnp.bfloat16)


def draw_kv_cache(key, part):
    first_key = jax.random.fold_in(jax.random.fold_in(key, 23), 0)
    complete_shape = (2, GROUP_REQUESTS, CACHE_SLOTS, KEY_HEADS * HEAD_WIDTH)
    base = jnp.clip(jax.random.normal(first_key, complete_shape, jnp.float32), -4.0, 4.0)
    return base.astype(jnp.bfloat16)


def level_of(key, extent, shards, smallest, top_value):
    factor_of = 1.0
    for axis_at, shards_of in shards:
        draws = jax.random.uniform(jax.random.fold_in(jax.random.fold_in(key, 6), axis_at), (shards_of,), jnp.float32, smallest / len(shards), top_value / len(shards))
        factor_of = factor_of * jnp.repeat(jnp.exp(draws), extent[axis_at] // shards_of).reshape((-1,) + (1,) * (len(extent) - 1 - axis_at))
    return factor_of


def profile(number_of, total, reach, slope):
    weights = [(1 << 20) // math.isqrt(standing ** slope) + 1 for standing in range(2, number_of + 1)]
    spare, holding = total - reach - (number_of - 1), [1] * (number_of - 1)
    while spare > 0:
        candidates = [i for i in range(number_of - 1) if holding[i] < reach]
        mass, left = sum([weights[i] for i in candidates]), spare
        for i in candidates:
            extra = min(reach - holding[i], max(1, left * weights[i] // mass), spare)
            holding[i] = holding[i] + extra
            spare = spare - extra
    return np.array([reach] + holding)


def uneven_parts(rng, number_of, total, bound, skew):
    if number_of == 2:
        one = jax.random.randint(rng, (), max(1, total - bound), min(bound, total - 1) + 1)
        return jnp.stack([one, total - one])
    tallies = jnp.asarray(profile(number_of, total, bound, skew), jnp.int32)
    twos = (number_of - 1) // 2
    giver, sink = tallies[1:1 + 2 * twos:2], tallies[2:2 + 2 * twos:2]
    slack = jnp.minimum(giver - 1, bound - sink)
    shifted = jax.random.randint(jax.random.fold_in(rng, 1), (twos,), 0, 1 << 20) % (slack + 1)
    tallies = tallies.at[1:1 + 2 * twos:2].set(giver - shifted).at[2:2 + 2 * twos:2].set(sink + shifted)
    return tallies[jax.random.permutation(jax.random.fold_in(rng, 2), number_of)]


def gaussian(key, extent, spread, limit, shards=(), kind=jnp.bfloat16):
    drawn = jax.random.normal(key, extent, jnp.float32) * spread
    if len(shards) > 0:
        drawn = level_of(key, extent, shards, -0.22, 0.18) * drawn
    return jnp.clip(drawn, min=-limit, max=limit).astype(kind)


def setup_inputs(seed: int = 0, part: int = 0) -> dict:
    key_list = jax.random.split(jax.random.key(seed), 14)
    part_keys = jax.random.split(jax.random.fold_in(key_list[13], part), 14)
    return {
        "tokens": draw_tokens(jax.random.fold_in(jax.random.fold_in(key_list[13], part), 71), part),
        "attn_gain": jnp.clip(1.0 + 0.15 * jax.random.normal(key_list[1], (MODEL_WIDTH,), jnp.float32), 0.25, 1.75).astype(jnp.bfloat16),
        "ffn_gain": jnp.clip(1.0 + 0.15 * jax.random.normal(key_list[2], (MODEL_WIDTH,), jnp.float32), 0.25, 1.75).astype(jnp.bfloat16),
        "w_query": gaussian(key_list[3], (MODEL_WIDTH, QUERY_HEADS * HEAD_WIDTH), MODEL_WIDTH ** -0.5, 0.0625, ((0, 4), (1, 4))),
        "key_matrix": gaussian(key_list[4], (MODEL_WIDTH, KEY_HEADS * HEAD_WIDTH), MODEL_WIDTH ** -0.5, 0.0625, ((0, 4), (1, 4))),
        "value_matrix": gaussian(key_list[5], (MODEL_WIDTH, KEY_HEADS * HEAD_WIDTH), MODEL_WIDTH ** -0.5, 0.0625, ((0, 4), (1, 4))),
        "w_out": gaussian(key_list[6], (QUERY_HEADS * HEAD_WIDTH, MODEL_WIDTH), (QUERY_HEADS * HEAD_WIDTH) ** -0.5, 0.0625, ((0, 4), (1, 4))),
        "w_gate": gaussian(key_list[7], (MODEL_WIDTH, FFW), MODEL_WIDTH ** -0.5, 0.0625, ((0, 4), (1, 4))),
        "w_up": gaussian(key_list[8], (MODEL_WIDTH, FFW), MODEL_WIDTH ** -0.5, 0.0625, ((0, 4), (1, 4))),
        "w_down": gaussian(key_list[9], (FFW, MODEL_WIDTH), FFW ** -0.5, 0.046875, ((0, 4), (1, 4))),
        "kv_cache": draw_kv_cache(jax.random.fold_in(jax.random.fold_in(key_list[13], part), 71), part),
        "lengths": uneven_parts(part_keys[11], GROUP_REQUESTS, GROUP_REQUESTS * CACHE_SLOTS // 2, CACHE_SLOTS, 2).astype(jnp.int32),
        "slots": jax.random.permutation(part_keys[12], GROUP_REQUESTS).astype(jnp.int32),
    }


epsilon = 1e-05
theta_base = 500000.0
neg_large = -1e+30

def rotary_tables(values, token_positions):
    half_width = values.shape[-1] // 2
    exponent = jnp.arange(half_width, dtype=jnp.float32) * (2.0 / values.shape[-1])
    angles = token_positions[:, None] * (theta_base ** (-exponent))[None, :]
    cosine = jnp.cos(angles)[:, None, :]
    sine_part = jnp.sin(angles)[:, None, :]
    front_half = values[..., :half_width]
    back_half = values[..., half_width:]
    return jnp.concatenate([front_half * cosine - back_half * sine_part, back_half * cosine + front_half * sine_part], axis=-1)

def reference(tokens, attn_gain, ffn_gain, w_query, key_matrix, value_matrix, w_out, w_gate, w_up, w_down, kv_cache, lengths, slots):
    token_row_count = tokens.shape[0]
    tokens_f = tokens.astype(jnp.float32)
    scale_in = lax.rsqrt(lax.optimization_barrier(jnp.mean(tokens_f * tokens_f, axis=1, keepdims=True)) + epsilon)
    normed = (tokens_f * scale_in * attn_gain.astype(jnp.float32)[None, :]).astype(jnp.bfloat16)
    query_sum = jnp.dot(normed, w_query, preferred_element_type=jnp.float32)
    key_total = jnp.dot(normed, key_matrix, preferred_element_type=jnp.float32)
    value_total = jnp.dot(normed, value_matrix, preferred_element_type=jnp.float32)
    token_positions = (jnp.repeat(lengths, DRAFT_TOKENS) + jnp.tile(jnp.arange(DRAFT_TOKENS, dtype=jnp.int32), GROUP_REQUESTS)).astype(jnp.float32)
    rotated_queries = (rotary_tables(query_sum.reshape(token_row_count, QUERY_HEADS, HEAD_WIDTH), token_positions) * HEAD_WIDTH ** (-0.5)).astype(jnp.bfloat16)
    rotated_keys = rotary_tables(key_total.reshape(token_row_count, KEY_HEADS, HEAD_WIDTH), token_positions).astype(jnp.bfloat16)
    fresh_value = value_total.reshape(token_row_count, KEY_HEADS, HEAD_WIDTH).astype(jnp.bfloat16)
    heads_per_group = QUERY_HEADS // KEY_HEADS
    causal = jnp.arange(DRAFT_TOKENS, dtype=jnp.int32)[None, :] <= jnp.arange(DRAFT_TOKENS, dtype=jnp.int32)[:, None]

    def attend(request):
        first_row_index = request * DRAFT_TOKENS
        query_tile_rows = lax.dynamic_slice_in_dim(rotated_queries, first_row_index, DRAFT_TOKENS, 0).reshape(DRAFT_TOKENS, KEY_HEADS, heads_per_group, HEAD_WIDTH).astype(jnp.float32)
        draft_keys = lax.dynamic_slice_in_dim(rotated_keys, first_row_index, DRAFT_TOKENS, 0).astype(jnp.float32)
        draft_vals = lax.dynamic_slice_in_dim(fresh_value, first_row_index, DRAFT_TOKENS, 0).astype(jnp.float32)
        cached_row_index = lax.dynamic_index_in_dim(kv_cache, slots[request], 1, keepdims=False)
        joined_keys = cached_row_index[0].reshape(CACHE_SLOTS, KEY_HEADS, HEAD_WIDTH).astype(jnp.float32)
        joined_values = cached_row_index[1].reshape(CACHE_SLOTS, KEY_HEADS, HEAD_WIDTH).astype(jnp.float32)
        scores = jnp.einsum('jkgd,pkd->kgjp', query_tile_rows, joined_keys)
        live_mask = jnp.arange(CACHE_SLOTS, dtype=jnp.int32) < lengths[request]
        masked = jnp.where(live_mask, scores, neg_large)
        draft_scores = jnp.einsum('jkgd,ikd->kgji', query_tile_rows, draft_keys)
        draft_masked = jnp.where(causal, draft_scores, neg_large)
        top_all = jnp.maximum(lax.optimization_barrier(jnp.max(masked, axis=-1)), lax.optimization_barrier(jnp.max(draft_masked, axis=-1)))
        weights = jnp.where(live_mask, jnp.exp(masked - top_all[..., None]), 0.0)
        draft_weights = jnp.where(causal, jnp.exp(draft_masked - top_all[..., None]), 0.0)
        denominator = lax.optimization_barrier(jnp.sum(weights, axis=-1)) + lax.optimization_barrier(jnp.sum(draft_weights, axis=-1))
        weights_b = lax.optimization_barrier(weights.astype(jnp.bfloat16)).astype(jnp.float32)
        draft_b = lax.optimization_barrier(draft_weights.astype(jnp.bfloat16)).astype(jnp.float32)
        accum = jnp.einsum('kgjp,pkd->kgjd', weights_b, joined_values) + jnp.einsum('kgji,ikd->kgjd', draft_b, draft_vals)
        result = accum / denominator[..., None]
        return result.transpose(2, 0, 1, 3).reshape(DRAFT_TOKENS, QUERY_HEADS * HEAD_WIDTH)
    attended = lax.map(attend, jnp.arange(GROUP_REQUESTS, dtype=jnp.int32)).reshape(token_row_count, QUERY_HEADS * HEAD_WIDTH).astype(jnp.bfloat16)
    resid = (tokens_f + jnp.dot(attended, w_out, preferred_element_type=jnp.float32)).astype(jnp.bfloat16)
    resid_f = resid.astype(jnp.float32)
    scale_mid = lax.rsqrt(lax.optimization_barrier(jnp.mean(resid_f * resid_f, axis=1, keepdims=True)) + epsilon)
    ffn_in = (resid_f * scale_mid * ffn_gain.astype(jnp.float32)[None, :]).astype(jnp.bfloat16)
    gate_sum = jnp.dot(ffn_in, w_gate, preferred_element_type=jnp.float32)
    up_sum = jnp.dot(ffn_in, w_up, preferred_element_type=jnp.float32)
    hidden = (jax.nn.silu(gate_sum) * up_sum).astype(jnp.bfloat16)
    return (resid_f + jnp.dot(hidden, w_down, preferred_element_type=jnp.float32)).astype(jnp.bfloat16)
```

```python
import jax
import jax.numpy as jnp
from jax import lax
from jax.experimental import pallas as pl
from jax.experimental.pallas import tpu as pltpu
from jax.sharding import PartitionSpec as P

HEAD_WIDTH = 128
DRAFT_TOKENS = 4
LANES = 128
MIB = 1 << 20

epsilon = 1e-05
theta_base = 500000.0
neg_large = -1e30

f32 = jnp.float32
bf16 = jnp.bfloat16
VMEM = pl.BlockSpec(memory_space=pltpu.VMEM)
SMEM = pl.BlockSpec(memory_space=pltpu.SMEM)
ANY = pl.BlockSpec(memory_space=pl.ANY)


def in_vmem(x):
    return pltpu.with_memory_space_constraint(x, pltpu.VMEM)


def cost(rows, *weights):
    size = sum(w.size for w in weights)
    return pl.CostEstimate(flops=2 * rows * size, bytes_accessed=2 * size, transcendentals=0)


def params(mib):
    return pltpu.CompilerParams(vmem_limit_bytes=mib * MIB)


def blocks_of(width, most):
    step = max(b for b in range(LANES, most + 1, LANES) if width % b == 0)
    return [(at, step) for at in range(0, width, step)]


def lanes(at):
    return slice(at * LANES, (at + 1) * LANES)


def project_kernel(chunks, at, tokens, gain, wq, wk, wv, out, own, tok, gain_f, norm, bq, bk, bv, acc, sems):
    rows, model = tok.shape
    depth, q_cols = bq.shape
    kv_cols = bk.shape[1]
    step = depth // chunks
    copies = [
        pltpu.make_async_copy(tokens, tok, sems.at[0]),
        pltpu.make_async_copy(wk, bk, sems.at[1]),
        pltpu.make_async_copy(wv, bv, sems.at[2]),
    ] + [
        pltpu.make_async_copy(
            wq.at[pl.ds(c * step, step)], bq.at[pl.ds(c * step, step)], sems.at[3 + c]
        )
        for c in range(chunks)
    ]
    for copy in copies:
        copy.start()
    gain_f[...] = gain[...].astype(f32)
    copies[0].wait()
    squares = jnp.zeros((rows, LANES), f32)
    for c in range(model // LANES):
        part = tok[:, lanes(c)].astype(f32)
        squares = squares + part * part
    scale = lax.rsqrt(jnp.sum(squares, axis=1, keepdims=True) / model + epsilon)
    count = depth // LANES
    for c in range(count):
        index = at[0] * count + c
        part = tok[:, pl.ds(pl.multiple_of(index * LANES, LANES), LANES)]
        own[:, lanes(c)] = part
        norm[:, lanes(c)] = (part.astype(f32) * scale * gain_f[pl.ds(index, 1), :]).astype(bf16)
    for copy, held, base in ((copies[1], bk, q_cols), (copies[2], bv, q_cols + kv_cols)):
        copy.wait()
        out[:, base : base + kv_cols] = jnp.dot(
            norm[...], held[...], preferred_element_type=f32
        ).astype(out.dtype)
    for c in range(chunks):
        copies[3 + c].wait()
        for start, size in blocks_of(q_cols, 512):
            cols = slice(start, start + size)
            term = jnp.dot(
                norm[:, c * step : (c + 1) * step],
                bq[c * step : (c + 1) * step, cols],
                preferred_element_type=f32,
            )
            if c:
                term = acc[:, cols] + term
            if c < chunks - 1:
                acc[:, cols] = term
            else:
                out[:, cols] = term.astype(out.dtype)


def project(at, tokens, gain, wq, wk, wv):
    rows, model = tokens.shape
    depth, q_cols = wq.shape
    kv_cols = wk.shape[1]
    chunks = max(1, min(8, depth // 256))
    return pl.pallas_call(
        lambda *refs: project_kernel(chunks, *refs),
        in_specs=[SMEM, ANY, VMEM, ANY, ANY, ANY],
        out_specs=[VMEM, VMEM],
        out_shape=[
            jax.ShapeDtypeStruct((rows, q_cols + 2 * kv_cols), bf16),
            jax.ShapeDtypeStruct((rows, depth), bf16),
        ],
        scratch_shapes=[
            pltpu.VMEM((rows, model), bf16),
            pltpu.VMEM((model // LANES, LANES), f32),
            pltpu.VMEM((rows, depth), bf16),
            pltpu.VMEM(wq.shape, bf16),
            pltpu.VMEM(wk.shape, bf16),
            pltpu.VMEM(wv.shape, bf16),
            pltpu.VMEM((rows, q_cols), f32),
            pltpu.SemaphoreType.DMA((3 + chunks,)),
        ],
        compiler_params=params(16),
        cost_estimate=cost(rows, wq, wk, wv),
        name="project",
    )(at, tokens, gain.reshape(model // LANES, LANES), wq, wk, wv)


def attend_kernel(n, at, lengths, slots, cos, sin, cache, *rest):
    parts, (out, lse_out, queries, total) = rest[:n], rest[n:]
    rows, q_cols = queries.shape
    context, kv_cols = cache.shape[2:]
    kv_heads = kv_cols // HEAD_WIDTH
    heads = q_cols // HEAD_WIDTH
    group = heads // kv_heads
    tile = 2 * DRAFT_TOKENS
    last = at[1]
    base = at[0] * context

    def column(c):
        return sum(p[:, lanes(c)].astype(f32) for p in parts)

    def rotated(x):
        return x * cos[...] + pltpu.roll(x, HEAD_WIDTH // 2, 1) * sin[...]

    for h in range(heads):
        queries[:, lanes(h)] = (rotated(column(h)) * HEAD_WIDTH ** (-0.5)).astype(bf16).astype(f32)
    new_keys = [rotated(column(heads + k)).astype(bf16) for k in range(kv_heads)]
    new_values = [column(heads + kv_heads + k).astype(bf16) for k in range(kv_heads)]

    high = group * tile
    row = lax.broadcasted_iota(jnp.int32, (high, 1), 0) % tile
    first = row < DRAFT_TOKENS
    position = lax.broadcasted_iota(jnp.int32, (high, context), 1) + base
    draft_col = lax.broadcasted_iota(jnp.int32, (high, rows), 1)
    lane = lax.broadcasted_iota(jnp.int32, (tile, LANES), 1)
    nt = (((1,), (1,)), ((), ()))
    for i in range(rows // tile):
        request = 2 * i
        limit = jnp.where(first, lengths[request], lengths[request + 1])
        live = position < limit
        own_at = tile * i + jnp.where(first, 0, DRAFT_TOKENS)
        seen = (draft_col >= own_at) & (draft_col <= tile * i + row) & (last > 0)
        stats = jnp.zeros((tile, LANES), f32)
        for k in range(kv_heads):
            q = jnp.concatenate(
                [queries[tile * i : tile * (i + 1), lanes(k * group + g)] for g in range(group)], axis=0
            ).astype(bf16)
            scores = [
                lax.dot_general(q, cache[0, slots[request + s], :, lanes(k)], nt, preferred_element_type=f32)
                for s in range(2)
            ]
            score = jnp.where(live, jnp.where(first, scores[0], scores[1]), neg_large)
            draft = lax.dot_general(q, new_keys[k], nt, preferred_element_type=f32)
            draft = jnp.where(seen, draft, neg_large)
            top = jnp.maximum(
                jnp.max(score, axis=1, keepdims=True), jnp.max(draft, axis=1, keepdims=True)
            )
            weight = jnp.where(live, jnp.exp(score - top), 0.0)
            draft_weight = jnp.where(seen, jnp.exp(draft - top), 0.0)
            mass = jnp.sum(weight, axis=1, keepdims=True) + jnp.sum(draft_weight, axis=1, keepdims=True)
            weight = weight.astype(bf16)
            sums = [
                jnp.dot(weight, cache[1, slots[request + s], :, lanes(k)], preferred_element_type=f32)
                for s in range(2)
            ]
            value = jnp.where(first, sums[0], sums[1]) + jnp.dot(
                draft_weight.astype(bf16), new_values[k], preferred_element_type=f32
            )
            some = mass > 0.0
            safe = jnp.where(some, mass, 1.0)
            value = value / safe
            lse = jnp.where(some, top + jnp.log(safe), neg_large)
            for g in range(group):
                at_rows = slice(tile * g, tile * (g + 1))
                total[tile * i : tile * (i + 1), lanes(k * group + g)] = value[at_rows]
                stats = jnp.where(lane == k * group + g, lse[at_rows], stats)
        lse_out[tile * i : tile * (i + 1), :] = stats
    out[...] = total[...].astype(bf16)


def attend(at, lengths, slots, cos, sin, cache, parts):
    rows, width = parts[0].shape
    q_cols = width - 2 * cache.shape[3]
    return pl.pallas_call(
        lambda *refs: attend_kernel(len(parts), *refs),
        in_specs=[SMEM] * 3 + [VMEM] * (3 + len(parts)),
        out_specs=[VMEM, VMEM],
        out_shape=[
            jax.ShapeDtypeStruct((rows, q_cols), bf16),
            jax.ShapeDtypeStruct((rows, LANES), f32),
        ],
        scratch_shapes=[pltpu.VMEM((rows, q_cols), f32), pltpu.VMEM((rows, q_cols), f32)],
        compiler_params=params(6),
        cost_estimate=cost(rows, cache),
        name="attend",
    )(at, lengths, slots, cos, sin, in_vmem(cache), *parts)


def output_kernel(n, w, *rest):
    values, stats, (out, attended) = rest[:n], rest[n : 2 * n], rest[2 * n :]
    heads = attended.shape[1] // HEAD_WIDTH
    top = stats[0][...]
    for s in stats[1:]:
        top = jnp.maximum(top, s[...])
    shares = [jnp.exp(s[...] - top) for s in stats]
    whole = sum(shares)
    shares = [s / whole for s in shares]
    for h in range(heads):
        attended[:, lanes(h)] = sum(
            v[:, lanes(h)].astype(f32) * s[:, h : h + 1] for v, s in zip(values, shares)
        ).astype(bf16)
    for start, size in blocks_of(w.shape[1], 512):
        cols = slice(start, start + size)
        out[:, cols] = jnp.dot(attended[...], w[:, cols], preferred_element_type=f32).astype(out.dtype)


def output(values, stats, w):
    rows = values[0].shape[0]
    return pl.pallas_call(
        lambda *refs: output_kernel(len(values), *refs),
        in_specs=[VMEM] * (1 + 2 * len(values)),
        out_specs=VMEM,
        out_shape=jax.ShapeDtypeStruct((rows, w.shape[1]), bf16),
        scratch_shapes=[pltpu.VMEM((rows, w.shape[0]), bf16)],
        compiler_params=params(4),
        cost_estimate=cost(rows, w),
        name="output",
    )(in_vmem(w), *values, *stats)


def half_of(side, x, wg, wu, out):
    half = wg.shape[1] // 2
    for base, w in ((0, wg), (half, wu)):
        for start, size in blocks_of(half, 512):
            cols = pl.ds(pl.multiple_of(side * half + start, LANES), size)
            out[:, base + start : base + start + size] = jnp.dot(
                x[...], w[:, cols], preferred_element_type=f32
            ).astype(out.dtype)


def expand_send_kernel(n, at, own, gain, wg, wu, *rest):
    parts, (out, resid, x, squares, gain_f) = rest[:n], rest[n:]
    rows = own.shape[0]
    gain_f[...] = gain[...].astype(f32)
    square = jnp.zeros((rows, LANES), f32)
    for c in range(own.shape[1] // LANES):
        value = own[:, lanes(c)].astype(f32) + sum(p[:, lanes(c)].astype(f32) for p in parts)
        value = value.astype(bf16)
        resid[:, lanes(c)] = value
        value = value.astype(f32)
        square = square + value * value
        x[:, lanes(c)] = (value * gain_f[c : c + 1, :]).astype(bf16)
    squares[...] = jnp.broadcast_to(jnp.sum(square, axis=1, keepdims=True), squares.shape)
    half_of(1 - at[2], x, wg, wu, out)


def expand_send(at, own, gain, parts, wg, wu):
    rows, depth = own.shape
    return pl.pallas_call(
        lambda *refs: expand_send_kernel(len(parts), *refs),
        in_specs=[SMEM] + [VMEM] * (4 + len(parts)),
        out_specs=[VMEM] * 4,
        out_shape=[
            jax.ShapeDtypeStruct((rows, wg.shape[1]), bf16),
            jax.ShapeDtypeStruct((rows, depth), bf16),
            jax.ShapeDtypeStruct((rows, depth), bf16),
            jax.ShapeDtypeStruct((rows, LANES), f32),
        ],
        scratch_shapes=[pltpu.VMEM((depth // LANES, LANES), f32)],
        compiler_params=params(4),
        cost_estimate=cost(rows, wg),
        name="expand_send",
    )(at, own, gain.reshape(depth // LANES, LANES), in_vmem(wg), in_vmem(wu), *parts)


def expand_keep_kernel(at, x, wg, wu, out):
    half_of(at[2], x, wg, wu, out)


def expand_keep(at, x, wg, wu):
    rows = x.shape[0]
    return pl.pallas_call(
        expand_keep_kernel,
        in_specs=[SMEM] + [VMEM] * 3,
        out_specs=VMEM,
        out_shape=jax.ShapeDtypeStruct((rows, wg.shape[1]), bf16),
        compiler_params=params(4),
        cost_estimate=cost(rows, wg),
        name="expand_keep",
    )(at, x, in_vmem(wg), in_vmem(wu))


def gated_kernel(n, model, squares_n, *rest):
    parts, squares, out = rest[:n], rest[n : n + squares_n], rest[-1]
    half = out.shape[1]
    scale = lax.rsqrt(sum(s[...] for s in squares) / model + epsilon)
    for c in range(half // LANES):
        gate = scale * sum(p[:, lanes(c)].astype(f32) for p in parts)
        up = scale * sum(p[:, half + c * LANES : half + (c + 1) * LANES].astype(f32) for p in parts)
        out[:, lanes(c)] = (gate / (1.0 + jnp.exp(-gate)) * up).astype(bf16)


def gated(model, parts, squares):
    rows, width = parts[0].shape
    return pl.pallas_call(
        lambda *refs: gated_kernel(len(parts), model, len(squares), *refs),
        in_specs=[VMEM] * (len(parts) + len(squares)),
        out_specs=VMEM,
        out_shape=jax.ShapeDtypeStruct((rows, width // 2), bf16),
        compiler_params=params(4),
        name="gated",
    )(*parts, *squares)


def contract_kernel(side, at, hidden, w, *rest):
    out = rest[-1]
    half = hidden.shape[1]
    from_row = pl.multiple_of((at[2] if side == 0 else 1 - at[2]) * half, LANES)
    for start, size in blocks_of(w.shape[1], 512):
        cols = slice(start, start + size)
        term = jnp.dot(hidden[...], w[pl.ds(from_row, half), cols], preferred_element_type=f32)
        if side:
            term = term + rest[0][:, cols]
        out[:, cols] = term.astype(out.dtype)


def contract(side, at, hidden, w, *before):
    rows = hidden.shape[0]
    return pl.pallas_call(
        lambda *refs: contract_kernel(side, *refs),
        in_specs=[SMEM] + [VMEM] * (2 + len(before)),
        out_specs=VMEM,
        out_shape=jax.ShapeDtypeStruct((rows, w.shape[1]), bf16 if side else f32),
        compiler_params=params(4),
        cost_estimate=cost(rows, w),
        name="contract",
    )(at, hidden, in_vmem(w), *before)


def swap(x, axis, bit):
    n = lax.axis_size(axis)
    return lax.ppermute(x, axis, [(i, i ^ bit) for i in range(n)])


def bits_of(axis):
    n = lax.axis_size(axis)
    return [1 << b for b in range(n.bit_length() - 1)]


def gathered(x, axis):
    parts = [x]
    for bit in reversed(bits_of(axis)):
        parts = parts + [swap(p, axis, bit) for p in parts]
    return parts


def summed(x, axis, bits):
    for bit in bits[:-1]:
        x = (x.astype(f32) + swap(x, axis, bit).astype(f32)).astype(bf16)
    return [x] + [swap(x, axis, bit) for bit in bits[-1:]]


def per_device(tokens, attn_gain, ffn_gain, w_query, key_matrix, value_matrix, w_out, w_gate, w_up, w_down, kv_cache, lengths, slots):
    rows, model = tokens.shape
    wide_at, head_at = lax.axis_index("wide"), lax.axis_index("head")
    wide_size, head_size = lax.axis_size("wide"), lax.axis_size("head")
    at = jnp.stack([wide_at, (wide_at == wide_size - 1).astype(jnp.int32), wide_at % 2]).astype(jnp.int32)

    half = HEAD_WIDTH // 2
    positions = (
        jnp.broadcast_to(lengths[:, None], (lengths.shape[0], DRAFT_TOKENS))
        + jnp.arange(DRAFT_TOKENS, dtype=jnp.int32)[None, :]
    ).reshape(rows).astype(f32)
    exponent = jnp.arange(half, dtype=f32) * (2.0 / HEAD_WIDTH)
    angles = positions[:, None] * (theta_base ** (-exponent))[None, :]
    cos, sin = jnp.cos(angles), jnp.sin(angles)
    cos = jnp.concatenate([cos, cos], axis=1)
    sin = jnp.concatenate([-sin, sin], axis=1)

    qkv, own = project(at, tokens, attn_gain, w_query, key_matrix, value_matrix)
    value, stats = attend(at, lengths, slots, cos, sin, kv_cache, gathered(qkv, "wide"))
    out_part = output(gathered(value, "wide"), gathered(stats, "wide"), w_out)
    parts = summed(out_part, "head", bits_of("head"))
    send, resid, x, squares = expand_send(at, own, ffn_gain, parts, w_gate, w_up)
    received = swap(send, "wide", 1)
    keep = expand_keep(at, x, w_gate, w_up)
    pair = (keep.astype(f32) + received.astype(f32)).astype(bf16)
    hidden = gated(model, summed(pair, "wide", bits_of("wide")[1:]), gathered(squares, "wide"))
    other = swap(hidden, "wide", 1)
    down = contract(0, at, hidden, w_down)
    down = contract(1, at, other, w_down, down)

    share = rows // head_size
    cols = down.shape[1]
    blocks = down.reshape(head_size, share, cols)

    def block(index):
        return lax.dynamic_index_in_dim(blocks, index, 0, keepdims=False)

    total = block(head_at).astype(f32)
    for s in range(1, head_size):
        total = total + swap(block(head_at ^ s), "head", s).astype(f32)
    resid_rows = lax.dynamic_slice_in_dim(resid, head_at * share, share, 0)
    return (resid_rows.astype(f32) + total).astype(bf16)


def solution(mesh):
    in_specs = (
        P("grp", None),
        P(),
        P("wide"),
        P("wide", "head"),
        P("wide", "head"),
        P("wide", "head"),
        P("head", "wide"),
        P("wide", "head"),
        P("wide", "head"),
        P("head", "wide"),
        P(None, "grp", "wide", "head"),
        P("grp"),
        P("grp"),
    )
    out_specs = P(("grp", "head"), "wide")
    return jax.shard_map(
        per_device, mesh=mesh, in_specs=in_specs, out_specs=out_specs, check_vma=False
    )
```

```python
import jax
import jax.numpy as jnp
from jax import lax
from jax.experimental import pallas as pl
from jax.experimental.pallas import tpu as pltpu
from jax.sharding import PartitionSpec as P

HEAD_WIDTH = 128
DRAFT_TOKENS = 4
LANES = 128
MIB = 1 << 20

epsilon = 1e-05
theta_base = 500000.0
neg_large = -1e30

f32 = jnp.float32
bf16 = jnp.bfloat16
ANY = pl.BlockSpec(memory_space=pl.ANY)
VMEM = pl.BlockSpec(memory_space=pltpu.VMEM)
SMEM = pl.BlockSpec(memory_space=pltpu.SMEM)
HBM = pl.BlockSpec(memory_space=pltpu.HBM)


def in_hbm(x):
    return pltpu.with_memory_space_constraint(x, pltpu.HBM)


def cost(rows, *weights):
    size = sum(w.size for w in weights)
    return pl.CostEstimate(flops=2 * rows * size, bytes_accessed=2 * size, transcendentals=0)


def params(mib):
    return pltpu.CompilerParams(vmem_limit_bytes=mib * MIB)


def blocks_of(width, most):
    step = max(b for b in range(LANES, most + 1, LANES) if width % b == 0)
    return [(at, step) for at in range(0, width, step)]


def thirds(x):
    high = x.astype(bf16)
    rest = x - high.astype(f32)
    middle = rest.astype(bf16)
    return high, middle, (rest - middle.astype(f32)).astype(bf16)


def lanes(at):
    return slice(at * LANES, (at + 1) * LANES)


def fetch_kernel(pieces, sides, at, _, *refs):
    n = len(sides)
    sources, held, token, sems = refs[:n], refs[n : 2 * n], refs[-2], refs[-1]
    copies = []
    for source, to, side in zip(sources, held, sides):
        step = max(1, to.shape[0] // pieces)
        base = 0
        if side is not None:
            base = pl.multiple_of((at[2] if side == 0 else 1 - at[2]) * to.shape[0], LANES)
        for p in range(to.shape[0] // step):
            copies.append(
                pltpu.make_async_copy(
                    source.at[pl.ds(base + p * step, step)],
                    to.at[pl.ds(p * step, step)],
                    sems.at[len(copies)],
                )
            )
    for copy in copies:
        copy.start()
    token[...] = jnp.zeros_like(token)
    for copy in copies:
        copy.wait()


def fetch(at, after, *wanted):
    pieces = 8
    sides = [w[1] if isinstance(w, tuple) else None for w in wanted]
    wanted = [w[0] if isinstance(w, tuple) else w for w in wanted]
    shapes = [
        w.shape if side is None else (w.shape[0] // 2,) + w.shape[1:] for w, side in zip(wanted, sides)
    ]
    size = sum(w.size // (1 if side is None else 2) for w, side in zip(wanted, sides))
    return pl.pallas_call(
        lambda *refs: fetch_kernel(pieces, sides, *refs),
        in_specs=[SMEM, ANY] + [HBM] * len(wanted),
        out_specs=[VMEM] * (len(wanted) + 1),
        out_shape=[pltpu.VMEM(shape, w.dtype) for shape, w in zip(shapes, wanted)]
        + [pltpu.VMEM((8, LANES), f32)],
        scratch_shapes=[pltpu.SemaphoreType.DMA((2 * pieces * len(wanted),))],
        compiler_params=params(2),
        cost_estimate=pl.CostEstimate(flops=0, bytes_accessed=4 * size, transcendentals=0),
        name="fetch",
    )(at, after, *[in_hbm(w) for w in wanted])


def project_kernel(chunks, at, tokens, gain, wq, wk, wv, out, own, tok, gain_f, norm, bq, bk, bv, acc, gain_b, sems):
    rows, model = tok.shape
    depth, q_cols = bq.shape
    kv_cols = bk.shape[1]
    step = depth // chunks
    gain_copy = pltpu.make_async_copy(gain, gain_b, sems.at[3 + chunks])
    gain_copy.start()
    copies = [
        pltpu.make_async_copy(tokens, tok, sems.at[0]),
        pltpu.make_async_copy(wk, bk, sems.at[1]),
        pltpu.make_async_copy(wv, bv, sems.at[2]),
    ] + [
        pltpu.make_async_copy(
            wq.at[pl.ds(c * step, step)], bq.at[pl.ds(c * step, step)], sems.at[3 + c]
        )
        for c in range(chunks)
    ]
    for copy in copies:
        copy.start()
    gain_copy.wait()
    gain_f[...] = gain_b[...].astype(f32)
    copies[0].wait()
    squares = jnp.zeros((rows, LANES), f32)
    for c in range(model // LANES):
        part = tok[:, lanes(c)].astype(f32)
        squares = squares + part * part
    scale = lax.rsqrt(jnp.sum(squares, axis=1, keepdims=True) / model + epsilon)
    count = depth // LANES
    for c in range(count):
        index = at[0] * count + c
        part = tok[:, pl.ds(pl.multiple_of(index * LANES, LANES), LANES)]
        own[:, lanes(c)] = part
        norm[:, lanes(c)] = (part.astype(f32) * scale * gain_f[pl.ds(index, 1), :]).astype(bf16)
    for copy, held, base in ((copies[1], bk, q_cols), (copies[2], bv, q_cols + kv_cols)):
        copy.wait()
        out[:, base : base + kv_cols] = jnp.dot(
            norm[...], held[...], preferred_element_type=f32
        ).astype(out.dtype)
    for c in range(chunks):
        copies[3 + c].wait()
        for start, size in blocks_of(q_cols, 512):
            cols = slice(start, start + size)
            term = jnp.dot(
                norm[:, c * step : (c + 1) * step],
                bq[c * step : (c + 1) * step, cols],
                preferred_element_type=f32,
            )
            if c:
                term = acc[:, cols] + term
            if c < chunks - 1:
                acc[:, cols] = term
            else:
                out[:, cols] = term.astype(out.dtype)


def project(at, tokens, gain, wq, wk, wv):
    rows, model = tokens.shape
    depth, q_cols = wq.shape
    kv_cols = wk.shape[1]
    chunks = max(1, min(8, depth // 256))
    return pl.pallas_call(
        lambda *refs: project_kernel(chunks, *refs),
        in_specs=[SMEM] + [HBM] * 5,
        out_specs=[VMEM, VMEM],
        out_shape=[
            jax.ShapeDtypeStruct((rows, q_cols + 2 * kv_cols), bf16),
            jax.ShapeDtypeStruct((rows, depth), bf16),
        ],
        scratch_shapes=[
            pltpu.VMEM((rows, model), bf16),
            pltpu.VMEM((model // LANES, LANES), f32),
            pltpu.VMEM((rows, depth), bf16),
            pltpu.VMEM(wq.shape, bf16),
            pltpu.VMEM(wk.shape, bf16),
            pltpu.VMEM(wv.shape, bf16),
            pltpu.VMEM((rows, q_cols), f32),
            pltpu.VMEM((model // LANES, LANES), bf16),
            pltpu.SemaphoreType.DMA((4 + chunks,)),
        ],
        compiler_params=params(16),
        cost_estimate=cost(rows, wq, wk, wv),
        name="project",
    )(at, in_hbm(tokens), in_hbm(gain.reshape(model // LANES, LANES)), in_hbm(wq), in_hbm(wk), in_hbm(wv))


def attend_kernel(n, at, cos, sin, cache, *rest):
    parts, (out, queries, total, stats_f) = rest[:n], rest[n:]
    rows, q_cols = queries.shape
    context, kv_cols = cache.shape[2:]
    kv_heads = kv_cols // HEAD_WIDTH
    heads = q_cols // HEAD_WIDTH
    group = heads // kv_heads
    tile = 2 * DRAFT_TOKENS
    requests = rows // DRAFT_TOKENS

    def length(r):
        return at[4 + r]

    def slot(r):
        return at[4 + requests + r]

    last = at[1]
    base = at[0] * context

    def column(c):
        return sum(p[:, lanes(c)].astype(f32) for p in parts)

    def rotated(x):
        return x * cos[...] + pltpu.roll(x, HEAD_WIDTH // 2, 1) * sin[...]

    for h in range(heads):
        queries[:, lanes(h)] = (rotated(column(h)) * HEAD_WIDTH ** (-0.5)).astype(bf16).astype(f32)
    new_keys = [rotated(column(heads + k)).astype(bf16) for k in range(kv_heads)]
    new_values = [column(heads + kv_heads + k).astype(bf16) for k in range(kv_heads)]

    high = group * tile
    row = lax.broadcasted_iota(jnp.int32, (high, 1), 0) % tile
    first = row < DRAFT_TOKENS
    position = lax.broadcasted_iota(jnp.int32, (high, context), 1) + base
    draft_col = lax.broadcasted_iota(jnp.int32, (high, rows), 1)
    lane = lax.broadcasted_iota(jnp.int32, (tile, LANES), 1)
    nt = (((1,), (1,)), ((), ()))
    for i in range(rows // tile):
        request = 2 * i
        limit = jnp.where(first, length(request), length(request + 1))
        live = position < limit
        own_at = tile * i + jnp.where(first, 0, DRAFT_TOKENS)
        seen = (draft_col >= own_at) & (draft_col <= tile * i + row) & (last > 0)
        stats = jnp.zeros((tile, LANES), f32)
        for k in range(kv_heads):
            q = jnp.concatenate(
                [queries[tile * i : tile * (i + 1), lanes(k * group + g)] for g in range(group)], axis=0
            ).astype(bf16)
            scores = [
                lax.dot_general(q, cache[0, slot(request + s), :, lanes(k)], nt, preferred_element_type=f32)
                for s in range(2)
            ]
            score = jnp.where(live, jnp.where(first, scores[0], scores[1]), neg_large)
            draft = lax.dot_general(q, new_keys[k], nt, preferred_element_type=f32)
            draft = jnp.where(seen, draft, neg_large)
            top = jnp.maximum(
                jnp.max(score, axis=1, keepdims=True), jnp.max(draft, axis=1, keepdims=True)
            )
            weight = jnp.where(live, jnp.exp(score - top), 0.0)
            draft_weight = jnp.where(seen, jnp.exp(draft - top), 0.0)
            mass = jnp.sum(weight, axis=1, keepdims=True) + jnp.sum(draft_weight, axis=1, keepdims=True)
            weight = weight.astype(bf16)
            sums = [
                jnp.dot(weight, cache[1, slot(request + s), :, lanes(k)], preferred_element_type=f32)
                for s in range(2)
            ]
            value = jnp.where(first, sums[0], sums[1]) + jnp.dot(
                draft_weight.astype(bf16), new_values[k], preferred_element_type=f32
            )
            some = mass > 0.0
            safe = jnp.where(some, mass, 1.0)
            value = value / safe
            lse = jnp.where(some, top + jnp.log(safe), neg_large)
            for g in range(group):
                at_rows = slice(tile * g, tile * (g + 1))
                total[tile * i : tile * (i + 1), lanes(k * group + g)] = value[at_rows]
                stats = jnp.where(lane == k * group + g, lse[at_rows], stats)
        stats_f[tile * i : tile * (i + 1), :] = stats
    out[:, :q_cols] = total[...].astype(bf16)
    for p, term in enumerate(thirds(stats_f[...])):
        out[:, q_cols + p * LANES : q_cols + (p + 1) * LANES] = term


def attend(at, cos, sin, cache, parts):
    rows, width = parts[0].shape
    q_cols = width - 2 * cache.shape[3]
    return pl.pallas_call(
        lambda *refs: attend_kernel(len(parts), *refs),
        in_specs=[SMEM] + [VMEM] * (3 + len(parts)),
        out_specs=VMEM,
        out_shape=jax.ShapeDtypeStruct((rows, q_cols + 3 * LANES), bf16),
        scratch_shapes=[
            pltpu.VMEM((rows, q_cols), f32),
            pltpu.VMEM((rows, q_cols), f32),
            pltpu.VMEM((rows, LANES), f32),
        ],
        compiler_params=params(6),
        cost_estimate=cost(rows, cache),
        name="attend",
    )(at, cos, sin, cache, *parts)


def joined(ref, start):
    return sum(ref[:, start + p * LANES : start + (p + 1) * LANES].astype(f32) for p in range(3))


def output_kernel(n, w, *rest):
    values, (out, attended) = rest[:n], rest[n:]
    heads = attended.shape[1] // HEAD_WIDTH
    stats = [joined(v, attended.shape[1]) for v in values]
    top = stats[0]
    for s in stats[1:]:
        top = jnp.maximum(top, s)
    shares = [jnp.exp(s - top) for s in stats]
    whole = sum(shares)
    shares = [s / whole for s in shares]
    for h in range(heads):
        attended[:, lanes(h)] = sum(
            v[:, lanes(h)].astype(f32) * s[:, h : h + 1] for v, s in zip(values, shares)
        ).astype(bf16)
    for start, size in blocks_of(w.shape[1], 512):
        cols = slice(start, start + size)
        out[:, cols] = jnp.dot(attended[...], w[:, cols], preferred_element_type=f32).astype(out.dtype)


def output(values, w, after):
    rows = values[0].shape[0]
    return pl.pallas_call(
        lambda _, *refs: output_kernel(len(values), *refs),
        in_specs=[ANY] + [VMEM] * (1 + len(values)),
        out_specs=VMEM,
        out_shape=jax.ShapeDtypeStruct((rows, w.shape[1]), bf16),
        scratch_shapes=[pltpu.VMEM((rows, w.shape[0]), bf16)],
        compiler_params=params(4),
        cost_estimate=cost(rows, w),
        name="output",
    )(after, w, *values)


def half_of(side, x, wg, wu, out):
    half = wg.shape[1] // 2
    for base, w in ((0, wg), (half, wu)):
        for start, size in blocks_of(half, 512):
            cols = pl.ds(pl.multiple_of(side * half + start, LANES), size)
            out[:, base + start : base + start + size] = jnp.dot(
                x[...], w[:, cols], preferred_element_type=f32
            ).astype(out.dtype)


def expand_send_kernel(n, at, own, gain, wg, wu, *rest):
    parts, (out, resid, x, gain_f) = rest[:n], rest[n:]
    rows = own.shape[0]
    gain_f[...] = gain[...].astype(f32)
    square = jnp.zeros((rows, LANES), f32)
    for c in range(own.shape[1] // LANES):
        value = own[:, lanes(c)].astype(f32) + sum(p[:, lanes(c)].astype(f32) for p in parts)
        value = value.astype(bf16)
        value = value.astype(f32)
        resid[:, lanes(c)] = value
        square = square + value * value
        x[:, lanes(c)] = (value * gain_f[c : c + 1, :]).astype(bf16)
    square = jnp.broadcast_to(jnp.sum(square, axis=1, keepdims=True), square.shape)
    for p, term in enumerate(thirds(square)):
        out[:, wg.shape[1] + p * LANES : wg.shape[1] + (p + 1) * LANES] = term
    half_of(1 - at[2], x, wg, wu, out)


def expand_send(at, own, gain, parts, wg, wu):
    rows, depth = own.shape
    return pl.pallas_call(
        lambda *refs: expand_send_kernel(len(parts), *refs),
        in_specs=[SMEM] + [VMEM] * (4 + len(parts)),
        out_specs=[VMEM] * 3,
        out_shape=[
            jax.ShapeDtypeStruct((rows, wg.shape[1] + 3 * LANES), bf16),
            jax.ShapeDtypeStruct((rows, depth), f32),
            jax.ShapeDtypeStruct((rows, depth), bf16),
        ],
        scratch_shapes=[pltpu.VMEM((depth // LANES, LANES), f32)],
        compiler_params=params(4),
        cost_estimate=cost(rows, wg),
        name="expand_send",
    )(at, own, gain.reshape(depth // LANES, LANES), wg, wu, *parts)


def expand_keep_kernel(at, x, wg, wu, out):
    half_of(at[2], x, wg, wu, out)


def expand_keep(at, x, wg, wu):
    rows = x.shape[0]
    return pl.pallas_call(
        expand_keep_kernel,
        in_specs=[SMEM] + [VMEM] * 3,
        out_specs=VMEM,
        out_shape=jax.ShapeDtypeStruct((rows, wg.shape[1]), bf16),
        compiler_params=params(4),
        cost_estimate=cost(rows, wg),
        name="expand_keep",
    )(at, x, wg, wu)


def pair_kernel(keep, received, stats, out):
    width = out.shape[1] - 3 * LANES
    for start, size in blocks_of(width, 512):
        cols = slice(start, start + size)
        out[:, cols] = (keep[:, cols].astype(f32) + received[:, cols].astype(f32)).astype(bf16)
    for p, term in enumerate(thirds(joined(stats, width) + joined(received, width))):
        out[:, width + p * LANES : width + (p + 1) * LANES] = term


def pair(keep, received, stats):
    return pl.pallas_call(
        pair_kernel,
        in_specs=[VMEM] * 3,
        out_specs=VMEM,
        out_shape=jax.ShapeDtypeStruct(received.shape, bf16),
        compiler_params=params(4),
        name="pair",
    )(keep, received, stats)


def gated_kernel(model, one, two, out):
    half = out.shape[1]
    scale = lax.rsqrt((joined(one, 2 * half) + joined(two, 2 * half)) / model + epsilon)
    for c in range(half // LANES):
        gate, up = (
            scale * (one[:, lanes(at)].astype(f32) + two[:, lanes(at)].astype(f32))
            for at in (c, half // LANES + c)
        )
        out[:, lanes(c)] = (gate / (1.0 + jnp.exp(-gate)) * up).astype(bf16)


def gated(model, one, two, after):
    rows, width = one.shape
    return pl.pallas_call(
        lambda _, *refs: gated_kernel(model, *refs),
        in_specs=[ANY] + [VMEM] * 2,
        out_specs=VMEM,
        out_shape=jax.ShapeDtypeStruct((rows, (width - 3 * LANES) // 2), bf16),
        compiler_params=params(4),
        name="gated",
    )(after, one, two)


def contract_kernel(hidden, w, out):
    for start, size in blocks_of(w.shape[1], 512):
        cols = slice(start, start + size)
        out[:, cols] = jnp.dot(hidden[...], w[:, cols], preferred_element_type=f32)


def contract(hidden, w):
    rows = hidden.shape[0]
    return pl.pallas_call(
        contract_kernel,
        in_specs=[VMEM] * 2,
        out_specs=VMEM,
        out_shape=jax.ShapeDtypeStruct((rows, w.shape[1]), f32),
        compiler_params=params(4),
        cost_estimate=cost(rows, w),
        name="contract",
    )(hidden, w)


def contract_last_kernel(n, at, hidden, w, before, resid, own, *rest):
    sends, acc = rest[:-1], rest[-1]
    share = own.shape[0]
    for start, size in blocks_of(w.shape[1], 512):
        cols = slice(start, start + size)
        acc[:, cols] = before[:, cols] + jnp.dot(hidden[...], w[:, cols], preferred_element_type=f32)

    def block(ref, index):
        if share % 8 == 0:
            return ref[pl.ds(pl.multiple_of(index * share, share), share), :]
        chosen = ref[:share, :]
        for b in range(1, n):
            chosen = jnp.where(index == b, ref[b * share : (b + 1) * share, :], chosen)
        return chosen

    own[...] = block(acc, at[3]) + block(resid, at[3])
    for s in range(1, n):
        sends[s - 1][...] = block(acc, at[3] ^ s).astype(bf16)


def contract_last(n, at, hidden, w, before, resid):
    rows, cols = before.shape
    share = rows // n
    return pl.pallas_call(
        lambda *refs: contract_last_kernel(n, *refs),
        in_specs=[SMEM] + [VMEM] * 4,
        out_specs=[VMEM] * n,
        out_shape=[jax.ShapeDtypeStruct((share, cols), f32)]
        + [jax.ShapeDtypeStruct((share, cols), bf16)] * (n - 1),
        scratch_shapes=[pltpu.VMEM((rows, cols), f32)],
        compiler_params=params(4),
        cost_estimate=cost(rows, w),
        name="contract_last",
    )(at, hidden, w, before, resid)


def add_kernel(_, one, two, out):
    for start, size in blocks_of(out.shape[1], 512):
        cols = slice(start, start + size)
        out[:, cols] = (one[:, cols].astype(f32) + two[:, cols].astype(f32)).astype(bf16)


def add(one, two, after):
    return pl.pallas_call(
        add_kernel,
        in_specs=[ANY] + [VMEM] * 2,
        out_specs=VMEM,
        out_shape=jax.ShapeDtypeStruct(one.shape, bf16),
        compiler_params=params(4),
        name="add",
    )(after, one, two)


def swap(x, axis, bit):
    n = lax.axis_size(axis)
    return lax.ppermute(x, axis, [(i, i ^ bit) for i in range(n)])


def bits_of(axis):
    n = lax.axis_size(axis)
    return [1 << b for b in range(n.bit_length() - 1)]


def gathered(x, axis):
    parts = [x]
    for bit in reversed(bits_of(axis)):
        parts = parts + [swap(p, axis, bit) for p in parts]
    return parts


def per_device(tokens, attn_gain, ffn_gain, w_query, key_matrix, value_matrix, w_out, w_gate, w_up, w_down, kv_cache, lengths, slots):
    rows, model = tokens.shape
    wide_at, head_at = lax.axis_index("wide"), lax.axis_index("head")
    wide_size, head_size = lax.axis_size("wide"), lax.axis_size("head")
    places = jnp.stack([wide_at, (wide_at == wide_size - 1).astype(jnp.int32), wide_at & 1, head_at])
    at = jnp.concatenate([places.astype(jnp.int32), lengths, slots])

    half = HEAD_WIDTH // 2
    positions = (
        jnp.broadcast_to(lengths[:, None], (lengths.shape[0], DRAFT_TOKENS))
        + jnp.arange(DRAFT_TOKENS, dtype=jnp.int32)[None, :]
    ).reshape(rows).astype(f32)
    exponent = jnp.arange(half, dtype=f32) * (2.0 / HEAD_WIDTH)
    angles = positions[:, None] * (theta_base ** (-exponent))[None, :]
    cos, sin = jnp.cos(angles), jnp.sin(angles)
    cos = jnp.concatenate([cos, cos], axis=1)
    sin = jnp.concatenate([-sin, sin], axis=1)

    qkv, own = project(at, tokens, attn_gain, w_query, key_matrix, value_matrix)
    cache, w_out, _ = fetch(at, qkv, kv_cache.reshape((-1,) + kv_cache.shape[2:]), w_out)
    cache = cache.reshape(kv_cache.shape)
    value = attend(at, cos, sin, cache, gathered(qkv, "wide"))
    w_gate, have_gate = fetch(at, value, w_gate)
    out_part = output(gathered(value, "wide"), w_out, have_gate)
    w_down_own, have_own = fetch(at, out_part, (w_down, 0))
    for bit in bits_of("head")[:-1]:
        out_part = add(out_part, swap(out_part, "head", bit), have_own)
    w_up, _ = fetch(at, out_part, w_up)
    parts = [out_part, swap(out_part, "head", bits_of("head")[-1])]
    send, resid, x = expand_send(at, own, ffn_gain, parts, w_gate, w_up)
    received = swap(send, "wide", 1)
    keep = expand_keep(at, x, w_gate, w_up)
    total = pair(keep, received, send)
    w_down_other, have_other = fetch(at, total, (w_down, 1))
    for bit in bits_of("wide")[1:-1]:
        there = swap(total, "wide", bit)
        total = pair(total, there, total)
    hidden = gated(model, total, swap(total, "wide", bits_of("wide")[-1]), have_other)
    other = swap(hidden, "wide", 1)
    total, *sends = contract_last(head_size, at, other, w_down_other, contract(hidden, w_down_own), resid)
    for s, send in enumerate(sends, 1):
        total = total + swap(send, "head", s).astype(f32)
    return total.astype(bf16)


def solution(mesh):
    in_specs = (
        P("grp", None),
        P(),
        P("wide"),
        P("wide", "head"),
        P("wide", "head"),
        P("wide", "head"),
        P("head", "wide"),
        P("wide", "head"),
        P("wide", "head"),
        P("head", "wide"),
        P(None, "grp", "wide", "head"),
        P("grp"),
        P("grp"),
    )
    out_specs = P(("grp", "head"), "wide")
    return jax.shard_map(
        per_device, mesh=mesh, in_specs=in_specs, out_specs=out_specs, check_vma=False
    )
```

```python
import math

import jax
import jax.numpy as jnp
from jax import lax
from jax.experimental import pallas as pl
from jax.experimental.pallas import tpu as pltpu
from jax.sharding import PartitionSpec as P

HEAD_WIDTH = 128
DRAFT_TOKENS = 4
LANES = 128
MIB = 1 << 20

epsilon = 1e-05
theta_base = 500000.0
neg_large = -1e30

f32 = jnp.float32
bf16 = jnp.bfloat16
ANY = pl.BlockSpec(memory_space=pl.ANY)
VMEM = pl.BlockSpec(memory_space=pltpu.VMEM)
SMEM = pl.BlockSpec(memory_space=pltpu.SMEM)
HBM = pl.BlockSpec(memory_space=pltpu.HBM)


def in_hbm(x):
    return pltpu.with_memory_space_constraint(x, pltpu.HBM)


def cost(rows, *weights):
    size = sum(w.size for w in weights)
    return pl.CostEstimate(flops=2 * rows * size, bytes_accessed=2 * size, transcendentals=0)


def params(mib):
    return pltpu.CompilerParams(vmem_limit_bytes=mib * MIB)


def blocks_of(width, most):
    step = max(b for b in range(LANES, most + 1, LANES) if width % b == 0)
    return [(at, step) for at in range(0, width, step)]


def thirds(x):
    high = x.astype(bf16)
    rest = x - high.astype(f32)
    middle = rest.astype(bf16)
    return high, middle, (rest - middle.astype(f32)).astype(bf16)


def lanes(at):
    return slice(at * LANES, (at + 1) * LANES)


PIECES = 8


class Part:
    def __init__(self, array, first=0, count=None, side=None):
        rows = array.shape[0]
        self.array, self.first, self.side = array, first, side
        self.count = rows // 2 if side is not None else rows if count is None else count
        self.shape = (self.count,) + array.shape[1:]
        self.out = pltpu.VMEM(self.shape, array.dtype)

    def copies(self, at, source, held, sems):
        step = max(1, self.count // PIECES)
        base = self.first
        if self.side is not None:
            base = pl.multiple_of((at[2] if self.side == 0 else 1 - at[2]) * self.count, LANES)
        return [
            pltpu.make_async_copy(
                source.at[pl.ds(base + p * step, step)], held.at[pl.ds(p * step, step)], sems.at[p]
            )
            for p in range(self.count // step)
        ]


def fetch_kernel(wanted, skip, at, *refs):
    n, refs = len(wanted), refs[skip:]
    sources, held, token, sems = refs[:n], refs[n : 2 * n], refs[2 * n], refs[2 * n + 1 :]
    copies = sum([w.copies(at, *refs) for w, *refs in zip(wanted, sources, held, sems)], [])
    for copy in copies:
        copy.start()
    token[...] = jnp.zeros_like(token)
    for copy in copies:
        copy.wait()


def fetch(at, after, *wanted):
    after = after if isinstance(after, (list, tuple)) else [after]
    size = sum(math.prod(w.shape) for w in wanted)
    return pl.pallas_call(
        lambda *refs: fetch_kernel(wanted, len(after), *refs),
        in_specs=[SMEM] + [ANY] * len(after) + [HBM] * len(wanted),
        out_specs=[VMEM] * (len(wanted) + 1),
        out_shape=[w.out for w in wanted] + [pltpu.VMEM((8, LANES), f32)],
        scratch_shapes=[pltpu.SemaphoreType.DMA((2 * PIECES,))] * len(wanted),
        compiler_params=params(2),
        cost_estimate=pl.CostEstimate(flops=0, bytes_accessed=4 * size, transcendentals=0),
        name="fetch",
    )(at, *after, *[in_hbm(w.array) for w in wanted])


def hold(x, token):
    return pl.pallas_call(
        lambda *_: None,
        in_specs=[VMEM, ANY],
        out_specs=VMEM,
        out_shape=jax.ShapeDtypeStruct(x.shape, x.dtype),
        input_output_aliases={0: 0},
        compiler_params=params(1),
        name="hold",
    )(x, token)


def project_kernel(chunks, at, tokens, gain, wq, wk, wv, out, own, tok, gain_f, norm, bq, bk, bv, acc, gain_b, sems):
    rows, model = tok.shape
    depth, q_cols = bq.shape
    kv_cols = bk.shape[1]
    step = depth // chunks
    gain_copy = pltpu.make_async_copy(gain, gain_b, sems.at[3 + chunks])
    gain_copy.start()
    copies = [
        pltpu.make_async_copy(tokens, tok, sems.at[0]),
        pltpu.make_async_copy(wk, bk, sems.at[1]),
        pltpu.make_async_copy(wv, bv, sems.at[2]),
    ] + [
        pltpu.make_async_copy(
            wq.at[pl.ds(c * step, step)], bq.at[pl.ds(c * step, step)], sems.at[3 + c]
        )
        for c in range(chunks)
    ]
    for copy in copies:
        copy.start()
    gain_copy.wait()
    gain_f[...] = gain_b[...].astype(f32)
    copies[0].wait()
    squares = jnp.zeros((rows, LANES), f32)
    for c in range(model // LANES):
        part = tok[:, lanes(c)].astype(f32)
        squares = squares + part * part
    scale = lax.rsqrt(jnp.sum(squares, axis=1, keepdims=True) / model + epsilon)
    count = depth // LANES
    for c in range(count):
        index = at[0] * count + c
        part = tok[:, pl.ds(pl.multiple_of(index * LANES, LANES), LANES)]
        own[:, lanes(c)] = part
        norm[:, lanes(c)] = (part.astype(f32) * scale * gain_f[pl.ds(index, 1), :]).astype(bf16)
    for copy, held, base in ((copies[1], bk, q_cols), (copies[2], bv, q_cols + kv_cols)):
        copy.wait()
        out[:, base : base + kv_cols] = jnp.dot(
            norm[...], held[...], preferred_element_type=f32
        ).astype(out.dtype)
    for c in range(chunks):
        copies[3 + c].wait()
        for start, size in blocks_of(q_cols, 512):
            cols = slice(start, start + size)
            term = jnp.dot(
                norm[:, c * step : (c + 1) * step],
                bq[c * step : (c + 1) * step, cols],
                preferred_element_type=f32,
            )
            if c:
                term = acc[:, cols] + term
            if c < chunks - 1:
                acc[:, cols] = term
            else:
                out[:, cols] = term.astype(out.dtype)


def project(at, tokens, gain, wq, wk, wv):
    rows, model = tokens.shape
    depth, q_cols = wq.shape
    kv_cols = wk.shape[1]
    chunks = max(1, min(8, depth // 256))
    return pl.pallas_call(
        lambda *refs: project_kernel(chunks, *refs),
        in_specs=[SMEM] + [HBM] * 5,
        out_specs=[VMEM, VMEM],
        out_shape=[
            jax.ShapeDtypeStruct((rows, q_cols + 2 * kv_cols), bf16),
            jax.ShapeDtypeStruct((rows, depth), bf16),
        ],
        scratch_shapes=[
            pltpu.VMEM((rows, model), bf16),
            pltpu.VMEM((model // LANES, LANES), f32),
            pltpu.VMEM((rows, depth), bf16),
            pltpu.VMEM(wq.shape, bf16),
            pltpu.VMEM(wk.shape, bf16),
            pltpu.VMEM(wv.shape, bf16),
            pltpu.VMEM((rows, q_cols), f32),
            pltpu.VMEM((model // LANES, LANES), bf16),
            pltpu.SemaphoreType.DMA((4 + chunks,)),
        ],
        compiler_params=params(16),
        cost_estimate=cost(rows, wq, wk, wv),
        name="project",
    )(at, in_hbm(tokens), in_hbm(gain.reshape(model // LANES, LANES)), in_hbm(wq), in_hbm(wk), in_hbm(wv))


def attend_kernel(n, part, at, cos, sin, cache, source, *rest):
    parts, (out, held, queries, total, stats_f, sems) = rest[:n], rest[n:]
    copies = part.copies(at, source, held, sems)
    for copy in copies:
        copy.start()
    rows, q_cols = queries.shape
    context, kv_cols = cache.shape[2:]
    kv_heads = kv_cols // HEAD_WIDTH
    heads = q_cols // HEAD_WIDTH
    group = heads // kv_heads
    tile = 2 * DRAFT_TOKENS
    requests = rows // DRAFT_TOKENS

    def length(r):
        return at[4 + r]

    def slot(r):
        return at[4 + requests + r]

    last = at[1]
    base = at[0] * context

    def column(c):
        return sum(p[:, lanes(c)].astype(f32) for p in parts)

    def rotated(x):
        return x * cos[...] + pltpu.roll(x, HEAD_WIDTH // 2, 1) * sin[...]

    for h in range(heads):
        queries[:, lanes(h)] = (rotated(column(h)) * HEAD_WIDTH ** (-0.5)).astype(bf16).astype(f32)
    new_keys = [rotated(column(heads + k)).astype(bf16) for k in range(kv_heads)]
    new_values = [column(heads + kv_heads + k).astype(bf16) for k in range(kv_heads)]

    high = group * tile
    row = lax.broadcasted_iota(jnp.int32, (high, 1), 0) % tile
    first = row < DRAFT_TOKENS
    position = lax.broadcasted_iota(jnp.int32, (high, context), 1) + base
    draft_col = lax.broadcasted_iota(jnp.int32, (high, rows), 1)
    lane = lax.broadcasted_iota(jnp.int32, (tile, LANES), 1)
    nt = (((1,), (1,)), ((), ()))
    for i in range(rows // tile):
        request = 2 * i
        limit = jnp.where(first, length(request), length(request + 1))
        live = position < limit
        own_at = tile * i + jnp.where(first, 0, DRAFT_TOKENS)
        seen = (draft_col >= own_at) & (draft_col <= tile * i + row) & (last > 0)
        stats = jnp.zeros((tile, LANES), f32)
        for k in range(kv_heads):
            q = jnp.concatenate(
                [queries[tile * i : tile * (i + 1), lanes(k * group + g)] for g in range(group)], axis=0
            ).astype(bf16)
            scores = [
                lax.dot_general(q, cache[0, slot(request + s), :, lanes(k)], nt, preferred_element_type=f32)
                for s in range(2)
            ]
            score = jnp.where(live, jnp.where(first, scores[0], scores[1]), neg_large)
            draft = lax.dot_general(q, new_keys[k], nt, preferred_element_type=f32)
            draft = jnp.where(seen, draft, neg_large)
            top = jnp.maximum(
                jnp.max(score, axis=1, keepdims=True), jnp.max(draft, axis=1, keepdims=True)
            )
            weight = jnp.where(live, jnp.exp(score - top), 0.0)
            draft_weight = jnp.where(seen, jnp.exp(draft - top), 0.0)
            mass = jnp.sum(weight, axis=1, keepdims=True) + jnp.sum(draft_weight, axis=1, keepdims=True)
            weight = weight.astype(bf16)
            sums = [
                jnp.dot(weight, cache[1, slot(request + s), :, lanes(k)], preferred_element_type=f32)
                for s in range(2)
            ]
            value = jnp.where(first, sums[0], sums[1]) + jnp.dot(
                draft_weight.astype(bf16), new_values[k], preferred_element_type=f32
            )
            some = mass > 0.0
            safe = jnp.where(some, mass, 1.0)
            value = value / safe
            lse = jnp.where(some, top + jnp.log(safe), neg_large)
            for g in range(group):
                at_rows = slice(tile * g, tile * (g + 1))
                total[tile * i : tile * (i + 1), lanes(k * group + g)] = value[at_rows]
                stats = jnp.where(lane == k * group + g, lse[at_rows], stats)
        stats_f[tile * i : tile * (i + 1), :] = stats
    out[:, :q_cols] = total[...].astype(bf16)
    for p, term in enumerate(thirds(stats_f[...])):
        out[:, q_cols + p * LANES : q_cols + (p + 1) * LANES] = term
    for copy in copies:
        copy.wait()


def attend(at, cos, sin, cache, parts, part):
    rows, width = parts[0].shape
    q_cols = width - 2 * cache.shape[3]
    return pl.pallas_call(
        lambda *refs: attend_kernel(len(parts), part, *refs),
        in_specs=[SMEM] + [VMEM] * 3 + [HBM] + [VMEM] * len(parts),
        out_specs=[VMEM, VMEM],
        out_shape=[jax.ShapeDtypeStruct((rows, q_cols + 3 * LANES), bf16), part.out],
        scratch_shapes=[
            pltpu.VMEM((rows, q_cols), f32),
            pltpu.VMEM((rows, q_cols), f32),
            pltpu.VMEM((rows, LANES), f32),
            pltpu.SemaphoreType.DMA((2 * PIECES,)),
        ],
        compiler_params=params(6),
        cost_estimate=cost(rows, cache),
        name="attend",
    )(at, cos, sin, cache, in_hbm(part.array), *parts)


def joined(ref, start):
    return sum(ref[:, start + p * LANES : start + (p + 1) * LANES].astype(f32) for p in range(3))


def product(x, w, out, base, width):
    for start, size in blocks_of(width, 512):
        out[:, start : start + size] = jnp.dot(
            x[...], w[:, base + start : base + start + size], preferred_element_type=f32
        ).astype(out.dtype)


def output_first_kernel(n, w, *rest):
    values, (out, attended) = rest[:n], rest[n:]
    heads = attended.shape[1] // HEAD_WIDTH
    stats = [joined(v, attended.shape[1]) for v in values]
    top = stats[0]
    for s in stats[1:]:
        top = jnp.maximum(top, s)
    shares = [jnp.exp(s - top) for s in stats]
    whole = sum(shares)
    shares = [s / whole for s in shares]
    for h in range(heads):
        attended[:, lanes(h)] = sum(
            v[:, lanes(h)].astype(f32) * s[:, h : h + 1] for v, s in zip(values, shares)
        ).astype(bf16)
    product(attended, w, out, 0, out.shape[1])


def output_first(values, w):
    rows, half = values[0].shape[0], w.shape[1] // 2
    return pl.pallas_call(
        lambda *refs: output_first_kernel(len(values), *refs),
        in_specs=[VMEM] * (1 + len(values)),
        out_specs=[VMEM, VMEM],
        out_shape=[
            jax.ShapeDtypeStruct((rows, half), bf16),
            jax.ShapeDtypeStruct((rows, w.shape[0]), bf16),
        ],
        compiler_params=params(4),
        cost_estimate=cost(rows, w),
        name="output_first",
    )(w, *values)


def output_second(attended, w):
    rows, half = attended.shape[0], w.shape[1] // 2
    return pl.pallas_call(
        lambda x, w, out: product(x, w, out, half, half),
        in_specs=[VMEM] * 2,
        out_specs=VMEM,
        out_shape=jax.ShapeDtypeStruct((rows, half), bf16),
        compiler_params=params(4),
        cost_estimate=cost(rows, w),
        name="output_second",
    )(attended, w)


def half_of(side, x, wg, wu, out, before=None):
    half = wg.shape[1] // 2
    for base, w in ((0, wg), (half, wu)):
        for start, size in blocks_of(half, 512):
            cols = pl.ds(pl.multiple_of(side * half + start, LANES), size)
            to = slice(base + start, base + start + size)
            term = jnp.dot(x[...], w[:, cols], preferred_element_type=f32)
            if before is not None:
                term = before[:, to] + term
            out[:, to] = term.astype(out.dtype)


def residual(which, own, gain, parts, resid, x, gain_f):
    gain_f[...] = gain[...].astype(f32)
    count = resid.shape[1] // LANES
    square = jnp.zeros((own.shape[0], LANES), f32)
    for c in range(count):
        at = which * count + c
        value = own[:, lanes(at)].astype(f32) + sum(p[:, lanes(c)].astype(f32) for p in parts)
        value = value.astype(bf16).astype(f32)
        resid[:, lanes(c)] = value
        square = square + value * value
        x[:, lanes(c)] = (value * gain_f[at : at + 1, :]).astype(bf16)
    return square


def expand_first_kernel(n, part, at, own, gain, wg, wu, _, source, *rest):
    parts, (send, keep, resid, squares, held, x, gain_f, sems) = rest[:n], rest[n:]
    copies = part.copies(at, source, held, sems)
    for copy in copies:
        copy.start()
    squares[...] = residual(0, own, gain, parts, resid, x, gain_f)
    half_of(1 - at[2], x, wg, wu, send)
    half_of(at[2], x, wg, wu, keep)
    for copy in copies:
        copy.wait()


def expand_first(at, own, gain, parts, wg, wu, part, after):
    rows, depth = own.shape
    width = wg.shape[1]
    return pl.pallas_call(
        lambda *refs: expand_first_kernel(len(parts), part, *refs),
        in_specs=[SMEM] + [VMEM] * 4 + [ANY, HBM] + [VMEM] * len(parts),
        out_specs=[VMEM] * 5,
        out_shape=[
            jax.ShapeDtypeStruct((rows, width), f32),
            jax.ShapeDtypeStruct((rows, width), f32),
            jax.ShapeDtypeStruct((rows, depth // 2), f32),
            jax.ShapeDtypeStruct((rows, LANES), f32),
            part.out,
        ],
        scratch_shapes=[
            pltpu.VMEM((rows, depth // 2), bf16),
            pltpu.VMEM((depth // LANES, LANES), f32),
            pltpu.SemaphoreType.DMA((2 * PIECES,)),
        ],
        compiler_params=params(4),
        cost_estimate=cost(rows, wg, wu),
        name="expand_first",
    )(at, own, gain, wg, wu, after, in_hbm(part.array), *parts)


def expand_send_kernel(n, at, own, gain, wg, wu, before, squares, *rest):
    parts, (out, resid, x, gain_f) = rest[:n], rest[n:]
    square = squares[...] + residual(1, own, gain, parts, resid, x, gain_f)
    square = jnp.broadcast_to(jnp.sum(square, axis=1, keepdims=True), square.shape)
    width = wg.shape[1]
    for p, term in enumerate(thirds(square)):
        out[:, width + p * LANES : width + (p + 1) * LANES] = term
    half_of(1 - at[2], x, wg, wu, out, before)


def expand_send(at, own, gain, parts, wg, wu, before, squares):
    rows, depth = own.shape
    return pl.pallas_call(
        lambda *refs: expand_send_kernel(len(parts), *refs),
        in_specs=[SMEM] + [VMEM] * (6 + len(parts)),
        out_specs=[VMEM] * 3,
        out_shape=[
            jax.ShapeDtypeStruct((rows, wg.shape[1] + 3 * LANES), bf16),
            jax.ShapeDtypeStruct((rows, depth // 2), f32),
            jax.ShapeDtypeStruct((rows, depth // 2), bf16),
        ],
        scratch_shapes=[pltpu.VMEM((depth // LANES, LANES), f32)],
        compiler_params=params(4),
        cost_estimate=cost(rows, wg),
        name="expand_send",
    )(at, own, gain, wg, wu, before, squares, *parts)


def expand_keep(at, x, wg, wu, before):
    rows = x.shape[0]
    return pl.pallas_call(
        lambda at, x, wg, wu, before, out: half_of(at[2], x, wg, wu, out, before),
        in_specs=[SMEM] + [VMEM] * 4,
        out_specs=VMEM,
        out_shape=jax.ShapeDtypeStruct((rows, wg.shape[1]), bf16),
        compiler_params=params(4),
        cost_estimate=cost(rows, wg),
        name="expand_keep",
    )(at, x, wg, wu, before)


def pair_kernel(keep, received, stats, out):
    width = out.shape[1] - 3 * LANES
    for start, size in blocks_of(width, 512):
        cols = slice(start, start + size)
        out[:, cols] = (keep[:, cols].astype(f32) + received[:, cols].astype(f32)).astype(bf16)
    for p, term in enumerate(thirds(joined(stats, width) + joined(received, width))):
        out[:, width + p * LANES : width + (p + 1) * LANES] = term


def pair(keep, received, stats):
    return pl.pallas_call(
        pair_kernel,
        in_specs=[VMEM] * 3,
        out_specs=VMEM,
        out_shape=jax.ShapeDtypeStruct(received.shape, bf16),
        compiler_params=params(4),
        name="pair",
    )(keep, received, stats)


def gated_kernel(model, one, two, out):
    half = out.shape[1]
    scale = lax.rsqrt((joined(one, 2 * half) + joined(two, 2 * half)) / model + epsilon)
    for c in range(half // LANES):
        gate, up = (
            scale * (one[:, lanes(at)].astype(f32) + two[:, lanes(at)].astype(f32))
            for at in (c, half // LANES + c)
        )
        out[:, lanes(c)] = (gate / (1.0 + jnp.exp(-gate)) * up).astype(bf16)


def gated(model, one, two, after):
    rows, width = one.shape
    return pl.pallas_call(
        lambda _, *refs: gated_kernel(model, *refs),
        in_specs=[ANY] + [VMEM] * 2,
        out_specs=VMEM,
        out_shape=jax.ShapeDtypeStruct((rows, (width - 3 * LANES) // 2), bf16),
        compiler_params=params(4),
        name="gated",
    )(after, one, two)


def contract_kernel(hidden, w, out):
    for start, size in blocks_of(w.shape[1], 512):
        cols = slice(start, start + size)
        out[:, cols] = jnp.dot(hidden[...], w[:, cols], preferred_element_type=f32)


def contract(hidden, w):
    rows = hidden.shape[0]
    return pl.pallas_call(
        contract_kernel,
        in_specs=[VMEM] * 2,
        out_specs=VMEM,
        out_shape=jax.ShapeDtypeStruct((rows, w.shape[1]), f32),
        compiler_params=params(4),
        cost_estimate=cost(rows, w),
        name="contract",
    )(hidden, w)


def contract_last_kernel(n, at, hidden, w, before, resid_0, resid_1, own, *rest):
    sends, acc = rest[:-1], rest[-1]
    share = own.shape[0]
    for start, size in blocks_of(w.shape[1], 512):
        cols = slice(start, start + size)
        acc[:, cols] = before[:, cols] + jnp.dot(hidden[...], w[:, cols], preferred_element_type=f32)

    def block(ref, index):
        if share % 8 == 0:
            return ref[pl.ds(pl.multiple_of(index * share, share), share), :]
        chosen = ref[:share, :]
        for b in range(1, n):
            chosen = jnp.where(index == b, ref[b * share : (b + 1) * share, :], chosen)
        return chosen

    half = resid_0.shape[1]
    mine = block(acc, at[3])
    own[:, :half] = mine[:, :half] + block(resid_0, at[3])
    own[:, half:] = mine[:, half:] + block(resid_1, at[3])
    for s in range(1, n):
        sends[s - 1][...] = block(acc, at[3] ^ s).astype(bf16)


def contract_last(n, at, hidden, w, before, *resid):
    rows, cols = before.shape
    share = rows // n
    return pl.pallas_call(
        lambda *refs: contract_last_kernel(n, *refs),
        in_specs=[SMEM] + [VMEM] * 5,
        out_specs=[VMEM] * n,
        out_shape=[jax.ShapeDtypeStruct((share, cols), f32)]
        + [jax.ShapeDtypeStruct((share, cols), bf16)] * (n - 1),
        scratch_shapes=[pltpu.VMEM((rows, cols), f32)],
        compiler_params=params(4),
        cost_estimate=cost(rows, w),
        name="contract_last",
    )(at, hidden, w, before, *resid)


def add_kernel(one, two, out):
    for start, size in blocks_of(out.shape[1], 512):
        cols = slice(start, start + size)
        out[:, cols] = (one[:, cols].astype(f32) + two[:, cols].astype(f32)).astype(bf16)


def add(one, two):
    return pl.pallas_call(
        add_kernel,
        in_specs=[VMEM] * 2,
        out_specs=VMEM,
        out_shape=jax.ShapeDtypeStruct(one.shape, bf16),
        compiler_params=params(4),
        name="add",
    )(one, two)


def swap(x, axis, bit):
    n = lax.axis_size(axis)
    return lax.ppermute(x, axis, [(i, i ^ bit) for i in range(n)])


def bits_of(axis):
    n = lax.axis_size(axis)
    return [1 << b for b in range(n.bit_length() - 1)]


def gathered(x, axis, token):
    parts = [x]
    for bit in reversed(bits_of(axis)):
        parts = parts + [swap(p, axis, bit) for p in parts]
        if bit > 1:
            parts = parts[:-1] + [hold(parts[-1], token)]
    return parts


def summed(x, axis):
    *bits, last = bits_of(axis)
    for bit in bits:
        x = add(x, swap(x, axis, bit))
    return x, swap(x, axis, last)


def per_device(tokens, attn_gain, ffn_gain, w_query, key_matrix, value_matrix, w_out, w_gate, w_up, w_down, kv_cache, lengths, slots):
    rows, model = tokens.shape
    wide_at, head_at = lax.axis_index("wide"), lax.axis_index("head")
    wide_size, head_size = lax.axis_size("wide"), lax.axis_size("head")
    places = jnp.stack([wide_at, (wide_at == wide_size - 1).astype(jnp.int32), wide_at & 1, head_at])
    at = places.astype(jnp.int32)

    half = HEAD_WIDTH // 2
    positions = (
        jnp.broadcast_to(lengths[:, None], (lengths.shape[0], DRAFT_TOKENS))
        + jnp.arange(DRAFT_TOKENS, dtype=jnp.int32)[None, :]
    ).reshape(rows).astype(f32)
    exponent = jnp.arange(half, dtype=f32) * (2.0 / HEAD_WIDTH)
    angles = positions[:, None] * (theta_base ** (-exponent))[None, :]
    cos, sin = jnp.cos(angles), jnp.sin(angles)
    cos = jnp.concatenate([cos, cos], axis=1)
    sin = jnp.concatenate([-sin, sin], axis=1)

    qkv, own = project(at, tokens, attn_gain, w_query, key_matrix, value_matrix)
    depth = own.shape[1]
    half = depth // 2
    gain = ffn_gain.reshape(depth // LANES, LANES)

    flat_cache = kv_cache.reshape((-1,) + kv_cache.shape[2:])
    meta = jnp.concatenate([at, lengths, slots])
    cache, gate_0, token = fetch(at, (qkv, meta, cos, sin), Part(flat_cache), Part(w_gate, 0, half))
    cache = cache.reshape(kv_cache.shape)
    value, w_out = attend(meta, cos, sin, cache, gathered(qkv, "wide", token), Part(w_out))

    up_0, token = fetch(at, value, Part(w_up, 0, half))
    out_0, attended = output_first(gathered(value, "wide", token), w_out)
    out_1 = output_second(attended, w_out)
    parts_0, parts_1 = summed(out_0, "head"), summed(out_1, "head")
    gate_1, token = fetch(at, parts_1[0], Part(w_gate, half, half))
    send, keep, resid_0, squares, up_1 = expand_first(
        at, own, gain, parts_0, gate_0, up_0, Part(w_up, half, half), token
    )
    send, resid_1, x = expand_send(at, own, gain, parts_1, gate_1, up_1, send, squares)
    received = swap(send, "wide", 1)
    total = pair(expand_keep(at, x, gate_1, up_1, keep), received, send)
    down_own, down_other, token = fetch(at, total, Part(w_down, side=0), Part(w_down, side=1))
    for bit in bits_of("wide")[1:-1]:
        there = swap(total, "wide", bit)
        total = pair(total, there, total)
    hidden = gated(model, total, swap(total, "wide", bits_of("wide")[-1]), token)
    other = swap(hidden, "wide", 1)
    total, *sends = contract_last(
        head_size, at, other, down_other, contract(hidden, down_own), resid_0, resid_1
    )
    for s, send in enumerate(sends, 1):
        total = total + swap(send, "head", s).astype(f32)
    return total.astype(bf16)


def solution(mesh):
    in_specs = (
        P("grp", None),
        P(),
        P("wide"),
        P("wide", "head"),
        P("wide", "head"),
        P("wide", "head"),
        P("head", "wide"),
        P("wide", "head"),
        P("wide", "head"),
        P("head", "wide"),
        P(None, "grp", "wide", "head"),
        P("grp"),
        P("grp"),
    )
    out_specs = P(("grp", "head"), "wide")
    return jax.shard_map(
        per_device, mesh=mesh, in_specs=in_specs, out_specs=out_specs, check_vma=False
    )
```

```python
import math

import jax
import jax.numpy as jnp
from jax import lax
from jax.experimental import pallas as pl
from jax.experimental.pallas import tpu as pltpu
from jax.sharding import PartitionSpec as P

HEAD_WIDTH = 128
DRAFT_TOKENS = 4
LANES = 128
MIB = 1 << 20

epsilon = 1e-05
theta_base = 500000.0
neg_large = -1e30

f32 = jnp.float32
bf16 = jnp.bfloat16
ANY = pl.BlockSpec(memory_space=pl.ANY)
VMEM = pl.BlockSpec(memory_space=pltpu.VMEM)
SMEM = pl.BlockSpec(memory_space=pltpu.SMEM)
HBM = pl.BlockSpec(memory_space=pltpu.HBM)


def in_hbm(x):
    return pltpu.with_memory_space_constraint(x, pltpu.HBM)


def cost(rows, *weights):
    size = sum(w.size for w in weights)
    return pl.CostEstimate(flops=2 * rows * size, bytes_accessed=2 * size, transcendentals=0)


def params(mib):
    return pltpu.CompilerParams(vmem_limit_bytes=mib * MIB)


def blocks_of(width, most):
    step = max(b for b in range(LANES, most + 1, LANES) if width % b == 0)
    return [(at, step) for at in range(0, width, step)]


def thirds(x):
    high = x.astype(bf16)
    rest = x - high.astype(f32)
    middle = rest.astype(bf16)
    return high, middle, (rest - middle.astype(f32)).astype(bf16)


def lanes(at):
    return slice(at * LANES, (at + 1) * LANES)


PIECES = 8


class Part:
    def __init__(self, array, first=0, count=None, side=None):
        rows = array.shape[0]
        self.array, self.first, self.side = array, first, side
        self.count = rows // 2 if side is not None else rows if count is None else count
        self.shape = (self.count,) + array.shape[1:]
        self.out = pltpu.VMEM(self.shape, array.dtype)

    def copies(self, at, source, held, sems):
        step = max(1, self.count // PIECES)
        base = self.first
        if self.side is not None:
            base = pl.multiple_of((at[2] if self.side == 0 else 1 - at[2]) * self.count, LANES)
        return [
            pltpu.make_async_copy(
                source.at[pl.ds(base + p * step, step)], held.at[pl.ds(p * step, step)], sems.at[p]
            )
            for p in range(self.count // step)
        ]


def beside(copies, at, compute):
    for copy in copies:
        copy.start()
    pl.when(at[2] >= 0)(compute)
    for copy in copies:
        copy.wait()


def fetch_kernel(wanted, skip, at, *refs):
    n, refs = len(wanted), refs[skip:]
    sources, held, token, sems = refs[:n], refs[n : 2 * n], refs[2 * n], refs[2 * n + 1 :]
    copies = sum([w.copies(at, *refs) for w, *refs in zip(wanted, sources, held, sems)], [])
    for copy in copies:
        copy.start()
    token[...] = jnp.zeros_like(token)
    for copy in copies:
        copy.wait()


def fetch(at, after, *wanted):
    after = after if isinstance(after, (list, tuple)) else [after]
    size = sum(math.prod(w.shape) for w in wanted)
    return pl.pallas_call(
        lambda *refs: fetch_kernel(wanted, len(after), *refs),
        in_specs=[SMEM] + [ANY] * len(after) + [HBM] * len(wanted),
        out_specs=[VMEM] * (len(wanted) + 1),
        out_shape=[w.out for w in wanted] + [pltpu.VMEM((8, LANES), f32)],
        scratch_shapes=[pltpu.SemaphoreType.DMA((2 * PIECES,))] * len(wanted),
        compiler_params=params(2),
        cost_estimate=pl.CostEstimate(flops=0, bytes_accessed=4 * size, transcendentals=0),
        name="fetch",
    )(at, *after, *[in_hbm(w.array) for w in wanted])


def hold(x, token):
    return pl.pallas_call(
        lambda *_: None,
        in_specs=[VMEM, ANY],
        out_specs=VMEM,
        out_shape=jax.ShapeDtypeStruct(x.shape, x.dtype),
        input_output_aliases={0: 0},
        compiler_params=params(1),
        name="hold",
    )(x, token)


def project_kernel(chunks, at, tokens, gain, wq, wk, wv, out, own, tok, gain_f, norm, bq, bk, bv, acc, gain_b, sems):
    rows, model = tok.shape
    depth, q_cols = bq.shape
    kv_cols = bk.shape[1]
    step = depth // chunks
    gain_copy = pltpu.make_async_copy(gain, gain_b, sems.at[3 + chunks])
    gain_copy.start()
    copies = [
        pltpu.make_async_copy(tokens, tok, sems.at[0]),
        pltpu.make_async_copy(wk, bk, sems.at[1]),
        pltpu.make_async_copy(wv, bv, sems.at[2]),
    ] + [
        pltpu.make_async_copy(
            wq.at[pl.ds(c * step, step)], bq.at[pl.ds(c * step, step)], sems.at[3 + c]
        )
        for c in range(chunks)
    ]
    for copy in copies:
        copy.start()
    gain_copy.wait()
    gain_f[...] = gain_b[...].astype(f32)
    copies[0].wait()
    squares = jnp.zeros((rows, LANES), f32)
    for c in range(model // LANES):
        part = tok[:, lanes(c)].astype(f32)
        squares = squares + part * part
    scale = lax.rsqrt(jnp.sum(squares, axis=1, keepdims=True) / model + epsilon)
    count = depth // LANES
    for c in range(count):
        index = at[0] * count + c
        part = tok[:, pl.ds(pl.multiple_of(index * LANES, LANES), LANES)]
        own[:, lanes(c)] = part
        norm[:, lanes(c)] = (part.astype(f32) * scale * gain_f[pl.ds(index, 1), :]).astype(bf16)
    for copy, held, base in ((copies[1], bk, q_cols), (copies[2], bv, q_cols + kv_cols)):
        copy.wait()
        out[:, base : base + kv_cols] = jnp.dot(
            norm[...], held[...], preferred_element_type=f32
        ).astype(out.dtype)
    for c in range(chunks):
        copies[3 + c].wait()
        for start, size in blocks_of(q_cols, 512):
            cols = slice(start, start + size)
            term = jnp.dot(
                norm[:, c * step : (c + 1) * step],
                bq[c * step : (c + 1) * step, cols],
                preferred_element_type=f32,
            )
            if c:
                term = acc[:, cols] + term
            if c < chunks - 1:
                acc[:, cols] = term
            else:
                out[:, cols] = term.astype(out.dtype)


def project(at, tokens, gain, wq, wk, wv):
    rows, model = tokens.shape
    depth, q_cols = wq.shape
    kv_cols = wk.shape[1]
    chunks = max(1, min(8, depth // 256))
    return pl.pallas_call(
        lambda *refs: project_kernel(chunks, *refs),
        in_specs=[SMEM] + [HBM] * 5,
        out_specs=[VMEM, VMEM],
        out_shape=[
            jax.ShapeDtypeStruct((rows, q_cols + 2 * kv_cols), bf16),
            jax.ShapeDtypeStruct((rows, depth), bf16),
        ],
        scratch_shapes=[
            pltpu.VMEM((rows, model), bf16),
            pltpu.VMEM((model // LANES, LANES), f32),
            pltpu.VMEM((rows, depth), bf16),
            pltpu.VMEM(wq.shape, bf16),
            pltpu.VMEM(wk.shape, bf16),
            pltpu.VMEM(wv.shape, bf16),
            pltpu.VMEM((rows, q_cols), f32),
            pltpu.VMEM((model // LANES, LANES), bf16),
            pltpu.SemaphoreType.DMA((4 + chunks,)),
        ],
        compiler_params=params(16),
        cost_estimate=cost(rows, wq, wk, wv),
        name="project",
    )(at, in_hbm(tokens), in_hbm(gain.reshape(model // LANES, LANES)), in_hbm(wq), in_hbm(wk), in_hbm(wv))


def attend_kernel(n, part, at, cos, sin, cache, source, *rest):
    parts, (out, held, queries, total, stats_f, sems) = rest[:n], rest[n:]
    beside(
        part.copies(at, source, held, sems),
        at,
        lambda: attention(at, cos, sin, cache, parts, out, queries, total, stats_f),
    )


def attention(at, cos, sin, cache, parts, out, queries, total, stats_f):
    rows, q_cols = queries.shape
    context, kv_cols = cache.shape[2:]
    kv_heads = kv_cols // HEAD_WIDTH
    heads = q_cols // HEAD_WIDTH
    group = heads // kv_heads
    tile = 2 * DRAFT_TOKENS
    requests = rows // DRAFT_TOKENS

    def length(r):
        return at[4 + r]

    def slot(r):
        return at[4 + requests + r]

    last = at[1]
    base = at[0] * context

    def column(c):
        return sum(p[:, lanes(c)].astype(f32) for p in parts)

    def rotated(x):
        return x * cos[...] + pltpu.roll(x, HEAD_WIDTH // 2, 1) * sin[...]

    for h in range(heads):
        queries[:, lanes(h)] = (rotated(column(h)) * HEAD_WIDTH ** (-0.5)).astype(bf16).astype(f32)
    new_keys = [rotated(column(heads + k)).astype(bf16) for k in range(kv_heads)]
    new_values = [column(heads + kv_heads + k).astype(bf16) for k in range(kv_heads)]

    high = group * tile
    row = lax.broadcasted_iota(jnp.int32, (high, 1), 0) % tile
    first = row < DRAFT_TOKENS
    position = lax.broadcasted_iota(jnp.int32, (high, context), 1) + base
    draft_col = lax.broadcasted_iota(jnp.int32, (high, rows), 1)
    lane = lax.broadcasted_iota(jnp.int32, (tile, LANES), 1)
    nt = (((1,), (1,)), ((), ()))
    for i in range(rows // tile):
        request = 2 * i
        limit = jnp.where(first, length(request), length(request + 1))
        live = position < limit
        own_at = tile * i + jnp.where(first, 0, DRAFT_TOKENS)
        seen = (draft_col >= own_at) & (draft_col <= tile * i + row) & (last > 0)
        stats = jnp.zeros((tile, LANES), f32)
        for k in range(kv_heads):
            q = jnp.concatenate(
                [queries[tile * i : tile * (i + 1), lanes(k * group + g)] for g in range(group)], axis=0
            ).astype(bf16)
            scores = [
                lax.dot_general(q, cache[0, slot(request + s), :, lanes(k)], nt, preferred_element_type=f32)
                for s in range(2)
            ]
            score = jnp.where(live, jnp.where(first, scores[0], scores[1]), neg_large)
            draft = lax.dot_general(q, new_keys[k], nt, preferred_element_type=f32)
            draft = jnp.where(seen, draft, neg_large)
            top = jnp.maximum(
                jnp.max(score, axis=1, keepdims=True), jnp.max(draft, axis=1, keepdims=True)
            )
            weight = jnp.where(live, jnp.exp(score - top), 0.0)
            draft_weight = jnp.where(seen, jnp.exp(draft - top), 0.0)
            mass = jnp.sum(weight, axis=1, keepdims=True) + jnp.sum(draft_weight, axis=1, keepdims=True)
            weight = weight.astype(bf16)
            sums = [
                jnp.dot(weight, cache[1, slot(request + s), :, lanes(k)], preferred_element_type=f32)
                for s in range(2)
            ]
            value = jnp.where(first, sums[0], sums[1]) + jnp.dot(
                draft_weight.astype(bf16), new_values[k], preferred_element_type=f32
            )
            some = mass > 0.0
            safe = jnp.where(some, mass, 1.0)
            value = value / safe
            lse = jnp.where(some, top + jnp.log(safe), neg_large)
            for g in range(group):
                at_rows = slice(tile * g, tile * (g + 1))
                total[tile * i : tile * (i + 1), lanes(k * group + g)] = value[at_rows]
                stats = jnp.where(lane == k * group + g, lse[at_rows], stats)
        stats_f[tile * i : tile * (i + 1), :] = stats
    out[:, :q_cols] = total[...].astype(bf16)
    for p, term in enumerate(thirds(stats_f[...])):
        out[:, q_cols + p * LANES : q_cols + (p + 1) * LANES] = term


def attend(at, cos, sin, cache, parts, part):
    rows, width = parts[0].shape
    q_cols = width - 2 * cache.shape[3]
    return pl.pallas_call(
        lambda *refs: attend_kernel(len(parts), part, *refs),
        in_specs=[SMEM] + [VMEM] * 3 + [HBM] + [VMEM] * len(parts),
        out_specs=[VMEM, VMEM],
        out_shape=[jax.ShapeDtypeStruct((rows, q_cols + 3 * LANES), bf16), part.out],
        scratch_shapes=[
            pltpu.VMEM((rows, q_cols), f32),
            pltpu.VMEM((rows, q_cols), f32),
            pltpu.VMEM((rows, LANES), f32),
            pltpu.SemaphoreType.DMA((2 * PIECES,)),
        ],
        compiler_params=params(6),
        cost_estimate=cost(rows, cache),
        name="attend",
    )(at, cos, sin, cache, in_hbm(part.array), *parts)


def joined(ref, start):
    return sum(ref[:, start + p * LANES : start + (p + 1) * LANES].astype(f32) for p in range(3))


def product(x, w, out, base, width):
    for start, size in blocks_of(width, 512):
        out[:, start : start + size] = jnp.dot(
            x[...], w[:, base + start : base + start + size], preferred_element_type=f32
        ).astype(out.dtype)


def output_first_kernel(n, part, at, w, source, *rest):
    values, (out, attended, held, sems) = rest[:n], rest[n:]
    beside(part.copies(at, source, held, sems), at, lambda: combine(w, values, out, attended))


def combine(w, values, out, attended):
    heads = attended.shape[1] // HEAD_WIDTH
    stats = [joined(v, attended.shape[1]) for v in values]
    top = stats[0]
    for s in stats[1:]:
        top = jnp.maximum(top, s)
    shares = [jnp.exp(s - top) for s in stats]
    whole = sum(shares)
    shares = [s / whole for s in shares]
    for h in range(heads):
        attended[:, lanes(h)] = sum(
            v[:, lanes(h)].astype(f32) * s[:, h : h + 1] for v, s in zip(values, shares)
        ).astype(bf16)
    product(attended, w, out, 0, out.shape[1])


def output_first(at, values, w, part):
    rows, half = values[0].shape[0], w.shape[1] // 2
    return pl.pallas_call(
        lambda *refs: output_first_kernel(len(values), part, *refs),
        in_specs=[SMEM, VMEM, HBM] + [VMEM] * len(values),
        out_specs=[VMEM] * 3,
        out_shape=[
            jax.ShapeDtypeStruct((rows, half), bf16),
            jax.ShapeDtypeStruct((rows, w.shape[0]), bf16),
            part.out,
        ],
        scratch_shapes=[pltpu.SemaphoreType.DMA((2 * PIECES,))],
        compiler_params=params(4),
        cost_estimate=cost(rows, w),
        name="output_first",
    )(at, w, in_hbm(part.array), *values)


def output_second(attended, w):
    rows, half = attended.shape[0], w.shape[1] // 2
    return pl.pallas_call(
        lambda x, w, out: product(x, w, out, half, half),
        in_specs=[VMEM] * 2,
        out_specs=VMEM,
        out_shape=jax.ShapeDtypeStruct((rows, half), bf16),
        compiler_params=params(4),
        cost_estimate=cost(rows, w),
        name="output_second",
    )(attended, w)


def half_of(side, x, wg, wu, out, before=None):
    half = wg[0].shape[1] // 2
    for base, pieces in ((0, wg), (half, wu)):
        for start, size in blocks_of(half, 512):
            cols = pl.ds(pl.multiple_of(side * half + start, LANES), size)
            to = slice(base + start, base + start + size)
            term = None if before is None else before[:, to]
            row = 0
            for w in pieces:
                more = jnp.dot(x[:, row : row + w.shape[0]], w[:, cols], preferred_element_type=f32)
                term = more if term is None else term + more
                row += w.shape[0]
            out[:, to] = term.astype(out.dtype)


def residual(which, own, gain, parts, resid, x, gain_f):
    gain_f[...] = gain[...].astype(f32)
    count = resid.shape[1] // LANES
    square = jnp.zeros((own.shape[0], LANES), f32)
    for c in range(count):
        at = which * count + c
        value = own[:, lanes(at)].astype(f32) + sum(p[:, lanes(c)].astype(f32) for p in parts)
        value = value.astype(bf16).astype(f32)
        resid[:, lanes(c)] = value
        square = square + value * value
        x[:, lanes(c)] = (value * gain_f[at : at + 1, :]).astype(bf16)
    return square


def expand_first_kernel(n, part, at, own, gain, wg, wu, source, *rest):
    parts, (send, keep, resid, squares, held, x, gain_f, sems) = rest[:n], rest[n:]

    def compute():
        squares[...] = residual(0, own, gain, parts, resid, x, gain_f)
        half_of(1 - at[2], x, [wg], [wu], send)
        half_of(at[2], x, [wg], [wu], keep)

    beside(part.copies(at, source, held, sems), at, compute)


def expand_first(at, own, gain, parts, wg, wu, part):
    rows, depth = own.shape
    width = wg.shape[1]
    return pl.pallas_call(
        lambda *refs: expand_first_kernel(len(parts), part, *refs),
        in_specs=[SMEM] + [VMEM] * 4 + [HBM] + [VMEM] * len(parts),
        out_specs=[VMEM] * 5,
        out_shape=[
            jax.ShapeDtypeStruct((rows, width), f32),
            jax.ShapeDtypeStruct((rows, width), f32),
            jax.ShapeDtypeStruct((rows, depth // 2), f32),
            jax.ShapeDtypeStruct((rows, LANES), f32),
            part.out,
        ],
        scratch_shapes=[
            pltpu.VMEM((rows, depth // 2), bf16),
            pltpu.VMEM((depth // LANES, LANES), f32),
            pltpu.SemaphoreType.DMA((2 * PIECES,)),
        ],
        compiler_params=params(4),
        cost_estimate=cost(rows, wg, wu),
        name="expand_first",
    )(at, own, gain, wg, wu, in_hbm(part.array), *parts)


def expand_send_kernel(n, g, at, own, gain, before, squares, *rest):
    wg, wu, parts, (out, resid, x, gain_f) = rest[:g], rest[g : g + 1], rest[g + 1 : g + 1 + n], rest[g + 1 + n :]
    square = squares[...] + residual(1, own, gain, parts, resid, x, gain_f)
    square = jnp.broadcast_to(jnp.sum(square, axis=1, keepdims=True), square.shape)
    width = wu[0].shape[1]
    for p, term in enumerate(thirds(square)):
        out[:, width + p * LANES : width + (p + 1) * LANES] = term
    half_of(1 - at[2], x, wg, wu, out, before)


def expand_send(at, own, gain, parts, wg, wu, before, squares):
    rows, depth = own.shape
    return pl.pallas_call(
        lambda *refs: expand_send_kernel(len(parts), len(wg), *refs),
        in_specs=[SMEM] + [VMEM] * (5 + len(wg) + len(parts)),
        out_specs=[VMEM] * 3,
        out_shape=[
            jax.ShapeDtypeStruct((rows, wu.shape[1] + 3 * LANES), bf16),
            jax.ShapeDtypeStruct((rows, depth // 2), f32),
            jax.ShapeDtypeStruct((rows, depth // 2), bf16),
        ],
        scratch_shapes=[pltpu.VMEM((depth // LANES, LANES), f32)],
        compiler_params=params(4),
        cost_estimate=cost(rows, wu),
        name="expand_send",
    )(at, own, gain, before, squares, *wg, wu, *parts)


def expand_keep(at, x, wg, wu, before):
    rows = x.shape[0]
    return pl.pallas_call(
        lambda at, x, before, *refs: half_of(at[2], x, refs[:-2], refs[-2:-1], refs[-1], before),
        in_specs=[SMEM] + [VMEM] * (3 + len(wg)),
        out_specs=VMEM,
        out_shape=jax.ShapeDtypeStruct((rows, wu.shape[1]), bf16),
        compiler_params=params(4),
        cost_estimate=cost(rows, wu),
        name="expand_keep",
    )(at, x, before, *wg, wu)


def pair_kernel(keep, received, stats, out):
    width = out.shape[1] - 3 * LANES
    for start, size in blocks_of(width, 512):
        cols = slice(start, start + size)
        out[:, cols] = (keep[:, cols].astype(f32) + received[:, cols].astype(f32)).astype(bf16)
    for p, term in enumerate(thirds(joined(stats, width) + joined(received, width))):
        out[:, width + p * LANES : width + (p + 1) * LANES] = term


def pair(keep, received, stats):
    return pl.pallas_call(
        pair_kernel,
        in_specs=[VMEM] * 3,
        out_specs=VMEM,
        out_shape=jax.ShapeDtypeStruct(received.shape, bf16),
        compiler_params=params(4),
        name="pair",
    )(keep, received, stats)


def gated_kernel(model, one, two, out):
    half = out.shape[1]
    scale = lax.rsqrt((joined(one, 2 * half) + joined(two, 2 * half)) / model + epsilon)
    for c in range(half // LANES):
        gate, up = (
            scale * (one[:, lanes(at)].astype(f32) + two[:, lanes(at)].astype(f32))
            for at in (c, half // LANES + c)
        )
        out[:, lanes(c)] = (gate / (1.0 + jnp.exp(-gate)) * up).astype(bf16)


def gated(model, one, two, after):
    rows, width = one.shape
    return pl.pallas_call(
        lambda _, *refs: gated_kernel(model, *refs),
        in_specs=[ANY] + [VMEM] * 2,
        out_specs=VMEM,
        out_shape=jax.ShapeDtypeStruct((rows, (width - 3 * LANES) // 2), bf16),
        compiler_params=params(4),
        name="gated",
    )(after, one, two)


def contract_kernel(hidden, w, out):
    for start, size in blocks_of(w.shape[1], 512):
        cols = slice(start, start + size)
        out[:, cols] = jnp.dot(hidden[...], w[:, cols], preferred_element_type=f32)


def contract(hidden, w):
    rows = hidden.shape[0]
    return pl.pallas_call(
        contract_kernel,
        in_specs=[VMEM] * 2,
        out_specs=VMEM,
        out_shape=jax.ShapeDtypeStruct((rows, w.shape[1]), f32),
        compiler_params=params(4),
        cost_estimate=cost(rows, w),
        name="contract",
    )(hidden, w)


def contract_last_kernel(n, at, hidden, w, before, resid_0, resid_1, own, *rest):
    sends, acc = rest[:-1], rest[-1]
    share = own.shape[0]
    for start, size in blocks_of(w.shape[1], 512):
        cols = slice(start, start + size)
        acc[:, cols] = before[:, cols] + jnp.dot(hidden[...], w[:, cols], preferred_element_type=f32)

    def block(ref, index):
        if share % 8 == 0:
            return ref[pl.ds(pl.multiple_of(index * share, share), share), :]
        chosen = ref[:share, :]
        for b in range(1, n):
            chosen = jnp.where(index == b, ref[b * share : (b + 1) * share, :], chosen)
        return chosen

    half = resid_0.shape[1]
    mine = block(acc, at[3])
    own[:, :half] = mine[:, :half] + block(resid_0, at[3])
    own[:, half:] = mine[:, half:] + block(resid_1, at[3])
    for s in range(1, n):
        sends[s - 1][...] = block(acc, at[3] ^ s).astype(bf16)


def contract_last(n, at, hidden, w, before, *resid):
    rows, cols = before.shape
    share = rows // n
    return pl.pallas_call(
        lambda *refs: contract_last_kernel(n, *refs),
        in_specs=[SMEM] + [VMEM] * 5,
        out_specs=[VMEM] * n,
        out_shape=[jax.ShapeDtypeStruct((share, cols), f32)]
        + [jax.ShapeDtypeStruct((share, cols), bf16)] * (n - 1),
        scratch_shapes=[pltpu.VMEM((rows, cols), f32)],
        compiler_params=params(4),
        cost_estimate=cost(rows, w),
        name="contract_last",
    )(at, hidden, w, before, *resid)


def add_kernel(one, two, out):
    for start, size in blocks_of(out.shape[1], 512):
        cols = slice(start, start + size)
        out[:, cols] = (one[:, cols].astype(f32) + two[:, cols].astype(f32)).astype(bf16)


def add(one, two):
    return pl.pallas_call(
        add_kernel,
        in_specs=[VMEM] * 2,
        out_specs=VMEM,
        out_shape=jax.ShapeDtypeStruct(one.shape, bf16),
        compiler_params=params(4),
        name="add",
    )(one, two)


def swap(x, axis, bit):
    n = lax.axis_size(axis)
    return lax.ppermute(x, axis, [(i, i ^ bit) for i in range(n)])


def bits_of(axis):
    n = lax.axis_size(axis)
    return [1 << b for b in range(n.bit_length() - 1)]


def gathered(x, axis, token):
    parts = [x]
    for bit in reversed(bits_of(axis)):
        parts = parts + [swap(p, axis, bit) for p in parts]
        if bit > 1:
            parts = parts[:-1] + [hold(parts[-1], token)]
    return parts


def summed(x, axis):
    *bits, last = bits_of(axis)
    for bit in bits:
        x = add(x, swap(x, axis, bit))
    return x, swap(x, axis, last)


def per_device(tokens, attn_gain, ffn_gain, w_query, key_matrix, value_matrix, w_out, w_gate, w_up, w_down, kv_cache, lengths, slots):
    rows, model = tokens.shape
    wide_at, head_at = lax.axis_index("wide"), lax.axis_index("head")
    wide_size, head_size = lax.axis_size("wide"), lax.axis_size("head")
    places = jnp.stack([wide_at, (wide_at == wide_size - 1).astype(jnp.int32), wide_at & 1, head_at])
    at = places.astype(jnp.int32)

    half = HEAD_WIDTH // 2
    positions = (
        jnp.broadcast_to(lengths[:, None], (lengths.shape[0], DRAFT_TOKENS))
        + jnp.arange(DRAFT_TOKENS, dtype=jnp.int32)[None, :]
    ).reshape(rows).astype(f32)
    exponent = jnp.arange(half, dtype=f32) * (2.0 / HEAD_WIDTH)
    angles = positions[:, None] * (theta_base ** (-exponent))[None, :]
    cos, sin = jnp.cos(angles), jnp.sin(angles)
    cos = jnp.concatenate([cos, cos], axis=1)
    sin = jnp.concatenate([-sin, sin], axis=1)

    qkv, own = project(at, tokens, attn_gain, w_query, key_matrix, value_matrix)
    depth = own.shape[1]
    half = depth // 2
    gain = ffn_gain.reshape(depth // LANES, LANES)

    flat_cache = kv_cache.reshape((-1,) + kv_cache.shape[2:])
    meta = jnp.concatenate([at, lengths, slots])
    cache, gate_0, token = fetch(at, (qkv, meta, cos, sin), Part(flat_cache), Part(w_gate, 0, half))
    cache = cache.reshape(kv_cache.shape)
    value, w_out = attend(meta, cos, sin, cache, gathered(qkv, "wide", token), Part(w_out))

    quarter = half // 2
    up_0, gate_1, token = fetch(at, value, Part(w_up, 0, half), Part(w_gate, half, quarter))
    out_0, attended, gate_2 = output_first(
        at, gathered(value, "wide", token), w_out, Part(w_gate, half + quarter, quarter)
    )
    out_1 = output_second(attended, w_out)
    parts_0, parts_1 = summed(out_0, "head"), summed(out_1, "head")
    send, keep, resid_0, squares, up_1 = expand_first(
        at, own, gain, parts_0, gate_0, up_0, Part(w_up, half, half)
    )
    gate_1 = (gate_1, gate_2)
    send, resid_1, x = expand_send(at, own, gain, parts_1, gate_1, up_1, send, squares)
    received = swap(send, "wide", 1)
    total = pair(expand_keep(at, x, gate_1, up_1, keep), received, send)
    down_own, down_other, token = fetch(at, total, Part(w_down, side=0), Part(w_down, side=1))
    for bit in bits_of("wide")[1:-1]:
        there = swap(total, "wide", bit)
        total = pair(total, there, total)
    hidden = gated(model, total, swap(total, "wide", bits_of("wide")[-1]), token)
    other = swap(hidden, "wide", 1)
    total, *sends = contract_last(
        head_size, at, other, down_other, contract(hidden, down_own), resid_0, resid_1
    )
    for s, send in enumerate(sends, 1):
        total = total + swap(send, "head", s).astype(f32)
    return total.astype(bf16)


def solution(mesh):
    in_specs = (
        P("grp", None),
        P(),
        P("wide"),
        P("wide", "head"),
        P("wide", "head"),
        P("wide", "head"),
        P("head", "wide"),
        P("wide", "head"),
        P("wide", "head"),
        P("head", "wide"),
        P(None, "grp", "wide", "head"),
        P("grp"),
        P("grp"),
    )
    out_specs = P(("grp", "head"), "wide")
    return jax.shard_map(
        per_device, mesh=mesh, in_specs=in_specs, out_specs=out_specs, check_vma=False
    )
```

```python
import math

import jax
import jax.numpy as jnp
from jax import lax
from jax.experimental import pallas as pl
from jax.experimental.pallas import tpu as pltpu
from jax.sharding import PartitionSpec as P

HEAD_WIDTH = 128
DRAFT_TOKENS = 4
LANES = 128
MIB = 1 << 20

epsilon = 1e-05
theta_base = 500000.0
neg_large = -1e30

f32 = jnp.float32
bf16 = jnp.bfloat16
ANY = pl.BlockSpec(memory_space=pl.ANY)
VMEM = pl.BlockSpec(memory_space=pltpu.VMEM)
SMEM = pl.BlockSpec(memory_space=pltpu.SMEM)
HBM = pl.BlockSpec(memory_space=pltpu.HBM)


def in_hbm(x):
    return pltpu.with_memory_space_constraint(x, pltpu.HBM)


def cost(rows, *weights):
    size = sum(w.size for w in weights)
    return pl.CostEstimate(flops=2 * rows * size, bytes_accessed=2 * size, transcendentals=0)


def params(mib):
    return pltpu.CompilerParams(vmem_limit_bytes=mib * MIB)


def blocks_of(width, most):
    step = max(b for b in range(LANES, most + 1, LANES) if width % b == 0)
    return [(at, step) for at in range(0, width, step)]


def thirds(x):
    high = x.astype(bf16)
    rest = x - high.astype(f32)
    middle = rest.astype(bf16)
    return high, middle, (rest - middle.astype(f32)).astype(bf16)


def lanes(at):
    return slice(at * LANES, (at + 1) * LANES)


PIECES = 8


class Part:
    def __init__(self, array, first=0, count=None, side=None):
        rows = array.shape[0]
        self.array, self.first, self.side = array, first, side
        self.count = rows // 2 if side is not None else rows if count is None else count
        self.shape = (self.count,) + array.shape[1:]
        self.out = pltpu.VMEM(self.shape, array.dtype)

    def copies(self, at, source, held, sems):
        step = max(1, self.count // PIECES)
        base = self.first
        if self.side is not None:
            base = pl.multiple_of((at[2] if self.side == 0 else 1 - at[2]) * self.count, LANES)
        return [
            pltpu.make_async_copy(
                source.at[pl.ds(base + p * step, step)], held.at[pl.ds(p * step, step)], sems.at[p]
            )
            for p in range(self.count // step)
        ]


def beside(copies, at, compute):
    for copy in copies:
        copy.start()
    pl.when(at[2] >= 0)(compute)
    for copy in copies:
        copy.wait()


def fetch_kernel(wanted, skip, at, *refs):
    n, refs = len(wanted), refs[skip:]
    sources, held, token, sems = refs[:n], refs[n : 2 * n], refs[2 * n], refs[2 * n + 1 :]
    copies = sum([w.copies(at, *refs) for w, *refs in zip(wanted, sources, held, sems)], [])
    for copy in copies:
        copy.start()
    token[...] = jnp.zeros_like(token)
    for copy in copies:
        copy.wait()


def fetch(at, after, *wanted):
    after = after if isinstance(after, (list, tuple)) else [after]
    size = sum(math.prod(w.shape) for w in wanted)
    return pl.pallas_call(
        lambda *refs: fetch_kernel(wanted, len(after), *refs),
        in_specs=[SMEM] + [ANY] * len(after) + [HBM] * len(wanted),
        out_specs=[VMEM] * (len(wanted) + 1),
        out_shape=[w.out for w in wanted] + [pltpu.VMEM((8, LANES), f32)],
        scratch_shapes=[pltpu.SemaphoreType.DMA((2 * PIECES,))] * len(wanted),
        compiler_params=params(2),
        cost_estimate=pl.CostEstimate(flops=0, bytes_accessed=4 * size, transcendentals=0),
        name="fetch",
    )(at, *after, *[in_hbm(w.array) for w in wanted])


def hold(x, token):
    return pl.pallas_call(
        lambda *_: None,
        in_specs=[VMEM, ANY],
        out_specs=VMEM,
        out_shape=jax.ShapeDtypeStruct(x.shape, x.dtype),
        input_output_aliases={0: 0},
        compiler_params=params(1),
        name="hold",
    )(x, token)


def project_kernel(chunks, at, tokens, gain, wq, wk, wv, out, own, tok, gain_f, norm, bq, bk, bv, acc, gain_b, sems):
    rows, model = tok.shape
    depth, q_cols = bq.shape
    kv_cols = bk.shape[1]
    step = depth // chunks
    gain_copy = pltpu.make_async_copy(gain, gain_b, sems.at[3 + chunks])
    gain_copy.start()
    copies = [
        pltpu.make_async_copy(tokens, tok, sems.at[0]),
        pltpu.make_async_copy(wk, bk, sems.at[1]),
        pltpu.make_async_copy(wv, bv, sems.at[2]),
    ] + [
        pltpu.make_async_copy(
            wq.at[pl.ds(c * step, step)], bq.at[pl.ds(c * step, step)], sems.at[3 + c]
        )
        for c in range(chunks)
    ]
    for copy in copies:
        copy.start()
    gain_copy.wait()
    gain_f[...] = gain_b[...].astype(f32)
    copies[0].wait()
    squares = jnp.zeros((rows, LANES), f32)
    for c in range(model // LANES):
        part = tok[:, lanes(c)].astype(f32)
        squares = squares + part * part
    scale = lax.rsqrt(jnp.sum(squares, axis=1, keepdims=True) / model + epsilon)
    count = depth // LANES
    for c in range(count):
        index = at[0] * count + c
        part = tok[:, pl.ds(pl.multiple_of(index * LANES, LANES), LANES)]
        own[:, lanes(c)] = part
        norm[:, lanes(c)] = (part.astype(f32) * scale * gain_f[pl.ds(index, 1), :]).astype(bf16)
    for copy, held, base in ((copies[1], bk, q_cols), (copies[2], bv, q_cols + kv_cols)):
        copy.wait()
        out[:, base : base + kv_cols] = jnp.dot(
            norm[...], held[...], preferred_element_type=f32
        ).astype(out.dtype)
    for c in range(chunks):
        copies[3 + c].wait()
        for start, size in blocks_of(q_cols, 512):
            cols = slice(start, start + size)
            term = jnp.dot(
                norm[:, c * step : (c + 1) * step],
                bq[c * step : (c + 1) * step, cols],
                preferred_element_type=f32,
            )
            if c:
                term = acc[:, cols] + term
            if c < chunks - 1:
                acc[:, cols] = term
            else:
                out[:, cols] = term.astype(out.dtype)


def project(at, tokens, gain, wq, wk, wv):
    rows, model = tokens.shape
    depth, q_cols = wq.shape
    kv_cols = wk.shape[1]
    chunks = max(1, min(8, depth // 256))
    return pl.pallas_call(
        lambda *refs: project_kernel(chunks, *refs),
        in_specs=[SMEM] + [HBM] * 5,
        out_specs=[VMEM, VMEM],
        out_shape=[
            jax.ShapeDtypeStruct((rows, q_cols + 2 * kv_cols), bf16),
            jax.ShapeDtypeStruct((rows, depth), bf16),
        ],
        scratch_shapes=[
            pltpu.VMEM((rows, model), bf16),
            pltpu.VMEM((model // LANES, LANES), f32),
            pltpu.VMEM((rows, depth), bf16),
            pltpu.VMEM(wq.shape, bf16),
            pltpu.VMEM(wk.shape, bf16),
            pltpu.VMEM(wv.shape, bf16),
            pltpu.VMEM((rows, q_cols), f32),
            pltpu.VMEM((model // LANES, LANES), bf16),
            pltpu.SemaphoreType.DMA((4 + chunks,)),
        ],
        compiler_params=params(16),
        cost_estimate=cost(rows, wq, wk, wv),
        name="project",
    )(at, in_hbm(tokens), in_hbm(gain.reshape(model // LANES, LANES)), in_hbm(wq), in_hbm(wk), in_hbm(wv))


def attend_kernel(n, part, at, cos, sin, cache, source, *rest):
    parts, (out, held, queries, total, stats_f, sems) = rest[:n], rest[n:]
    beside(
        part.copies(at, source, held, sems),
        at,
        lambda: attention(at, cos, sin, cache, parts, out, queries, total, stats_f),
    )


def attention(at, cos, sin, cache, parts, out, queries, total, stats_f):
    rows, q_cols = queries.shape
    context, kv_cols = cache.shape[2:]
    kv_heads = kv_cols // HEAD_WIDTH
    heads = q_cols // HEAD_WIDTH
    group = heads // kv_heads
    tile = 2 * DRAFT_TOKENS
    requests = rows // DRAFT_TOKENS

    def length(r):
        return at[4 + r]

    def slot(r):
        return at[4 + requests + r]

    last = at[1]
    base = at[0] * context

    def column(c):
        return sum(p[:, lanes(c)].astype(f32) for p in parts)

    def rotated(x):
        return x * cos[...] + pltpu.roll(x, HEAD_WIDTH // 2, 1) * sin[...]

    for h in range(heads):
        queries[:, lanes(h)] = (rotated(column(h)) * HEAD_WIDTH ** (-0.5)).astype(bf16).astype(f32)
    new_keys = [rotated(column(heads + k)).astype(bf16) for k in range(kv_heads)]
    new_values = [column(heads + kv_heads + k).astype(bf16) for k in range(kv_heads)]

    high = group * tile
    row = lax.broadcasted_iota(jnp.int32, (high, 1), 0) % tile
    first = row < DRAFT_TOKENS
    position = lax.broadcasted_iota(jnp.int32, (high, context), 1) + base
    draft_col = lax.broadcasted_iota(jnp.int32, (high, rows), 1)
    lane = lax.broadcasted_iota(jnp.int32, (tile, LANES), 1)
    nt = (((1,), (1,)), ((), ()))
    for i in range(rows // tile):
        request = 2 * i
        limit = jnp.where(first, length(request), length(request + 1))
        live = position < limit
        own_at = tile * i + jnp.where(first, 0, DRAFT_TOKENS)
        seen = (draft_col >= own_at) & (draft_col <= tile * i + row) & (last > 0)
        stats = jnp.zeros((tile, LANES), f32)
        for k in range(kv_heads):
            q = jnp.concatenate(
                [queries[tile * i : tile * (i + 1), lanes(k * group + g)] for g in range(group)], axis=0
            ).astype(bf16)
            scores = [
                lax.dot_general(q, cache[0, slot(request + s), :, lanes(k)], nt, preferred_element_type=f32)
                for s in range(2)
            ]
            score = jnp.where(live, jnp.where(first, scores[0], scores[1]), neg_large)
            draft = lax.dot_general(q, new_keys[k], nt, preferred_element_type=f32)
            draft = jnp.where(seen, draft, neg_large)
            top = jnp.maximum(
                jnp.max(score, axis=1, keepdims=True), jnp.max(draft, axis=1, keepdims=True)
            )
            weight = jnp.where(live, jnp.exp(score - top), 0.0)
            draft_weight = jnp.where(seen, jnp.exp(draft - top), 0.0)
            mass = jnp.sum(weight, axis=1, keepdims=True) + jnp.sum(draft_weight, axis=1, keepdims=True)
            weight = weight.astype(bf16)
            sums = [
                jnp.dot(weight, cache[1, slot(request + s), :, lanes(k)], preferred_element_type=f32)
                for s in range(2)
            ]
            value = jnp.where(first, sums[0], sums[1]) + jnp.dot(
                draft_weight.astype(bf16), new_values[k], preferred_element_type=f32
            )
            some = mass > 0.0
            safe = jnp.where(some, mass, 1.0)
            value = value / safe
            lse = jnp.where(some, top + jnp.log(safe), neg_large)
            for g in range(group):
                at_rows = slice(tile * g, tile * (g + 1))
                total[tile * i : tile * (i + 1), lanes(k * group + g)] = value[at_rows]
                stats = jnp.where(lane == k * group + g, lse[at_rows], stats)
        stats_f[tile * i : tile * (i + 1), :] = stats
    out[:, :q_cols] = total[...].astype(bf16)
    for p, term in enumerate(thirds(stats_f[...])):
        out[:, q_cols + p * LANES : q_cols + (p + 1) * LANES] = term


def attend(at, cos, sin, cache, parts, part):
    rows, width = parts[0].shape
    q_cols = width - 2 * cache.shape[3]
    return pl.pallas_call(
        lambda *refs: attend_kernel(len(parts), part, *refs),
        in_specs=[SMEM] + [VMEM] * 3 + [HBM] + [VMEM] * len(parts),
        out_specs=[VMEM, VMEM],
        out_shape=[jax.ShapeDtypeStruct((rows, q_cols + 3 * LANES), bf16), part.out],
        scratch_shapes=[
            pltpu.VMEM((rows, q_cols), f32),
            pltpu.VMEM((rows, q_cols), f32),
            pltpu.VMEM((rows, LANES), f32),
            pltpu.SemaphoreType.DMA((2 * PIECES,)),
        ],
        compiler_params=params(6),
        cost_estimate=cost(rows, cache),
        name="attend",
    )(at, cos, sin, cache, in_hbm(part.array), *parts)


def joined(ref, start):
    return sum(ref[:, start + p * LANES : start + (p + 1) * LANES].astype(f32) for p in range(3))


def product(x, w, out, base, width):
    for start, size in blocks_of(width, 512):
        out[:, start : start + size] = jnp.dot(
            x[...], w[:, base + start : base + start + size], preferred_element_type=f32
        ).astype(out.dtype)


def output_first_kernel(n, part, at, w, source, *rest):
    values, (out, attended, held, sems) = rest[:n], rest[n:]
    beside(part.copies(at, source, held, sems), at, lambda: combine(w, values, out, attended))


def combine(w, values, out, attended):
    heads = attended.shape[1] // HEAD_WIDTH
    stats = [joined(v, attended.shape[1]) for v in values]
    top = stats[0]
    for s in stats[1:]:
        top = jnp.maximum(top, s)
    shares = [jnp.exp(s - top) for s in stats]
    whole = sum(shares)
    shares = [s / whole for s in shares]
    for h in range(heads):
        attended[:, lanes(h)] = sum(
            v[:, lanes(h)].astype(f32) * s[:, h : h + 1] for v, s in zip(values, shares)
        ).astype(bf16)
    product(attended, w, out, 0, out.shape[1])


def output_first(at, values, w, part):
    rows, half = values[0].shape[0], w.shape[1] // 2
    return pl.pallas_call(
        lambda *refs: output_first_kernel(len(values), part, *refs),
        in_specs=[SMEM, VMEM, HBM] + [VMEM] * len(values),
        out_specs=[VMEM] * 3,
        out_shape=[
            jax.ShapeDtypeStruct((rows, half), bf16),
            jax.ShapeDtypeStruct((rows, w.shape[0]), bf16),
            part.out,
        ],
        scratch_shapes=[pltpu.SemaphoreType.DMA((2 * PIECES,))],
        compiler_params=params(4),
        cost_estimate=cost(rows, w),
        name="output_first",
    )(at, w, in_hbm(part.array), *values)


def output_second(attended, w):
    rows, half = attended.shape[0], w.shape[1] // 2
    return pl.pallas_call(
        lambda x, w, out: product(x, w, out, half, half),
        in_specs=[VMEM] * 2,
        out_specs=VMEM,
        out_shape=jax.ShapeDtypeStruct((rows, half), bf16),
        compiler_params=params(4),
        cost_estimate=cost(rows, w),
        name="output_second",
    )(attended, w)


def half_of(side, x, wg, wu, out, before=None):
    half = wg[0].shape[1] // 2
    for base, pieces in ((0, wg), (half, wu)):
        for start, size in blocks_of(half, 512):
            cols = pl.ds(pl.multiple_of(side * half + start, LANES), size)
            to = slice(base + start, base + start + size)
            term = None if before is None else before[:, to]
            row = 0
            for w in pieces:
                more = jnp.dot(x[:, row : row + w.shape[0]], w[:, cols], preferred_element_type=f32)
                term = more if term is None else term + more
                row += w.shape[0]
            out[:, to] = term.astype(out.dtype)


def residual(which, own, gain, parts, resid, x, gain_f):
    gain_f[...] = gain[...].astype(f32)
    count = resid.shape[1] // LANES
    square = jnp.zeros((own.shape[0], LANES), f32)
    for c in range(count):
        at = which * count + c
        value = own[:, lanes(at)].astype(f32) + sum(p[:, lanes(c)].astype(f32) for p in parts)
        value = value.astype(bf16).astype(f32)
        resid[:, lanes(c)] = value
        square = square + value * value
        x[:, lanes(c)] = (value * gain_f[at : at + 1, :]).astype(bf16)
    return square


def expand_first_kernel(n, part, at, own, gain, wg, wu, source, *rest):
    parts, (send, keep, resid, squares, held, x, gain_f, sems) = rest[:n], rest[n:]

    def compute():
        squares[...] = residual(0, own, gain, parts, resid, x, gain_f)
        half_of(1 - at[2], x, [wg], [wu], send)
        half_of(at[2], x, [wg], [wu], keep)

    beside(part.copies(at, source, held, sems), at, compute)


def expand_first(at, own, gain, parts, wg, wu, part):
    rows, depth = own.shape
    width = wg.shape[1]
    return pl.pallas_call(
        lambda *refs: expand_first_kernel(len(parts), part, *refs),
        in_specs=[SMEM] + [VMEM] * 4 + [HBM] + [VMEM] * len(parts),
        out_specs=[VMEM] * 5,
        out_shape=[
            jax.ShapeDtypeStruct((rows, width), f32),
            jax.ShapeDtypeStruct((rows, width), f32),
            jax.ShapeDtypeStruct((rows, depth // 2), f32),
            jax.ShapeDtypeStruct((rows, LANES), f32),
            part.out,
        ],
        scratch_shapes=[
            pltpu.VMEM((rows, depth // 2), bf16),
            pltpu.VMEM((depth // LANES, LANES), f32),
            pltpu.SemaphoreType.DMA((2 * PIECES,)),
        ],
        compiler_params=params(4),
        cost_estimate=cost(rows, wg, wu),
        name="expand_first",
    )(at, own, gain, wg, wu, in_hbm(part.array), *parts)


def expand_send_kernel(n, g, at, own, gain, before, squares, *rest):
    wg, wu, parts, (out, resid, x, gain_f) = rest[:g], rest[g : g + 1], rest[g + 1 : g + 1 + n], rest[g + 1 + n :]
    square = squares[...] + residual(1, own, gain, parts, resid, x, gain_f)
    square = jnp.broadcast_to(jnp.sum(square, axis=1, keepdims=True), square.shape)
    width = wu[0].shape[1]
    for p, term in enumerate(thirds(square)):
        out[:, width + p * LANES : width + (p + 1) * LANES] = term
    half_of(1 - at[2], x, wg, wu, out, before)


def expand_send(at, own, gain, parts, wg, wu, before, squares):
    rows, depth = own.shape
    return pl.pallas_call(
        lambda *refs: expand_send_kernel(len(parts), len(wg), *refs),
        in_specs=[SMEM] + [VMEM] * (5 + len(wg) + len(parts)),
        out_specs=[VMEM] * 3,
        out_shape=[
            jax.ShapeDtypeStruct((rows, wu.shape[1] + 3 * LANES), bf16),
            jax.ShapeDtypeStruct((rows, depth // 2), f32),
            jax.ShapeDtypeStruct((rows, depth // 2), bf16),
        ],
        scratch_shapes=[pltpu.VMEM((depth // LANES, LANES), f32)],
        compiler_params=params(4),
        cost_estimate=cost(rows, wu),
        name="expand_send",
    )(at, own, gain, before, squares, *wg, wu, *parts)


def expand_keep(at, x, wg, wu, before):
    rows = x.shape[0]
    return pl.pallas_call(
        lambda at, x, before, *refs: half_of(at[2], x, refs[:-2], refs[-2:-1], refs[-1], before),
        in_specs=[SMEM] + [VMEM] * (3 + len(wg)),
        out_specs=VMEM,
        out_shape=jax.ShapeDtypeStruct((rows, wu.shape[1]), bf16),
        compiler_params=params(4),
        cost_estimate=cost(rows, wu),
        name="expand_keep",
    )(at, x, before, *wg, wu)


def pair_kernel(keep, received, stats, out):
    width = out.shape[1] - 3 * LANES
    for start, size in blocks_of(width, 512):
        cols = slice(start, start + size)
        out[:, cols] = (keep[:, cols].astype(f32) + received[:, cols].astype(f32)).astype(bf16)
    for p, term in enumerate(thirds(joined(stats, width) + joined(received, width))):
        out[:, width + p * LANES : width + (p + 1) * LANES] = term


def pair(keep, received, stats):
    return pl.pallas_call(
        pair_kernel,
        in_specs=[VMEM] * 3,
        out_specs=VMEM,
        out_shape=jax.ShapeDtypeStruct(received.shape, bf16),
        compiler_params=params(4),
        name="pair",
    )(keep, received, stats)


def gated_kernel(model, one, two, out):
    half = out.shape[1]
    scale = lax.rsqrt((joined(one, 2 * half) + joined(two, 2 * half)) / model + epsilon)
    for c in range(half // LANES):
        gate, up = (
            scale * (one[:, lanes(at)].astype(f32) + two[:, lanes(at)].astype(f32))
            for at in (c, half // LANES + c)
        )
        out[:, lanes(c)] = (gate / (1.0 + jnp.exp(-gate)) * up).astype(bf16)


def gated(model, one, two, after):
    rows, width = one.shape
    return pl.pallas_call(
        lambda _, *refs: gated_kernel(model, *refs),
        in_specs=[ANY] + [VMEM] * 2,
        out_specs=VMEM,
        out_shape=jax.ShapeDtypeStruct((rows, (width - 3 * LANES) // 2), bf16),
        compiler_params=params(4),
        name="gated",
    )(after, one, two)


def contract_kernel(hidden, w, out):
    for start, size in blocks_of(w.shape[1], 512):
        cols = slice(start, start + size)
        out[:, cols] = jnp.dot(hidden[...], w[:, cols], preferred_element_type=f32)


def contract(hidden, w):
    rows = hidden.shape[0]
    return pl.pallas_call(
        contract_kernel,
        in_specs=[VMEM] * 2,
        out_specs=VMEM,
        out_shape=jax.ShapeDtypeStruct((rows, w.shape[1]), f32),
        compiler_params=params(4),
        cost_estimate=cost(rows, w),
        name="contract",
    )(hidden, w)


def contract_last_kernel(n, at, hidden, w, before, resid_0, resid_1, own, *rest):
    sends, acc = rest[:-1], rest[-1]
    share = own.shape[0]
    for start, size in blocks_of(w.shape[1], 512):
        cols = slice(start, start + size)
        acc[:, cols] = before[:, cols] + jnp.dot(hidden[...], w[:, cols], preferred_element_type=f32)

    def block(ref, index):
        if share % 8 == 0:
            return ref[pl.ds(pl.multiple_of(index * share, share), share), :]
        chosen = ref[:share, :]
        for b in range(1, n):
            chosen = jnp.where(index == b, ref[b * share : (b + 1) * share, :], chosen)
        return chosen

    half = resid_0.shape[1]
    mine = block(acc, at[3])
    own[:, :half] = mine[:, :half] + block(resid_0, at[3])
    own[:, half:] = mine[:, half:] + block(resid_1, at[3])
    for s in range(1, n):
        sends[s - 1][...] = block(acc, at[3] ^ s).astype(bf16)


def contract_last(n, at, hidden, w, before, *resid):
    rows, cols = before.shape
    share = rows // n
    return pl.pallas_call(
        lambda *refs: contract_last_kernel(n, *refs),
        in_specs=[SMEM] + [VMEM] * 5,
        out_specs=[VMEM] * n,
        out_shape=[jax.ShapeDtypeStruct((share, cols), f32)]
        + [jax.ShapeDtypeStruct((share, cols), bf16)] * (n - 1),
        scratch_shapes=[pltpu.VMEM((rows, cols), f32)],
        compiler_params=params(4),
        cost_estimate=cost(rows, w),
        name="contract_last",
    )(at, hidden, w, before, *resid)


def add_kernel(one, two, out):
    for start, size in blocks_of(out.shape[1], 512):
        cols = slice(start, start + size)
        out[:, cols] = (one[:, cols].astype(f32) + two[:, cols].astype(f32)).astype(bf16)


def add(one, two):
    return pl.pallas_call(
        add_kernel,
        in_specs=[VMEM] * 2,
        out_specs=VMEM,
        out_shape=jax.ShapeDtypeStruct(one.shape, bf16),
        compiler_params=params(4),
        name="add",
    )(one, two)


def swap(x, axis, bit):
    n = lax.axis_size(axis)
    return lax.ppermute(x, axis, [(i, i ^ bit) for i in range(n)])


def bits_of(axis):
    n = lax.axis_size(axis)
    return [1 << b for b in range(n.bit_length() - 1)]


def gathered(x, axis, token):
    parts = [x]
    for bit in reversed(bits_of(axis)):
        parts = parts + [swap(p, axis, bit) for p in parts]
        if bit > 1:
            parts = parts[:-1] + [hold(parts[-1], token)]
    return parts


def summed(x, axis, order):
    *bits, last = bits_of(axis)[::order]
    for bit in bits:
        x = add(x, swap(x, axis, bit))
    return x, swap(x, axis, last)


def per_device(tokens, attn_gain, ffn_gain, w_query, key_matrix, value_matrix, w_out, w_gate, w_up, w_down, kv_cache, lengths, slots):
    rows, model = tokens.shape
    wide_at, head_at = lax.axis_index("wide"), lax.axis_index("head")
    wide_size, head_size = lax.axis_size("wide"), lax.axis_size("head")
    places = jnp.stack([wide_at, (wide_at == wide_size - 1).astype(jnp.int32), wide_at & 1, head_at])
    at = places.astype(jnp.int32)

    half = HEAD_WIDTH // 2
    positions = (
        jnp.broadcast_to(lengths[:, None], (lengths.shape[0], DRAFT_TOKENS))
        + jnp.arange(DRAFT_TOKENS, dtype=jnp.int32)[None, :]
    ).reshape(rows).astype(f32)
    exponent = jnp.arange(half, dtype=f32) * (2.0 / HEAD_WIDTH)
    angles = positions[:, None] * (theta_base ** (-exponent))[None, :]
    cos, sin = jnp.cos(angles), jnp.sin(angles)
    cos = jnp.concatenate([cos, cos], axis=1)
    sin = jnp.concatenate([-sin, sin], axis=1)

    qkv, own = project(at, tokens, attn_gain, w_query, key_matrix, value_matrix)
    depth = own.shape[1]
    half = depth // 2
    gain = ffn_gain.reshape(depth // LANES, LANES)

    flat_cache = kv_cache.reshape((-1,) + kv_cache.shape[2:])
    meta = jnp.concatenate([at, lengths, slots])
    cache, gate_0, token = fetch(at, (qkv, meta, cos, sin), Part(flat_cache), Part(w_gate, 0, half))
    cache = cache.reshape(kv_cache.shape)
    value, w_out = attend(meta, cos, sin, cache, gathered(qkv, "wide", token), Part(w_out))

    quarter = half // 2
    up_0, gate_1, token = fetch(at, value, Part(w_up, 0, half), Part(w_gate, half, quarter))
    out_0, attended, gate_2 = output_first(
        at, gathered(value, "wide", token), w_out, Part(w_gate, half + quarter, quarter)
    )
    out_1 = output_second(attended, w_out)
    parts_0, parts_1 = summed(out_0, "head", 1), summed(out_1, "head", -1)
    send, keep, resid_0, squares, up_1 = expand_first(
        at, own, gain, parts_0, gate_0, up_0, Part(w_up, half, half)
    )
    gate_1 = (gate_1, gate_2)
    send, resid_1, x = expand_send(at, own, gain, parts_1, gate_1, up_1, send, squares)
    received = swap(send, "wide", 1)
    total = pair(expand_keep(at, x, gate_1, up_1, keep), received, send)
    down_own, down_other, token = fetch(at, total, Part(w_down, side=0), Part(w_down, side=1))
    for bit in bits_of("wide")[1:-1]:
        there = swap(total, "wide", bit)
        total = pair(total, there, total)
    hidden = gated(model, total, swap(total, "wide", bits_of("wide")[-1]), token)
    other = swap(hidden, "wide", 1)
    total, *sends = contract_last(
        head_size, at, other, down_other, contract(hidden, down_own), resid_0, resid_1
    )
    for s, send in enumerate(sends, 1):
        total = total + swap(send, "head", s).astype(f32)
    return total.astype(bf16)


def solution(mesh):
    in_specs = (
        P("grp", None),
        P(),
        P("wide"),
        P("wide", "head"),
        P("wide", "head"),
        P("wide", "head"),
        P("head", "wide"),
        P("wide", "head"),
        P("wide", "head"),
        P("head", "wide"),
        P(None, "grp", "wide", "head"),
        P("grp"),
        P("grp"),
    )
    out_specs = P(("grp", "head"), "wide")
    return jax.shard_map(
        per_device, mesh=mesh, in_specs=in_specs, out_specs=out_specs, check_vma=False
    )
```

```python
import math

import jax
import jax.numpy as jnp
from jax import lax
from jax.experimental import pallas as pl
from jax.experimental.pallas import tpu as pltpu
from jax.sharding import PartitionSpec as P

HEAD_WIDTH = 128
DRAFT_TOKENS = 4
LANES = 128
MIB = 1 << 20

epsilon = 1e-05
theta_base = 500000.0
neg_large = -1e30

f32 = jnp.float32
bf16 = jnp.bfloat16
ANY = pl.BlockSpec(memory_space=pl.ANY)
VMEM = pl.BlockSpec(memory_space=pltpu.VMEM)
SMEM = pl.BlockSpec(memory_space=pltpu.SMEM)
HBM = pl.BlockSpec(memory_space=pltpu.HBM)


def in_hbm(x):
    return pltpu.with_memory_space_constraint(x, pltpu.HBM)


def cost(rows, *weights):
    size = sum(w.size for w in weights)
    return pl.CostEstimate(flops=2 * rows * size, bytes_accessed=2 * size, transcendentals=0)


def params(mib):
    return pltpu.CompilerParams(vmem_limit_bytes=mib * MIB)


def blocks_of(width, most):
    step = max(b for b in range(LANES, most + 1, LANES) if width % b == 0)
    return [(at, step) for at in range(0, width, step)]


def thirds(x):
    high = x.astype(bf16)
    rest = x - high.astype(f32)
    middle = rest.astype(bf16)
    return high, middle, (rest - middle.astype(f32)).astype(bf16)


def lanes(at):
    return slice(at * LANES, (at + 1) * LANES)


PIECES = 8


class Part:
    def __init__(self, array, first=0, count=None, side=None):
        rows = array.shape[0]
        self.array, self.first, self.side = array, first, side
        self.count = rows // 2 if side is not None else rows if count is None else count
        self.shape = (self.count,) + array.shape[1:]
        self.out = pltpu.VMEM(self.shape, array.dtype)

    def copies(self, at, source, held, sems):
        step = max(1, self.count // PIECES)
        base = self.first
        if self.side is not None:
            base = pl.multiple_of((at[2] if self.side == 0 else 1 - at[2]) * self.count, LANES)
        return [
            pltpu.make_async_copy(
                source.at[pl.ds(base + p * step, step)], held.at[pl.ds(p * step, step)], sems.at[p]
            )
            for p in range(self.count // step)
        ]


def fetch_kernel(wanted, skip, at, *refs):
    n, refs = len(wanted), refs[skip:]
    sources, held, token, sems = refs[:n], refs[n : 2 * n], refs[2 * n], refs[2 * n + 1 :]
    copies = sum([w.copies(at, *refs) for w, *refs in zip(wanted, sources, held, sems)], [])
    for copy in copies:
        copy.start()
    token[...] = jnp.zeros_like(token)
    for copy in copies:
        copy.wait()


def fetch(at, after, *wanted):
    after = after if isinstance(after, (list, tuple)) else [after]
    size = sum(math.prod(w.shape) for w in wanted)
    return pl.pallas_call(
        lambda *refs: fetch_kernel(wanted, len(after), *refs),
        in_specs=[SMEM] + [ANY] * len(after) + [HBM] * len(wanted),
        out_specs=[VMEM] * (len(wanted) + 1),
        out_shape=[w.out for w in wanted] + [pltpu.VMEM((8, LANES), f32)],
        scratch_shapes=[pltpu.SemaphoreType.DMA((2 * PIECES,))] * len(wanted),
        compiler_params=params(2),
        cost_estimate=pl.CostEstimate(flops=0, bytes_accessed=4 * size, transcendentals=0),
        name="fetch",
    )(at, *after, *[in_hbm(w.array) for w in wanted])


def hold(x, token):
    return pl.pallas_call(
        lambda *_: None,
        in_specs=[VMEM, ANY],
        out_specs=VMEM,
        out_shape=jax.ShapeDtypeStruct(x.shape, x.dtype),
        input_output_aliases={0: 0},
        compiler_params=params(1),
        name="hold",
    )(x, token)


def project_kernel(chunks, at, tokens, gain, wq, wk, wv, out, own, tok, gain_f, norm, bq, bk, bv, acc, gain_b, sems):
    rows, model = tok.shape
    depth, q_cols = bq.shape
    kv_cols = bk.shape[1]
    step = depth // chunks
    gain_copy = pltpu.make_async_copy(gain, gain_b, sems.at[3 + chunks])
    gain_copy.start()
    copies = [
        pltpu.make_async_copy(tokens, tok, sems.at[0]),
        pltpu.make_async_copy(wk, bk, sems.at[1]),
        pltpu.make_async_copy(wv, bv, sems.at[2]),
    ] + [
        pltpu.make_async_copy(
            wq.at[pl.ds(c * step, step)], bq.at[pl.ds(c * step, step)], sems.at[3 + c]
        )
        for c in range(chunks)
    ]
    for copy in copies:
        copy.start()
    gain_copy.wait()
    gain_f[...] = gain_b[...].astype(f32)
    copies[0].wait()
    squares = jnp.zeros((rows, LANES), f32)
    for c in range(model // LANES):
        part = tok[:, lanes(c)].astype(f32)
        squares = squares + part * part
    scale = lax.rsqrt(jnp.sum(squares, axis=1, keepdims=True) / model + epsilon)
    count = depth // LANES
    for c in range(count):
        index = at[0] * count + c
        part = tok[:, pl.ds(pl.multiple_of(index * LANES, LANES), LANES)]
        own[:, lanes(c)] = part
        norm[:, lanes(c)] = (part.astype(f32) * scale * gain_f[pl.ds(index, 1), :]).astype(bf16)
    for copy, held, base in ((copies[1], bk, q_cols), (copies[2], bv, q_cols + kv_cols)):
        copy.wait()
        out[:, base : base + kv_cols] = jnp.dot(
            norm[...], held[...], preferred_element_type=f32
        ).astype(out.dtype)
    for c in range(chunks):
        copies[3 + c].wait()
        for start, size in blocks_of(q_cols, 512):
            cols = slice(start, start + size)
            term = jnp.dot(
                norm[:, c * step : (c + 1) * step],
                bq[c * step : (c + 1) * step, cols],
                preferred_element_type=f32,
            )
            if c:
                term = acc[:, cols] + term
            if c < chunks - 1:
                acc[:, cols] = term
            else:
                out[:, cols] = term.astype(out.dtype)


def project(at, tokens, gain, wq, wk, wv):
    rows, model = tokens.shape
    depth, q_cols = wq.shape
    kv_cols = wk.shape[1]
    chunks = max(1, min(8, depth // 256))
    return pl.pallas_call(
        lambda *refs: project_kernel(chunks, *refs),
        in_specs=[SMEM] + [HBM] * 5,
        out_specs=[VMEM, VMEM],
        out_shape=[
            jax.ShapeDtypeStruct((rows, q_cols + 2 * kv_cols), bf16),
            jax.ShapeDtypeStruct((rows, depth), bf16),
        ],
        scratch_shapes=[
            pltpu.VMEM((rows, model), bf16),
            pltpu.VMEM((model // LANES, LANES), f32),
            pltpu.VMEM((rows, depth), bf16),
            pltpu.VMEM(wq.shape, bf16),
            pltpu.VMEM(wk.shape, bf16),
            pltpu.VMEM(wv.shape, bf16),
            pltpu.VMEM((rows, q_cols), f32),
            pltpu.VMEM((model // LANES, LANES), bf16),
            pltpu.SemaphoreType.DMA((4 + chunks,)),
        ],
        compiler_params=params(16),
        cost_estimate=cost(rows, wq, wk, wv),
        name="project",
    )(at, in_hbm(tokens), in_hbm(gain.reshape(model // LANES, LANES)), in_hbm(wq), in_hbm(wk), in_hbm(wv))


def attend_kernel(n, at, cos, sin, cache, *rest):
    parts, (out, queries, total, stats_f) = rest[:n], rest[n:]
    rows, q_cols = queries.shape
    context, kv_cols = cache.shape[2:]
    kv_heads = kv_cols // HEAD_WIDTH
    heads = q_cols // HEAD_WIDTH
    group = heads // kv_heads
    tile = 2 * DRAFT_TOKENS
    requests = rows // DRAFT_TOKENS

    def length(r):
        return at[4 + r]

    def slot(r):
        return at[4 + requests + r]

    last = at[1]
    base = at[0] * context

    def column(c):
        return sum(p[:, lanes(c)].astype(f32) for p in parts)

    def rotated(x):
        return x * cos[...] + pltpu.roll(x, HEAD_WIDTH // 2, 1) * sin[...]

    for h in range(heads):
        queries[:, lanes(h)] = (rotated(column(h)) * HEAD_WIDTH ** (-0.5)).astype(bf16).astype(f32)
    new_keys = [rotated(column(heads + k)).astype(bf16) for k in range(kv_heads)]
    new_values = [column(heads + kv_heads + k).astype(bf16) for k in range(kv_heads)]

    high = group * tile
    row = lax.broadcasted_iota(jnp.int32, (high, 1), 0) % tile
    first = row < DRAFT_TOKENS
    position = lax.broadcasted_iota(jnp.int32, (high, context), 1) + base
    draft_col = lax.broadcasted_iota(jnp.int32, (high, rows), 1)
    lane = lax.broadcasted_iota(jnp.int32, (tile, LANES), 1)
    nt = (((1,), (1,)), ((), ()))
    for i in range(rows // tile):
        request = 2 * i
        limit = jnp.where(first, length(request), length(request + 1))
        live = position < limit
        own_at = tile * i + jnp.where(first, 0, DRAFT_TOKENS)
        seen = (draft_col >= own_at) & (draft_col <= tile * i + row) & (last > 0)
        stats = jnp.zeros((tile, LANES), f32)
        for k in range(kv_heads):
            q = jnp.concatenate(
                [queries[tile * i : tile * (i + 1), lanes(k * group + g)] for g in range(group)], axis=0
            ).astype(bf16)
            scores = [
                lax.dot_general(q, cache[0, slot(request + s), :, lanes(k)], nt, preferred_element_type=f32)
                for s in range(2)
            ]
            score = jnp.where(live, jnp.where(first, scores[0], scores[1]), neg_large)
            draft = lax.dot_general(q, new_keys[k], nt, preferred_element_type=f32)
            draft = jnp.where(seen, draft, neg_large)
            top = jnp.maximum(
                jnp.max(score, axis=1, keepdims=True), jnp.max(draft, axis=1, keepdims=True)
            )
            weight = jnp.where(live, jnp.exp(score - top), 0.0)
            draft_weight = jnp.where(seen, jnp.exp(draft - top), 0.0)
            mass = jnp.sum(weight, axis=1, keepdims=True) + jnp.sum(draft_weight, axis=1, keepdims=True)
            weight = weight.astype(bf16)
            sums = [
                jnp.dot(weight, cache[1, slot(request + s), :, lanes(k)], preferred_element_type=f32)
                for s in range(2)
            ]
            value = jnp.where(first, sums[0], sums[1]) + jnp.dot(
                draft_weight.astype(bf16), new_values[k], preferred_element_type=f32
            )
            some = mass > 0.0
            safe = jnp.where(some, mass, 1.0)
            value = value / safe
            lse = jnp.where(some, top + jnp.log(safe), neg_large)
            for g in range(group):
                at_rows = slice(tile * g, tile * (g + 1))
                total[tile * i : tile * (i + 1), lanes(k * group + g)] = value[at_rows]
                stats = jnp.where(lane == k * group + g, lse[at_rows], stats)
        stats_f[tile * i : tile * (i + 1), :] = stats
    out[:, :q_cols] = total[...].astype(bf16)
    for p, term in enumerate(thirds(stats_f[...])):
        out[:, q_cols + p * LANES : q_cols + (p + 1) * LANES] = term


def attend(at, cos, sin, cache, parts):
    rows, width = parts[0].shape
    q_cols = width - 2 * cache.shape[3]
    return pl.pallas_call(
        lambda *refs: attend_kernel(len(parts), *refs),
        in_specs=[SMEM] + [VMEM] * (3 + len(parts)),
        out_specs=VMEM,
        out_shape=jax.ShapeDtypeStruct((rows, q_cols + 3 * LANES), bf16),
        scratch_shapes=[
            pltpu.VMEM((rows, q_cols), f32),
            pltpu.VMEM((rows, q_cols), f32),
            pltpu.VMEM((rows, LANES), f32),
        ],
        compiler_params=params(6),
        cost_estimate=cost(rows, cache),
        name="attend",
    )(at, cos, sin, cache, *parts)


def joined(ref, start):
    return sum(ref[:, start + p * LANES : start + (p + 1) * LANES].astype(f32) for p in range(3))


def product(x, w, out, base, width):
    for start, size in blocks_of(width, 512):
        out[:, start : start + size] = jnp.dot(
            x[...], w[:, base + start : base + start + size], preferred_element_type=f32
        ).astype(out.dtype)


def output_first_kernel(n, w, *rest):
    values, (out, attended) = rest[:n], rest[n:]
    heads = attended.shape[1] // HEAD_WIDTH
    stats = [joined(v, attended.shape[1]) for v in values]
    top = stats[0]
    for s in stats[1:]:
        top = jnp.maximum(top, s)
    shares = [jnp.exp(s - top) for s in stats]
    whole = sum(shares)
    shares = [s / whole for s in shares]
    for h in range(heads):
        attended[:, lanes(h)] = sum(
            v[:, lanes(h)].astype(f32) * s[:, h : h + 1] for v, s in zip(values, shares)
        ).astype(bf16)
    product(attended, w, out, 0, out.shape[1])


def output_first(values, w):
    rows, half = values[0].shape[0], w.shape[1] // 2
    return pl.pallas_call(
        lambda *refs: output_first_kernel(len(values), *refs),
        in_specs=[VMEM] * (1 + len(values)),
        out_specs=[VMEM] * 2,
        out_shape=[
            jax.ShapeDtypeStruct((rows, half), bf16),
            jax.ShapeDtypeStruct((rows, w.shape[0]), bf16),
        ],
        compiler_params=params(4),
        cost_estimate=cost(rows, w),
        name="output_first",
    )(w, *values)


def output_second(attended, w):
    rows, half = attended.shape[0], w.shape[1] // 2
    return pl.pallas_call(
        lambda x, w, out: product(x, w, out, half, half),
        in_specs=[VMEM] * 2,
        out_specs=VMEM,
        out_shape=jax.ShapeDtypeStruct((rows, half), bf16),
        compiler_params=params(4),
        cost_estimate=cost(rows, w),
        name="output_second",
    )(attended, w)


SLOTS = 3
WIDE = 896


def half_of(sides, x, row, wg, wu, held, sems):
    count, half = x.shape[1], wg.shape[1] // 2
    jobs = []
    for side, out, before in sides:
        for base, w in ((0, wg), (half, wu)):
            for start, size in blocks_of(half, WIDE):
                slot = len(jobs) % SLOTS
                cols = pl.ds(pl.multiple_of(side * half + start, LANES), size)
                copy = pltpu.make_async_copy(
                    w.at[pl.ds(row, count), cols], held.at[slot, :, pl.ds(0, size)], sems.at[slot]
                )
                jobs.append((copy, slot, size, base + start, out, before))
    for copy, *_ in jobs[: SLOTS - 1]:
        copy.start()
    for n, (copy, slot, size, to, out, before) in enumerate(jobs):
        copy.wait()
        if n + SLOTS - 1 < len(jobs):
            jobs[n + SLOTS - 1][0].start()
        term = jnp.dot(x[...], held[slot, :, :size], preferred_element_type=f32)
        cols = slice(to, to + size)
        if before is not None:
            term = before[:, cols] + term
        out[:, cols] = term.astype(out.dtype)


def block_scratch(count, half):
    width = max(size for _, size in blocks_of(half, WIDE))
    return [pltpu.VMEM((SLOTS, count, width), bf16), pltpu.SemaphoreType.DMA((SLOTS,))]


def residual(which, own, gain, parts, resid, x, gain_f):
    gain_f[...] = gain[...].astype(f32)
    count = resid.shape[1] // LANES
    square = jnp.zeros((own.shape[0], LANES), f32)
    for c in range(count):
        at = which * count + c
        value = own[:, lanes(at)].astype(f32) + sum(p[:, lanes(c)].astype(f32) for p in parts)
        value = value.astype(bf16).astype(f32)
        resid[:, lanes(c)] = value
        square = square + value * value
        x[:, lanes(c)] = (value * gain_f[at : at + 1, :]).astype(bf16)
    return square


def expand_first_kernel(n, at, own, gain, wg, wu, *rest):
    parts, (send, keep, resid, squares, x, gain_f, held, sems) = rest[:n], rest[n:]
    squares[...] = residual(0, own, gain, parts, resid, x, gain_f)
    half_of([(1 - at[2], send, None), (at[2], keep, None)], x, 0, wg, wu, held, sems)


def expand_first(at, own, gain, parts, wg, wu):
    rows, depth = own.shape
    width = wg.shape[1]
    return pl.pallas_call(
        lambda *refs: expand_first_kernel(len(parts), *refs),
        in_specs=[SMEM] + [VMEM] * 2 + [ANY] * 2 + [VMEM] * len(parts),
        out_specs=[VMEM] * 4,
        out_shape=[
            jax.ShapeDtypeStruct((rows, width), f32),
            jax.ShapeDtypeStruct((rows, width), f32),
            jax.ShapeDtypeStruct((rows, depth // 2), f32),
            jax.ShapeDtypeStruct((rows, LANES), f32),
        ],
        scratch_shapes=[
            pltpu.VMEM((rows, depth // 2), bf16),
            pltpu.VMEM((depth // LANES, LANES), f32),
        ]
        + block_scratch(depth // 2, width // 2),
        compiler_params=params(9),
        cost_estimate=cost(rows, wg, wu),
        name="expand_first",
    )(at, own, gain, wg, wu, *parts)


def expand_send_kernel(n, at, own, gain, before, squares, wg, wu, *rest):
    parts, (out, resid, x, gain_f, held, sems) = rest[:n], rest[n:]
    square = squares[...] + residual(1, own, gain, parts, resid, x, gain_f)
    square = jnp.broadcast_to(jnp.sum(square, axis=1, keepdims=True), square.shape)
    width = wu.shape[1]
    for p, term in enumerate(thirds(square)):
        out[:, width + p * LANES : width + (p + 1) * LANES] = term
    half_of([(1 - at[2], out, before)], x, x.shape[1], wg, wu, held, sems)


def expand_send(at, own, gain, parts, wg, wu, before, squares):
    rows, depth = own.shape
    return pl.pallas_call(
        lambda *refs: expand_send_kernel(len(parts), *refs),
        in_specs=[SMEM] + [VMEM] * 4 + [ANY] * 2 + [VMEM] * len(parts),
        out_specs=[VMEM] * 3,
        out_shape=[
            jax.ShapeDtypeStruct((rows, wu.shape[1] + 3 * LANES), bf16),
            jax.ShapeDtypeStruct((rows, depth // 2), f32),
            jax.ShapeDtypeStruct((rows, depth // 2), bf16),
        ],
        scratch_shapes=[pltpu.VMEM((depth // LANES, LANES), f32)]
        + block_scratch(depth // 2, wu.shape[1] // 2),
        compiler_params=params(9),
        cost_estimate=cost(rows, wu),
        name="expand_send",
    )(at, own, gain, before, squares, wg, wu, *parts)


def expand_keep_kernel(at, x, before, wg, wu, out, held, sems):
    half_of([(at[2], out, before)], x, x.shape[1], wg, wu, held, sems)


def expand_keep(at, x, wg, wu, before):
    rows = x.shape[0]
    return pl.pallas_call(
        expand_keep_kernel,
        in_specs=[SMEM] + [VMEM] * 2 + [ANY] * 2,
        out_specs=VMEM,
        out_shape=jax.ShapeDtypeStruct((rows, wu.shape[1]), bf16),
        scratch_shapes=block_scratch(x.shape[1], wu.shape[1] // 2),
        compiler_params=params(9),
        cost_estimate=cost(rows, wu),
        name="expand_keep",
    )(at, x, before, wg, wu)


def pair_kernel(keep, received, stats, out):
    width = out.shape[1] - 3 * LANES
    for start, size in blocks_of(width, 512):
        cols = slice(start, start + size)
        out[:, cols] = (keep[:, cols].astype(f32) + received[:, cols].astype(f32)).astype(bf16)
    for p, term in enumerate(thirds(joined(stats, width) + joined(received, width))):
        out[:, width + p * LANES : width + (p + 1) * LANES] = term


def pair(keep, received, stats):
    return pl.pallas_call(
        pair_kernel,
        in_specs=[VMEM] * 3,
        out_specs=VMEM,
        out_shape=jax.ShapeDtypeStruct(received.shape, bf16),
        compiler_params=params(4),
        name="pair",
    )(keep, received, stats)


def gated_kernel(model, one, two, out):
    half = out.shape[1]
    scale = lax.rsqrt((joined(one, 2 * half) + joined(two, 2 * half)) / model + epsilon)
    for c in range(half // LANES):
        gate, up = (
            scale * (one[:, lanes(at)].astype(f32) + two[:, lanes(at)].astype(f32))
            for at in (c, half // LANES + c)
        )
        out[:, lanes(c)] = (gate / (1.0 + jnp.exp(-gate)) * up).astype(bf16)


def gated(model, one, two, after):
    rows, width = one.shape
    return pl.pallas_call(
        lambda _, *refs: gated_kernel(model, *refs),
        in_specs=[ANY] + [VMEM] * 2,
        out_specs=VMEM,
        out_shape=jax.ShapeDtypeStruct((rows, (width - 3 * LANES) // 2), bf16),
        compiler_params=params(4),
        name="gated",
    )(after, one, two)


def contract_kernel(hidden, w, out):
    for start, size in blocks_of(w.shape[1], 512):
        cols = slice(start, start + size)
        out[:, cols] = jnp.dot(hidden[...], w[:, cols], preferred_element_type=f32)


def contract(hidden, w):
    rows = hidden.shape[0]
    return pl.pallas_call(
        contract_kernel,
        in_specs=[VMEM] * 2,
        out_specs=VMEM,
        out_shape=jax.ShapeDtypeStruct((rows, w.shape[1]), f32),
        compiler_params=params(4),
        cost_estimate=cost(rows, w),
        name="contract",
    )(hidden, w)


def contract_last_kernel(n, at, hidden, w, before, resid_0, resid_1, own, *rest):
    sends, acc = rest[:-1], rest[-1]
    share = own.shape[0]
    for start, size in blocks_of(w.shape[1], 512):
        cols = slice(start, start + size)
        acc[:, cols] = before[:, cols] + jnp.dot(hidden[...], w[:, cols], preferred_element_type=f32)

    def block(ref, index):
        if share % 8 == 0:
            return ref[pl.ds(pl.multiple_of(index * share, share), share), :]
        chosen = ref[:share, :]
        for b in range(1, n):
            chosen = jnp.where(index == b, ref[b * share : (b + 1) * share, :], chosen)
        return chosen

    half = resid_0.shape[1]
    mine = block(acc, at[3])
    own[:, :half] = mine[:, :half] + block(resid_0, at[3])
    own[:, half:] = mine[:, half:] + block(resid_1, at[3])
    for s in range(1, n):
        sends[s - 1][...] = block(acc, at[3] ^ s).astype(bf16)


def contract_last(n, at, hidden, w, before, *resid):
    rows, cols = before.shape
    share = rows // n
    return pl.pallas_call(
        lambda *refs: contract_last_kernel(n, *refs),
        in_specs=[SMEM] + [VMEM] * 5,
        out_specs=[VMEM] * n,
        out_shape=[jax.ShapeDtypeStruct((share, cols), f32)]
        + [jax.ShapeDtypeStruct((share, cols), bf16)] * (n - 1),
        scratch_shapes=[pltpu.VMEM((rows, cols), f32)],
        compiler_params=params(4),
        cost_estimate=cost(rows, w),
        name="contract_last",
    )(at, hidden, w, before, *resid)


def add_kernel(one, two, out):
    for start, size in blocks_of(out.shape[1], 512):
        cols = slice(start, start + size)
        out[:, cols] = (one[:, cols].astype(f32) + two[:, cols].astype(f32)).astype(bf16)


def add(one, two):
    return pl.pallas_call(
        add_kernel,
        in_specs=[VMEM] * 2,
        out_specs=VMEM,
        out_shape=jax.ShapeDtypeStruct(one.shape, bf16),
        compiler_params=params(4),
        name="add",
    )(one, two)


def swap(x, axis, bit):
    n = lax.axis_size(axis)
    return lax.ppermute(x, axis, [(i, i ^ bit) for i in range(n)])


def bits_of(axis):
    n = lax.axis_size(axis)
    return [1 << b for b in range(n.bit_length() - 1)]


def gathered(x, axis, token=None):
    parts = [x]
    for bit in reversed(bits_of(axis)):
        parts = parts + [swap(p, axis, bit) for p in parts]
        if bit > 1 and token is not None:
            parts = parts[:-1] + [hold(parts[-1], token)]
    return parts


def summed(x, axis, order):
    *bits, last = bits_of(axis)[::order]
    for bit in bits:
        x = add(x, swap(x, axis, bit))
    return x, swap(x, axis, last)


def per_device(tokens, attn_gain, ffn_gain, w_query, key_matrix, value_matrix, w_out, w_gate, w_up, w_down, kv_cache, lengths, slots):
    rows, model = tokens.shape
    wide_at, head_at = lax.axis_index("wide"), lax.axis_index("head")
    wide_size, head_size = lax.axis_size("wide"), lax.axis_size("head")
    places = jnp.stack([wide_at, (wide_at == wide_size - 1).astype(jnp.int32), wide_at & 1, head_at])
    at = places.astype(jnp.int32)

    half = HEAD_WIDTH // 2
    positions = (
        jnp.broadcast_to(lengths[:, None], (lengths.shape[0], DRAFT_TOKENS))
        + jnp.arange(DRAFT_TOKENS, dtype=jnp.int32)[None, :]
    ).reshape(rows).astype(f32)
    exponent = jnp.arange(half, dtype=f32) * (2.0 / HEAD_WIDTH)
    angles = positions[:, None] * (theta_base ** (-exponent))[None, :]
    cos, sin = jnp.cos(angles), jnp.sin(angles)
    cos = jnp.concatenate([cos, cos], axis=1)
    sin = jnp.concatenate([-sin, sin], axis=1)

    qkv, own = project(at, tokens, attn_gain, w_query, key_matrix, value_matrix)
    depth = own.shape[1]
    half = depth // 2
    gain = ffn_gain.reshape(depth // LANES, LANES)

    flat_cache = kv_cache.reshape((-1,) + kv_cache.shape[2:])
    meta = jnp.concatenate([at, lengths, slots])
    cache, w_out, token = fetch(at, (qkv, meta, cos, sin), Part(flat_cache), Part(w_out))
    cache = cache.reshape(kv_cache.shape)
    value = attend(meta, cos, sin, cache, gathered(qkv, "wide", token))
    out_0, attended = output_first(gathered(value, "wide"), w_out)
    out_1 = output_second(attended, w_out)
    parts_0, parts_1 = summed(out_0, "head", 1), summed(out_1, "head", -1)
    send, keep, resid_0, squares = expand_first(at, own, gain, parts_0, w_gate, w_up)
    send, resid_1, x = expand_send(at, own, gain, parts_1, w_gate, w_up, send, squares)
    received = swap(send, "wide", 1)
    total = pair(expand_keep(at, x, w_gate, w_up, keep), received, send)
    down_own, down_other, token = fetch(at, total, Part(w_down, side=0), Part(w_down, side=1))
    for bit in bits_of("wide")[1:-1]:
        there = swap(total, "wide", bit)
        total = pair(total, there, total)
    hidden = gated(model, total, swap(total, "wide", bits_of("wide")[-1]), token)
    other = swap(hidden, "wide", 1)
    total, *sends = contract_last(
        head_size, at, other, down_other, contract(hidden, down_own), resid_0, resid_1
    )
    for s, send in enumerate(sends, 1):
        total = total + swap(send, "head", s).astype(f32)
    return total.astype(bf16)


def solution(mesh):
    in_specs = (
        P("grp", None),
        P(),
        P("wide"),
        P("wide", "head"),
        P("wide", "head"),
        P("wide", "head"),
        P("head", "wide"),
        P("wide", "head"),
        P("wide", "head"),
        P("head", "wide"),
        P(None, "grp", "wide", "head"),
        P("grp"),
        P("grp"),
    )
    out_specs = P(("grp", "head"), "wide")
    return jax.shard_map(
        per_device, mesh=mesh, in_specs=in_specs, out_specs=out_specs, check_vma=False
    )
```

```python
import math

import jax
import jax.numpy as jnp
from jax import lax
from jax.experimental import pallas as pl
from jax.experimental.pallas import tpu as pltpu
from jax.sharding import PartitionSpec as P

HEAD_WIDTH = 128
DRAFT_TOKENS = 4
LANES = 128
MIB = 1 << 20

epsilon = 1e-05
theta_base = 500000.0
neg_large = -1e30

f32 = jnp.float32
bf16 = jnp.bfloat16
ANY = pl.BlockSpec(memory_space=pl.ANY)
VMEM = pl.BlockSpec(memory_space=pltpu.VMEM)
SMEM = pl.BlockSpec(memory_space=pltpu.SMEM)
HBM = pl.BlockSpec(memory_space=pltpu.HBM)


def in_hbm(x):
    return pltpu.with_memory_space_constraint(x, pltpu.HBM)


def cost(rows, *weights):
    size = sum(w.size for w in weights)
    return pl.CostEstimate(flops=2 * rows * size, bytes_accessed=2 * size, transcendentals=0)


def params(mib):
    return pltpu.CompilerParams(vmem_limit_bytes=mib * MIB)


def blocks_of(width, most):
    step = max(b for b in range(LANES, most + 1, LANES) if width % b == 0)
    return [(at, step) for at in range(0, width, step)]


def thirds(x):
    high = x.astype(bf16)
    rest = x - high.astype(f32)
    middle = rest.astype(bf16)
    return high, middle, (rest - middle.astype(f32)).astype(bf16)


def lanes(at):
    return slice(at * LANES, (at + 1) * LANES)


PIECES = 8


class Part:
    def __init__(self, array, first=0, count=None, side=None):
        rows = array.shape[0]
        self.array, self.first, self.side = array, first, side
        self.count = rows // 2 if side is not None else rows if count is None else count
        self.shape = (self.count,) + array.shape[1:]
        self.out = pltpu.VMEM(self.shape, array.dtype)

    def copies(self, at, source, held, sems):
        step = max(1, self.count // PIECES)
        base = self.first
        if self.side is not None:
            base = pl.multiple_of((at[2] if self.side == 0 else 1 - at[2]) * self.count, LANES)
        return [
            pltpu.make_async_copy(
                source.at[pl.ds(base + p * step, step)], held.at[pl.ds(p * step, step)], sems.at[p]
            )
            for p in range(self.count // step)
        ]


def fetch_kernel(wanted, skip, at, *refs):
    n, refs = len(wanted), refs[skip:]
    sources, held, token, sems = refs[:n], refs[n : 2 * n], refs[2 * n], refs[2 * n + 1 :]
    copies = sum([w.copies(at, *refs) for w, *refs in zip(wanted, sources, held, sems)], [])
    for copy in copies:
        copy.start()
    token[...] = jnp.zeros_like(token)
    for copy in copies:
        copy.wait()


def fetch(at, after, *wanted):
    after = after if isinstance(after, (list, tuple)) else [after]
    size = sum(math.prod(w.shape) for w in wanted)
    return pl.pallas_call(
        lambda *refs: fetch_kernel(wanted, len(after), *refs),
        in_specs=[SMEM] + [ANY] * len(after) + [HBM] * len(wanted),
        out_specs=[VMEM] * (len(wanted) + 1),
        out_shape=[w.out for w in wanted] + [pltpu.VMEM((8, LANES), f32)],
        scratch_shapes=[pltpu.SemaphoreType.DMA((2 * PIECES,))] * len(wanted),
        compiler_params=params(2),
        cost_estimate=pl.CostEstimate(flops=0, bytes_accessed=4 * size, transcendentals=0),
        name="fetch",
    )(at, *after, *[in_hbm(w.array) for w in wanted])


def hold(x, token):
    return pl.pallas_call(
        lambda *_: None,
        in_specs=[VMEM, ANY],
        out_specs=VMEM,
        out_shape=jax.ShapeDtypeStruct(x.shape, x.dtype),
        input_output_aliases={0: 0},
        compiler_params=params(1),
        name="hold",
    )(x, token)


def project_kernel(chunks, at, tokens, gain, wq, wk, wv, out, own, tok, gain_f, norm, bq, bk, bv, acc, gain_b, sems):
    rows, model = tok.shape
    depth, q_cols = bq.shape
    kv_cols = bk.shape[1]
    step = depth // chunks
    gain_copy = pltpu.make_async_copy(gain, gain_b, sems.at[3 + chunks])
    gain_copy.start()
    copies = [
        pltpu.make_async_copy(tokens, tok, sems.at[0]),
        pltpu.make_async_copy(wk, bk, sems.at[1]),
        pltpu.make_async_copy(wv, bv, sems.at[2]),
    ] + [
        pltpu.make_async_copy(
            wq.at[pl.ds(c * step, step)], bq.at[pl.ds(c * step, step)], sems.at[3 + c]
        )
        for c in range(chunks)
    ]
    for copy in copies:
        copy.start()
    gain_copy.wait()
    gain_f[...] = gain_b[...].astype(f32)
    copies[0].wait()
    squares = jnp.zeros((rows, LANES), f32)
    for c in range(model // LANES):
        part = tok[:, lanes(c)].astype(f32)
        squares = squares + part * part
    scale = lax.rsqrt(jnp.sum(squares, axis=1, keepdims=True) / model + epsilon)
    count = depth // LANES
    for c in range(count):
        index = at[0] * count + c
        part = tok[:, pl.ds(pl.multiple_of(index * LANES, LANES), LANES)]
        own[:, lanes(c)] = part
        norm[:, lanes(c)] = (part.astype(f32) * scale * gain_f[pl.ds(index, 1), :]).astype(bf16)
    for copy, held, base in ((copies[1], bk, q_cols), (copies[2], bv, q_cols + kv_cols)):
        copy.wait()
        out[:, base : base + kv_cols] = jnp.dot(
            norm[...], held[...], preferred_element_type=f32
        ).astype(out.dtype)
    for c in range(chunks):
        copies[3 + c].wait()
        for start, size in blocks_of(q_cols, 512):
            cols = slice(start, start + size)
            term = jnp.dot(
                norm[:, c * step : (c + 1) * step],
                bq[c * step : (c + 1) * step, cols],
                preferred_element_type=f32,
            )
            if c:
                term = acc[:, cols] + term
            if c < chunks - 1:
                acc[:, cols] = term
            else:
                out[:, cols] = term.astype(out.dtype)


def project(at, tokens, gain, wq, wk, wv):
    rows, model = tokens.shape
    depth, q_cols = wq.shape
    kv_cols = wk.shape[1]
    chunks = max(1, min(8, depth // 256))
    return pl.pallas_call(
        lambda *refs: project_kernel(chunks, *refs),
        in_specs=[SMEM] + [HBM] * 5,
        out_specs=[VMEM, VMEM],
        out_shape=[
            jax.ShapeDtypeStruct((rows, q_cols + 2 * kv_cols), bf16),
            jax.ShapeDtypeStruct((rows, depth), bf16),
        ],
        scratch_shapes=[
            pltpu.VMEM((rows, model), bf16),
            pltpu.VMEM((model // LANES, LANES), f32),
            pltpu.VMEM((rows, depth), bf16),
            pltpu.VMEM(wq.shape, bf16),
            pltpu.VMEM(wk.shape, bf16),
            pltpu.VMEM(wv.shape, bf16),
            pltpu.VMEM((rows, q_cols), f32),
            pltpu.VMEM((model // LANES, LANES), bf16),
            pltpu.SemaphoreType.DMA((4 + chunks,)),
        ],
        compiler_params=params(16),
        cost_estimate=cost(rows, wq, wk, wv),
        name="project",
    )(at, in_hbm(tokens), in_hbm(gain.reshape(model // LANES, LANES)), in_hbm(wq), in_hbm(wk), in_hbm(wv))


def attend_kernel(n, at, cos, sin, cache, *rest):
    parts, (out, queries, total, stats_f) = rest[:n], rest[n:]
    rows, q_cols = queries.shape
    context, kv_cols = cache.shape[2:]
    kv_heads = kv_cols // HEAD_WIDTH
    heads = q_cols // HEAD_WIDTH
    group = heads // kv_heads
    tile = 2 * DRAFT_TOKENS
    requests = rows // DRAFT_TOKENS

    def length(r):
        return at[4 + r]

    def slot(r):
        return at[4 + requests + r]

    last = at[1]
    base = at[0] * context

    def column(c):
        return sum(p[:, lanes(c)].astype(f32) for p in parts)

    def rotated(x):
        return x * cos[...] + pltpu.roll(x, HEAD_WIDTH // 2, 1) * sin[...]

    for h in range(heads):
        queries[:, lanes(h)] = (rotated(column(h)) * HEAD_WIDTH ** (-0.5)).astype(bf16).astype(f32)
    new_keys = [rotated(column(heads + k)).astype(bf16) for k in range(kv_heads)]
    new_values = [column(heads + kv_heads + k).astype(bf16) for k in range(kv_heads)]

    high = group * tile
    row = lax.broadcasted_iota(jnp.int32, (high, 1), 0) % tile
    first = row < DRAFT_TOKENS
    position = lax.broadcasted_iota(jnp.int32, (high, context), 1) + base
    draft_col = lax.broadcasted_iota(jnp.int32, (high, rows), 1)
    lane = lax.broadcasted_iota(jnp.int32, (tile, LANES), 1)
    nt = (((1,), (1,)), ((), ()))
    for i in range(rows // tile):
        request = 2 * i
        limit = jnp.where(first, length(request), length(request + 1))
        live = position < limit
        own_at = tile * i + jnp.where(first, 0, DRAFT_TOKENS)
        seen = (draft_col >= own_at) & (draft_col <= tile * i + row) & (last > 0)
        stats = jnp.zeros((tile, LANES), f32)
        for k in range(kv_heads):
            q = jnp.concatenate(
                [queries[tile * i : tile * (i + 1), lanes(k * group + g)] for g in range(group)], axis=0
            ).astype(bf16)
            scores = [
                lax.dot_general(q, cache[0, slot(request + s), :, lanes(k)], nt, preferred_element_type=f32)
                for s in range(2)
            ]
            score = jnp.where(live, jnp.where(first, scores[0], scores[1]), neg_large)
            draft = lax.dot_general(q, new_keys[k], nt, preferred_element_type=f32)
            draft = jnp.where(seen, draft, neg_large)
            top = jnp.maximum(
                jnp.max(score, axis=1, keepdims=True), jnp.max(draft, axis=1, keepdims=True)
            )
            weight = jnp.where(live, jnp.exp(score - top), 0.0)
            draft_weight = jnp.where(seen, jnp.exp(draft - top), 0.0)
            mass = jnp.sum(weight, axis=1, keepdims=True) + jnp.sum(draft_weight, axis=1, keepdims=True)
            weight = weight.astype(bf16)
            sums = [
                jnp.dot(weight, cache[1, slot(request + s), :, lanes(k)], preferred_element_type=f32)
                for s in range(2)
            ]
            value = jnp.where(first, sums[0], sums[1]) + jnp.dot(
                draft_weight.astype(bf16), new_values[k], preferred_element_type=f32
            )
            some = mass > 0.0
            safe = jnp.where(some, mass, 1.0)
            value = value / safe
            lse = jnp.where(some, top + jnp.log(safe), neg_large)
            for g in range(group):
                at_rows = slice(tile * g, tile * (g + 1))
                total[tile * i : tile * (i + 1), lanes(k * group + g)] = value[at_rows]
                stats = jnp.where(lane == k * group + g, lse[at_rows], stats)
        stats_f[tile * i : tile * (i + 1), :] = stats
    out[:, :q_cols] = total[...].astype(bf16)
    for p, term in enumerate(thirds(stats_f[...])):
        out[:, q_cols + p * LANES : q_cols + (p + 1) * LANES] = term


def attend(at, cos, sin, cache, parts):
    rows, width = parts[0].shape
    q_cols = width - 2 * cache.shape[3]
    return pl.pallas_call(
        lambda *refs: attend_kernel(len(parts), *refs),
        in_specs=[SMEM] + [VMEM] * (3 + len(parts)),
        out_specs=VMEM,
        out_shape=jax.ShapeDtypeStruct((rows, q_cols + 3 * LANES), bf16),
        scratch_shapes=[
            pltpu.VMEM((rows, q_cols), f32),
            pltpu.VMEM((rows, q_cols), f32),
            pltpu.VMEM((rows, LANES), f32),
        ],
        compiler_params=params(6),
        cost_estimate=cost(rows, cache),
        name="attend",
    )(at, cos, sin, cache, *parts)


def joined(ref, start):
    return sum(ref[:, start + p * LANES : start + (p + 1) * LANES].astype(f32) for p in range(3))


def product(x, w, out, base, width):
    for start, size in blocks_of(width, 512):
        out[:, start : start + size] = jnp.dot(
            x[...], w[:, base + start : base + start + size], preferred_element_type=f32
        ).astype(out.dtype)


def output_first_kernel(n, w, *rest):
    values, (out, attended) = rest[:n], rest[n:]
    heads = attended.shape[1] // HEAD_WIDTH
    stats = [joined(v, attended.shape[1]) for v in values]
    top = stats[0]
    for s in stats[1:]:
        top = jnp.maximum(top, s)
    shares = [jnp.exp(s - top) for s in stats]
    whole = sum(shares)
    shares = [s / whole for s in shares]
    for h in range(heads):
        attended[:, lanes(h)] = sum(
            v[:, lanes(h)].astype(f32) * s[:, h : h + 1] for v, s in zip(values, shares)
        ).astype(bf16)
    product(attended, w, out, 0, out.shape[1])


def output_first(values, w):
    rows, half = values[0].shape[0], w.shape[1] // 2
    return pl.pallas_call(
        lambda *refs: output_first_kernel(len(values), *refs),
        in_specs=[VMEM] * (1 + len(values)),
        out_specs=[VMEM] * 2,
        out_shape=[
            jax.ShapeDtypeStruct((rows, half), bf16),
            jax.ShapeDtypeStruct((rows, w.shape[0]), bf16),
        ],
        compiler_params=params(4),
        cost_estimate=cost(rows, w),
        name="output_first",
    )(w, *values)


def output_second(attended, w):
    rows, half = attended.shape[0], w.shape[1] // 2
    return pl.pallas_call(
        lambda x, w, out: product(x, w, out, half, half),
        in_specs=[VMEM] * 2,
        out_specs=VMEM,
        out_shape=jax.ShapeDtypeStruct((rows, half), bf16),
        compiler_params=params(4),
        cost_estimate=cost(rows, w),
        name="output_second",
    )(attended, w)


WIDE = 896
SPLIT = 4


def half_of(at, sides, x, row, wg, wu, held, sems, prepare=None):
    count, half = x.shape[1], wg.shape[1] // 2
    step = count // SPLIT
    jobs = []
    for side, out, before in sides:
        for base, w in ((0, wg), (half, wu)):
            for start, size in blocks_of(half, WIDE):
                n = len(jobs)
                cols = pl.ds(pl.multiple_of(side * half + start, LANES), size)
                copies = [
                    pltpu.make_async_copy(
                        w.at[pl.ds(row + p * step, step), cols],
                        held.at[n, pl.ds(p * step, step)],
                        sems.at[n * SPLIT + p],
                    )
                    for p in range(SPLIT)
                ]
                jobs.append((copies, slice(base + start, base + start + size), out, before))
    for copies, *_ in jobs:
        for copy in copies:
            copy.start()
    if prepare is not None:
        pl.when(at[2] >= 0)(prepare)
    for n, (copies, cols, out, before) in enumerate(jobs):
        for copy in copies:
            copy.wait()
        term = jnp.dot(x[...], held[n], preferred_element_type=f32)
        if before is not None:
            term = before[:, cols] + term
        out[:, cols] = term.astype(out.dtype)


def block_scratch(sides, count, half):
    blocks = blocks_of(half, WIDE)
    number = sides * 2 * len(blocks)
    return [
        pltpu.VMEM((number, count, blocks[0][1]), bf16),
        pltpu.SemaphoreType.DMA((number * SPLIT,)),
    ]


def residual(which, own, gain, parts, resid, x, gain_f):
    gain_f[...] = gain[...].astype(f32)
    count = resid.shape[1] // LANES
    square = jnp.zeros((own.shape[0], LANES), f32)
    for c in range(count):
        at = which * count + c
        value = own[:, lanes(at)].astype(f32) + sum(p[:, lanes(c)].astype(f32) for p in parts)
        value = value.astype(bf16).astype(f32)
        resid[:, lanes(c)] = value
        square = square + value * value
        x[:, lanes(c)] = (value * gain_f[at : at + 1, :]).astype(bf16)
    return square


def expand_first_kernel(n, at, own, gain, wg, wu, *rest):
    parts, (send, keep, resid, squares, x, gain_f, held, sems) = rest[:n], rest[n:]

    def prepare():
        squares[...] = residual(0, own, gain, parts, resid, x, gain_f)

    half_of(
        at, [(1 - at[2], send, None), (at[2], keep, None)], x, 0, wg, wu, held, sems, prepare
    )


def expand_first(at, own, gain, parts, wg, wu):
    rows, depth = own.shape
    width = wg.shape[1]
    return pl.pallas_call(
        lambda *refs: expand_first_kernel(len(parts), *refs),
        in_specs=[SMEM] + [VMEM] * 2 + [ANY] * 2 + [VMEM] * len(parts),
        out_specs=[VMEM] * 4,
        out_shape=[
            jax.ShapeDtypeStruct((rows, width), f32),
            jax.ShapeDtypeStruct((rows, width), f32),
            jax.ShapeDtypeStruct((rows, depth // 2), f32),
            jax.ShapeDtypeStruct((rows, LANES), f32),
        ],
        scratch_shapes=[
            pltpu.VMEM((rows, depth // 2), bf16),
            pltpu.VMEM((depth // LANES, LANES), f32),
        ]
        + block_scratch(2, depth // 2, width // 2),
        compiler_params=params(18),
        cost_estimate=cost(rows, wg, wu),
        name="expand_first",
    )(at, own, gain, wg, wu, *parts)


def expand_send_kernel(n, at, own, gain, before, squares, wg, wu, *rest):
    parts, (out, resid, x, gain_f, held, sems) = rest[:n], rest[n:]
    width = wu.shape[1]

    def prepare():
        square = squares[...] + residual(1, own, gain, parts, resid, x, gain_f)
        square = jnp.broadcast_to(jnp.sum(square, axis=1, keepdims=True), square.shape)
        for p, term in enumerate(thirds(square)):
            out[:, width + p * LANES : width + (p + 1) * LANES] = term

    half_of(at, [(1 - at[2], out, before)], x, x.shape[1], wg, wu, held, sems, prepare)


def expand_send(at, own, gain, parts, wg, wu, before, squares):
    rows, depth = own.shape
    return pl.pallas_call(
        lambda *refs: expand_send_kernel(len(parts), *refs),
        in_specs=[SMEM] + [VMEM] * 4 + [ANY] * 2 + [VMEM] * len(parts),
        out_specs=[VMEM] * 3,
        out_shape=[
            jax.ShapeDtypeStruct((rows, wu.shape[1] + 3 * LANES), bf16),
            jax.ShapeDtypeStruct((rows, depth // 2), f32),
            jax.ShapeDtypeStruct((rows, depth // 2), bf16),
        ],
        scratch_shapes=[pltpu.VMEM((depth // LANES, LANES), f32)]
        + block_scratch(1, depth // 2, wu.shape[1] // 2),
        compiler_params=params(10),
        cost_estimate=cost(rows, wu),
        name="expand_send",
    )(at, own, gain, before, squares, wg, wu, *parts)


def expand_keep_kernel(at, x, before, wg, wu, out, held, sems):
    half_of(at, [(at[2], out, before)], x, x.shape[1], wg, wu, held, sems)


def expand_keep(at, x, wg, wu, before):
    rows = x.shape[0]
    return pl.pallas_call(
        expand_keep_kernel,
        in_specs=[SMEM] + [VMEM] * 2 + [ANY] * 2,
        out_specs=VMEM,
        out_shape=jax.ShapeDtypeStruct((rows, wu.shape[1]), bf16),
        scratch_shapes=block_scratch(1, x.shape[1], wu.shape[1] // 2),
        compiler_params=params(10),
        cost_estimate=cost(rows, wu),
        name="expand_keep",
    )(at, x, before, wg, wu)


def pair_kernel(keep, received, stats, out):
    width = out.shape[1] - 3 * LANES
    for start, size in blocks_of(width, 512):
        cols = slice(start, start + size)
        out[:, cols] = (keep[:, cols].astype(f32) + received[:, cols].astype(f32)).astype(bf16)
    for p, term in enumerate(thirds(joined(stats, width) + joined(received, width))):
        out[:, width + p * LANES : width + (p + 1) * LANES] = term


def pair(keep, received, stats):
    return pl.pallas_call(
        pair_kernel,
        in_specs=[VMEM] * 3,
        out_specs=VMEM,
        out_shape=jax.ShapeDtypeStruct(received.shape, bf16),
        compiler_params=params(4),
        name="pair",
    )(keep, received, stats)


def gated_kernel(model, one, two, out):
    half = out.shape[1]
    scale = lax.rsqrt((joined(one, 2 * half) + joined(two, 2 * half)) / model + epsilon)
    for c in range(half // LANES):
        gate, up = (
            scale * (one[:, lanes(at)].astype(f32) + two[:, lanes(at)].astype(f32))
            for at in (c, half // LANES + c)
        )
        out[:, lanes(c)] = (gate / (1.0 + jnp.exp(-gate)) * up).astype(bf16)


def gated(model, one, two, after):
    rows, width = one.shape
    return pl.pallas_call(
        lambda _, *refs: gated_kernel(model, *refs),
        in_specs=[ANY] + [VMEM] * 2,
        out_specs=VMEM,
        out_shape=jax.ShapeDtypeStruct((rows, (width - 3 * LANES) // 2), bf16),
        compiler_params=params(4),
        name="gated",
    )(after, one, two)


def contract_kernel(hidden, w, out):
    for start, size in blocks_of(w.shape[1], 512):
        cols = slice(start, start + size)
        out[:, cols] = jnp.dot(hidden[...], w[:, cols], preferred_element_type=f32)


def contract(hidden, w):
    rows = hidden.shape[0]
    return pl.pallas_call(
        contract_kernel,
        in_specs=[VMEM] * 2,
        out_specs=VMEM,
        out_shape=jax.ShapeDtypeStruct((rows, w.shape[1]), f32),
        compiler_params=params(4),
        cost_estimate=cost(rows, w),
        name="contract",
    )(hidden, w)


def contract_last_kernel(n, at, hidden, w, before, resid_0, resid_1, own, *rest):
    sends, acc = rest[:-1], rest[-1]
    share = own.shape[0]
    for start, size in blocks_of(w.shape[1], 512):
        cols = slice(start, start + size)
        acc[:, cols] = before[:, cols] + jnp.dot(hidden[...], w[:, cols], preferred_element_type=f32)

    def block(ref, index):
        if share % 8 == 0:
            return ref[pl.ds(pl.multiple_of(index * share, share), share), :]
        chosen = ref[:share, :]
        for b in range(1, n):
            chosen = jnp.where(index == b, ref[b * share : (b + 1) * share, :], chosen)
        return chosen

    half = resid_0.shape[1]
    mine = block(acc, at[3])
    own[:, :half] = mine[:, :half] + block(resid_0, at[3])
    own[:, half:] = mine[:, half:] + block(resid_1, at[3])
    for s in range(1, n):
        sends[s - 1][...] = block(acc, at[3] ^ s).astype(bf16)


def contract_last(n, at, hidden, w, before, *resid):
    rows, cols = before.shape
    share = rows // n
    return pl.pallas_call(
        lambda *refs: contract_last_kernel(n, *refs),
        in_specs=[SMEM] + [VMEM] * 5,
        out_specs=[VMEM] * n,
        out_shape=[jax.ShapeDtypeStruct((share, cols), f32)]
        + [jax.ShapeDtypeStruct((share, cols), bf16)] * (n - 1),
        scratch_shapes=[pltpu.VMEM((rows, cols), f32)],
        compiler_params=params(4),
        cost_estimate=cost(rows, w),
        name="contract_last",
    )(at, hidden, w, before, *resid)


def add_kernel(one, two, out):
    for start, size in blocks_of(out.shape[1], 512):
        cols = slice(start, start + size)
        out[:, cols] = (one[:, cols].astype(f32) + two[:, cols].astype(f32)).astype(bf16)


def add(one, two):
    return pl.pallas_call(
        add_kernel,
        in_specs=[VMEM] * 2,
        out_specs=VMEM,
        out_shape=jax.ShapeDtypeStruct(one.shape, bf16),
        compiler_params=params(4),
        name="add",
    )(one, two)


def swap(x, axis, bit):
    n = lax.axis_size(axis)
    return lax.ppermute(x, axis, [(i, i ^ bit) for i in range(n)])


def bits_of(axis):
    n = lax.axis_size(axis)
    return [1 << b for b in range(n.bit_length() - 1)]


def gathered(x, axis, token=None):
    parts = [x]
    for bit in reversed(bits_of(axis)):
        parts = parts + [swap(p, axis, bit) for p in parts]
        if bit > 1 and token is not None:
            parts = parts[:-1] + [hold(parts[-1], token)]
    return parts


def summed(x, axis, order):
    *bits, last = bits_of(axis)[::order]
    for bit in bits:
        x = add(x, swap(x, axis, bit))
    return x, swap(x, axis, last)


def per_device(tokens, attn_gain, ffn_gain, w_query, key_matrix, value_matrix, w_out, w_gate, w_up, w_down, kv_cache, lengths, slots):
    rows, model = tokens.shape
    wide_at, head_at = lax.axis_index("wide"), lax.axis_index("head")
    wide_size, head_size = lax.axis_size("wide"), lax.axis_size("head")
    places = jnp.stack([wide_at, (wide_at == wide_size - 1).astype(jnp.int32), wide_at & 1, head_at])
    at = places.astype(jnp.int32)

    half = HEAD_WIDTH // 2
    positions = (
        jnp.broadcast_to(lengths[:, None], (lengths.shape[0], DRAFT_TOKENS))
        + jnp.arange(DRAFT_TOKENS, dtype=jnp.int32)[None, :]
    ).reshape(rows).astype(f32)
    exponent = jnp.arange(half, dtype=f32) * (2.0 / HEAD_WIDTH)
    angles = positions[:, None] * (theta_base ** (-exponent))[None, :]
    cos, sin = jnp.cos(angles), jnp.sin(angles)
    cos = jnp.concatenate([cos, cos], axis=1)
    sin = jnp.concatenate([-sin, sin], axis=1)

    qkv, own = project(at, tokens, attn_gain, w_query, key_matrix, value_matrix)
    depth = own.shape[1]
    half = depth // 2
    gain = ffn_gain.reshape(depth // LANES, LANES)

    flat_cache = kv_cache.reshape((-1,) + kv_cache.shape[2:])
    meta = jnp.concatenate([at, lengths, slots])
    cache, w_out, token = fetch(at, (qkv, meta, cos, sin), Part(flat_cache), Part(w_out))
    cache = cache.reshape(kv_cache.shape)
    value = attend(meta, cos, sin, cache, gathered(qkv, "wide", token))
    out_0, attended = output_first(gathered(value, "wide"), w_out)
    out_1 = output_second(attended, w_out)
    parts_0, parts_1 = summed(out_0, "head", 1), summed(out_1, "head", -1)
    send, keep, resid_0, squares = expand_first(at, own, gain, parts_0, w_gate, w_up)
    send, resid_1, x = expand_send(at, own, gain, parts_1, w_gate, w_up, send, squares)
    received = swap(send, "wide", 1)
    total = pair(expand_keep(at, x, w_gate, w_up, keep), received, send)
    down_own, down_other, token = fetch(at, total, Part(w_down, side=0), Part(w_down, side=1))
    for bit in bits_of("wide")[1:-1]:
        there = swap(total, "wide", bit)
        total = pair(total, there, total)
    hidden = gated(model, total, swap(total, "wide", bits_of("wide")[-1]), token)
    other = swap(hidden, "wide", 1)
    total, *sends = contract_last(
        head_size, at, other, down_other, contract(hidden, down_own), resid_0, resid_1
    )
    for s, send in enumerate(sends, 1):
        total = total + swap(send, "head", s).astype(f32)
    return total.astype(bf16)


def solution(mesh):
    in_specs = (
        P("grp", None),
        P(),
        P("wide"),
        P("wide", "head"),
        P("wide", "head"),
        P("wide", "head"),
        P("head", "wide"),
        P("wide", "head"),
        P("wide", "head"),
        P("head", "wide"),
        P(None, "grp", "wide", "head"),
        P("grp"),
        P("grp"),
    )
    out_specs = P(("grp", "head"), "wide")
    return jax.shard_map(
        per_device, mesh=mesh, in_specs=in_specs, out_specs=out_specs, check_vma=False
    )
```

```python
import math

import jax
import jax.numpy as jnp
from jax import lax
from jax.experimental import pallas as pl
from jax.experimental.pallas import tpu as pltpu
from jax.sharding import PartitionSpec as P

HEAD_WIDTH = 128
DRAFT_TOKENS = 4
LANES = 128
MIB = 1 << 20

epsilon = 1e-05
theta_base = 500000.0
neg_large = -1e30

f32 = jnp.float32
bf16 = jnp.bfloat16
ANY = pl.BlockSpec(memory_space=pl.ANY)
VMEM = pl.BlockSpec(memory_space=pltpu.VMEM)
SMEM = pl.BlockSpec(memory_space=pltpu.SMEM)
HBM = pl.BlockSpec(memory_space=pltpu.HBM)


def in_hbm(x):
    return pltpu.with_memory_space_constraint(x, pltpu.HBM)


def cost(rows, *weights):
    size = sum(w.size for w in weights)
    return pl.CostEstimate(flops=2 * rows * size, bytes_accessed=2 * size, transcendentals=0)


def params(mib):
    return pltpu.CompilerParams(vmem_limit_bytes=mib * MIB)


def blocks_of(width, most):
    step = max(b for b in range(LANES, most + 1, LANES) if width % b == 0)
    return [(at, step) for at in range(0, width, step)]


def thirds(x):
    high = x.astype(bf16)
    rest = x - high.astype(f32)
    middle = rest.astype(bf16)
    return high, middle, (rest - middle.astype(f32)).astype(bf16)


def lanes(at):
    return slice(at * LANES, (at + 1) * LANES)


PIECES = 8


class Part:
    def __init__(self, array, first=0, count=None, side=None):
        rows = array.shape[0]
        self.array, self.first, self.side = array, first, side
        self.count = rows // 2 if side is not None else rows if count is None else count
        self.shape = (self.count,) + array.shape[1:]
        self.out = pltpu.VMEM(self.shape, array.dtype)

    def copies(self, at, source, held, sems):
        step = max(1, self.count // PIECES)
        base = self.first
        if self.side is not None:
            base = pl.multiple_of((at[2] if self.side == 0 else 1 - at[2]) * self.count, LANES)
        return [
            pltpu.make_async_copy(
                source.at[pl.ds(base + p * step, step)], held.at[pl.ds(p * step, step)], sems.at[p]
            )
            for p in range(self.count // step)
        ]


def fetch_kernel(wanted, skip, at, *refs):
    n, refs = len(wanted), refs[skip:]
    sources, held, token, sems = refs[:n], refs[n : 2 * n], refs[2 * n], refs[2 * n + 1 :]
    copies = sum([w.copies(at, *refs) for w, *refs in zip(wanted, sources, held, sems)], [])
    for copy in copies:
        copy.start()
    token[...] = jnp.zeros_like(token)
    for copy in copies:
        copy.wait()


def fetch(at, after, *wanted):
    after = after if isinstance(after, (list, tuple)) else [after]
    size = sum(math.prod(w.shape) for w in wanted)
    return pl.pallas_call(
        lambda *refs: fetch_kernel(wanted, len(after), *refs),
        in_specs=[SMEM] + [ANY] * len(after) + [HBM] * len(wanted),
        out_specs=[VMEM] * (len(wanted) + 1),
        out_shape=[w.out for w in wanted] + [pltpu.VMEM((8, LANES), f32)],
        scratch_shapes=[pltpu.SemaphoreType.DMA((2 * PIECES,))] * len(wanted),
        compiler_params=params(2),
        cost_estimate=pl.CostEstimate(flops=0, bytes_accessed=4 * size, transcendentals=0),
        name="fetch",
    )(at, *after, *[in_hbm(w.array) for w in wanted])


def hold(x, token):
    return pl.pallas_call(
        lambda *_: None,
        in_specs=[VMEM, ANY],
        out_specs=VMEM,
        out_shape=jax.ShapeDtypeStruct(x.shape, x.dtype),
        input_output_aliases={0: 0},
        compiler_params=params(1),
        name="hold",
    )(x, token)


def project_kernel(chunks, at, tokens, gain, wq, wk, wv, out, own, tok, gain_f, norm, bq, bk, bv, acc, gain_b, sems):
    rows, model = tok.shape
    depth, q_cols = bq.shape
    kv_cols = bk.shape[1]
    step = depth // chunks
    gain_copy = pltpu.make_async_copy(gain, gain_b, sems.at[3 + chunks])
    gain_copy.start()
    copies = [
        pltpu.make_async_copy(tokens, tok, sems.at[0]),
        pltpu.make_async_copy(wk, bk, sems.at[1]),
        pltpu.make_async_copy(wv, bv, sems.at[2]),
    ] + [
        pltpu.make_async_copy(
            wq.at[pl.ds(c * step, step)], bq.at[pl.ds(c * step, step)], sems.at[3 + c]
        )
        for c in range(chunks)
    ]
    for copy in copies:
        copy.start()
    gain_copy.wait()
    gain_f[...] = gain_b[...].astype(f32)
    copies[0].wait()
    squares = jnp.zeros((rows, LANES), f32)
    for c in range(model // LANES):
        part = tok[:, lanes(c)].astype(f32)
        squares = squares + part * part
    scale = lax.rsqrt(jnp.sum(squares, axis=1, keepdims=True) / model + epsilon)
    count = depth // LANES
    for c in range(count):
        index = at[0] * count + c
        part = tok[:, pl.ds(pl.multiple_of(index * LANES, LANES), LANES)]
        own[:, lanes(c)] = part
        norm[:, lanes(c)] = (part.astype(f32) * scale * gain_f[pl.ds(index, 1), :]).astype(bf16)
    for copy, held, base in ((copies[1], bk, q_cols), (copies[2], bv, q_cols + kv_cols)):
        copy.wait()
        out[:, base : base + kv_cols] = jnp.dot(
            norm[...], held[...], preferred_element_type=f32
        ).astype(out.dtype)
    for c in range(chunks):
        copies[3 + c].wait()
        for start, size in blocks_of(q_cols, 512):
            cols = slice(start, start + size)
            term = jnp.dot(
                norm[:, c * step : (c + 1) * step],
                bq[c * step : (c + 1) * step, cols],
                preferred_element_type=f32,
            )
            if c:
                term = acc[:, cols] + term
            if c < chunks - 1:
                acc[:, cols] = term
            else:
                out[:, cols] = term.astype(out.dtype)


def project(at, tokens, gain, wq, wk, wv):
    rows, model = tokens.shape
    depth, q_cols = wq.shape
    kv_cols = wk.shape[1]
    chunks = max(1, min(8, depth // 256))
    return pl.pallas_call(
        lambda *refs: project_kernel(chunks, *refs),
        in_specs=[SMEM] + [HBM] * 5,
        out_specs=[VMEM, VMEM],
        out_shape=[
            jax.ShapeDtypeStruct((rows, q_cols + 2 * kv_cols), bf16),
            jax.ShapeDtypeStruct((rows, depth), bf16),
        ],
        scratch_shapes=[
            pltpu.VMEM((rows, model), bf16),
            pltpu.VMEM((model // LANES, LANES), f32),
            pltpu.VMEM((rows, depth), bf16),
            pltpu.VMEM(wq.shape, bf16),
            pltpu.VMEM(wk.shape, bf16),
            pltpu.VMEM(wv.shape, bf16),
            pltpu.VMEM((rows, q_cols), f32),
            pltpu.VMEM((model // LANES, LANES), bf16),
            pltpu.SemaphoreType.DMA((4 + chunks,)),
        ],
        compiler_params=params(16),
        cost_estimate=cost(rows, wq, wk, wv),
        name="project",
    )(at, in_hbm(tokens), in_hbm(gain.reshape(model // LANES, LANES)), in_hbm(wq), in_hbm(wk), in_hbm(wv))


def attend_kernel(n, at, cos, sin, cache, *rest):
    parts, (out, queries, total, stats_f) = rest[:n], rest[n:]
    rows, q_cols = queries.shape
    context, kv_cols = cache.shape[2:]
    kv_heads = kv_cols // HEAD_WIDTH
    heads = q_cols // HEAD_WIDTH
    group = heads // kv_heads
    tile = 2 * DRAFT_TOKENS
    requests = rows // DRAFT_TOKENS

    def length(r):
        return at[4 + r]

    def slot(r):
        return at[4 + requests + r]

    last = at[1]
    base = at[0] * context

    def column(c):
        return sum(p[:, lanes(c)].astype(f32) for p in parts)

    def rotated(x):
        return x * cos[...] + pltpu.roll(x, HEAD_WIDTH // 2, 1) * sin[...]

    for h in range(heads):
        queries[:, lanes(h)] = (rotated(column(h)) * HEAD_WIDTH ** (-0.5)).astype(bf16).astype(f32)
    new_keys = [rotated(column(heads + k)).astype(bf16) for k in range(kv_heads)]
    new_values = [column(heads + kv_heads + k).astype(bf16) for k in range(kv_heads)]

    high = group * tile
    row = lax.broadcasted_iota(jnp.int32, (high, 1), 0) % tile
    first = row < DRAFT_TOKENS
    position = lax.broadcasted_iota(jnp.int32, (high, context), 1) + base
    draft_col = lax.broadcasted_iota(jnp.int32, (high, rows), 1)
    lane = lax.broadcasted_iota(jnp.int32, (tile, LANES), 1)
    nt = (((1,), (1,)), ((), ()))
    for i in range(rows // tile):
        request = 2 * i
        limit = jnp.where(first, length(request), length(request + 1))
        live = position < limit
        own_at = tile * i + jnp.where(first, 0, DRAFT_TOKENS)
        seen = (draft_col >= own_at) & (draft_col <= tile * i + row) & (last > 0)
        stats = jnp.zeros((tile, LANES), f32)
        for k in range(kv_heads):
            q = jnp.concatenate(
                [queries[tile * i : tile * (i + 1), lanes(k * group + g)] for g in range(group)], axis=0
            ).astype(bf16)
            scores = [
                lax.dot_general(q, cache[0, slot(request + s), :, lanes(k)], nt, preferred_element_type=f32)
                for s in range(2)
            ]
            score = jnp.where(live, jnp.where(first, scores[0], scores[1]), neg_large)
            draft = lax.dot_general(q, new_keys[k], nt, preferred_element_type=f32)
            draft = jnp.where(seen, draft, neg_large)
            top = jnp.maximum(
                jnp.max(score, axis=1, keepdims=True), jnp.max(draft, axis=1, keepdims=True)
            )
            weight = jnp.where(live, jnp.exp(score - top), 0.0)
            draft_weight = jnp.where(seen, jnp.exp(draft - top), 0.0)
            mass = jnp.sum(weight, axis=1, keepdims=True) + jnp.sum(draft_weight, axis=1, keepdims=True)
            weight = weight.astype(bf16)
            sums = [
                jnp.dot(weight, cache[1, slot(request + s), :, lanes(k)], preferred_element_type=f32)
                for s in range(2)
            ]
            value = jnp.where(first, sums[0], sums[1]) + jnp.dot(
                draft_weight.astype(bf16), new_values[k], preferred_element_type=f32
            )
            some = mass > 0.0
            safe = jnp.where(some, mass, 1.0)
            value = value / safe
            lse = jnp.where(some, top + jnp.log(safe), neg_large)
            for g in range(group):
                at_rows = slice(tile * g, tile * (g + 1))
                total[tile * i : tile * (i + 1), lanes(k * group + g)] = value[at_rows]
                stats = jnp.where(lane == k * group + g, lse[at_rows], stats)
        stats_f[tile * i : tile * (i + 1), :] = stats
    out[:, :q_cols] = total[...].astype(bf16)
    for p, term in enumerate(thirds(stats_f[...])):
        out[:, q_cols + p * LANES : q_cols + (p + 1) * LANES] = term


def attend(at, cos, sin, cache, parts):
    rows, width = parts[0].shape
    q_cols = width - 2 * cache.shape[3]
    return pl.pallas_call(
        lambda *refs: attend_kernel(len(parts), *refs),
        in_specs=[SMEM] + [VMEM] * (3 + len(parts)),
        out_specs=VMEM,
        out_shape=jax.ShapeDtypeStruct((rows, q_cols + 3 * LANES), bf16),
        scratch_shapes=[
            pltpu.VMEM((rows, q_cols), f32),
            pltpu.VMEM((rows, q_cols), f32),
            pltpu.VMEM((rows, LANES), f32),
        ],
        compiler_params=params(6),
        cost_estimate=cost(rows, cache),
        name="attend",
    )(at, cos, sin, cache, *parts)


def joined(ref, start):
    return sum(ref[:, start + p * LANES : start + (p + 1) * LANES].astype(f32) for p in range(3))


def product(x, w, out, base, width):
    for start, size in blocks_of(width, 512):
        out[:, start : start + size] = jnp.dot(
            x[...], w[:, base + start : base + start + size], preferred_element_type=f32
        ).astype(out.dtype)


def output_first_kernel(n, w, *rest):
    values, (out, attended) = rest[:n], rest[n:]
    heads = attended.shape[1] // HEAD_WIDTH
    stats = [joined(v, attended.shape[1]) for v in values]
    top = stats[0]
    for s in stats[1:]:
        top = jnp.maximum(top, s)
    shares = [jnp.exp(s - top) for s in stats]
    whole = sum(shares)
    shares = [s / whole for s in shares]
    for h in range(heads):
        attended[:, lanes(h)] = sum(
            v[:, lanes(h)].astype(f32) * s[:, h : h + 1] for v, s in zip(values, shares)
        ).astype(bf16)
    product(attended, w, out, 0, out.shape[1])


def output_first(values, w):
    rows, half = values[0].shape[0], w.shape[1] // 2
    return pl.pallas_call(
        lambda *refs: output_first_kernel(len(values), *refs),
        in_specs=[VMEM] * (1 + len(values)),
        out_specs=[VMEM] * 2,
        out_shape=[
            jax.ShapeDtypeStruct((rows, half), bf16),
            jax.ShapeDtypeStruct((rows, w.shape[0]), bf16),
        ],
        compiler_params=params(4),
        cost_estimate=cost(rows, w),
        name="output_first",
    )(w, *values)


def output_second(attended, w):
    rows, half = attended.shape[0], w.shape[1] // 2
    return pl.pallas_call(
        lambda x, w, out: product(x, w, out, half, half),
        in_specs=[VMEM] * 2,
        out_specs=VMEM,
        out_shape=jax.ShapeDtypeStruct((rows, half), bf16),
        compiler_params=params(4),
        cost_estimate=cost(rows, w),
        name="output_second",
    )(attended, w)


WIDE = 1792
SPLIT = 4


def half_of(at, sides, x, row, wg, wu, held, sems, prepare=None):
    count, half = x.shape[1], wg.shape[1] // 2
    step = count // SPLIT
    jobs = []
    for side, out, before in sides:
        for base, w in ((0, wg), (half, wu)):
            for start, size in blocks_of(half, WIDE):
                n = len(jobs)
                cols = pl.ds(pl.multiple_of(side * half + start, LANES), size)
                copies = [
                    pltpu.make_async_copy(
                        w.at[pl.ds(row + p * step, step), cols],
                        held.at[n, pl.ds(p * step, step)],
                        sems.at[n * SPLIT + p],
                    )
                    for p in range(SPLIT)
                ]
                jobs.append((copies, slice(base + start, base + start + size), out, before))
    for copies, *_ in jobs:
        for copy in copies:
            copy.start()
    if prepare is not None:
        pl.when(at[2] >= 0)(prepare)
    for n, (copies, cols, out, before) in enumerate(jobs):
        for copy in copies:
            copy.wait()
        term = jnp.dot(x[...], held[n], preferred_element_type=f32)
        if before is not None:
            term = before[:, cols] + term
        out[:, cols] = term.astype(out.dtype)


def block_scratch(sides, count, half):
    blocks = blocks_of(half, WIDE)
    number = sides * 2 * len(blocks)
    return [
        pltpu.VMEM((number, count, blocks[0][1]), bf16),
        pltpu.SemaphoreType.DMA((number * SPLIT,)),
    ]


def residual(which, own, gain, parts, resid, x, gain_f):
    gain_f[...] = gain[...].astype(f32)
    count = resid.shape[1] // LANES
    square = jnp.zeros((own.shape[0], LANES), f32)
    for c in range(count):
        at = which * count + c
        value = own[:, lanes(at)].astype(f32) + sum(p[:, lanes(c)].astype(f32) for p in parts)
        value = value.astype(bf16).astype(f32)
        resid[:, lanes(c)] = value
        square = square + value * value
        x[:, lanes(c)] = (value * gain_f[at : at + 1, :]).astype(bf16)
    return square


def expand_first_kernel(n, at, own, gain, wg, wu, *rest):
    parts, (send, keep, resid, squares, x, gain_f, held, sems) = rest[:n], rest[n:]

    def prepare():
        squares[...] = residual(0, own, gain, parts, resid, x, gain_f)

    half_of(
        at, [(1 - at[2], send, None), (at[2], keep, None)], x, 0, wg, wu, held, sems, prepare
    )


def expand_first(at, own, gain, parts, wg, wu):
    rows, depth = own.shape
    width = wg.shape[1]
    return pl.pallas_call(
        lambda *refs: expand_first_kernel(len(parts), *refs),
        in_specs=[SMEM] + [VMEM] * 2 + [ANY] * 2 + [VMEM] * len(parts),
        out_specs=[VMEM] * 4,
        out_shape=[
            jax.ShapeDtypeStruct((rows, width), f32),
            jax.ShapeDtypeStruct((rows, width), f32),
            jax.ShapeDtypeStruct((rows, depth // 2), f32),
            jax.ShapeDtypeStruct((rows, LANES), f32),
        ],
        scratch_shapes=[
            pltpu.VMEM((rows, depth // 2), bf16),
            pltpu.VMEM((depth // LANES, LANES), f32),
        ]
        + block_scratch(2, depth // 2, width // 2),
        compiler_params=params(18),
        cost_estimate=cost(rows, wg, wu),
        name="expand_first",
    )(at, own, gain, wg, wu, *parts)


def expand_send_kernel(n, at, own, gain, before, squares, wg, wu, *rest):
    parts, (out, resid, x, gain_f, held, sems) = rest[:n], rest[n:]
    width = wu.shape[1]

    def prepare():
        square = squares[...] + residual(1, own, gain, parts, resid, x, gain_f)
        square = jnp.broadcast_to(jnp.sum(square, axis=1, keepdims=True), square.shape)
        for p, term in enumerate(thirds(square)):
            out[:, width + p * LANES : width + (p + 1) * LANES] = term

    half_of(at, [(1 - at[2], out, before)], x, x.shape[1], wg, wu, held, sems, prepare)


def expand_send(at, own, gain, parts, wg, wu, before, squares):
    rows, depth = own.shape
    return pl.pallas_call(
        lambda *refs: expand_send_kernel(len(parts), *refs),
        in_specs=[SMEM] + [VMEM] * 4 + [ANY] * 2 + [VMEM] * len(parts),
        out_specs=[VMEM] * 3,
        out_shape=[
            jax.ShapeDtypeStruct((rows, wu.shape[1] + 3 * LANES), bf16),
            jax.ShapeDtypeStruct((rows, depth // 2), f32),
            jax.ShapeDtypeStruct((rows, depth // 2), bf16),
        ],
        scratch_shapes=[pltpu.VMEM((depth // LANES, LANES), f32)]
        + block_scratch(1, depth // 2, wu.shape[1] // 2),
        compiler_params=params(10),
        cost_estimate=cost(rows, wu),
        name="expand_send",
    )(at, own, gain, before, squares, wg, wu, *parts)


def expand_keep_kernel(at, x, before, wg, wu, out, held, sems):
    half_of(at, [(at[2], out, before)], x, x.shape[1], wg, wu, held, sems)


def expand_keep(at, x, wg, wu, before):
    rows = x.shape[0]
    return pl.pallas_call(
        expand_keep_kernel,
        in_specs=[SMEM] + [VMEM] * 2 + [ANY] * 2,
        out_specs=VMEM,
        out_shape=jax.ShapeDtypeStruct((rows, wu.shape[1]), bf16),
        scratch_shapes=block_scratch(1, x.shape[1], wu.shape[1] // 2),
        compiler_params=params(10),
        cost_estimate=cost(rows, wu),
        name="expand_keep",
    )(at, x, before, wg, wu)


def pair_kernel(keep, received, stats, out):
    width = out.shape[1] - 3 * LANES
    for start, size in blocks_of(width, 512):
        cols = slice(start, start + size)
        out[:, cols] = (keep[:, cols].astype(f32) + received[:, cols].astype(f32)).astype(bf16)
    for p, term in enumerate(thirds(joined(stats, width) + joined(received, width))):
        out[:, width + p * LANES : width + (p + 1) * LANES] = term


def pair(keep, received, stats):
    return pl.pallas_call(
        pair_kernel,
        in_specs=[VMEM] * 3,
        out_specs=VMEM,
        out_shape=jax.ShapeDtypeStruct(received.shape, bf16),
        compiler_params=params(4),
        name="pair",
    )(keep, received, stats)


def gated_kernel(model, one, two, out):
    half = out.shape[1]
    scale = lax.rsqrt((joined(one, 2 * half) + joined(two, 2 * half)) / model + epsilon)
    for c in range(half // LANES):
        gate, up = (
            scale * (one[:, lanes(at)].astype(f32) + two[:, lanes(at)].astype(f32))
            for at in (c, half // LANES + c)
        )
        out[:, lanes(c)] = (gate / (1.0 + jnp.exp(-gate)) * up).astype(bf16)


def gated(model, one, two, after):
    rows, width = one.shape
    return pl.pallas_call(
        lambda _, *refs: gated_kernel(model, *refs),
        in_specs=[ANY] + [VMEM] * 2,
        out_specs=VMEM,
        out_shape=jax.ShapeDtypeStruct((rows, (width - 3 * LANES) // 2), bf16),
        compiler_params=params(4),
        name="gated",
    )(after, one, two)


def contract_kernel(hidden, w, out):
    for start, size in blocks_of(w.shape[1], 512):
        cols = slice(start, start + size)
        out[:, cols] = jnp.dot(hidden[...], w[:, cols], preferred_element_type=f32)


def contract(hidden, w):
    rows = hidden.shape[0]
    return pl.pallas_call(
        contract_kernel,
        in_specs=[VMEM] * 2,
        out_specs=VMEM,
        out_shape=jax.ShapeDtypeStruct((rows, w.shape[1]), f32),
        compiler_params=params(4),
        cost_estimate=cost(rows, w),
        name="contract",
    )(hidden, w)


def contract_last_kernel(n, at, hidden, w, before, resid_0, resid_1, own, *rest):
    sends, acc = rest[:-1], rest[-1]
    share = own.shape[0]
    for start, size in blocks_of(w.shape[1], 512):
        cols = slice(start, start + size)
        acc[:, cols] = before[:, cols] + jnp.dot(hidden[...], w[:, cols], preferred_element_type=f32)

    def block(ref, index):
        if share % 8 == 0:
            return ref[pl.ds(pl.multiple_of(index * share, share), share), :]
        chosen = ref[:share, :]
        for b in range(1, n):
            chosen = jnp.where(index == b, ref[b * share : (b + 1) * share, :], chosen)
        return chosen

    half = resid_0.shape[1]
    mine = block(acc, at[3])
    own[:, :half] = mine[:, :half] + block(resid_0, at[3])
    own[:, half:] = mine[:, half:] + block(resid_1, at[3])
    for s in range(1, n):
        sends[s - 1][...] = block(acc, at[3] ^ s).astype(bf16)


def contract_last(n, at, hidden, w, before, *resid):
    rows, cols = before.shape
    share = rows // n
    return pl.pallas_call(
        lambda *refs: contract_last_kernel(n, *refs),
        in_specs=[SMEM] + [VMEM] * 5,
        out_specs=[VMEM] * n,
        out_shape=[jax.ShapeDtypeStruct((share, cols), f32)]
        + [jax.ShapeDtypeStruct((share, cols), bf16)] * (n - 1),
        scratch_shapes=[pltpu.VMEM((rows, cols), f32)],
        compiler_params=params(4),
        cost_estimate=cost(rows, w),
        name="contract_last",
    )(at, hidden, w, before, *resid)


def add_kernel(one, two, out):
    for start, size in blocks_of(out.shape[1], 512):
        cols = slice(start, start + size)
        out[:, cols] = (one[:, cols].astype(f32) + two[:, cols].astype(f32)).astype(bf16)


def add(one, two):
    return pl.pallas_call(
        add_kernel,
        in_specs=[VMEM] * 2,
        out_specs=VMEM,
        out_shape=jax.ShapeDtypeStruct(one.shape, bf16),
        compiler_params=params(4),
        name="add",
    )(one, two)


def swap(x, axis, bit):
    n = lax.axis_size(axis)
    return lax.ppermute(x, axis, [(i, i ^ bit) for i in range(n)])


def bits_of(axis):
    n = lax.axis_size(axis)
    return [1 << b for b in range(n.bit_length() - 1)]


def gathered(x, axis, token=None):
    parts = [x]
    for bit in reversed(bits_of(axis)):
        parts = parts + [swap(p, axis, bit) for p in parts]
        if bit > 1 and token is not None:
            parts = parts[:-1] + [hold(parts[-1], token)]
    return parts


def summed(x, axis, order):
    *bits, last = bits_of(axis)[::order]
    for bit in bits:
        x = add(x, swap(x, axis, bit))
    return x, swap(x, axis, last)


def per_device(tokens, attn_gain, ffn_gain, w_query, key_matrix, value_matrix, w_out, w_gate, w_up, w_down, kv_cache, lengths, slots):
    rows, model = tokens.shape
    wide_at, head_at = lax.axis_index("wide"), lax.axis_index("head")
    wide_size, head_size = lax.axis_size("wide"), lax.axis_size("head")
    places = jnp.stack([wide_at, (wide_at == wide_size - 1).astype(jnp.int32), wide_at & 1, head_at])
    at = places.astype(jnp.int32)

    half = HEAD_WIDTH // 2
    positions = (
        jnp.broadcast_to(lengths[:, None], (lengths.shape[0], DRAFT_TOKENS))
        + jnp.arange(DRAFT_TOKENS, dtype=jnp.int32)[None, :]
    ).reshape(rows).astype(f32)
    exponent = jnp.arange(half, dtype=f32) * (2.0 / HEAD_WIDTH)
    angles = positions[:, None] * (theta_base ** (-exponent))[None, :]
    cos, sin = jnp.cos(angles), jnp.sin(angles)
    cos = jnp.concatenate([cos, cos], axis=1)
    sin = jnp.concatenate([-sin, sin], axis=1)

    qkv, own = project(at, tokens, attn_gain, w_query, key_matrix, value_matrix)
    depth = own.shape[1]
    half = depth // 2
    gain = ffn_gain.reshape(depth // LANES, LANES)

    flat_cache = kv_cache.reshape((-1,) + kv_cache.shape[2:])
    meta = jnp.concatenate([at, lengths, slots])
    cache, w_out, token = fetch(at, (qkv, meta, cos, sin), Part(flat_cache), Part(w_out))
    cache = cache.reshape(kv_cache.shape)
    value = attend(meta, cos, sin, cache, gathered(qkv, "wide", token))
    out_0, attended = output_first(gathered(value, "wide"), w_out)
    out_1 = output_second(attended, w_out)
    parts_0, parts_1 = summed(out_0, "head", 1), summed(out_1, "head", -1)
    send, keep, resid_0, squares = expand_first(at, own, gain, parts_0, w_gate, w_up)
    send, resid_1, x = expand_send(at, own, gain, parts_1, w_gate, w_up, send, squares)
    received = swap(send, "wide", 1)
    total = pair(expand_keep(at, x, w_gate, w_up, keep), received, send)
    down_own, down_other, token = fetch(at, total, Part(w_down, side=0), Part(w_down, side=1))
    for bit in bits_of("wide")[1:-1]:
        there = swap(total, "wide", bit)
        total = pair(total, there, total)
    hidden = gated(model, total, swap(total, "wide", bits_of("wide")[-1]), token)
    other = swap(hidden, "wide", 1)
    total, *sends = contract_last(
        head_size, at, other, down_other, contract(hidden, down_own), resid_0, resid_1
    )
    for s, send in enumerate(sends, 1):
        total = total + swap(send, "head", s).astype(f32)
    return total.astype(bf16)


def solution(mesh):
    in_specs = (
        P("grp", None),
        P(),
        P("wide"),
        P("wide", "head"),
        P("wide", "head"),
        P("wide", "head"),
        P("head", "wide"),
        P("wide", "head"),
        P("wide", "head"),
        P("head", "wide"),
        P(None, "grp", "wide", "head"),
        P("grp"),
        P("grp"),
    )
    out_specs = P(("grp", "head"), "wide")
    return jax.shard_map(
        per_device, mesh=mesh, in_specs=in_specs, out_specs=out_specs, check_vma=False
    )
```

```python
import math

import jax
import jax.numpy as jnp
from jax import lax
from jax.experimental import pallas as pl
from jax.experimental.pallas import tpu as pltpu
from jax.sharding import PartitionSpec as P

HEAD_WIDTH = 128
DRAFT_TOKENS = 4
LANES = 128
MIB = 1 << 20

epsilon = 1e-05
theta_base = 500000.0
neg_large = -1e30

f32 = jnp.float32
bf16 = jnp.bfloat16
ANY = pl.BlockSpec(memory_space=pl.ANY)
VMEM = pl.BlockSpec(memory_space=pltpu.VMEM)
SMEM = pl.BlockSpec(memory_space=pltpu.SMEM)
HBM = pl.BlockSpec(memory_space=pltpu.HBM)


def in_hbm(x):
    return pltpu.with_memory_space_constraint(x, pltpu.HBM)


def cost(rows, *weights):
    size = sum(w.size for w in weights)
    return pl.CostEstimate(flops=2 * rows * size, bytes_accessed=2 * size, transcendentals=0)


def params(mib):
    return pltpu.CompilerParams(vmem_limit_bytes=mib * MIB)


def blocks_of(width, most):
    step = max(b for b in range(LANES, most + 1, LANES) if width % b == 0)
    return [(at, step) for at in range(0, width, step)]


def thirds(x):
    high = x.astype(bf16)
    rest = x - high.astype(f32)
    middle = rest.astype(bf16)
    return high, middle, (rest - middle.astype(f32)).astype(bf16)


def lanes(at):
    return slice(at * LANES, (at + 1) * LANES)


PIECES = 8


class Part:
    def __init__(self, array, first=0, count=None, side=None):
        rows = array.shape[0]
        self.array, self.first, self.side = array, first, side
        self.count = rows // 2 if side is not None else rows if count is None else count
        self.shape = (self.count,) + array.shape[1:]
        self.out = pltpu.VMEM(self.shape, array.dtype)

    def copies(self, at, source, held, sems):
        step = max(1, self.count // PIECES)
        base = self.first
        if self.side is not None:
            base = pl.multiple_of((at[2] if self.side == 0 else 1 - at[2]) * self.count, LANES)
        return [
            pltpu.make_async_copy(
                source.at[pl.ds(base + p * step, step)], held.at[pl.ds(p * step, step)], sems.at[p]
            )
            for p in range(self.count // step)
        ]


def fetch_kernel(wanted, skip, at, *refs):
    n, refs = len(wanted), refs[skip:]
    sources, held, token, sems = refs[:n], refs[n : 2 * n], refs[2 * n], refs[2 * n + 1 :]
    copies = sum([w.copies(at, *refs) for w, *refs in zip(wanted, sources, held, sems)], [])
    for copy in copies:
        copy.start()
    token[...] = jnp.zeros_like(token)
    for copy in copies:
        copy.wait()


def fetch(at, after, *wanted):
    after = after if isinstance(after, (list, tuple)) else [after]
    size = sum(math.prod(w.shape) for w in wanted)
    return pl.pallas_call(
        lambda *refs: fetch_kernel(wanted, len(after), *refs),
        in_specs=[SMEM] + [ANY] * len(after) + [HBM] * len(wanted),
        out_specs=[VMEM] * (len(wanted) + 1),
        out_shape=[w.out for w in wanted] + [pltpu.VMEM((8, LANES), f32)],
        scratch_shapes=[pltpu.SemaphoreType.DMA((2 * PIECES,))] * len(wanted),
        compiler_params=params(2),
        cost_estimate=pl.CostEstimate(flops=0, bytes_accessed=4 * size, transcendentals=0),
        name="fetch",
    )(at, *after, *[in_hbm(w.array) for w in wanted])


def hold(x, token):
    return pl.pallas_call(
        lambda *_: None,
        in_specs=[VMEM, ANY],
        out_specs=VMEM,
        out_shape=jax.ShapeDtypeStruct(x.shape, x.dtype),
        input_output_aliases={0: 0},
        compiler_params=params(1),
        name="hold",
    )(x, token)


def project_kernel(chunks, at, tokens, gain, wq, wk, wv, out, own, tok, gain_f, norm, bq, bk, bv, acc, gain_b, sems):
    rows, model = tok.shape
    depth, q_cols = bq.shape
    kv_cols = bk.shape[1]
    step = depth // chunks
    gain_copy = pltpu.make_async_copy(gain, gain_b, sems.at[3 + chunks])
    gain_copy.start()
    copies = [
        pltpu.make_async_copy(tokens, tok, sems.at[0]),
        pltpu.make_async_copy(wk, bk, sems.at[1]),
        pltpu.make_async_copy(wv, bv, sems.at[2]),
    ] + [
        pltpu.make_async_copy(
            wq.at[pl.ds(c * step, step)], bq.at[pl.ds(c * step, step)], sems.at[3 + c]
        )
        for c in range(chunks)
    ]
    for copy in copies:
        copy.start()
    gain_copy.wait()
    gain_f[...] = gain_b[...].astype(f32)
    copies[0].wait()
    squares = jnp.zeros((rows, LANES), f32)
    for c in range(model // LANES):
        part = tok[:, lanes(c)].astype(f32)
        squares = squares + part * part
    scale = lax.rsqrt(jnp.sum(squares, axis=1, keepdims=True) / model + epsilon)
    count = depth // LANES
    for c in range(count):
        index = at[0] * count + c
        part = tok[:, pl.ds(pl.multiple_of(index * LANES, LANES), LANES)]
        own[:, lanes(c)] = part
        norm[:, lanes(c)] = (part.astype(f32) * scale * gain_f[pl.ds(index, 1), :]).astype(bf16)
    for copy, held, base in ((copies[1], bk, q_cols), (copies[2], bv, q_cols + kv_cols)):
        copy.wait()
        out[:, base : base + kv_cols] = jnp.dot(
            norm[...], held[...], preferred_element_type=f32
        ).astype(out.dtype)
    for c in range(chunks):
        copies[3 + c].wait()
        for start, size in blocks_of(q_cols, 512):
            cols = slice(start, start + size)
            term = jnp.dot(
                norm[:, c * step : (c + 1) * step],
                bq[c * step : (c + 1) * step, cols],
                preferred_element_type=f32,
            )
            if c:
                term = acc[:, cols] + term
            if c < chunks - 1:
                acc[:, cols] = term
            else:
                out[:, cols] = term.astype(out.dtype)


def project(at, tokens, gain, wq, wk, wv):
    rows, model = tokens.shape
    depth, q_cols = wq.shape
    kv_cols = wk.shape[1]
    chunks = max(1, min(8, depth // 256))
    return pl.pallas_call(
        lambda *refs: project_kernel(chunks, *refs),
        in_specs=[SMEM] + [HBM] * 5,
        out_specs=[VMEM, VMEM],
        out_shape=[
            jax.ShapeDtypeStruct((rows, q_cols + 2 * kv_cols), bf16),
            jax.ShapeDtypeStruct((rows, depth), bf16),
        ],
        scratch_shapes=[
            pltpu.VMEM((rows, model), bf16),
            pltpu.VMEM((model // LANES, LANES), f32),
            pltpu.VMEM((rows, depth), bf16),
            pltpu.VMEM(wq.shape, bf16),
            pltpu.VMEM(wk.shape, bf16),
            pltpu.VMEM(wv.shape, bf16),
            pltpu.VMEM((rows, q_cols), f32),
            pltpu.VMEM((model // LANES, LANES), bf16),
            pltpu.SemaphoreType.DMA((4 + chunks,)),
        ],
        compiler_params=params(16),
        cost_estimate=cost(rows, wq, wk, wv),
        name="project",
    )(at, in_hbm(tokens), in_hbm(gain.reshape(model // LANES, LANES)), in_hbm(wq), in_hbm(wk), in_hbm(wv))


def attend_kernel(n, at, cos, sin, cache, *rest):
    parts, (out, queries, total, stats_f) = rest[:n], rest[n:]
    rows, q_cols = queries.shape
    context, kv_cols = cache.shape[2:]
    kv_heads = kv_cols // HEAD_WIDTH
    heads = q_cols // HEAD_WIDTH
    group = heads // kv_heads
    tile = 2 * DRAFT_TOKENS
    requests = rows // DRAFT_TOKENS

    def length(r):
        return at[4 + r]

    def slot(r):
        return at[4 + requests + r]

    last = at[1]
    base = at[0] * context

    def column(c):
        return sum(p[:, lanes(c)].astype(f32) for p in parts)

    def rotated(x):
        return x * cos[...] + pltpu.roll(x, HEAD_WIDTH // 2, 1) * sin[...]

    for h in range(heads):
        queries[:, lanes(h)] = (rotated(column(h)) * HEAD_WIDTH ** (-0.5)).astype(bf16).astype(f32)
    new_keys = [rotated(column(heads + k)).astype(bf16) for k in range(kv_heads)]
    new_values = [column(heads + kv_heads + k).astype(bf16) for k in range(kv_heads)]

    high = group * tile
    row = lax.broadcasted_iota(jnp.int32, (high, 1), 0) % tile
    first = row < DRAFT_TOKENS
    position = lax.broadcasted_iota(jnp.int32, (high, context), 1) + base
    draft_col = lax.broadcasted_iota(jnp.int32, (high, rows), 1)
    lane = lax.broadcasted_iota(jnp.int32, (tile, LANES), 1)
    nt = (((1,), (1,)), ((), ()))
    for i in range(rows // tile):
        request = 2 * i
        limit = jnp.where(first, length(request), length(request + 1))
        live = position < limit
        own_at = tile * i + jnp.where(first, 0, DRAFT_TOKENS)
        seen = (draft_col >= own_at) & (draft_col <= tile * i + row) & (last > 0)
        stats = jnp.zeros((tile, LANES), f32)
        for k in range(kv_heads):
            q = jnp.concatenate(
                [queries[tile * i : tile * (i + 1), lanes(k * group + g)] for g in range(group)], axis=0
            ).astype(bf16)
            scores = [
                lax.dot_general(q, cache[0, slot(request + s), :, lanes(k)], nt, preferred_element_type=f32)
                for s in range(2)
            ]
            score = jnp.where(live, jnp.where(first, scores[0], scores[1]), neg_large)
            draft = lax.dot_general(q, new_keys[k], nt, preferred_element_type=f32)
            draft = jnp.where(seen, draft, neg_large)
            top = jnp.maximum(
                jnp.max(score, axis=1, keepdims=True), jnp.max(draft, axis=1, keepdims=True)
            )
            weight = jnp.where(live, jnp.exp(score - top), 0.0)
            draft_weight = jnp.where(seen, jnp.exp(draft - top), 0.0)
            mass = jnp.sum(weight, axis=1, keepdims=True) + jnp.sum(draft_weight, axis=1, keepdims=True)
            weight = weight.astype(bf16)
            sums = [
                jnp.dot(weight, cache[1, slot(request + s), :, lanes(k)], preferred_element_type=f32)
                for s in range(2)
            ]
            value = jnp.where(first, sums[0], sums[1]) + jnp.dot(
                draft_weight.astype(bf16), new_values[k], preferred_element_type=f32
            )
            some = mass > 0.0
            safe = jnp.where(some, mass, 1.0)
            value = value / safe
            lse = jnp.where(some, top + jnp.log(safe), neg_large)
            for g in range(group):
                at_rows = slice(tile * g, tile * (g + 1))
                total[tile * i : tile * (i + 1), lanes(k * group + g)] = value[at_rows]
                stats = jnp.where(lane == k * group + g, lse[at_rows], stats)
        stats_f[tile * i : tile * (i + 1), :] = stats
    out[:, :q_cols] = total[...].astype(bf16)
    for p, term in enumerate(thirds(stats_f[...])):
        out[:, q_cols + p * LANES : q_cols + (p + 1) * LANES] = term


def attend(at, cos, sin, cache, parts):
    rows, width = parts[0].shape
    q_cols = width - 2 * cache.shape[3]
    return pl.pallas_call(
        lambda *refs: attend_kernel(len(parts), *refs),
        in_specs=[SMEM] + [VMEM] * (3 + len(parts)),
        out_specs=VMEM,
        out_shape=jax.ShapeDtypeStruct((rows, q_cols + 3 * LANES), bf16),
        scratch_shapes=[
            pltpu.VMEM((rows, q_cols), f32),
            pltpu.VMEM((rows, q_cols), f32),
            pltpu.VMEM((rows, LANES), f32),
        ],
        compiler_params=params(6),
        cost_estimate=cost(rows, cache),
        name="attend",
    )(at, cos, sin, cache, *parts)


def joined(ref, start):
    return sum(ref[:, start + p * LANES : start + (p + 1) * LANES].astype(f32) for p in range(3))


def product(x, w, out, base, width):
    for start, size in blocks_of(width, 512):
        out[:, start : start + size] = jnp.dot(
            x[...], w[:, base + start : base + start + size], preferred_element_type=f32
        ).astype(out.dtype)


def output_first_kernel(n, w, *rest):
    values, (out, attended) = rest[:n], rest[n:]
    heads = attended.shape[1] // HEAD_WIDTH
    stats = [joined(v, attended.shape[1]) for v in values]
    top = stats[0]
    for s in stats[1:]:
        top = jnp.maximum(top, s)
    shares = [jnp.exp(s - top) for s in stats]
    whole = sum(shares)
    shares = [s / whole for s in shares]
    for h in range(heads):
        attended[:, lanes(h)] = sum(
            v[:, lanes(h)].astype(f32) * s[:, h : h + 1] for v, s in zip(values, shares)
        ).astype(bf16)
    product(attended, w, out, 0, out.shape[1])


def output_first(values, w):
    rows, half = values[0].shape[0], w.shape[1] // 2
    return pl.pallas_call(
        lambda *refs: output_first_kernel(len(values), *refs),
        in_specs=[VMEM] * (1 + len(values)),
        out_specs=[VMEM] * 2,
        out_shape=[
            jax.ShapeDtypeStruct((rows, half), bf16),
            jax.ShapeDtypeStruct((rows, w.shape[0]), bf16),
        ],
        compiler_params=params(4),
        cost_estimate=cost(rows, w),
        name="output_first",
    )(w, *values)


def output_second(attended, w):
    rows, half = attended.shape[0], w.shape[1] // 2
    return pl.pallas_call(
        lambda x, w, out: product(x, w, out, half, half),
        in_specs=[VMEM] * 2,
        out_specs=VMEM,
        out_shape=jax.ShapeDtypeStruct((rows, half), bf16),
        compiler_params=params(4),
        cost_estimate=cost(rows, w),
        name="output_second",
    )(attended, w)


WIDE = 256
AHEAD = 8


def half_of(at, sides, x, row, wg, wu, held, sems, prepare=None):
    half = wg.shape[1] // 2
    jobs = []
    for side, out, before in sides:
        for base, w in ((0, wg), (half, wu)):
            for start, size in blocks_of(half, WIDE):
                n = len(jobs)
                cols = pl.ds(pl.multiple_of(side * half + start, LANES), size)
                copy = pltpu.make_async_copy(
                    w.at[pl.ds(row, x.shape[1]), cols], held.at[n], sems.at[n]
                )
                jobs.append((copy, slice(base + start, base + start + size), out, before))
    for copy, *_ in jobs[:AHEAD]:
        copy.start()
    if prepare is not None:
        pl.when(at[2] >= 0)(prepare)
    for n, (copy, cols, out, before) in enumerate(jobs):
        copy.wait()
        if n + AHEAD < len(jobs):
            jobs[n + AHEAD][0].start()
        term = jnp.dot(x[...], held[n], preferred_element_type=f32)
        if before is not None:
            term = before[:, cols] + term
        out[:, cols] = term.astype(out.dtype)


def block_scratch(sides, count, half):
    blocks = blocks_of(half, WIDE)
    number = sides * 2 * len(blocks)
    return [pltpu.VMEM((number, count, blocks[0][1]), bf16), pltpu.SemaphoreType.DMA((number,))]


def residual(which, own, gain, parts, resid, x, gain_f):
    gain_f[...] = gain[...].astype(f32)
    count = resid.shape[1] // LANES
    square = jnp.zeros((own.shape[0], LANES), f32)
    for c in range(count):
        at = which * count + c
        value = own[:, lanes(at)].astype(f32) + sum(p[:, lanes(c)].astype(f32) for p in parts)
        value = value.astype(bf16).astype(f32)
        resid[:, lanes(c)] = value
        square = square + value * value
        x[:, lanes(c)] = (value * gain_f[at : at + 1, :]).astype(bf16)
    return square


def expand_first_kernel(n, at, own, gain, wg, wu, *rest):
    parts, (send, keep, resid, squares, x, gain_f, held, sems) = rest[:n], rest[n:]

    def prepare():
        squares[...] = residual(0, own, gain, parts, resid, x, gain_f)

    half_of(
        at, [(1 - at[2], send, None), (at[2], keep, None)], x, 0, wg, wu, held, sems, prepare
    )


def expand_first(at, own, gain, parts, wg, wu):
    rows, depth = own.shape
    width = wg.shape[1]
    return pl.pallas_call(
        lambda *refs: expand_first_kernel(len(parts), *refs),
        in_specs=[SMEM] + [VMEM] * 2 + [ANY] * 2 + [VMEM] * len(parts),
        out_specs=[VMEM] * 4,
        out_shape=[
            jax.ShapeDtypeStruct((rows, width), f32),
            jax.ShapeDtypeStruct((rows, width), f32),
            jax.ShapeDtypeStruct((rows, depth // 2), f32),
            jax.ShapeDtypeStruct((rows, LANES), f32),
        ],
        scratch_shapes=[
            pltpu.VMEM((rows, depth // 2), bf16),
            pltpu.VMEM((depth // LANES, LANES), f32),
        ]
        + block_scratch(2, depth // 2, width // 2),
        compiler_params=params(18),
        cost_estimate=cost(rows, wg, wu),
        name="expand_first",
    )(at, own, gain, wg, wu, *parts)


def expand_send_kernel(n, at, own, gain, before, squares, wg, wu, *rest):
    parts, (out, resid, x, gain_f, held, sems) = rest[:n], rest[n:]
    width = wu.shape[1]

    def prepare():
        square = squares[...] + residual(1, own, gain, parts, resid, x, gain_f)
        square = jnp.broadcast_to(jnp.sum(square, axis=1, keepdims=True), square.shape)
        for p, term in enumerate(thirds(square)):
            out[:, width + p * LANES : width + (p + 1) * LANES] = term

    half_of(at, [(1 - at[2], out, before)], x, x.shape[1], wg, wu, held, sems, prepare)


def expand_send(at, own, gain, parts, wg, wu, before, squares):
    rows, depth = own.shape
    return pl.pallas_call(
        lambda *refs: expand_send_kernel(len(parts), *refs),
        in_specs=[SMEM] + [VMEM] * 4 + [ANY] * 2 + [VMEM] * len(parts),
        out_specs=[VMEM] * 3,
        out_shape=[
            jax.ShapeDtypeStruct((rows, wu.shape[1] + 3 * LANES), bf16),
            jax.ShapeDtypeStruct((rows, depth // 2), f32),
            jax.ShapeDtypeStruct((rows, depth // 2), bf16),
        ],
        scratch_shapes=[pltpu.VMEM((depth // LANES, LANES), f32)]
        + block_scratch(1, depth // 2, wu.shape[1] // 2),
        compiler_params=params(10),
        cost_estimate=cost(rows, wu),
        name="expand_send",
    )(at, own, gain, before, squares, wg, wu, *parts)


def expand_keep_kernel(at, x, before, wg, wu, out, held, sems):
    half_of(at, [(at[2], out, before)], x, x.shape[1], wg, wu, held, sems)


def expand_keep(at, x, wg, wu, before):
    rows = x.shape[0]
    return pl.pallas_call(
        expand_keep_kernel,
        in_specs=[SMEM] + [VMEM] * 2 + [ANY] * 2,
        out_specs=VMEM,
        out_shape=jax.ShapeDtypeStruct((rows, wu.shape[1]), bf16),
        scratch_shapes=block_scratch(1, x.shape[1], wu.shape[1] // 2),
        compiler_params=params(10),
        cost_estimate=cost(rows, wu),
        name="expand_keep",
    )(at, x, before, wg, wu)


def pair_kernel(keep, received, stats, out):
    width = out.shape[1] - 3 * LANES
    for start, size in blocks_of(width, 512):
        cols = slice(start, start + size)
        out[:, cols] = (keep[:, cols].astype(f32) + received[:, cols].astype(f32)).astype(bf16)
    for p, term in enumerate(thirds(joined(stats, width) + joined(received, width))):
        out[:, width + p * LANES : width + (p + 1) * LANES] = term


def pair(keep, received, stats):
    return pl.pallas_call(
        pair_kernel,
        in_specs=[VMEM] * 3,
        out_specs=VMEM,
        out_shape=jax.ShapeDtypeStruct(received.shape, bf16),
        compiler_params=params(4),
        name="pair",
    )(keep, received, stats)


def gated_kernel(model, one, two, out):
    half = out.shape[1]
    scale = lax.rsqrt((joined(one, 2 * half) + joined(two, 2 * half)) / model + epsilon)
    for c in range(half // LANES):
        gate, up = (
            scale * (one[:, lanes(at)].astype(f32) + two[:, lanes(at)].astype(f32))
            for at in (c, half // LANES + c)
        )
        out[:, lanes(c)] = (gate / (1.0 + jnp.exp(-gate)) * up).astype(bf16)


def gated(model, one, two, after):
    rows, width = one.shape
    return pl.pallas_call(
        lambda _, *refs: gated_kernel(model, *refs),
        in_specs=[ANY] + [VMEM] * 2,
        out_specs=VMEM,
        out_shape=jax.ShapeDtypeStruct((rows, (width - 3 * LANES) // 2), bf16),
        compiler_params=params(4),
        name="gated",
    )(after, one, two)


def contract_kernel(hidden, w, out):
    for start, size in blocks_of(w.shape[1], 512):
        cols = slice(start, start + size)
        out[:, cols] = jnp.dot(hidden[...], w[:, cols], preferred_element_type=f32)


def contract(hidden, w):
    rows = hidden.shape[0]
    return pl.pallas_call(
        contract_kernel,
        in_specs=[VMEM] * 2,
        out_specs=VMEM,
        out_shape=jax.ShapeDtypeStruct((rows, w.shape[1]), f32),
        compiler_params=params(4),
        cost_estimate=cost(rows, w),
        name="contract",
    )(hidden, w)


def contract_last_kernel(n, at, hidden, w, before, resid_0, resid_1, own, *rest):
    sends, acc = rest[:-1], rest[-1]
    share = own.shape[0]
    for start, size in blocks_of(w.shape[1], 512):
        cols = slice(start, start + size)
        acc[:, cols] = before[:, cols] + jnp.dot(hidden[...], w[:, cols], preferred_element_type=f32)

    def block(ref, index):
        if share % 8 == 0:
            return ref[pl.ds(pl.multiple_of(index * share, share), share), :]
        chosen = ref[:share, :]
        for b in range(1, n):
            chosen = jnp.where(index == b, ref[b * share : (b + 1) * share, :], chosen)
        return chosen

    half = resid_0.shape[1]
    mine = block(acc, at[3])
    own[:, :half] = mine[:, :half] + block(resid_0, at[3])
    own[:, half:] = mine[:, half:] + block(resid_1, at[3])
    for s in range(1, n):
        sends[s - 1][...] = block(acc, at[3] ^ s).astype(bf16)


def contract_last(n, at, hidden, w, before, *resid):
    rows, cols = before.shape
    share = rows // n
    return pl.pallas_call(
        lambda *refs: contract_last_kernel(n, *refs),
        in_specs=[SMEM] + [VMEM] * 5,
        out_specs=[VMEM] * n,
        out_shape=[jax.ShapeDtypeStruct((share, cols), f32)]
        + [jax.ShapeDtypeStruct((share, cols), bf16)] * (n - 1),
        scratch_shapes=[pltpu.VMEM((rows, cols), f32)],
        compiler_params=params(4),
        cost_estimate=cost(rows, w),
        name="contract_last",
    )(at, hidden, w, before, *resid)


def add_kernel(one, two, out):
    for start, size in blocks_of(out.shape[1], 512):
        cols = slice(start, start + size)
        out[:, cols] = (one[:, cols].astype(f32) + two[:, cols].astype(f32)).astype(bf16)


def add(one, two):
    return pl.pallas_call(
        add_kernel,
        in_specs=[VMEM] * 2,
        out_specs=VMEM,
        out_shape=jax.ShapeDtypeStruct(one.shape, bf16),
        compiler_params=params(4),
        name="add",
    )(one, two)


def swap(x, axis, bit):
    n = lax.axis_size(axis)
    return lax.ppermute(x, axis, [(i, i ^ bit) for i in range(n)])


def bits_of(axis):
    n = lax.axis_size(axis)
    return [1 << b for b in range(n.bit_length() - 1)]


def gathered(x, axis, token=None):
    parts = [x]
    for bit in reversed(bits_of(axis)):
        parts = parts + [swap(p, axis, bit) for p in parts]
        if bit > 1 and token is not None:
            parts = parts[:-1] + [hold(parts[-1], token)]
    return parts


def summed(x, axis, order):
    *bits, last = bits_of(axis)[::order]
    for bit in bits:
        x = add(x, swap(x, axis, bit))
    return x, swap(x, axis, last)


def per_device(tokens, attn_gain, ffn_gain, w_query, key_matrix, value_matrix, w_out, w_gate, w_up, w_down, kv_cache, lengths, slots):
    rows, model = tokens.shape
    wide_at, head_at = lax.axis_index("wide"), lax.axis_index("head")
    wide_size, head_size = lax.axis_size("wide"), lax.axis_size("head")
    places = jnp.stack([wide_at, (wide_at == wide_size - 1).astype(jnp.int32), wide_at & 1, head_at])
    at = places.astype(jnp.int32)

    half = HEAD_WIDTH // 2
    positions = (
        jnp.broadcast_to(lengths[:, None], (lengths.shape[0], DRAFT_TOKENS))
        + jnp.arange(DRAFT_TOKENS, dtype=jnp.int32)[None, :]
    ).reshape(rows).astype(f32)
    exponent = jnp.arange(half, dtype=f32) * (2.0 / HEAD_WIDTH)
    angles = positions[:, None] * (theta_base ** (-exponent))[None, :]
    cos, sin = jnp.cos(angles), jnp.sin(angles)
    cos = jnp.concatenate([cos, cos], axis=1)
    sin = jnp.concatenate([-sin, sin], axis=1)

    qkv, own = project(at, tokens, attn_gain, w_query, key_matrix, value_matrix)
    depth = own.shape[1]
    half = depth // 2
    gain = ffn_gain.reshape(depth // LANES, LANES)

    flat_cache = kv_cache.reshape((-1,) + kv_cache.shape[2:])
    meta = jnp.concatenate([at, lengths, slots])
    cache, w_out, token = fetch(at, (qkv, meta, cos, sin), Part(flat_cache), Part(w_out))
    cache = cache.reshape(kv_cache.shape)
    value = attend(meta, cos, sin, cache, gathered(qkv, "wide", token))
    out_0, attended = output_first(gathered(value, "wide"), w_out)
    out_1 = output_second(attended, w_out)
    parts_0, parts_1 = summed(out_0, "head", 1), summed(out_1, "head", -1)
    send, keep, resid_0, squares = expand_first(at, own, gain, parts_0, w_gate, w_up)
    send, resid_1, x = expand_send(at, own, gain, parts_1, w_gate, w_up, send, squares)
    received = swap(send, "wide", 1)
    total = pair(expand_keep(at, x, w_gate, w_up, keep), received, send)
    down_own, down_other, token = fetch(at, total, Part(w_down, side=0), Part(w_down, side=1))
    for bit in bits_of("wide")[1:-1]:
        there = swap(total, "wide", bit)
        total = pair(total, there, total)
    hidden = gated(model, total, swap(total, "wide", bits_of("wide")[-1]), token)
    other = swap(hidden, "wide", 1)
    total, *sends = contract_last(
        head_size, at, other, down_other, contract(hidden, down_own), resid_0, resid_1
    )
    for s, send in enumerate(sends, 1):
        total = total + swap(send, "head", s).astype(f32)
    return total.astype(bf16)


def solution(mesh):
    in_specs = (
        P("grp", None),
        P(),
        P("wide"),
        P("wide", "head"),
        P("wide", "head"),
        P("wide", "head"),
        P("head", "wide"),
        P("wide", "head"),
        P("wide", "head"),
        P("head", "wide"),
        P(None, "grp", "wide", "head"),
        P("grp"),
        P("grp"),
    )
    out_specs = P(("grp", "head"), "wide")
    return jax.shard_map(
        per_device, mesh=mesh, in_specs=in_specs, out_specs=out_specs, check_vma=False
    )
```

```python
import math

import jax
import jax.numpy as jnp
from jax import lax
from jax.experimental import pallas as pl
from jax.experimental.pallas import tpu as pltpu
from jax.sharding import PartitionSpec as P

HEAD_WIDTH = 128
DRAFT_TOKENS = 4
LANES = 128
MIB = 1 << 20

epsilon = 1e-05
theta_base = 500000.0
neg_large = -1e30

f32 = jnp.float32
bf16 = jnp.bfloat16
ANY = pl.BlockSpec(memory_space=pl.ANY)
VMEM = pl.BlockSpec(memory_space=pltpu.VMEM)
SMEM = pl.BlockSpec(memory_space=pltpu.SMEM)
HBM = pl.BlockSpec(memory_space=pltpu.HBM)


def in_hbm(x):
    return pltpu.with_memory_space_constraint(x, pltpu.HBM)


def cost(rows, *weights):
    size = sum(w.size for w in weights)
    return pl.CostEstimate(flops=2 * rows * size, bytes_accessed=2 * size, transcendentals=0)


def params(mib):
    return pltpu.CompilerParams(vmem_limit_bytes=mib * MIB)


def blocks_of(width, most):
    step = max(b for b in range(LANES, most + 1, LANES) if width % b == 0)
    return [(at, step) for at in range(0, width, step)]


def thirds(x):
    high = x.astype(bf16)
    rest = x - high.astype(f32)
    middle = rest.astype(bf16)
    return high, middle, (rest - middle.astype(f32)).astype(bf16)


def lanes(at):
    return slice(at * LANES, (at + 1) * LANES)


PIECES = 8


class Part:
    def __init__(self, array, first=0, count=None, side=None):
        rows = array.shape[0]
        self.array, self.first, self.side = array, first, side
        self.count = rows // 2 if side is not None else rows if count is None else count
        self.shape = (self.count,) + array.shape[1:]
        self.out = pltpu.VMEM(self.shape, array.dtype)

    def copies(self, at, source, held, sems):
        step = max(1, self.count // PIECES)
        base = self.first
        if self.side is not None:
            base = pl.multiple_of((at[2] if self.side == 0 else 1 - at[2]) * self.count, LANES)
        return [
            pltpu.make_async_copy(
                source.at[pl.ds(base + p * step, step)], held.at[pl.ds(p * step, step)], sems.at[p]
            )
            for p in range(self.count // step)
        ]


def fetch_kernel(wanted, skip, at, *refs):
    n, refs = len(wanted), refs[skip:]
    sources, held, token, sems = refs[:n], refs[n : 2 * n], refs[2 * n], refs[2 * n + 1 :]
    copies = sum([w.copies(at, *refs) for w, *refs in zip(wanted, sources, held, sems)], [])
    for copy in copies:
        copy.start()
    token[...] = jnp.zeros_like(token)
    for copy in copies:
        copy.wait()


def fetch(at, after, *wanted):
    after = after if isinstance(after, (list, tuple)) else [after]
    size = sum(math.prod(w.shape) for w in wanted)
    return pl.pallas_call(
        lambda *refs: fetch_kernel(wanted, len(after), *refs),
        in_specs=[SMEM] + [ANY] * len(after) + [HBM] * len(wanted),
        out_specs=[VMEM] * (len(wanted) + 1),
        out_shape=[w.out for w in wanted] + [pltpu.VMEM((8, LANES), f32)],
        scratch_shapes=[pltpu.SemaphoreType.DMA((2 * PIECES,))] * len(wanted),
        compiler_params=params(2),
        cost_estimate=pl.CostEstimate(flops=0, bytes_accessed=4 * size, transcendentals=0),
        name="fetch",
    )(at, *after, *[in_hbm(w.array) for w in wanted])


def hold(x, token):
    return pl.pallas_call(
        lambda *_: None,
        in_specs=[VMEM, ANY],
        out_specs=VMEM,
        out_shape=jax.ShapeDtypeStruct(x.shape, x.dtype),
        input_output_aliases={0: 0},
        compiler_params=params(1),
        name="hold",
    )(x, token)


def project_kernel(chunks, at, tokens, gain, wq, wk, wv, out, own, tok, gain_f, norm, bq, bk, bv, acc, gain_b, sems):
    rows, model = tok.shape
    depth, q_cols = bq.shape
    kv_cols = bk.shape[1]
    step = depth // chunks
    gain_copy = pltpu.make_async_copy(gain, gain_b, sems.at[3 + chunks])
    gain_copy.start()
    copies = [
        pltpu.make_async_copy(tokens, tok, sems.at[0]),
        pltpu.make_async_copy(wk, bk, sems.at[1]),
        pltpu.make_async_copy(wv, bv, sems.at[2]),
    ] + [
        pltpu.make_async_copy(
            wq.at[pl.ds(c * step, step)], bq.at[pl.ds(c * step, step)], sems.at[3 + c]
        )
        for c in range(chunks)
    ]
    for copy in copies:
        copy.start()
    gain_copy.wait()
    gain_f[...] = gain_b[...].astype(f32)
    copies[0].wait()
    squares = jnp.zeros((rows, LANES), f32)
    for c in range(model // LANES):
        part = tok[:, lanes(c)].astype(f32)
        squares = squares + part * part
    scale = lax.rsqrt(jnp.sum(squares, axis=1, keepdims=True) / model + epsilon)
    count = depth // LANES
    for c in range(count):
        index = at[0] * count + c
        part = tok[:, pl.ds(pl.multiple_of(index * LANES, LANES), LANES)]
        own[:, lanes(c)] = part
        norm[:, lanes(c)] = (part.astype(f32) * scale * gain_f[pl.ds(index, 1), :]).astype(bf16)
    for copy, held, base in ((copies[1], bk, q_cols), (copies[2], bv, q_cols + kv_cols)):
        copy.wait()
        out[:, base : base + kv_cols] = jnp.dot(
            norm[...], held[...], preferred_element_type=f32
        ).astype(out.dtype)
    for c in range(chunks):
        copies[3 + c].wait()
        for start, size in blocks_of(q_cols, 512):
            cols = slice(start, start + size)
            term = jnp.dot(
                norm[:, c * step : (c + 1) * step],
                bq[c * step : (c + 1) * step, cols],
                preferred_element_type=f32,
            )
            if c:
                term = acc[:, cols] + term
            if c < chunks - 1:
                acc[:, cols] = term
            else:
                out[:, cols] = term.astype(out.dtype)


def project(at, tokens, gain, wq, wk, wv):
    rows, model = tokens.shape
    depth, q_cols = wq.shape
    kv_cols = wk.shape[1]
    chunks = max(1, min(8, depth // 256))
    return pl.pallas_call(
        lambda *refs: project_kernel(chunks, *refs),
        in_specs=[SMEM] + [HBM] * 5,
        out_specs=[VMEM, VMEM],
        out_shape=[
            jax.ShapeDtypeStruct((rows, q_cols + 2 * kv_cols), bf16),
            jax.ShapeDtypeStruct((rows, depth), bf16),
        ],
        scratch_shapes=[
            pltpu.VMEM((rows, model), bf16),
            pltpu.VMEM((model // LANES, LANES), f32),
            pltpu.VMEM((rows, depth), bf16),
            pltpu.VMEM(wq.shape, bf16),
            pltpu.VMEM(wk.shape, bf16),
            pltpu.VMEM(wv.shape, bf16),
            pltpu.VMEM((rows, q_cols), f32),
            pltpu.VMEM((model // LANES, LANES), bf16),
            pltpu.SemaphoreType.DMA((4 + chunks,)),
        ],
        compiler_params=params(16),
        cost_estimate=cost(rows, wq, wk, wv),
        name="project",
    )(at, in_hbm(tokens), in_hbm(gain.reshape(model // LANES, LANES)), in_hbm(wq), in_hbm(wk), in_hbm(wv))


def attend_kernel(n, at, cos, sin, cache, *rest):
    parts, (out, queries, total, stats_f) = rest[:n], rest[n:]
    rows, q_cols = queries.shape
    context, kv_cols = cache.shape[2:]
    kv_heads = kv_cols // HEAD_WIDTH
    heads = q_cols // HEAD_WIDTH
    group = heads // kv_heads
    tile = 2 * DRAFT_TOKENS
    requests = rows // DRAFT_TOKENS

    def length(r):
        return at[4 + r]

    def slot(r):
        return at[4 + requests + r]

    last = at[1]
    base = at[0] * context

    def column(c):
        return sum(p[:, lanes(c)].astype(f32) for p in parts)

    def rotated(x):
        return x * cos[...] + pltpu.roll(x, HEAD_WIDTH // 2, 1) * sin[...]

    for h in range(heads):
        queries[:, lanes(h)] = (rotated(column(h)) * HEAD_WIDTH ** (-0.5)).astype(bf16).astype(f32)
    new_keys = [rotated(column(heads + k)).astype(bf16) for k in range(kv_heads)]
    new_values = [column(heads + kv_heads + k).astype(bf16) for k in range(kv_heads)]

    high = group * tile
    row = lax.broadcasted_iota(jnp.int32, (high, 1), 0) % tile
    first = row < DRAFT_TOKENS
    position = lax.broadcasted_iota(jnp.int32, (high, context), 1) + base
    draft_col = lax.broadcasted_iota(jnp.int32, (high, rows), 1)
    lane = lax.broadcasted_iota(jnp.int32, (tile, LANES), 1)
    nt = (((1,), (1,)), ((), ()))
    for i in range(rows // tile):
        request = 2 * i
        limit = jnp.where(first, length(request), length(request + 1))
        live = position < limit
        own_at = tile * i + jnp.where(first, 0, DRAFT_TOKENS)
        seen = (draft_col >= own_at) & (draft_col <= tile * i + row) & (last > 0)
        stats = jnp.zeros((tile, LANES), f32)
        for k in range(kv_heads):
            q = jnp.concatenate(
                [queries[tile * i : tile * (i + 1), lanes(k * group + g)] for g in range(group)], axis=0
            ).astype(bf16)
            scores = [
                lax.dot_general(q, cache[0, slot(request + s), :, lanes(k)], nt, preferred_element_type=f32)
                for s in range(2)
            ]
            score = jnp.where(live, jnp.where(first, scores[0], scores[1]), neg_large)
            draft = lax.dot_general(q, new_keys[k], nt, preferred_element_type=f32)
            draft = jnp.where(seen, draft, neg_large)
            top = jnp.maximum(
                jnp.max(score, axis=1, keepdims=True), jnp.max(draft, axis=1, keepdims=True)
            )
            weight = jnp.where(live, jnp.exp(score - top), 0.0)
            draft_weight = jnp.where(seen, jnp.exp(draft - top), 0.0)
            mass = jnp.sum(weight, axis=1, keepdims=True) + jnp.sum(draft_weight, axis=1, keepdims=True)
            weight = weight.astype(bf16)
            sums = [
                jnp.dot(weight, cache[1, slot(request + s), :, lanes(k)], preferred_element_type=f32)
                for s in range(2)
            ]
            value = jnp.where(first, sums[0], sums[1]) + jnp.dot(
                draft_weight.astype(bf16), new_values[k], preferred_element_type=f32
            )
            some = mass > 0.0
            safe = jnp.where(some, mass, 1.0)
            value = value / safe
            lse = jnp.where(some, top + jnp.log(safe), neg_large)
            for g in range(group):
                at_rows = slice(tile * g, tile * (g + 1))
                total[tile * i : tile * (i + 1), lanes(k * group + g)] = value[at_rows]
                stats = jnp.where(lane == k * group + g, lse[at_rows], stats)
        stats_f[tile * i : tile * (i + 1), :] = stats
    out[:, :q_cols] = total[...].astype(bf16)
    for p, term in enumerate(thirds(stats_f[...])):
        out[:, q_cols + p * LANES : q_cols + (p + 1) * LANES] = term


def attend(at, cos, sin, cache, parts):
    rows, width = parts[0].shape
    q_cols = width - 2 * cache.shape[3]
    return pl.pallas_call(
        lambda *refs: attend_kernel(len(parts), *refs),
        in_specs=[SMEM] + [VMEM] * (3 + len(parts)),
        out_specs=VMEM,
        out_shape=jax.ShapeDtypeStruct((rows, q_cols + 3 * LANES), bf16),
        scratch_shapes=[
            pltpu.VMEM((rows, q_cols), f32),
            pltpu.VMEM((rows, q_cols), f32),
            pltpu.VMEM((rows, LANES), f32),
        ],
        compiler_params=params(6),
        cost_estimate=cost(rows, cache),
        name="attend",
    )(at, cos, sin, cache, *parts)


def joined(ref, start):
    return sum(ref[:, start + p * LANES : start + (p + 1) * LANES].astype(f32) for p in range(3))


def product(x, w, out, base, width):
    for start, size in blocks_of(width, 512):
        out[:, start : start + size] = jnp.dot(
            x[...], w[:, base + start : base + start + size], preferred_element_type=f32
        ).astype(out.dtype)


def output_first_kernel(n, w, *rest):
    values, (out, attended) = rest[:n], rest[n:]
    heads = attended.shape[1] // HEAD_WIDTH
    stats = [joined(v, attended.shape[1]) for v in values]
    top = stats[0]
    for s in stats[1:]:
        top = jnp.maximum(top, s)
    shares = [jnp.exp(s - top) for s in stats]
    whole = sum(shares)
    shares = [s / whole for s in shares]
    for h in range(heads):
        attended[:, lanes(h)] = sum(
            v[:, lanes(h)].astype(f32) * s[:, h : h + 1] for v, s in zip(values, shares)
        ).astype(bf16)
    product(attended, w, out, 0, out.shape[1])


def output_first(values, w):
    rows, half = values[0].shape[0], w.shape[1] // 2
    return pl.pallas_call(
        lambda *refs: output_first_kernel(len(values), *refs),
        in_specs=[VMEM] * (1 + len(values)),
        out_specs=[VMEM] * 2,
        out_shape=[
            jax.ShapeDtypeStruct((rows, half), bf16),
            jax.ShapeDtypeStruct((rows, w.shape[0]), bf16),
        ],
        compiler_params=params(4),
        cost_estimate=cost(rows, w),
        name="output_first",
    )(w, *values)


def output_second(attended, w):
    rows, half = attended.shape[0], w.shape[1] // 2
    return pl.pallas_call(
        lambda x, w, out: product(x, w, out, half, half),
        in_specs=[VMEM] * 2,
        out_specs=VMEM,
        out_shape=jax.ShapeDtypeStruct((rows, half), bf16),
        compiler_params=params(4),
        cost_estimate=cost(rows, w),
        name="output_second",
    )(attended, w)


def chunks_of(count):
    return max(1, min(4, count // 256))


def half_of(at, sides, x, row, weights, held, sems, prepare):
    count, half = x.shape[1], weights[0].shape[1] // 2
    chunks = chunks_of(count)
    step = count // chunks
    copies = [
        pltpu.make_async_copy(
            w.at[pl.ds(row + c * step, step)], h.at[pl.ds(c * step, step)], sems.at[i * chunks + c]
        )
        for i, (w, h) in enumerate(zip(weights, held))
        for c in range(chunks)
    ]
    for copy in copies[:chunks]:
        copy.start()
    pl.when(at[2] >= 0)(prepare)
    for n, copy in enumerate(copies):
        copy.wait()
        i, c = divmod(n, chunks)
        part = slice(c * step, (c + 1) * step)
        for side, out, total, before in sides:
            for start, size in blocks_of(half, 512):
                cols = pl.ds(pl.multiple_of(side * half + start, LANES), size)
                to = slice(i * half + start, i * half + start + size)
                term = jnp.dot(x[:, part], held[i][part, cols], preferred_element_type=f32)
                if c:
                    term = total[:, to] + term
                elif before is not None:
                    term = before[:, to] + term
                if c < chunks - 1:
                    total[:, to] = term
                else:
                    out[:, to] = term.astype(out.dtype)
        if n < chunks:
            copies[n + chunks].start()


def residual(which, own, gain, parts, resid, x, gain_f):
    gain_f[...] = gain[...].astype(f32)
    count = resid.shape[1] // LANES
    square = jnp.zeros((own.shape[0], LANES), f32)
    for c in range(count):
        at = which * count + c
        value = own[:, lanes(at)].astype(f32) + sum(p[:, lanes(c)].astype(f32) for p in parts)
        value = value.astype(bf16).astype(f32)
        resid[:, lanes(c)] = value
        square = square + value * value
        x[:, lanes(c)] = (value * gain_f[at : at + 1, :]).astype(bf16)
    return square


def expand_first_kernel(n, at, own, gain, wg, wu, *rest):
    parts, (send, keep, resid, squares, x, gain_f, held, sems) = rest[:n], rest[n:]

    def prepare():
        squares[...] = residual(0, own, gain, parts, resid, x, gain_f)

    sides = [(1 - at[2], send, send, None), (at[2], keep, keep, None)]
    half_of(at, sides, x, 0, (wg, wu), (held, held), sems, prepare)


def expand_first(at, own, gain, parts, wg, wu):
    rows, depth = own.shape
    width = wg.shape[1]
    return pl.pallas_call(
        lambda *refs: expand_first_kernel(len(parts), *refs),
        in_specs=[SMEM] + [VMEM] * 2 + [ANY] * 2 + [VMEM] * len(parts),
        out_specs=[VMEM] * 4,
        out_shape=[
            jax.ShapeDtypeStruct((rows, width), f32),
            jax.ShapeDtypeStruct((rows, width), f32),
            jax.ShapeDtypeStruct((rows, depth // 2), f32),
            jax.ShapeDtypeStruct((rows, LANES), f32),
        ],
        scratch_shapes=[
            pltpu.VMEM((rows, depth // 2), bf16),
            pltpu.VMEM((depth // LANES, LANES), f32),
            pltpu.VMEM((depth // 2, width), bf16),
            pltpu.SemaphoreType.DMA((2 * chunks_of(depth // 2),)),
        ],
        compiler_params=params(11),
        cost_estimate=cost(rows, wg, wu),
        name="expand_first",
    )(at, own, gain, wg, wu, *parts)


def expand_send_kernel(n, at, own, gain, before, squares, wg, wu, *rest):
    parts, (out, resid, x, hg, hu, gain_f, total, sems) = rest[:n], rest[n:]
    width = wu.shape[1]

    def prepare():
        square = squares[...] + residual(1, own, gain, parts, resid, x, gain_f)
        square = jnp.broadcast_to(jnp.sum(square, axis=1, keepdims=True), square.shape)
        for p, term in enumerate(thirds(square)):
            out[:, width + p * LANES : width + (p + 1) * LANES] = term

    sides = [(1 - at[2], out, total, before)]
    half_of(at, sides, x, x.shape[1], (wg, wu), (hg, hu), sems, prepare)


def expand_send(at, own, gain, parts, wg, wu, before, squares):
    rows, depth = own.shape
    width = wg.shape[1]
    return pl.pallas_call(
        lambda *refs: expand_send_kernel(len(parts), *refs),
        in_specs=[SMEM] + [VMEM] * 4 + [ANY] * 2 + [VMEM] * len(parts),
        out_specs=[VMEM] * 5,
        out_shape=[
            jax.ShapeDtypeStruct((rows, width + 3 * LANES), bf16),
            jax.ShapeDtypeStruct((rows, depth // 2), f32),
            jax.ShapeDtypeStruct((rows, depth // 2), bf16),
            pltpu.VMEM((depth // 2, width), bf16),
            pltpu.VMEM((depth // 2, width), bf16),
        ],
        scratch_shapes=[
            pltpu.VMEM((depth // LANES, LANES), f32),
            pltpu.VMEM((rows, width), f32),
            pltpu.SemaphoreType.DMA((2 * chunks_of(depth // 2),)),
        ],
        compiler_params=params(4),
        cost_estimate=cost(rows, wu),
        name="expand_send",
    )(at, own, gain, before, squares, wg, wu, *parts)


def expand_keep_kernel(at, x, before, wg, wu, out):
    half = wg.shape[1] // 2
    for base, w in ((0, wg), (half, wu)):
        for start, size in blocks_of(half, 512):
            cols = pl.ds(pl.multiple_of(at[2] * half + start, LANES), size)
            to = slice(base + start, base + start + size)
            term = before[:, to] + jnp.dot(x[...], w[:, cols], preferred_element_type=f32)
            out[:, to] = term.astype(out.dtype)


def expand_keep(at, x, wg, wu, before):
    rows = x.shape[0]
    return pl.pallas_call(
        expand_keep_kernel,
        in_specs=[SMEM] + [VMEM] * 4,
        out_specs=VMEM,
        out_shape=jax.ShapeDtypeStruct((rows, wu.shape[1]), bf16),
        compiler_params=params(4),
        cost_estimate=cost(rows, wu),
        name="expand_keep",
    )(at, x, before, wg, wu)


def pair_kernel(keep, received, stats, out):
    width = out.shape[1] - 3 * LANES
    for start, size in blocks_of(width, 512):
        cols = slice(start, start + size)
        out[:, cols] = (keep[:, cols].astype(f32) + received[:, cols].astype(f32)).astype(bf16)
    for p, term in enumerate(thirds(joined(stats, width) + joined(received, width))):
        out[:, width + p * LANES : width + (p + 1) * LANES] = term


def pair(keep, received, stats):
    return pl.pallas_call(
        pair_kernel,
        in_specs=[VMEM] * 3,
        out_specs=VMEM,
        out_shape=jax.ShapeDtypeStruct(received.shape, bf16),
        compiler_params=params(4),
        name="pair",
    )(keep, received, stats)


def gated_kernel(model, one, two, out):
    half = out.shape[1]
    scale = lax.rsqrt((joined(one, 2 * half) + joined(two, 2 * half)) / model + epsilon)
    for c in range(half // LANES):
        gate, up = (
            scale * (one[:, lanes(at)].astype(f32) + two[:, lanes(at)].astype(f32))
            for at in (c, half // LANES + c)
        )
        out[:, lanes(c)] = (gate / (1.0 + jnp.exp(-gate)) * up).astype(bf16)


def gated(model, one, two, after):
    rows, width = one.shape
    return pl.pallas_call(
        lambda _, *refs: gated_kernel(model, *refs),
        in_specs=[ANY] + [VMEM] * 2,
        out_specs=VMEM,
        out_shape=jax.ShapeDtypeStruct((rows, (width - 3 * LANES) // 2), bf16),
        compiler_params=params(4),
        name="gated",
    )(after, one, two)


def contract_kernel(hidden, w, out):
    for start, size in blocks_of(w.shape[1], 512):
        cols = slice(start, start + size)
        out[:, cols] = jnp.dot(hidden[...], w[:, cols], preferred_element_type=f32)


def contract(hidden, w):
    rows = hidden.shape[0]
    return pl.pallas_call(
        contract_kernel,
        in_specs=[VMEM] * 2,
        out_specs=VMEM,
        out_shape=jax.ShapeDtypeStruct((rows, w.shape[1]), f32),
        compiler_params=params(4),
        cost_estimate=cost(rows, w),
        name="contract",
    )(hidden, w)


def contract_last_kernel(n, at, hidden, w, before, resid_0, resid_1, own, *rest):
    sends, acc = rest[:-1], rest[-1]
    share = own.shape[0]
    for start, size in blocks_of(w.shape[1], 512):
        cols = slice(start, start + size)
        acc[:, cols] = before[:, cols] + jnp.dot(hidden[...], w[:, cols], preferred_element_type=f32)

    def block(ref, index):
        if share % 8 == 0:
            return ref[pl.ds(pl.multiple_of(index * share, share), share), :]
        chosen = ref[:share, :]
        for b in range(1, n):
            chosen = jnp.where(index == b, ref[b * share : (b + 1) * share, :], chosen)
        return chosen

    half = resid_0.shape[1]
    mine = block(acc, at[3])
    own[:, :half] = mine[:, :half] + block(resid_0, at[3])
    own[:, half:] = mine[:, half:] + block(resid_1, at[3])
    for s in range(1, n):
        sends[s - 1][...] = block(acc, at[3] ^ s).astype(bf16)


def contract_last(n, at, hidden, w, before, *resid):
    rows, cols = before.shape
    share = rows // n
    return pl.pallas_call(
        lambda *refs: contract_last_kernel(n, *refs),
        in_specs=[SMEM] + [VMEM] * 5,
        out_specs=[VMEM] * n,
        out_shape=[jax.ShapeDtypeStruct((share, cols), f32)]
        + [jax.ShapeDtypeStruct((share, cols), bf16)] * (n - 1),
        scratch_shapes=[pltpu.VMEM((rows, cols), f32)],
        compiler_params=params(4),
        cost_estimate=cost(rows, w),
        name="contract_last",
    )(at, hidden, w, before, *resid)


def add_kernel(one, two, out):
    for start, size in blocks_of(out.shape[1], 512):
        cols = slice(start, start + size)
        out[:, cols] = (one[:, cols].astype(f32) + two[:, cols].astype(f32)).astype(bf16)


def add(one, two):
    return pl.pallas_call(
        add_kernel,
        in_specs=[VMEM] * 2,
        out_specs=VMEM,
        out_shape=jax.ShapeDtypeStruct(one.shape, bf16),
        compiler_params=params(4),
        name="add",
    )(one, two)


def swap(x, axis, bit):
    n = lax.axis_size(axis)
    return lax.ppermute(x, axis, [(i, i ^ bit) for i in range(n)])


def bits_of(axis):
    n = lax.axis_size(axis)
    return [1 << b for b in range(n.bit_length() - 1)]


def gathered(x, axis, token=None):
    parts = [x]
    for bit in reversed(bits_of(axis)):
        parts = parts + [swap(p, axis, bit) for p in parts]
        if bit > 1 and token is not None:
            parts = parts[:-1] + [hold(parts[-1], token)]
    return parts


def summed(x, axis, order):
    *bits, last = bits_of(axis)[::order]
    for bit in bits:
        x = add(x, swap(x, axis, bit))
    return x, swap(x, axis, last)


def per_device(tokens, attn_gain, ffn_gain, w_query, key_matrix, value_matrix, w_out, w_gate, w_up, w_down, kv_cache, lengths, slots):
    rows, model = tokens.shape
    wide_at, head_at = lax.axis_index("wide"), lax.axis_index("head")
    wide_size, head_size = lax.axis_size("wide"), lax.axis_size("head")
    places = jnp.stack([wide_at, (wide_at == wide_size - 1).astype(jnp.int32), wide_at & 1, head_at])
    at = places.astype(jnp.int32)

    half = HEAD_WIDTH // 2
    positions = (
        jnp.broadcast_to(lengths[:, None], (lengths.shape[0], DRAFT_TOKENS))
        + jnp.arange(DRAFT_TOKENS, dtype=jnp.int32)[None, :]
    ).reshape(rows).astype(f32)
    exponent = jnp.arange(half, dtype=f32) * (2.0 / HEAD_WIDTH)
    angles = positions[:, None] * (theta_base ** (-exponent))[None, :]
    cos, sin = jnp.cos(angles), jnp.sin(angles)
    cos = jnp.concatenate([cos, cos], axis=1)
    sin = jnp.concatenate([-sin, sin], axis=1)

    qkv, own = project(at, tokens, attn_gain, w_query, key_matrix, value_matrix)
    depth = own.shape[1]
    half = depth // 2
    gain = ffn_gain.reshape(depth // LANES, LANES)

    flat_cache = kv_cache.reshape((-1,) + kv_cache.shape[2:])
    meta = jnp.concatenate([at, lengths, slots])
    cache, w_out, token = fetch(at, (qkv, meta, cos, sin), Part(flat_cache), Part(w_out))
    cache = cache.reshape(kv_cache.shape)
    value = attend(meta, cos, sin, cache, gathered(qkv, "wide", token))
    out_0, attended = output_first(gathered(value, "wide"), w_out)
    out_1 = output_second(attended, w_out)
    parts_0, parts_1 = summed(out_0, "head", 1), summed(out_1, "head", -1)
    send, keep, resid_0, squares = expand_first(at, own, gain, parts_0, w_gate, w_up)
    send, resid_1, x, gate_1, up_1 = expand_send(at, own, gain, parts_1, w_gate, w_up, send, squares)
    received = swap(send, "wide", 1)
    total = pair(expand_keep(at, x, gate_1, up_1, keep), received, send)
    down_own, down_other, token = fetch(at, total, Part(w_down, side=0), Part(w_down, side=1))
    for bit in bits_of("wide")[1:-1]:
        there = swap(total, "wide", bit)
        total = pair(total, there, total)
    hidden = gated(model, total, swap(total, "wide", bits_of("wide")[-1]), token)
    other = swap(hidden, "wide", 1)
    total, *sends = contract_last(
        head_size, at, other, down_other, contract(hidden, down_own), resid_0, resid_1
    )
    for s, send in enumerate(sends, 1):
        total = total + swap(send, "head", s).astype(f32)
    return total.astype(bf16)


def solution(mesh):
    in_specs = (
        P("grp", None),
        P(),
        P("wide"),
        P("wide", "head"),
        P("wide", "head"),
        P("wide", "head"),
        P("head", "wide"),
        P("wide", "head"),
        P("wide", "head"),
        P("head", "wide"),
        P(None, "grp", "wide", "head"),
        P("grp"),
        P("grp"),
    )
    out_specs = P(("grp", "head"), "wide")
    return jax.shard_map(
        per_device, mesh=mesh, in_specs=in_specs, out_specs=out_specs, check_vma=False
    )
```

```python
import math

import jax
import jax.numpy as jnp
from jax import lax
from jax.experimental import pallas as pl
from jax.experimental.pallas import tpu as pltpu
from jax.sharding import PartitionSpec as P

HEAD_WIDTH = 128
DRAFT_TOKENS = 4
LANES = 128
MIB = 1 << 20

epsilon = 1e-05
theta_base = 500000.0
neg_large = -1e30

f32 = jnp.float32
bf16 = jnp.bfloat16
ANY = pl.BlockSpec(memory_space=pl.ANY)
VMEM = pl.BlockSpec(memory_space=pltpu.VMEM)
SMEM = pl.BlockSpec(memory_space=pltpu.SMEM)
HBM = pl.BlockSpec(memory_space=pltpu.HBM)


def in_hbm(x):
    return pltpu.with_memory_space_constraint(x, pltpu.HBM)


def cost(rows, *weights):
    size = sum(w.size for w in weights)
    return pl.CostEstimate(flops=2 * rows * size, bytes_accessed=2 * size, transcendentals=0)


def params(mib):
    return pltpu.CompilerParams(vmem_limit_bytes=mib * MIB)


def blocks_of(width, most):
    step = max(b for b in range(LANES, most + 1, LANES) if width % b == 0)
    return [(at, step) for at in range(0, width, step)]


def thirds(x):
    high = x.astype(bf16)
    rest = x - high.astype(f32)
    middle = rest.astype(bf16)
    return high, middle, (rest - middle.astype(f32)).astype(bf16)


def lanes(at):
    return slice(at * LANES, (at + 1) * LANES)


PIECES = 8


class Part:
    def __init__(self, array, first=0, count=None, side=None):
        rows = array.shape[0]
        self.array, self.first, self.side = array, first, side
        self.count = rows // 2 if side is not None else rows if count is None else count
        self.shape = (self.count,) + array.shape[1:]
        self.out = pltpu.VMEM(self.shape, array.dtype)

    def copies(self, at, source, held, sems):
        step = max(1, self.count // PIECES)
        base = self.first
        if self.side is not None:
            base = pl.multiple_of((at[2] if self.side == 0 else 1 - at[2]) * self.count, LANES)
        return [
            pltpu.make_async_copy(
                source.at[pl.ds(base + p * step, step)], held.at[pl.ds(p * step, step)], sems.at[p]
            )
            for p in range(self.count // step)
        ]


def fetch_kernel(wanted, skip, at, *refs):
    n, refs = len(wanted), refs[skip:]
    sources, held, token, sems = refs[:n], refs[n : 2 * n], refs[2 * n], refs[2 * n + 1 :]
    copies = sum([w.copies(at, *refs) for w, *refs in zip(wanted, sources, held, sems)], [])
    for copy in copies:
        copy.start()
    token[...] = jnp.zeros_like(token)
    for copy in copies:
        copy.wait()


def fetch(at, after, *wanted):
    after = after if isinstance(after, (list, tuple)) else [after]
    size = sum(math.prod(w.shape) for w in wanted)
    return pl.pallas_call(
        lambda *refs: fetch_kernel(wanted, len(after), *refs),
        in_specs=[SMEM] + [ANY] * len(after) + [HBM] * len(wanted),
        out_specs=[VMEM] * (len(wanted) + 1),
        out_shape=[w.out for w in wanted] + [pltpu.VMEM((8, LANES), f32)],
        scratch_shapes=[pltpu.SemaphoreType.DMA((2 * PIECES,))] * len(wanted),
        compiler_params=params(2),
        cost_estimate=pl.CostEstimate(flops=0, bytes_accessed=4 * size, transcendentals=0),
        name="fetch",
    )(at, *after, *[in_hbm(w.array) for w in wanted])


def hold(x, token):
    return pl.pallas_call(
        lambda *_: None,
        in_specs=[VMEM, ANY],
        out_specs=VMEM,
        out_shape=jax.ShapeDtypeStruct(x.shape, x.dtype),
        input_output_aliases={0: 0},
        compiler_params=params(1),
        name="hold",
    )(x, token)


def project_kernel(chunks, at, tokens, gain, wq, wk, wv, out, own, tok, gain_f, norm, bq, bk, bv, acc, gain_b, sems):
    rows, model = tok.shape
    depth, q_cols = bq.shape
    kv_cols = bk.shape[1]
    step = depth // chunks
    gain_copy = pltpu.make_async_copy(gain, gain_b, sems.at[3 + chunks])
    gain_copy.start()
    copies = [
        pltpu.make_async_copy(tokens, tok, sems.at[0]),
        pltpu.make_async_copy(wk, bk, sems.at[1]),
        pltpu.make_async_copy(wv, bv, sems.at[2]),
    ] + [
        pltpu.make_async_copy(
            wq.at[pl.ds(c * step, step)], bq.at[pl.ds(c * step, step)], sems.at[3 + c]
        )
        for c in range(chunks)
    ]
    for copy in copies:
        copy.start()
    gain_copy.wait()
    gain_f[...] = gain_b[...].astype(f32)
    copies[0].wait()
    squares = jnp.zeros((rows, LANES), f32)
    for c in range(model // LANES):
        part = tok[:, lanes(c)].astype(f32)
        squares = squares + part * part
    scale = lax.rsqrt(jnp.sum(squares, axis=1, keepdims=True) / model + epsilon)
    count = depth // LANES
    for c in range(count):
        index = at[0] * count + c
        part = tok[:, pl.ds(pl.multiple_of(index * LANES, LANES), LANES)]
        own[:, lanes(c)] = part
        norm[:, lanes(c)] = (part.astype(f32) * scale * gain_f[pl.ds(index, 1), :]).astype(bf16)
    for copy, held, base in ((copies[1], bk, q_cols), (copies[2], bv, q_cols + kv_cols)):
        copy.wait()
        out[:, base : base + kv_cols] = jnp.dot(
            norm[...], held[...], preferred_element_type=f32
        ).astype(out.dtype)
    for c in range(chunks):
        copies[3 + c].wait()
        for start, size in blocks_of(q_cols, 512):
            cols = slice(start, start + size)
            term = jnp.dot(
                norm[:, c * step : (c + 1) * step],
                bq[c * step : (c + 1) * step, cols],
                preferred_element_type=f32,
            )
            if c:
                term = acc[:, cols] + term
            if c < chunks - 1:
                acc[:, cols] = term
            else:
                out[:, cols] = term.astype(out.dtype)


def project(at, tokens, gain, wq, wk, wv):
    rows, model = tokens.shape
    depth, q_cols = wq.shape
    kv_cols = wk.shape[1]
    chunks = max(1, min(8, depth // 256))
    return pl.pallas_call(
        lambda *refs: project_kernel(chunks, *refs),
        in_specs=[SMEM] + [HBM] * 5,
        out_specs=[VMEM, VMEM],
        out_shape=[
            jax.ShapeDtypeStruct((rows, q_cols + 2 * kv_cols), bf16),
            jax.ShapeDtypeStruct((rows, depth), bf16),
        ],
        scratch_shapes=[
            pltpu.VMEM((rows, model), bf16),
            pltpu.VMEM((model // LANES, LANES), f32),
            pltpu.VMEM((rows, depth), bf16),
            pltpu.VMEM(wq.shape, bf16),
            pltpu.VMEM(wk.shape, bf16),
            pltpu.VMEM(wv.shape, bf16),
            pltpu.VMEM((rows, q_cols), f32),
            pltpu.VMEM((model // LANES, LANES), bf16),
            pltpu.SemaphoreType.DMA((4 + chunks,)),
        ],
        compiler_params=params(16),
        cost_estimate=cost(rows, wq, wk, wv),
        name="project",
    )(at, in_hbm(tokens), in_hbm(gain.reshape(model // LANES, LANES)), in_hbm(wq), in_hbm(wk), in_hbm(wv))


def attend_kernel(n, at, cos, sin, cache, *rest):
    parts, (out, queries, total, stats_f) = rest[:n], rest[n:]
    rows, q_cols = queries.shape
    context, kv_cols = cache.shape[2:]
    kv_heads = kv_cols // HEAD_WIDTH
    heads = q_cols // HEAD_WIDTH
    group = heads // kv_heads
    tile = 2 * DRAFT_TOKENS
    requests = rows // DRAFT_TOKENS

    def length(r):
        return at[4 + r]

    def slot(r):
        return at[4 + requests + r]

    last = at[1]
    base = at[0] * context

    def column(c):
        return sum(p[:, lanes(c)].astype(f32) for p in parts)

    def rotated(x):
        return x * cos[...] + pltpu.roll(x, HEAD_WIDTH // 2, 1) * sin[...]

    for h in range(heads):
        queries[:, lanes(h)] = (rotated(column(h)) * HEAD_WIDTH ** (-0.5)).astype(bf16).astype(f32)
    new_keys = [rotated(column(heads + k)).astype(bf16) for k in range(kv_heads)]
    new_values = [column(heads + kv_heads + k).astype(bf16) for k in range(kv_heads)]

    high = group * tile
    row = lax.broadcasted_iota(jnp.int32, (high, 1), 0) % tile
    first = row < DRAFT_TOKENS
    position = lax.broadcasted_iota(jnp.int32, (high, context), 1) + base
    draft_col = lax.broadcasted_iota(jnp.int32, (high, rows), 1)
    lane = lax.broadcasted_iota(jnp.int32, (tile, LANES), 1)
    nt = (((1,), (1,)), ((), ()))
    for i in range(rows // tile):
        request = 2 * i
        limit = jnp.where(first, length(request), length(request + 1))
        live = position < limit
        own_at = tile * i + jnp.where(first, 0, DRAFT_TOKENS)
        seen = (draft_col >= own_at) & (draft_col <= tile * i + row) & (last > 0)
        stats = jnp.zeros((tile, LANES), f32)
        for k in range(kv_heads):
            q = jnp.concatenate(
                [queries[tile * i : tile * (i + 1), lanes(k * group + g)] for g in range(group)], axis=0
            ).astype(bf16)
            scores = [
                lax.dot_general(q, cache[0, slot(request + s), :, lanes(k)], nt, preferred_element_type=f32)
                for s in range(2)
            ]
            score = jnp.where(live, jnp.where(first, scores[0], scores[1]), neg_large)
            draft = lax.dot_general(q, new_keys[k], nt, preferred_element_type=f32)
            draft = jnp.where(seen, draft, neg_large)
            top = jnp.maximum(
                jnp.max(score, axis=1, keepdims=True), jnp.max(draft, axis=1, keepdims=True)
            )
            weight = jnp.where(live, jnp.exp(score - top), 0.0)
            draft_weight = jnp.where(seen, jnp.exp(draft - top), 0.0)
            mass = jnp.sum(weight, axis=1, keepdims=True) + jnp.sum(draft_weight, axis=1, keepdims=True)
            weight = weight.astype(bf16)
            sums = [
                jnp.dot(weight, cache[1, slot(request + s), :, lanes(k)], preferred_element_type=f32)
                for s in range(2)
            ]
            value = jnp.where(first, sums[0], sums[1]) + jnp.dot(
                draft_weight.astype(bf16), new_values[k], preferred_element_type=f32
            )
            some = mass > 0.0
            safe = jnp.where(some, mass, 1.0)
            value = value / safe
            lse = jnp.where(some, top + jnp.log(safe), neg_large)
            for g in range(group):
                at_rows = slice(tile * g, tile * (g + 1))
                total[tile * i : tile * (i + 1), lanes(k * group + g)] = value[at_rows]
                stats = jnp.where(lane == k * group + g, lse[at_rows], stats)
        stats_f[tile * i : tile * (i + 1), :] = stats
    out[:, :q_cols] = total[...].astype(bf16)
    for p, term in enumerate(thirds(stats_f[...])):
        out[:, q_cols + p * LANES : q_cols + (p + 1) * LANES] = term


def attend(at, cos, sin, cache, parts):
    rows, width = parts[0].shape
    q_cols = width - 2 * cache.shape[3]
    return pl.pallas_call(
        lambda *refs: attend_kernel(len(parts), *refs),
        in_specs=[SMEM] + [VMEM] * (3 + len(parts)),
        out_specs=VMEM,
        out_shape=jax.ShapeDtypeStruct((rows, q_cols + 3 * LANES), bf16),
        scratch_shapes=[
            pltpu.VMEM((rows, q_cols), f32),
            pltpu.VMEM((rows, q_cols), f32),
            pltpu.VMEM((rows, LANES), f32),
        ],
        compiler_params=params(6),
        cost_estimate=cost(rows, cache),
        name="attend",
    )(at, cos, sin, cache, *parts)


def joined(ref, start):
    return sum(ref[:, start + p * LANES : start + (p + 1) * LANES].astype(f32) for p in range(3))


def product(x, w, out, base, width):
    for start, size in blocks_of(width, 512):
        out[:, start : start + size] = jnp.dot(
            x[...], w[:, base + start : base + start + size], preferred_element_type=f32
        ).astype(out.dtype)


def output_first_kernel(n, w, *rest):
    values, (out, attended) = rest[:n], rest[n:]
    heads = attended.shape[1] // HEAD_WIDTH
    stats = [joined(v, attended.shape[1]) for v in values]
    top = stats[0]
    for s in stats[1:]:
        top = jnp.maximum(top, s)
    shares = [jnp.exp(s - top) for s in stats]
    whole = sum(shares)
    shares = [s / whole for s in shares]
    for h in range(heads):
        attended[:, lanes(h)] = sum(
            v[:, lanes(h)].astype(f32) * s[:, h : h + 1] for v, s in zip(values, shares)
        ).astype(bf16)
    product(attended, w, out, 0, out.shape[1])


def output_first(values, w):
    rows, half = values[0].shape[0], w.shape[1] // 2
    return pl.pallas_call(
        lambda *refs: output_first_kernel(len(values), *refs),
        in_specs=[VMEM] * (1 + len(values)),
        out_specs=[VMEM] * 2,
        out_shape=[
            jax.ShapeDtypeStruct((rows, half), bf16),
            jax.ShapeDtypeStruct((rows, w.shape[0]), bf16),
        ],
        compiler_params=params(4),
        cost_estimate=cost(rows, w),
        name="output_first",
    )(w, *values)


def output_second(attended, w):
    rows, half = attended.shape[0], w.shape[1] // 2
    return pl.pallas_call(
        lambda x, w, out: product(x, w, out, half, half),
        in_specs=[VMEM] * 2,
        out_specs=VMEM,
        out_shape=jax.ShapeDtypeStruct((rows, half), bf16),
        compiler_params=params(4),
        cost_estimate=cost(rows, w),
        name="output_second",
    )(attended, w)


def side_of(side, x, w, base, out, before=None):
    half = w.shape[1] // 2
    for start, size in blocks_of(half, 512):
        cols = pl.ds(pl.multiple_of(side * half + start, LANES), size)
        to = slice(base + start, base + start + size)
        term = jnp.dot(x[...], w[:, cols], preferred_element_type=f32)
        if before is not None:
            term = before[:, to] + term
        out[:, to] = term.astype(out.dtype)


def residual(which, own, gain, parts, resid, x, gain_f):
    gain_f[...] = gain[...].astype(f32)
    count = resid.shape[1] // LANES
    square = jnp.zeros((own.shape[0], LANES), f32)
    for c in range(count):
        at = which * count + c
        value = own[:, lanes(at)].astype(f32) + sum(p[:, lanes(c)].astype(f32) for p in parts)
        value = value.astype(bf16).astype(f32)
        resid[:, lanes(c)] = value
        square = square + value * value
        x[:, lanes(c)] = (value * gain_f[at : at + 1, :]).astype(bf16)
    return square


def expand_first_kernel(n, parts_of, at, own, gain, wu, *rest):
    sources, parts, (send, keep, resid, squares, up, wg, x, gain_f, *sems) = rest[:2], rest[2 : 2 + n], rest[2 + n :]
    gate_copies, up_copies = (
        p.copies(at, source, held, sem) for p, source, held, sem in zip(parts_of, sources, (wg, up), sems)
    )
    sides = ((1 - at[2], send), (at[2], keep))
    half = wu.shape[1] // 2
    for copy in gate_copies + up_copies:
        copy.start()

    @pl.when(at[2] >= 0)
    def _():
        squares[...] = residual(0, own, gain, parts, resid, x, gain_f)
        for side, out in sides:
            side_of(side, x, wu, half, out)

    for copy in gate_copies:
        copy.wait()
    for side, out in sides:
        side_of(side, x, wg, 0, out)
    for copy in up_copies:
        copy.wait()


def expand_first(at, own, gain, parts, gate, wu, up):
    rows, depth = own.shape
    width = wu.shape[1]
    return pl.pallas_call(
        lambda *refs: expand_first_kernel(len(parts), (gate, up), *refs),
        in_specs=[SMEM] + [VMEM] * 3 + [ANY, HBM] + [VMEM] * len(parts),
        out_specs=[VMEM] * 5,
        out_shape=[
            jax.ShapeDtypeStruct((rows, width), f32),
            jax.ShapeDtypeStruct((rows, width), f32),
            jax.ShapeDtypeStruct((rows, depth // 2), f32),
            jax.ShapeDtypeStruct((rows, LANES), f32),
            up.out,
        ],
        scratch_shapes=[
            pltpu.VMEM(gate.shape, bf16),
            pltpu.VMEM((rows, depth // 2), bf16),
            pltpu.VMEM((depth // LANES, LANES), f32),
            pltpu.SemaphoreType.DMA((2 * PIECES,)),
            pltpu.SemaphoreType.DMA((2 * PIECES,)),
        ],
        compiler_params=params(11),
        cost_estimate=cost(rows, wu, wu),
        name="expand_first",
    )(at, own, gain, wu, gate.array, in_hbm(up.array), *parts)


def expand_send_kernel(n, gate, at, own, gain, before, squares, wu, source, *rest):
    parts, (out, resid, x, wg, gain_f, sems) = rest[:n], rest[n:]
    side, width = 1 - at[2], wu.shape[1]
    copies = gate.copies(at, source, wg, sems)
    for copy in copies:
        copy.start()

    @pl.when(at[2] >= 0)
    def _():
        square = squares[...] + residual(1, own, gain, parts, resid, x, gain_f)
        square = jnp.broadcast_to(jnp.sum(square, axis=1, keepdims=True), square.shape)
        for p, term in enumerate(thirds(square)):
            out[:, width + p * LANES : width + (p + 1) * LANES] = term
        side_of(side, x, wu, width // 2, out, before)

    for copy in copies:
        copy.wait()
    side_of(side, x, wg, 0, out, before)


def expand_send(at, own, gain, parts, gate, wu, before, squares):
    rows, depth = own.shape
    width = wu.shape[1]
    return pl.pallas_call(
        lambda *refs: expand_send_kernel(len(parts), gate, *refs),
        in_specs=[SMEM] + [VMEM] * 5 + [ANY] + [VMEM] * len(parts),
        out_specs=[VMEM] * 4,
        out_shape=[
            jax.ShapeDtypeStruct((rows, width + 3 * LANES), bf16),
            jax.ShapeDtypeStruct((rows, depth // 2), f32),
            jax.ShapeDtypeStruct((rows, depth // 2), bf16),
            gate.out,
        ],
        scratch_shapes=[
            pltpu.VMEM((depth // LANES, LANES), f32),
            pltpu.SemaphoreType.DMA((2 * PIECES,)),
        ],
        compiler_params=params(4),
        cost_estimate=cost(rows, wu),
        name="expand_send",
    )(at, own, gain, before, squares, wu, gate.array, *parts)


def expand_keep_kernel(at, x, before, wg, wu, out):
    side_of(at[2], x, wg, 0, out, before)
    side_of(at[2], x, wu, wu.shape[1] // 2, out, before)


def expand_keep(at, x, wg, wu, before):
    rows = x.shape[0]
    return pl.pallas_call(
        expand_keep_kernel,
        in_specs=[SMEM] + [VMEM] * 4,
        out_specs=VMEM,
        out_shape=jax.ShapeDtypeStruct((rows, wu.shape[1]), bf16),
        compiler_params=params(4),
        cost_estimate=cost(rows, wu),
        name="expand_keep",
    )(at, x, before, wg, wu)


def pair_kernel(keep, received, stats, out):
    width = out.shape[1] - 3 * LANES
    for start, size in blocks_of(width, 512):
        cols = slice(start, start + size)
        out[:, cols] = (keep[:, cols].astype(f32) + received[:, cols].astype(f32)).astype(bf16)
    for p, term in enumerate(thirds(joined(stats, width) + joined(received, width))):
        out[:, width + p * LANES : width + (p + 1) * LANES] = term


def pair(keep, received, stats):
    return pl.pallas_call(
        pair_kernel,
        in_specs=[VMEM] * 3,
        out_specs=VMEM,
        out_shape=jax.ShapeDtypeStruct(received.shape, bf16),
        compiler_params=params(4),
        name="pair",
    )(keep, received, stats)


def gated_kernel(model, one, two, out):
    half = out.shape[1]
    scale = lax.rsqrt((joined(one, 2 * half) + joined(two, 2 * half)) / model + epsilon)
    for c in range(half // LANES):
        gate, up = (
            scale * (one[:, lanes(at)].astype(f32) + two[:, lanes(at)].astype(f32))
            for at in (c, half // LANES + c)
        )
        out[:, lanes(c)] = (gate / (1.0 + jnp.exp(-gate)) * up).astype(bf16)


def gated(model, one, two, after):
    rows, width = one.shape
    return pl.pallas_call(
        lambda _, *refs: gated_kernel(model, *refs),
        in_specs=[ANY] + [VMEM] * 2,
        out_specs=VMEM,
        out_shape=jax.ShapeDtypeStruct((rows, (width - 3 * LANES) // 2), bf16),
        compiler_params=params(4),
        name="gated",
    )(after, one, two)


def contract_kernel(hidden, w, out):
    for start, size in blocks_of(w.shape[1], 512):
        cols = slice(start, start + size)
        out[:, cols] = jnp.dot(hidden[...], w[:, cols], preferred_element_type=f32)


def contract(hidden, w):
    rows = hidden.shape[0]
    return pl.pallas_call(
        contract_kernel,
        in_specs=[VMEM] * 2,
        out_specs=VMEM,
        out_shape=jax.ShapeDtypeStruct((rows, w.shape[1]), f32),
        compiler_params=params(4),
        cost_estimate=cost(rows, w),
        name="contract",
    )(hidden, w)


def contract_last_kernel(n, at, hidden, w, before, resid_0, resid_1, own, *rest):
    sends, acc = rest[:-1], rest[-1]
    share = own.shape[0]
    for start, size in blocks_of(w.shape[1], 512):
        cols = slice(start, start + size)
        acc[:, cols] = before[:, cols] + jnp.dot(hidden[...], w[:, cols], preferred_element_type=f32)

    def block(ref, index):
        if share % 8 == 0:
            return ref[pl.ds(pl.multiple_of(index * share, share), share), :]
        chosen = ref[:share, :]
        for b in range(1, n):
            chosen = jnp.where(index == b, ref[b * share : (b + 1) * share, :], chosen)
        return chosen

    half = resid_0.shape[1]
    mine = block(acc, at[3])
    own[:, :half] = mine[:, :half] + block(resid_0, at[3])
    own[:, half:] = mine[:, half:] + block(resid_1, at[3])
    for s in range(1, n):
        sends[s - 1][...] = block(acc, at[3] ^ s).astype(bf16)


def contract_last(n, at, hidden, w, before, *resid):
    rows, cols = before.shape
    share = rows // n
    return pl.pallas_call(
        lambda *refs: contract_last_kernel(n, *refs),
        in_specs=[SMEM] + [VMEM] * 5,
        out_specs=[VMEM] * n,
        out_shape=[jax.ShapeDtypeStruct((share, cols), f32)]
        + [jax.ShapeDtypeStruct((share, cols), bf16)] * (n - 1),
        scratch_shapes=[pltpu.VMEM((rows, cols), f32)],
        compiler_params=params(4),
        cost_estimate=cost(rows, w),
        name="contract_last",
    )(at, hidden, w, before, *resid)


def add_kernel(one, two, out):
    for start, size in blocks_of(out.shape[1], 512):
        cols = slice(start, start + size)
        out[:, cols] = (one[:, cols].astype(f32) + two[:, cols].astype(f32)).astype(bf16)


def add(one, two):
    return pl.pallas_call(
        add_kernel,
        in_specs=[VMEM] * 2,
        out_specs=VMEM,
        out_shape=jax.ShapeDtypeStruct(one.shape, bf16),
        compiler_params=params(4),
        name="add",
    )(one, two)


def swap(x, axis, bit):
    n = lax.axis_size(axis)
    return lax.ppermute(x, axis, [(i, i ^ bit) for i in range(n)])


def bits_of(axis):
    n = lax.axis_size(axis)
    return [1 << b for b in range(n.bit_length() - 1)]


def gathered(x, axis, token=None):
    parts = [x]
    for bit in reversed(bits_of(axis)):
        parts = parts + [swap(p, axis, bit) for p in parts]
        if bit > 1 and token is not None:
            parts = parts[:-1] + [hold(parts[-1], token)]
    return parts


def summed(x, axis, order):
    *bits, last = bits_of(axis)[::order]
    for bit in bits:
        x = add(x, swap(x, axis, bit))
    return x, swap(x, axis, last)


def per_device(tokens, attn_gain, ffn_gain, w_query, key_matrix, value_matrix, w_out, w_gate, w_up, w_down, kv_cache, lengths, slots):
    rows, model = tokens.shape
    wide_at, head_at = lax.axis_index("wide"), lax.axis_index("head")
    wide_size, head_size = lax.axis_size("wide"), lax.axis_size("head")
    places = jnp.stack([wide_at, (wide_at == wide_size - 1).astype(jnp.int32), wide_at & 1, head_at])
    at = places.astype(jnp.int32)

    half = HEAD_WIDTH // 2
    positions = (
        jnp.broadcast_to(lengths[:, None], (lengths.shape[0], DRAFT_TOKENS))
        + jnp.arange(DRAFT_TOKENS, dtype=jnp.int32)[None, :]
    ).reshape(rows).astype(f32)
    exponent = jnp.arange(half, dtype=f32) * (2.0 / HEAD_WIDTH)
    angles = positions[:, None] * (theta_base ** (-exponent))[None, :]
    cos, sin = jnp.cos(angles), jnp.sin(angles)
    cos = jnp.concatenate([cos, cos], axis=1)
    sin = jnp.concatenate([-sin, sin], axis=1)

    qkv, own = project(at, tokens, attn_gain, w_query, key_matrix, value_matrix)
    depth = own.shape[1]
    half = depth // 2
    gain = ffn_gain.reshape(depth // LANES, LANES)

    flat_cache = kv_cache.reshape((-1,) + kv_cache.shape[2:])
    meta = jnp.concatenate([at, lengths, slots])
    cache, w_out, token = fetch(at, (qkv, meta, cos, sin), Part(flat_cache), Part(w_out))
    cache = cache.reshape(kv_cache.shape)
    value = attend(meta, cos, sin, cache, gathered(qkv, "wide", token))
    up_0, token = fetch(at, value, Part(w_up, 0, half))
    out_0, attended = output_first(gathered(value, "wide", token), w_out)
    out_1 = output_second(attended, w_out)
    parts_0, parts_1 = summed(out_0, "head", 1), summed(out_1, "head", -1)
    send, keep, resid_0, squares, up_1 = expand_first(
        at, own, gain, parts_0, Part(w_gate, 0, half), up_0, Part(w_up, half, half)
    )
    send, resid_1, x, gate_1 = expand_send(
        at, own, gain, parts_1, Part(w_gate, half, half), up_1, send, squares
    )
    received = swap(send, "wide", 1)
    total = pair(expand_keep(at, x, gate_1, up_1, keep), received, send)
    down_own, down_other, token = fetch(at, total, Part(w_down, side=0), Part(w_down, side=1))
    for bit in bits_of("wide")[1:-1]:
        there = swap(total, "wide", bit)
        total = pair(total, there, total)
    hidden = gated(model, total, swap(total, "wide", bits_of("wide")[-1]), token)
    other = swap(hidden, "wide", 1)
    total, *sends = contract_last(
        head_size, at, other, down_other, contract(hidden, down_own), resid_0, resid_1
    )
    for s, send in enumerate(sends, 1):
        total = total + swap(send, "head", s).astype(f32)
    return total.astype(bf16)


def solution(mesh):
    in_specs = (
        P("grp", None),
        P(),
        P("wide"),
        P("wide", "head"),
        P("wide", "head"),
        P("wide", "head"),
        P("head", "wide"),
        P("wide", "head"),
        P("wide", "head"),
        P("head", "wide"),
        P(None, "grp", "wide", "head"),
        P("grp"),
        P("grp"),
    )
    out_specs = P(("grp", "head"), "wide")
    return jax.shard_map(
        per_device, mesh=mesh, in_specs=in_specs, out_specs=out_specs, check_vma=False
    )
```

```python
import math

import jax
import jax.numpy as jnp
from jax import lax
from jax.experimental import pallas as pl
from jax.experimental.pallas import tpu as pltpu
from jax.sharding import PartitionSpec as P

HEAD_WIDTH = 128
DRAFT_TOKENS = 4
LANES = 128
MIB = 1 << 20

epsilon = 1e-05
theta_base = 500000.0
neg_large = -1e30

f32 = jnp.float32
bf16 = jnp.bfloat16
ANY = pl.BlockSpec(memory_space=pl.ANY)
VMEM = pl.BlockSpec(memory_space=pltpu.VMEM)
SMEM = pl.BlockSpec(memory_space=pltpu.SMEM)
HBM = pl.BlockSpec(memory_space=pltpu.HBM)


def in_hbm(x):
    return pltpu.with_memory_space_constraint(x, pltpu.HBM)


def cost(rows, *weights):
    size = sum(w.size for w in weights)
    return pl.CostEstimate(flops=2 * rows * size, bytes_accessed=2 * size, transcendentals=0)


def params(mib):
    return pltpu.CompilerParams(vmem_limit_bytes=mib * MIB)


def blocks_of(width, most):
    step = max(b for b in range(LANES, most + 1, LANES) if width % b == 0)
    return [(at, step) for at in range(0, width, step)]


def thirds(x):
    high = x.astype(bf16)
    rest = x - high.astype(f32)
    middle = rest.astype(bf16)
    return high, middle, (rest - middle.astype(f32)).astype(bf16)


def lanes(at):
    return slice(at * LANES, (at + 1) * LANES)


PIECES = 8


class Part:
    def __init__(self, array, first=0, count=None, side=None):
        rows = array.shape[0]
        self.array, self.first, self.side = array, first, side
        self.count = rows // 2 if side is not None else rows if count is None else count
        self.shape = (self.count,) + array.shape[1:]
        self.out = pltpu.VMEM(self.shape, array.dtype)

    def copies(self, at, source, held, sems):
        step = max(1, self.count // PIECES)
        base = self.first
        if self.side is not None:
            base = pl.multiple_of((at[2] if self.side == 0 else 1 - at[2]) * self.count, LANES)
        return [
            pltpu.make_async_copy(
                source.at[pl.ds(base + p * step, step)], held.at[pl.ds(p * step, step)], sems.at[p]
            )
            for p in range(self.count // step)
        ]


def beside(copies, at, compute):
    for copy in copies:
        copy.start()
    pl.when(at[2] >= 0)(compute)
    for copy in copies:
        copy.wait()


def fetch_kernel(wanted, skip, at, *refs):
    n, refs = len(wanted), refs[skip:]
    sources, held, token, sems = refs[:n], refs[n : 2 * n], refs[2 * n], refs[2 * n + 1 :]
    copies = sum([w.copies(at, *refs) for w, *refs in zip(wanted, sources, held, sems)], [])
    for copy in copies:
        copy.start()
    token[...] = jnp.zeros_like(token)
    for copy in copies:
        copy.wait()


def fetch(at, after, *wanted):
    after = after if isinstance(after, (list, tuple)) else [after]
    size = sum(math.prod(w.shape) for w in wanted)
    return pl.pallas_call(
        lambda *refs: fetch_kernel(wanted, len(after), *refs),
        in_specs=[SMEM] + [ANY] * len(after) + [HBM] * len(wanted),
        out_specs=[VMEM] * (len(wanted) + 1),
        out_shape=[w.out for w in wanted] + [pltpu.VMEM((8, LANES), f32)],
        scratch_shapes=[pltpu.SemaphoreType.DMA((2 * PIECES,))] * len(wanted),
        compiler_params=params(2),
        cost_estimate=pl.CostEstimate(flops=0, bytes_accessed=4 * size, transcendentals=0),
        name="fetch",
    )(at, *after, *[in_hbm(w.array) for w in wanted])


def hold(x, token):
    return pl.pallas_call(
        lambda *_: None,
        in_specs=[VMEM, ANY],
        out_specs=VMEM,
        out_shape=jax.ShapeDtypeStruct(x.shape, x.dtype),
        input_output_aliases={0: 0},
        compiler_params=params(1),
        name="hold",
    )(x, token)


def project_kernel(chunks, at, tokens, gain, wq, wk, wv, out, own, tok, gain_f, norm, bq, bk, bv, acc, gain_b, sems):
    rows, model = tok.shape
    depth, q_cols = bq.shape
    kv_cols = bk.shape[1]
    step = depth // chunks
    gain_copy = pltpu.make_async_copy(gain, gain_b, sems.at[3 + chunks])
    gain_copy.start()
    copies = [
        pltpu.make_async_copy(tokens, tok, sems.at[0]),
        pltpu.make_async_copy(wk, bk, sems.at[1]),
        pltpu.make_async_copy(wv, bv, sems.at[2]),
    ] + [
        pltpu.make_async_copy(
            wq.at[pl.ds(c * step, step)], bq.at[pl.ds(c * step, step)], sems.at[3 + c]
        )
        for c in range(chunks)
    ]
    for copy in copies:
        copy.start()
    gain_copy.wait()
    gain_f[...] = gain_b[...].astype(f32)
    copies[0].wait()
    squares = jnp.zeros((rows, LANES), f32)
    for c in range(model // LANES):
        part = tok[:, lanes(c)].astype(f32)
        squares = squares + part * part
    scale = lax.rsqrt(jnp.sum(squares, axis=1, keepdims=True) / model + epsilon)
    count = depth // LANES
    for c in range(count):
        index = at[0] * count + c
        part = tok[:, pl.ds(pl.multiple_of(index * LANES, LANES), LANES)]
        own[:, lanes(c)] = part
        norm[:, lanes(c)] = (part.astype(f32) * scale * gain_f[pl.ds(index, 1), :]).astype(bf16)
    for copy, held, base in ((copies[1], bk, q_cols), (copies[2], bv, q_cols + kv_cols)):
        copy.wait()
        out[:, base : base + kv_cols] = jnp.dot(
            norm[...], held[...], preferred_element_type=f32
        ).astype(out.dtype)
    for c in range(chunks):
        copies[3 + c].wait()
        for start, size in blocks_of(q_cols, 512):
            cols = slice(start, start + size)
            term = jnp.dot(
                norm[:, c * step : (c + 1) * step],
                bq[c * step : (c + 1) * step, cols],
                preferred_element_type=f32,
            )
            if c:
                term = acc[:, cols] + term
            if c < chunks - 1:
                acc[:, cols] = term
            else:
                out[:, cols] = term.astype(out.dtype)


def project(at, tokens, gain, wq, wk, wv):
    rows, model = tokens.shape
    depth, q_cols = wq.shape
    kv_cols = wk.shape[1]
    chunks = max(1, min(8, depth // 256))
    return pl.pallas_call(
        lambda *refs: project_kernel(chunks, *refs),
        in_specs=[SMEM] + [HBM] * 5,
        out_specs=[VMEM, VMEM],
        out_shape=[
            jax.ShapeDtypeStruct((rows, q_cols + 2 * kv_cols), bf16),
            jax.ShapeDtypeStruct((rows, depth), bf16),
        ],
        scratch_shapes=[
            pltpu.VMEM((rows, model), bf16),
            pltpu.VMEM((model // LANES, LANES), f32),
            pltpu.VMEM((rows, depth), bf16),
            pltpu.VMEM(wq.shape, bf16),
            pltpu.VMEM(wk.shape, bf16),
            pltpu.VMEM(wv.shape, bf16),
            pltpu.VMEM((rows, q_cols), f32),
            pltpu.VMEM((model // LANES, LANES), bf16),
            pltpu.SemaphoreType.DMA((4 + chunks,)),
        ],
        compiler_params=params(16),
        cost_estimate=cost(rows, wq, wk, wv),
        name="project",
    )(at, in_hbm(tokens), in_hbm(gain.reshape(model // LANES, LANES)), in_hbm(wq), in_hbm(wk), in_hbm(wv))


def attend_kernel(n, part, at, cos, sin, cache, source, *rest):
    parts, (out, held, queries, total, stats_f, sems) = rest[:n], rest[n:]
    beside(
        part.copies(at, source, held, sems),
        at,
        lambda: attention(at, cos, sin, cache, parts, out, queries, total, stats_f),
    )


def attention(at, cos, sin, cache, parts, out, queries, total, stats_f):
    rows, q_cols = queries.shape
    context, kv_cols = cache.shape[2:]
    kv_heads = kv_cols // HEAD_WIDTH
    heads = q_cols // HEAD_WIDTH
    group = heads // kv_heads
    tile = 2 * DRAFT_TOKENS
    requests = rows // DRAFT_TOKENS

    def length(r):
        return at[4 + r]

    def slot(r):
        return at[4 + requests + r]

    last = at[1]
    base = at[0] * context

    def column(c):
        return sum(p[:, lanes(c)].astype(f32) for p in parts)

    def rotated(x):
        return x * cos[...] + pltpu.roll(x, HEAD_WIDTH // 2, 1) * sin[...]

    for h in range(heads):
        queries[:, lanes(h)] = (rotated(column(h)) * HEAD_WIDTH ** (-0.5)).astype(bf16).astype(f32)
    new_keys = [rotated(column(heads + k)).astype(bf16) for k in range(kv_heads)]
    new_values = [column(heads + kv_heads + k).astype(bf16) for k in range(kv_heads)]

    high = group * tile
    row = lax.broadcasted_iota(jnp.int32, (high, 1), 0) % tile
    first = row < DRAFT_TOKENS
    position = lax.broadcasted_iota(jnp.int32, (high, context), 1) + base
    draft_col = lax.broadcasted_iota(jnp.int32, (high, rows), 1)
    lane = lax.broadcasted_iota(jnp.int32, (tile, LANES), 1)
    nt = (((1,), (1,)), ((), ()))
    for i in range(rows // tile):
        request = 2 * i
        limit = jnp.where(first, length(request), length(request + 1))
        live = position < limit
        own_at = tile * i + jnp.where(first, 0, DRAFT_TOKENS)
        seen = (draft_col >= own_at) & (draft_col <= tile * i + row) & (last > 0)
        stats = jnp.zeros((tile, LANES), f32)
        for k in range(kv_heads):
            q = jnp.concatenate(
                [queries[tile * i : tile * (i + 1), lanes(k * group + g)] for g in range(group)], axis=0
            ).astype(bf16)
            scores = [
                lax.dot_general(q, cache[0, slot(request + s), :, lanes(k)], nt, preferred_element_type=f32)
                for s in range(2)
            ]
            score = jnp.where(live, jnp.where(first, scores[0], scores[1]), neg_large)
            draft = lax.dot_general(q, new_keys[k], nt, preferred_element_type=f32)
            draft = jnp.where(seen, draft, neg_large)
            top = jnp.maximum(
                jnp.max(score, axis=1, keepdims=True), jnp.max(draft, axis=1, keepdims=True)
            )
            weight = jnp.where(live, jnp.exp(score - top), 0.0)
            draft_weight = jnp.where(seen, jnp.exp(draft - top), 0.0)
            mass = jnp.sum(weight, axis=1, keepdims=True) + jnp.sum(draft_weight, axis=1, keepdims=True)
            weight = weight.astype(bf16)
            sums = [
                jnp.dot(weight, cache[1, slot(request + s), :, lanes(k)], preferred_element_type=f32)
                for s in range(2)
            ]
            value = jnp.where(first, sums[0], sums[1]) + jnp.dot(
                draft_weight.astype(bf16), new_values[k], preferred_element_type=f32
            )
            some = mass > 0.0
            safe = jnp.where(some, mass, 1.0)
            value = value / safe
            lse = jnp.where(some, top + jnp.log(safe), neg_large)
            for g in range(group):
                at_rows = slice(tile * g, tile * (g + 1))
                total[tile * i : tile * (i + 1), lanes(k * group + g)] = value[at_rows]
                stats = jnp.where(lane == k * group + g, lse[at_rows], stats)
        stats_f[tile * i : tile * (i + 1), :] = stats
    out[:, :q_cols] = total[...].astype(bf16)
    for p, term in enumerate(thirds(stats_f[...])):
        out[:, q_cols + p * LANES : q_cols + (p + 1) * LANES] = term


def attend(at, cos, sin, cache, parts, part):
    rows, width = parts[0].shape
    q_cols = width - 2 * cache.shape[3]
    return pl.pallas_call(
        lambda *refs: attend_kernel(len(parts), part, *refs),
        in_specs=[SMEM] + [VMEM] * 3 + [HBM] + [VMEM] * len(parts),
        out_specs=[VMEM, VMEM],
        out_shape=[jax.ShapeDtypeStruct((rows, q_cols + 3 * LANES), bf16), part.out],
        scratch_shapes=[
            pltpu.VMEM((rows, q_cols), f32),
            pltpu.VMEM((rows, q_cols), f32),
            pltpu.VMEM((rows, LANES), f32),
            pltpu.SemaphoreType.DMA((2 * PIECES,)),
        ],
        compiler_params=params(6),
        cost_estimate=cost(rows, cache),
        name="attend",
    )(at, cos, sin, cache, in_hbm(part.array), *parts)


def joined(ref, start):
    return sum(ref[:, start + p * LANES : start + (p + 1) * LANES].astype(f32) for p in range(3))


def product(x, w, out, base, width):
    for start, size in blocks_of(width, 512):
        out[:, start : start + size] = jnp.dot(
            x[...], w[:, base + start : base + start + size], preferred_element_type=f32
        ).astype(out.dtype)


def output_first_kernel(n, w, *rest):
    values, (out, attended) = rest[:n], rest[n:]
    heads = attended.shape[1] // HEAD_WIDTH
    stats = [joined(v, attended.shape[1]) for v in values]
    top = stats[0]
    for s in stats[1:]:
        top = jnp.maximum(top, s)
    shares = [jnp.exp(s - top) for s in stats]
    whole = sum(shares)
    shares = [s / whole for s in shares]
    for h in range(heads):
        attended[:, lanes(h)] = sum(
            v[:, lanes(h)].astype(f32) * s[:, h : h + 1] for v, s in zip(values, shares)
        ).astype(bf16)
    product(attended, w, out, 0, out.shape[1])


def output_first(values, w):
    rows, half = values[0].shape[0], w.shape[1] // 2
    return pl.pallas_call(
        lambda *refs: output_first_kernel(len(values), *refs),
        in_specs=[VMEM] * (1 + len(values)),
        out_specs=[VMEM] * 2,
        out_shape=[
            jax.ShapeDtypeStruct((rows, half), bf16),
            jax.ShapeDtypeStruct((rows, w.shape[0]), bf16),
        ],
        compiler_params=params(4),
        cost_estimate=cost(rows, w),
        name="output_first",
    )(w, *values)


def output_second(attended, w):
    rows, half = attended.shape[0], w.shape[1] // 2
    return pl.pallas_call(
        lambda x, w, out: product(x, w, out, half, half),
        in_specs=[VMEM] * 2,
        out_specs=VMEM,
        out_shape=jax.ShapeDtypeStruct((rows, half), bf16),
        compiler_params=params(4),
        cost_estimate=cost(rows, w),
        name="output_second",
    )(attended, w)


def half_of(side, x, wg, wu, out, before=None):
    half = wg[0].shape[1] // 2
    for base, pieces in ((0, wg), (half, wu)):
        for start, size in blocks_of(half, 512):
            cols = pl.ds(pl.multiple_of(side * half + start, LANES), size)
            to = slice(base + start, base + start + size)
            term = None if before is None else before[:, to]
            row = 0
            for w in pieces:
                more = jnp.dot(x[:, row : row + w.shape[0]], w[:, cols], preferred_element_type=f32)
                term = more if term is None else term + more
                row += w.shape[0]
            out[:, to] = term.astype(out.dtype)


def residual(which, own, gain, parts, resid, x, gain_f):
    gain_f[...] = gain[...].astype(f32)
    count = resid.shape[1] // LANES
    square = jnp.zeros((own.shape[0], LANES), f32)
    for c in range(count):
        at = which * count + c
        value = own[:, lanes(at)].astype(f32) + sum(p[:, lanes(c)].astype(f32) for p in parts)
        value = value.astype(bf16).astype(f32)
        resid[:, lanes(c)] = value
        square = square + value * value
        x[:, lanes(c)] = (value * gain_f[at : at + 1, :]).astype(bf16)
    return square


def expand_first_kernel(n, part, at, own, gain, wg, wu, source, *rest):
    parts, (send, keep, resid, squares, held, x, gain_f, sems) = rest[:n], rest[n:]

    def compute():
        squares[...] = residual(0, own, gain, parts, resid, x, gain_f)
        half_of(1 - at[2], x, [wg], [wu], send)
        half_of(at[2], x, [wg], [wu], keep)

    beside(part.copies(at, source, held, sems), at, compute)


def expand_first(at, own, gain, parts, wg, wu, part):
    rows, depth = own.shape
    width = wg.shape[1]
    return pl.pallas_call(
        lambda *refs: expand_first_kernel(len(parts), part, *refs),
        in_specs=[SMEM] + [VMEM] * 4 + [HBM] + [VMEM] * len(parts),
        out_specs=[VMEM] * 5,
        out_shape=[
            jax.ShapeDtypeStruct((rows, width), f32),
            jax.ShapeDtypeStruct((rows, width), f32),
            jax.ShapeDtypeStruct((rows, depth // 2), f32),
            jax.ShapeDtypeStruct((rows, LANES), f32),
            part.out,
        ],
        scratch_shapes=[
            pltpu.VMEM((rows, depth // 2), bf16),
            pltpu.VMEM((depth // LANES, LANES), f32),
            pltpu.SemaphoreType.DMA((2 * PIECES,)),
        ],
        compiler_params=params(4),
        cost_estimate=cost(rows, wg, wu),
        name="expand_first",
    )(at, own, gain, wg, wu, in_hbm(part.array), *parts)


def expand_send_kernel(n, g, at, own, gain, before, squares, *rest):
    wg, wu, parts, (out, resid, x, gain_f) = rest[:g], rest[g : g + 1], rest[g + 1 : g + 1 + n], rest[g + 1 + n :]
    square = squares[...] + residual(1, own, gain, parts, resid, x, gain_f)
    square = jnp.broadcast_to(jnp.sum(square, axis=1, keepdims=True), square.shape)
    width = wu[0].shape[1]
    for p, term in enumerate(thirds(square)):
        out[:, width + p * LANES : width + (p + 1) * LANES] = term
    half_of(1 - at[2], x, wg, wu, out, before)


def expand_send(at, own, gain, parts, wg, wu, before, squares):
    rows, depth = own.shape
    return pl.pallas_call(
        lambda *refs: expand_send_kernel(len(parts), len(wg), *refs),
        in_specs=[SMEM] + [VMEM] * (5 + len(wg) + len(parts)),
        out_specs=[VMEM] * 3,
        out_shape=[
            jax.ShapeDtypeStruct((rows, wu.shape[1] + 3 * LANES), bf16),
            jax.ShapeDtypeStruct((rows, depth // 2), f32),
            jax.ShapeDtypeStruct((rows, depth // 2), bf16),
        ],
        scratch_shapes=[pltpu.VMEM((depth // LANES, LANES), f32)],
        compiler_params=params(4),
        cost_estimate=cost(rows, wu),
        name="expand_send",
    )(at, own, gain, before, squares, *wg, wu, *parts)


def expand_keep(at, x, wg, wu, before):
    rows = x.shape[0]
    return pl.pallas_call(
        lambda at, x, before, *refs: half_of(at[2], x, refs[:-2], refs[-2:-1], refs[-1], before),
        in_specs=[SMEM] + [VMEM] * (3 + len(wg)),
        out_specs=VMEM,
        out_shape=jax.ShapeDtypeStruct((rows, wu.shape[1]), bf16),
        compiler_params=params(4),
        cost_estimate=cost(rows, wu),
        name="expand_keep",
    )(at, x, before, *wg, wu)


def pair_kernel(keep, received, stats, out):
    width = out.shape[1] - 3 * LANES
    for start, size in blocks_of(width, 512):
        cols = slice(start, start + size)
        out[:, cols] = (keep[:, cols].astype(f32) + received[:, cols].astype(f32)).astype(bf16)
    for p, term in enumerate(thirds(joined(stats, width) + joined(received, width))):
        out[:, width + p * LANES : width + (p + 1) * LANES] = term


def pair(keep, received, stats):
    return pl.pallas_call(
        pair_kernel,
        in_specs=[VMEM] * 3,
        out_specs=VMEM,
        out_shape=jax.ShapeDtypeStruct(received.shape, bf16),
        compiler_params=params(4),
        name="pair",
    )(keep, received, stats)


def gated_kernel(model, one, two, out):
    half = out.shape[1]
    scale = lax.rsqrt((joined(one, 2 * half) + joined(two, 2 * half)) / model + epsilon)
    for c in range(half // LANES):
        gate, up = (
            scale * (one[:, lanes(at)].astype(f32) + two[:, lanes(at)].astype(f32))
            for at in (c, half // LANES + c)
        )
        out[:, lanes(c)] = (gate / (1.0 + jnp.exp(-gate)) * up).astype(bf16)


def gated(model, one, two, after):
    rows, width = one.shape
    return pl.pallas_call(
        lambda _, *refs: gated_kernel(model, *refs),
        in_specs=[ANY] + [VMEM] * 2,
        out_specs=VMEM,
        out_shape=jax.ShapeDtypeStruct((rows, (width - 3 * LANES) // 2), bf16),
        compiler_params=params(4),
        name="gated",
    )(after, one, two)


def contract_kernel(hidden, w, out):
    for start, size in blocks_of(w.shape[1], 512):
        cols = slice(start, start + size)
        out[:, cols] = jnp.dot(hidden[...], w[:, cols], preferred_element_type=f32)


def contract(hidden, w):
    rows = hidden.shape[0]
    return pl.pallas_call(
        contract_kernel,
        in_specs=[VMEM] * 2,
        out_specs=VMEM,
        out_shape=jax.ShapeDtypeStruct((rows, w.shape[1]), f32),
        compiler_params=params(4),
        cost_estimate=cost(rows, w),
        name="contract",
    )(hidden, w)


def contract_last_kernel(n, at, hidden, w, before, resid_0, resid_1, own, *rest):
    sends, acc = rest[:-1], rest[-1]
    share = own.shape[0]
    for start, size in blocks_of(w.shape[1], 512):
        cols = slice(start, start + size)
        acc[:, cols] = before[:, cols] + jnp.dot(hidden[...], w[:, cols], preferred_element_type=f32)

    def block(ref, index):
        if share % 8 == 0:
            return ref[pl.ds(pl.multiple_of(index * share, share), share), :]
        chosen = ref[:share, :]
        for b in range(1, n):
            chosen = jnp.where(index == b, ref[b * share : (b + 1) * share, :], chosen)
        return chosen

    half = resid_0.shape[1]
    mine = block(acc, at[3])
    own[:, :half] = mine[:, :half] + block(resid_0, at[3])
    own[:, half:] = mine[:, half:] + block(resid_1, at[3])
    for s in range(1, n):
        sends[s - 1][...] = block(acc, at[3] ^ s).astype(bf16)


def contract_last(n, at, hidden, w, before, *resid):
    rows, cols = before.shape
    share = rows // n
    return pl.pallas_call(
        lambda *refs: contract_last_kernel(n, *refs),
        in_specs=[SMEM] + [VMEM] * 5,
        out_specs=[VMEM] * n,
        out_shape=[jax.ShapeDtypeStruct((share, cols), f32)]
        + [jax.ShapeDtypeStruct((share, cols), bf16)] * (n - 1),
        scratch_shapes=[pltpu.VMEM((rows, cols), f32)],
        compiler_params=params(4),
        cost_estimate=cost(rows, w),
        name="contract_last",
    )(at, hidden, w, before, *resid)


def add_kernel(one, two, *rest):
    out = rest[-1]
    for start, size in blocks_of(out.shape[1], 512):
        cols = slice(start, start + size)
        out[:, cols] = (one[:, cols].astype(f32) + two[:, cols].astype(f32)).astype(bf16)


def add(one, two, *tokens):
    return pl.pallas_call(
        add_kernel,
        in_specs=[VMEM] * 2 + [ANY] * len(tokens),
        out_specs=VMEM,
        out_shape=jax.ShapeDtypeStruct(one.shape, bf16),
        compiler_params=params(4),
        name="add",
    )(one, two, *tokens)


def swap(x, axis, bit):
    n = lax.axis_size(axis)
    return lax.ppermute(x, axis, [(i, i ^ bit) for i in range(n)])


def bits_of(axis):
    n = lax.axis_size(axis)
    return [1 << b for b in range(n.bit_length() - 1)]


def gathered(x, axis, token):
    parts = [x]
    for bit in reversed(bits_of(axis)):
        parts = parts + [swap(p, axis, bit) for p in parts]
        if bit > 1:
            parts = parts[:-1] + [hold(parts[-1], token)]
    return parts


def summed(x, axis, order, *tokens):
    *bits, last = bits_of(axis)[::order]
    for bit in bits:
        x = add(x, swap(x, axis, bit), *(tokens if bit == bits[-1] else ()))
    return x, swap(x, axis, last)


def per_device(tokens, attn_gain, ffn_gain, w_query, key_matrix, value_matrix, w_out, w_gate, w_up, w_down, kv_cache, lengths, slots):
    rows, model = tokens.shape
    wide_at, head_at = lax.axis_index("wide"), lax.axis_index("head")
    wide_size, head_size = lax.axis_size("wide"), lax.axis_size("head")
    places = jnp.stack([wide_at, (wide_at == wide_size - 1).astype(jnp.int32), wide_at & 1, head_at])
    at = places.astype(jnp.int32)

    half = HEAD_WIDTH // 2
    positions = (
        jnp.broadcast_to(lengths[:, None], (lengths.shape[0], DRAFT_TOKENS))
        + jnp.arange(DRAFT_TOKENS, dtype=jnp.int32)[None, :]
    ).reshape(rows).astype(f32)
    exponent = jnp.arange(half, dtype=f32) * (2.0 / HEAD_WIDTH)
    angles = positions[:, None] * (theta_base ** (-exponent))[None, :]
    cos, sin = jnp.cos(angles), jnp.sin(angles)
    cos = jnp.concatenate([cos, cos], axis=1)
    sin = jnp.concatenate([-sin, sin], axis=1)

    qkv, own = project(at, tokens, attn_gain, w_query, key_matrix, value_matrix)
    depth = own.shape[1]
    half = depth // 2
    gain = ffn_gain.reshape(depth // LANES, LANES)

    flat_cache = kv_cache.reshape((-1,) + kv_cache.shape[2:])
    meta = jnp.concatenate([at, lengths, slots])
    cache, gate_0, token = fetch(at, (qkv, meta, cos, sin), Part(flat_cache), Part(w_gate, 0, half))
    cache = cache.reshape(kv_cache.shape)
    value, w_out = attend(meta, cos, sin, cache, gathered(qkv, "wide", token), Part(w_out))

    quarter = half // 2
    up_0, gate_1, token = fetch(at, value, Part(w_up, 0, half), Part(w_gate, half, quarter))
    out_0, attended = output_first(gathered(value, "wide", token), w_out)
    out_1 = output_second(attended, w_out)
    parts_0 = summed(out_0, "head", 1)
    gate_2, token = fetch(at, parts_0[0], Part(w_gate, half + quarter, quarter))
    parts_1 = summed(out_1, "head", -1, token)
    send, keep, resid_0, squares, up_1 = expand_first(
        at, own, gain, parts_0, gate_0, up_0, Part(w_up, half, half)
    )
    gate_1 = (gate_1, gate_2)
    send, resid_1, x = expand_send(at, own, gain, parts_1, gate_1, up_1, send, squares)
    received = swap(send, "wide", 1)
    total = pair(expand_keep(at, x, gate_1, up_1, keep), received, send)
    down_own, down_other, token = fetch(at, total, Part(w_down, side=0), Part(w_down, side=1))
    for bit in bits_of("wide")[1:-1]:
        there = swap(total, "wide", bit)
        total = pair(total, there, total)
    hidden = gated(model, total, swap(total, "wide", bits_of("wide")[-1]), token)
    other = swap(hidden, "wide", 1)
    total, *sends = contract_last(
        head_size, at, other, down_other, contract(hidden, down_own), resid_0, resid_1
    )
    for s, send in enumerate(sends, 1):
        total = total + swap(send, "head", s).astype(f32)
    return total.astype(bf16)


def solution(mesh):
    in_specs = (
        P("grp", None),
        P(),
        P("wide"),
        P("wide", "head"),
        P("wide", "head"),
        P("wide", "head"),
        P("head", "wide"),
        P("wide", "head"),
        P("wide", "head"),
        P("head", "wide"),
        P(None, "grp", "wide", "head"),
        P("grp"),
        P("grp"),
    )
    out_specs = P(("grp", "head"), "wide")
    return jax.shard_map(
        per_device, mesh=mesh, in_specs=in_specs, out_specs=out_specs, check_vma=False
    )
```

```python
import math

import jax
import jax.numpy as jnp
from jax import lax
from jax.experimental import pallas as pl
from jax.experimental.pallas import tpu as pltpu
from jax.sharding import PartitionSpec as P

HEAD_WIDTH = 128
DRAFT_TOKENS = 4
LANES = 128
MIB = 1 << 20

epsilon = 1e-05
theta_base = 500000.0
neg_large = -1e30

f32 = jnp.float32
bf16 = jnp.bfloat16
ANY = pl.BlockSpec(memory_space=pl.ANY)
VMEM = pl.BlockSpec(memory_space=pltpu.VMEM)
SMEM = pl.BlockSpec(memory_space=pltpu.SMEM)
HBM = pl.BlockSpec(memory_space=pltpu.HBM)


def in_hbm(x):
    return pltpu.with_memory_space_constraint(x, pltpu.HBM)


def cost(rows, *weights):
    size = sum(w.size for w in weights)
    return pl.CostEstimate(flops=2 * rows * size, bytes_accessed=2 * size, transcendentals=0)


def params(mib):
    return pltpu.CompilerParams(vmem_limit_bytes=mib * MIB)


def blocks_of(width, most):
    step = max(b for b in range(LANES, most + 1, LANES) if width % b == 0)
    return [(at, step) for at in range(0, width, step)]


def thirds(x):
    high = x.astype(bf16)
    rest = x - high.astype(f32)
    middle = rest.astype(bf16)
    return high, middle, (rest - middle.astype(f32)).astype(bf16)


def lanes(at):
    return slice(at * LANES, (at + 1) * LANES)


PIECES = 8


class Part:
    def __init__(self, array, first=0, count=None, side=None):
        rows = array.shape[0]
        self.array, self.first, self.side = array, first, side
        self.count = rows // 2 if side is not None else rows if count is None else count
        self.shape = (self.count,) + array.shape[1:]
        self.out = pltpu.VMEM(self.shape, array.dtype)

    def copies(self, at, source, held, sems):
        step = max(1, self.count // PIECES)
        base = self.first
        if self.side is not None:
            base = pl.multiple_of((at[2] if self.side == 0 else 1 - at[2]) * self.count, LANES)
        return [
            pltpu.make_async_copy(
                source.at[pl.ds(base + p * step, step)], held.at[pl.ds(p * step, step)], sems.at[p]
            )
            for p in range(self.count // step)
        ]


def beside(copies, at, compute):
    for copy in copies:
        copy.start()
    pl.when(at[2] >= 0)(compute)
    for copy in copies:
        copy.wait()


def fetch_kernel(wanted, skip, at, *refs):
    n, refs = len(wanted), refs[skip:]
    sources, held, token, sems = refs[:n], refs[n : 2 * n], refs[2 * n], refs[2 * n + 1 :]
    copies = sum([w.copies(at, *refs) for w, *refs in zip(wanted, sources, held, sems)], [])
    for copy in copies:
        copy.start()
    token[...] = jnp.zeros_like(token)
    for copy in copies:
        copy.wait()


def fetch(at, after, *wanted):
    after = after if isinstance(after, (list, tuple)) else [after]
    size = sum(math.prod(w.shape) for w in wanted)
    return pl.pallas_call(
        lambda *refs: fetch_kernel(wanted, len(after), *refs),
        in_specs=[SMEM] + [ANY] * len(after) + [HBM] * len(wanted),
        out_specs=[VMEM] * (len(wanted) + 1),
        out_shape=[w.out for w in wanted] + [pltpu.VMEM((8, LANES), f32)],
        scratch_shapes=[pltpu.SemaphoreType.DMA((2 * PIECES,))] * len(wanted),
        compiler_params=params(2),
        cost_estimate=pl.CostEstimate(flops=0, bytes_accessed=4 * size, transcendentals=0),
        name="fetch",
    )(at, *after, *[in_hbm(w.array) for w in wanted])


def hold(x, token):
    return pl.pallas_call(
        lambda *_: None,
        in_specs=[VMEM, ANY],
        out_specs=VMEM,
        out_shape=jax.ShapeDtypeStruct(x.shape, x.dtype),
        input_output_aliases={0: 0},
        compiler_params=params(1),
        name="hold",
    )(x, token)


def project_kernel(chunks, at, tokens, gain, wq, wk, wv, out, own, tok, gain_f, norm, bq, bk, bv, acc, gain_b, sems):
    rows, model = tok.shape
    depth, q_cols = bq.shape
    kv_cols = bk.shape[1]
    step = depth // chunks
    gain_copy = pltpu.make_async_copy(gain, gain_b, sems.at[3 + chunks])
    gain_copy.start()
    copies = [
        pltpu.make_async_copy(tokens, tok, sems.at[0]),
        pltpu.make_async_copy(wk, bk, sems.at[1]),
        pltpu.make_async_copy(wv, bv, sems.at[2]),
    ] + [
        pltpu.make_async_copy(
            wq.at[pl.ds(c * step, step)], bq.at[pl.ds(c * step, step)], sems.at[3 + c]
        )
        for c in range(chunks)
    ]
    for copy in copies:
        copy.start()
    gain_copy.wait()
    gain_f[...] = gain_b[...].astype(f32)
    copies[0].wait()
    squares = jnp.zeros((rows, LANES), f32)
    for c in range(model // LANES):
        part = tok[:, lanes(c)].astype(f32)
        squares = squares + part * part
    scale = lax.rsqrt(jnp.sum(squares, axis=1, keepdims=True) / model + epsilon)
    count = depth // LANES
    for c in range(count):
        index = at[0] * count + c
        part = tok[:, pl.ds(pl.multiple_of(index * LANES, LANES), LANES)]
        own[:, lanes(c)] = part
        norm[:, lanes(c)] = (part.astype(f32) * scale * gain_f[pl.ds(index, 1), :]).astype(bf16)
    for copy, held, base in ((copies[1], bk, q_cols), (copies[2], bv, q_cols + kv_cols)):
        copy.wait()
        out[:, base : base + kv_cols] = jnp.dot(
            norm[...], held[...], preferred_element_type=f32
        ).astype(out.dtype)
    for c in range(chunks):
        copies[3 + c].wait()
        for start, size in blocks_of(q_cols, 512):
            cols = slice(start, start + size)
            term = jnp.dot(
                norm[:, c * step : (c + 1) * step],
                bq[c * step : (c + 1) * step, cols],
                preferred_element_type=f32,
            )
            if c:
                term = acc[:, cols] + term
            if c < chunks - 1:
                acc[:, cols] = term
            else:
                out[:, cols] = term.astype(out.dtype)


def project(at, tokens, gain, wq, wk, wv):
    rows, model = tokens.shape
    depth, q_cols = wq.shape
    kv_cols = wk.shape[1]
    chunks = max(1, min(8, depth // 256))
    return pl.pallas_call(
        lambda *refs: project_kernel(chunks, *refs),
        in_specs=[SMEM] + [HBM] * 5,
        out_specs=[VMEM, VMEM],
        out_shape=[
            jax.ShapeDtypeStruct((rows, q_cols + 2 * kv_cols), bf16),
            jax.ShapeDtypeStruct((rows, depth), bf16),
        ],
        scratch_shapes=[
            pltpu.VMEM((rows, model), bf16),
            pltpu.VMEM((model // LANES, LANES), f32),
            pltpu.VMEM((rows, depth), bf16),
            pltpu.VMEM(wq.shape, bf16),
            pltpu.VMEM(wk.shape, bf16),
            pltpu.VMEM(wv.shape, bf16),
            pltpu.VMEM((rows, q_cols), f32),
            pltpu.VMEM((model // LANES, LANES), bf16),
            pltpu.SemaphoreType.DMA((4 + chunks,)),
        ],
        compiler_params=params(16),
        cost_estimate=cost(rows, wq, wk, wv),
        name="project",
    )(at, in_hbm(tokens), in_hbm(gain.reshape(model // LANES, LANES)), in_hbm(wq), in_hbm(wk), in_hbm(wv))


def attend_kernel(n, part, at, cos, sin, cache, source, *rest):
    parts, (out, held, queries, total, stats_f, sems) = rest[:n], rest[n:]
    beside(
        part.copies(at, source, held, sems),
        at,
        lambda: attention(at, cos, sin, cache, parts, out, queries, total, stats_f),
    )


def attention(at, cos, sin, cache, parts, out, queries, total, stats_f):
    rows, q_cols = queries.shape
    context, kv_cols = cache.shape[2:]
    kv_heads = kv_cols // HEAD_WIDTH
    heads = q_cols // HEAD_WIDTH
    group = heads // kv_heads
    tile = 2 * DRAFT_TOKENS
    requests = rows // DRAFT_TOKENS

    def length(r):
        return at[4 + r]

    def slot(r):
        return at[4 + requests + r]

    last = at[1]
    base = at[0] * context

    def column(c):
        return sum(p[:, lanes(c)].astype(f32) for p in parts)

    def rotated(x):
        return x * cos[...] + pltpu.roll(x, HEAD_WIDTH // 2, 1) * sin[...]

    for h in range(heads):
        queries[:, lanes(h)] = (rotated(column(h)) * HEAD_WIDTH ** (-0.5)).astype(bf16).astype(f32)
    new_keys = [rotated(column(heads + k)).astype(bf16) for k in range(kv_heads)]
    new_values = [column(heads + kv_heads + k).astype(bf16) for k in range(kv_heads)]

    high = group * tile
    row = lax.broadcasted_iota(jnp.int32, (high, 1), 0) % tile
    first = row < DRAFT_TOKENS
    position = lax.broadcasted_iota(jnp.int32, (high, context), 1) + base
    draft_col = lax.broadcasted_iota(jnp.int32, (high, rows), 1)
    lane = lax.broadcasted_iota(jnp.int32, (tile, LANES), 1)
    nt = (((1,), (1,)), ((), ()))
    for i in range(rows // tile):
        request = 2 * i
        limit = jnp.where(first, length(request), length(request + 1))
        live = position < limit
        own_at = tile * i + jnp.where(first, 0, DRAFT_TOKENS)
        seen = (draft_col >= own_at) & (draft_col <= tile * i + row) & (last > 0)
        stats = jnp.zeros((tile, LANES), f32)
        for k in range(kv_heads):
            q = jnp.concatenate(
                [queries[tile * i : tile * (i + 1), lanes(k * group + g)] for g in range(group)], axis=0
            ).astype(bf16)
            scores = [
                lax.dot_general(q, cache[0, slot(request + s), :, lanes(k)], nt, preferred_element_type=f32)
                for s in range(2)
            ]
            score = jnp.where(live, jnp.where(first, scores[0], scores[1]), neg_large)
            draft = lax.dot_general(q, new_keys[k], nt, preferred_element_type=f32)
            draft = jnp.where(seen, draft, neg_large)
            top = jnp.maximum(
                jnp.max(score, axis=1, keepdims=True), jnp.max(draft, axis=1, keepdims=True)
            )
            weight = jnp.where(live, jnp.exp(score - top), 0.0)
            draft_weight = jnp.where(seen, jnp.exp(draft - top), 0.0)
            mass = jnp.sum(weight, axis=1, keepdims=True) + jnp.sum(draft_weight, axis=1, keepdims=True)
            weight = weight.astype(bf16)
            sums = [
                jnp.dot(weight, cache[1, slot(request + s), :, lanes(k)], preferred_element_type=f32)
                for s in range(2)
            ]
            value = jnp.where(first, sums[0], sums[1]) + jnp.dot(
                draft_weight.astype(bf16), new_values[k], preferred_element_type=f32
            )
            some = mass > 0.0
            safe = jnp.where(some, mass, 1.0)
            value = value / safe
            lse = jnp.where(some, top + jnp.log(safe), neg_large)
            for g in range(group):
                at_rows = slice(tile * g, tile * (g + 1))
                total[tile * i : tile * (i + 1), lanes(k * group + g)] = value[at_rows]
                stats = jnp.where(lane == k * group + g, lse[at_rows], stats)
        stats_f[tile * i : tile * (i + 1), :] = stats
    out[:, :q_cols] = total[...].astype(bf16)
    for p, term in enumerate(thirds(stats_f[...])):
        out[:, q_cols + p * LANES : q_cols + (p + 1) * LANES] = term


def attend(at, cos, sin, cache, parts, part):
    rows, width = parts[0].shape
    q_cols = width - 2 * cache.shape[3]
    return pl.pallas_call(
        lambda *refs: attend_kernel(len(parts), part, *refs),
        in_specs=[SMEM] + [VMEM] * 3 + [HBM] + [VMEM] * len(parts),
        out_specs=[VMEM, VMEM],
        out_shape=[jax.ShapeDtypeStruct((rows, q_cols + 3 * LANES), bf16), part.out],
        scratch_shapes=[
            pltpu.VMEM((rows, q_cols), f32),
            pltpu.VMEM((rows, q_cols), f32),
            pltpu.VMEM((rows, LANES), f32),
            pltpu.SemaphoreType.DMA((2 * PIECES,)),
        ],
        compiler_params=params(6),
        cost_estimate=cost(rows, cache),
        name="attend",
    )(at, cos, sin, cache, in_hbm(part.array), *parts)


def joined(ref, start):
    return sum(ref[:, start + p * LANES : start + (p + 1) * LANES].astype(f32) for p in range(3))


def product(x, w, out, base, width):
    for start, size in blocks_of(width, 512):
        out[:, start : start + size] = jnp.dot(
            x[...], w[:, base + start : base + start + size], preferred_element_type=f32
        ).astype(out.dtype)


def output_first_kernel(n, w, *rest):
    values, (out, attended) = rest[:n], rest[n:]
    heads = attended.shape[1] // HEAD_WIDTH
    stats = [joined(v, attended.shape[1]) for v in values]
    top = stats[0]
    for s in stats[1:]:
        top = jnp.maximum(top, s)
    shares = [jnp.exp(s - top) for s in stats]
    whole = sum(shares)
    shares = [s / whole for s in shares]
    for h in range(heads):
        attended[:, lanes(h)] = sum(
            v[:, lanes(h)].astype(f32) * s[:, h : h + 1] for v, s in zip(values, shares)
        ).astype(bf16)
    product(attended, w, out, 0, out.shape[1])


def output_first(values, w):
    rows, half = values[0].shape[0], w.shape[1] // 2
    return pl.pallas_call(
        lambda *refs: output_first_kernel(len(values), *refs),
        in_specs=[VMEM] * (1 + len(values)),
        out_specs=[VMEM] * 2,
        out_shape=[
            jax.ShapeDtypeStruct((rows, half), bf16),
            jax.ShapeDtypeStruct((rows, w.shape[0]), bf16),
        ],
        compiler_params=params(4),
        cost_estimate=cost(rows, w),
        name="output_first",
    )(w, *values)


def output_second(attended, w):
    rows, half = attended.shape[0], w.shape[1] // 2
    return pl.pallas_call(
        lambda x, w, out: product(x, w, out, half, half),
        in_specs=[VMEM] * 2,
        out_specs=VMEM,
        out_shape=jax.ShapeDtypeStruct((rows, half), bf16),
        compiler_params=params(4),
        cost_estimate=cost(rows, w),
        name="output_second",
    )(attended, w)


def half_of(side, x, wg, wu, out, before=None):
    half = wg[0].shape[1] // 2
    for base, pieces in ((0, wg), (half, wu)):
        for start, size in blocks_of(half, 512):
            cols = pl.ds(pl.multiple_of(side * half + start, LANES), size)
            to = slice(base + start, base + start + size)
            term = None if before is None else before[:, to]
            row = 0
            for w in pieces:
                more = jnp.dot(x[:, row : row + w.shape[0]], w[:, cols], preferred_element_type=f32)
                term = more if term is None else term + more
                row += w.shape[0]
            out[:, to] = term.astype(out.dtype)


def residual(which, own, gain, parts, resid, x, gain_f):
    gain_f[...] = gain[...].astype(f32)
    count = resid.shape[1] // LANES
    square = jnp.zeros((own.shape[0], LANES), f32)
    for c in range(count):
        at = which * count + c
        value = own[:, lanes(at)].astype(f32) + sum(p[:, lanes(c)].astype(f32) for p in parts)
        value = value.astype(bf16).astype(f32)
        resid[:, lanes(c)] = value
        square = square + value * value
        x[:, lanes(c)] = (value * gain_f[at : at + 1, :]).astype(bf16)
    return square


def expand_first_kernel(n, part, at, own, gain, wg, wu, source, *rest):
    parts, (send, keep, resid, squares, held, x, gain_f, sems) = rest[:n], rest[n:]

    def compute():
        squares[...] = residual(0, own, gain, parts, resid, x, gain_f)
        half_of(1 - at[2], x, [wg], [wu], send)
        half_of(at[2], x, [wg], [wu], keep)

    beside(part.copies(at, source, held, sems), at, compute)


def expand_first(at, own, gain, parts, wg, wu, part):
    rows, depth = own.shape
    width = wg.shape[1]
    return pl.pallas_call(
        lambda *refs: expand_first_kernel(len(parts), part, *refs),
        in_specs=[SMEM] + [VMEM] * 4 + [HBM] + [VMEM] * len(parts),
        out_specs=[VMEM] * 5,
        out_shape=[
            jax.ShapeDtypeStruct((rows, width), f32),
            jax.ShapeDtypeStruct((rows, width), f32),
            jax.ShapeDtypeStruct((rows, depth // 2), f32),
            jax.ShapeDtypeStruct((rows, LANES), f32),
            part.out,
        ],
        scratch_shapes=[
            pltpu.VMEM((rows, depth // 2), bf16),
            pltpu.VMEM((depth // LANES, LANES), f32),
            pltpu.SemaphoreType.DMA((2 * PIECES,)),
        ],
        compiler_params=params(4),
        cost_estimate=cost(rows, wg, wu),
        name="expand_first",
    )(at, own, gain, wg, wu, in_hbm(part.array), *parts)


def expand_send_kernel(n, g, at, own, gain, before, squares, *rest):
    wg, wu, parts, (out, resid, x, gain_f) = rest[:g], rest[g : g + 1], rest[g + 1 : g + 1 + n], rest[g + 1 + n :]
    square = squares[...] + residual(1, own, gain, parts, resid, x, gain_f)
    square = jnp.broadcast_to(jnp.sum(square, axis=1, keepdims=True), square.shape)
    width = wu[0].shape[1]
    for p, term in enumerate(thirds(square)):
        out[:, width + p * LANES : width + (p + 1) * LANES] = term
    half_of(1 - at[2], x, wg, wu, out, before)


def expand_send(at, own, gain, parts, wg, wu, before, squares):
    rows, depth = own.shape
    return pl.pallas_call(
        lambda *refs: expand_send_kernel(len(parts), len(wg), *refs),
        in_specs=[SMEM] + [VMEM] * (5 + len(wg) + len(parts)),
        out_specs=[VMEM] * 3,
        out_shape=[
            jax.ShapeDtypeStruct((rows, wu.shape[1] + 3 * LANES), bf16),
            jax.ShapeDtypeStruct((rows, depth // 2), f32),
            jax.ShapeDtypeStruct((rows, depth // 2), bf16),
        ],
        scratch_shapes=[pltpu.VMEM((depth // LANES, LANES), f32)],
        compiler_params=params(4),
        cost_estimate=cost(rows, wu),
        name="expand_send",
    )(at, own, gain, before, squares, *wg, wu, *parts)


def expand_keep(at, x, wg, wu, before):
    rows = x.shape[0]
    return pl.pallas_call(
        lambda at, x, before, *refs: half_of(at[2], x, refs[:-2], refs[-2:-1], refs[-1], before),
        in_specs=[SMEM] + [VMEM] * (3 + len(wg)),
        out_specs=VMEM,
        out_shape=jax.ShapeDtypeStruct((rows, wu.shape[1]), bf16),
        compiler_params=params(4),
        cost_estimate=cost(rows, wu),
        name="expand_keep",
    )(at, x, before, *wg, wu)


def pair_kernel(keep, received, stats, out):
    width = out.shape[1] - 3 * LANES
    for start, size in blocks_of(width, 512):
        cols = slice(start, start + size)
        out[:, cols] = (keep[:, cols].astype(f32) + received[:, cols].astype(f32)).astype(bf16)
    for p, term in enumerate(thirds(joined(stats, width) + joined(received, width))):
        out[:, width + p * LANES : width + (p + 1) * LANES] = term


def pair(keep, received, stats):
    return pl.pallas_call(
        pair_kernel,
        in_specs=[VMEM] * 3,
        out_specs=VMEM,
        out_shape=jax.ShapeDtypeStruct(received.shape, bf16),
        compiler_params=params(4),
        name="pair",
    )(keep, received, stats)


def gated_kernel(model, one, two, out):
    half = out.shape[1]
    scale = lax.rsqrt((joined(one, 2 * half) + joined(two, 2 * half)) / model + epsilon)
    for c in range(half // LANES):
        gate, up = (
            scale * (one[:, lanes(at)].astype(f32) + two[:, lanes(at)].astype(f32))
            for at in (c, half // LANES + c)
        )
        out[:, lanes(c)] = (gate / (1.0 + jnp.exp(-gate)) * up).astype(bf16)


def gated(model, one, two, after):
    rows, width = one.shape
    return pl.pallas_call(
        lambda _, *refs: gated_kernel(model, *refs),
        in_specs=[ANY] + [VMEM] * 2,
        out_specs=VMEM,
        out_shape=jax.ShapeDtypeStruct((rows, (width - 3 * LANES) // 2), bf16),
        compiler_params=params(4),
        name="gated",
    )(after, one, two)


def contract_kernel(hidden, w, out):
    for start, size in blocks_of(w.shape[1], 512):
        cols = slice(start, start + size)
        out[:, cols] = jnp.dot(hidden[...], w[:, cols], preferred_element_type=f32)


def contract(hidden, w):
    rows = hidden.shape[0]
    return pl.pallas_call(
        contract_kernel,
        in_specs=[VMEM] * 2,
        out_specs=VMEM,
        out_shape=jax.ShapeDtypeStruct((rows, w.shape[1]), f32),
        compiler_params=params(4),
        cost_estimate=cost(rows, w),
        name="contract",
    )(hidden, w)


def contract_last_kernel(n, at, hidden, w, before, resid_0, resid_1, own, *rest):
    sends, acc = rest[:-1], rest[-1]
    share = own.shape[0]
    for start, size in blocks_of(w.shape[1], 512):
        cols = slice(start, start + size)
        acc[:, cols] = before[:, cols] + jnp.dot(hidden[...], w[:, cols], preferred_element_type=f32)

    def block(ref, index):
        if share % 8 == 0:
            return ref[pl.ds(pl.multiple_of(index * share, share), share), :]
        chosen = ref[:share, :]
        for b in range(1, n):
            chosen = jnp.where(index == b, ref[b * share : (b + 1) * share, :], chosen)
        return chosen

    half = resid_0.shape[1]
    mine = block(acc, at[3])
    own[:, :half] = mine[:, :half] + block(resid_0, at[3])
    own[:, half:] = mine[:, half:] + block(resid_1, at[3])
    for s in range(1, n):
        sends[s - 1][...] = block(acc, at[3] ^ s).astype(bf16)


def contract_last(n, at, hidden, w, before, *resid):
    rows, cols = before.shape
    share = rows // n
    return pl.pallas_call(
        lambda *refs: contract_last_kernel(n, *refs),
        in_specs=[SMEM] + [VMEM] * 5,
        out_specs=[VMEM] * n,
        out_shape=[jax.ShapeDtypeStruct((share, cols), f32)]
        + [jax.ShapeDtypeStruct((share, cols), bf16)] * (n - 1),
        scratch_shapes=[pltpu.VMEM((rows, cols), f32)],
        compiler_params=params(4),
        cost_estimate=cost(rows, w),
        name="contract_last",
    )(at, hidden, w, before, *resid)


def add_kernel(one, two, *rest):
    out = rest[-1]
    for start, size in blocks_of(out.shape[1], 512):
        cols = slice(start, start + size)
        out[:, cols] = (one[:, cols].astype(f32) + two[:, cols].astype(f32)).astype(bf16)


def add(one, two, *tokens):
    return pl.pallas_call(
        add_kernel,
        in_specs=[VMEM] * 2 + [ANY] * len(tokens),
        out_specs=VMEM,
        out_shape=jax.ShapeDtypeStruct(one.shape, bf16),
        compiler_params=params(4),
        name="add",
    )(one, two, *tokens)


def swap(x, axis, bit):
    n = lax.axis_size(axis)
    return lax.ppermute(x, axis, [(i, i ^ bit) for i in range(n)])


def bits_of(axis):
    n = lax.axis_size(axis)
    return [1 << b for b in range(n.bit_length() - 1)]


def gathered(x, axis, token):
    parts = [x]
    for bit in reversed(bits_of(axis)):
        parts = parts + [swap(p, axis, bit) for p in parts]
        if bit > 1:
            parts = parts[:-1] + [hold(parts[-1], token)]
    return parts


def summed(x, axis, order, *tokens):
    *bits, last = bits_of(axis)[::order]
    for bit in bits:
        x = add(x, swap(x, axis, bit), *(tokens if bit == bits[-1] else ()))
    return x, swap(x, axis, last)


def per_device(tokens, attn_gain, ffn_gain, w_query, key_matrix, value_matrix, w_out, w_gate, w_up, w_down, kv_cache, lengths, slots):
    rows, model = tokens.shape
    wide_at, head_at = lax.axis_index("wide"), lax.axis_index("head")
    wide_size, head_size = lax.axis_size("wide"), lax.axis_size("head")
    places = jnp.stack([wide_at, (wide_at == wide_size - 1).astype(jnp.int32), wide_at & 1, head_at])
    at = places.astype(jnp.int32)

    half = HEAD_WIDTH // 2
    positions = (
        jnp.broadcast_to(lengths[:, None], (lengths.shape[0], DRAFT_TOKENS))
        + jnp.arange(DRAFT_TOKENS, dtype=jnp.int32)[None, :]
    ).reshape(rows).astype(f32)
    exponent = jnp.arange(half, dtype=f32) * (2.0 / HEAD_WIDTH)
    angles = positions[:, None] * (theta_base ** (-exponent))[None, :]
    cos, sin = jnp.cos(angles), jnp.sin(angles)
    cos = jnp.concatenate([cos, cos], axis=1)
    sin = jnp.concatenate([-sin, sin], axis=1)

    qkv, own = project(at, tokens, attn_gain, w_query, key_matrix, value_matrix)
    depth = own.shape[1]
    half = depth // 2
    gain = ffn_gain.reshape(depth // LANES, LANES)

    flat_cache = kv_cache.reshape((-1,) + kv_cache.shape[2:])
    meta = jnp.concatenate([at, lengths, slots])
    cache, gate_0, token = fetch(at, (qkv, meta, cos, sin), Part(flat_cache), Part(w_gate, 0, half))
    cache = cache.reshape(kv_cache.shape)
    value, w_out = attend(meta, cos, sin, cache, gathered(qkv, "wide", token), Part(w_out))

    quarter = half // 2
    up_0, gate_1, token = fetch(at, value, Part(w_up, 0, half), Part(w_gate, half, quarter))
    out_0, attended = output_first(gathered(value, "wide", token), w_out)
    out_1 = output_second(attended, w_out)
    parts_0 = summed(out_0, "head", 1)
    gate_2, token = fetch(at, parts_0[0], Part(w_gate, half + quarter, quarter))
    parts_1 = summed(out_1, "head", -1, token)
    send, keep, resid_0, squares, up_1 = expand_first(
        at, own, gain, parts_0, gate_0, up_0, Part(w_up, half, half)
    )
    gate_1 = (gate_1, gate_2)
    send, resid_1, x = expand_send(at, own, gain, parts_1, gate_1, up_1, send, squares)
    received = swap(send, "wide", 1)
    total = pair(expand_keep(at, x, gate_1, up_1, keep), received, send)
    down_own, down_other, token = fetch(at, total, Part(w_down, side=0), Part(w_down, side=1))
    for bit in bits_of("wide")[1:-1]:
        there = swap(total, "wide", bit)
        total = pair(total, there, total)
    hidden = gated(model, total, swap(total, "wide", bits_of("wide")[-1]), token)
    other = swap(hidden, "wide", 1)
    total, *sends = contract_last(
        head_size, at, other, down_other, contract(hidden, down_own), resid_0, resid_1
    )
    for s, send in reversed(list(enumerate(sends, 1))):
        total = total + swap(send, "head", s).astype(f32)
    return total.astype(bf16)


def solution(mesh):
    in_specs = (
        P("grp", None),
        P(),
        P("wide"),
        P("wide", "head"),
        P("wide", "head"),
        P("wide", "head"),
        P("head", "wide"),
        P("wide", "head"),
        P("wide", "head"),
        P("head", "wide"),
        P(None, "grp", "wide", "head"),
        P("grp"),
        P("grp"),
    )
    out_specs = P(("grp", "head"), "wide")
    return jax.shard_map(
        per_device, mesh=mesh, in_specs=in_specs, out_specs=out_specs, check_vma=False
    )
```

```python
import math

import jax
import jax.numpy as jnp
from jax import lax
from jax.experimental import pallas as pl
from jax.experimental.pallas import tpu as pltpu
from jax.sharding import PartitionSpec as P

HEAD_WIDTH = 128
DRAFT_TOKENS = 4
LANES = 128
MIB = 1 << 20

epsilon = 1e-05
theta_base = 500000.0
neg_large = -1e30

f32 = jnp.float32
bf16 = jnp.bfloat16
ANY = pl.BlockSpec(memory_space=pl.ANY)
VMEM = pl.BlockSpec(memory_space=pltpu.VMEM)
SMEM = pl.BlockSpec(memory_space=pltpu.SMEM)
HBM = pl.BlockSpec(memory_space=pltpu.HBM)


def in_hbm(x):
    return pltpu.with_memory_space_constraint(x, pltpu.HBM)


def cost(rows, *weights):
    size = sum(w.size for w in weights)
    return pl.CostEstimate(flops=2 * rows * size, bytes_accessed=2 * size, transcendentals=0)


def params(mib):
    return pltpu.CompilerParams(vmem_limit_bytes=mib * MIB)


def blocks_of(width, most):
    step = max(b for b in range(LANES, most + 1, LANES) if width % b == 0)
    return [(at, step) for at in range(0, width, step)]


def thirds(x):
    high = x.astype(bf16)
    rest = x - high.astype(f32)
    middle = rest.astype(bf16)
    return high, middle, (rest - middle.astype(f32)).astype(bf16)


def lanes(at):
    return slice(at * LANES, (at + 1) * LANES)


PIECES = 8


class Part:
    def __init__(self, array, first=0, count=None, side=None):
        rows = array.shape[0]
        self.array, self.first, self.side = array, first, side
        self.count = rows // 2 if side is not None else rows if count is None else count
        self.shape = (self.count,) + array.shape[1:]
        self.out = pltpu.VMEM(self.shape, array.dtype)

    def copies(self, at, source, held, sems):
        step = max(1, self.count // PIECES)
        base = self.first
        if self.side is not None:
            base = pl.multiple_of((at[2] if self.side == 0 else 1 - at[2]) * self.count, LANES)
        return [
            pltpu.make_async_copy(
                source.at[pl.ds(base + p * step, step)], held.at[pl.ds(p * step, step)], sems.at[p]
            )
            for p in range(self.count // step)
        ]


def beside(copies, at, compute):
    for copy in copies:
        copy.start()
    pl.when(at[2] >= 0)(compute)
    for copy in copies:
        copy.wait()


def fetch_kernel(wanted, skip, at, *refs):
    n, refs = len(wanted), refs[skip:]
    sources, held, token, sems = refs[:n], refs[n : 2 * n], refs[2 * n], refs[2 * n + 1 :]
    copies = sum([w.copies(at, *refs) for w, *refs in zip(wanted, sources, held, sems)], [])
    for copy in copies:
        copy.start()
    token[...] = jnp.zeros_like(token)
    for copy in copies:
        copy.wait()


def fetch(at, after, *wanted):
    after = after if isinstance(after, (list, tuple)) else [after]
    size = sum(math.prod(w.shape) for w in wanted)
    return pl.pallas_call(
        lambda *refs: fetch_kernel(wanted, len(after), *refs),
        in_specs=[SMEM] + [ANY] * len(after) + [HBM] * len(wanted),
        out_specs=[VMEM] * (len(wanted) + 1),
        out_shape=[w.out for w in wanted] + [pltpu.VMEM((8, LANES), f32)],
        scratch_shapes=[pltpu.SemaphoreType.DMA((2 * PIECES,))] * len(wanted),
        compiler_params=params(2),
        cost_estimate=pl.CostEstimate(flops=0, bytes_accessed=4 * size, transcendentals=0),
        name="fetch",
    )(at, *after, *[in_hbm(w.array) for w in wanted])


def hold(x, token):
    return pl.pallas_call(
        lambda *_: None,
        in_specs=[VMEM, ANY],
        out_specs=VMEM,
        out_shape=jax.ShapeDtypeStruct(x.shape, x.dtype),
        input_output_aliases={0: 0},
        compiler_params=params(1),
        name="hold",
    )(x, token)


def project_kernel(chunks, at, tokens, gain, wq, wk, wv, out, own, tok, gain_f, norm, bq, bk, bv, acc, gain_b, sems):
    rows, model = tok.shape
    depth, q_cols = bq.shape
    kv_cols = bk.shape[1]
    step = depth // chunks
    gain_copy = pltpu.make_async_copy(gain, gain_b, sems.at[3 + chunks])
    gain_copy.start()
    copies = [
        pltpu.make_async_copy(tokens, tok, sems.at[0]),
        pltpu.make_async_copy(wk, bk, sems.at[1]),
        pltpu.make_async_copy(wv, bv, sems.at[2]),
    ] + [
        pltpu.make_async_copy(
            wq.at[pl.ds(c * step, step)], bq.at[pl.ds(c * step, step)], sems.at[3 + c]
        )
        for c in range(chunks)
    ]
    for copy in copies:
        copy.start()
    gain_copy.wait()
    gain_f[...] = gain_b[...].astype(f32)
    copies[0].wait()
    squares = jnp.zeros((rows, LANES), f32)
    for c in range(model // LANES):
        part = tok[:, lanes(c)].astype(f32)
        squares = squares + part * part
    scale = lax.rsqrt(jnp.sum(squares, axis=1, keepdims=True) / model + epsilon)
    count = depth // LANES
    for c in range(count):
        index = at[0] * count + c
        part = tok[:, pl.ds(pl.multiple_of(index * LANES, LANES), LANES)]
        own[:, lanes(c)] = part
        norm[:, lanes(c)] = (part.astype(f32) * scale * gain_f[pl.ds(index, 1), :]).astype(bf16)
    for copy, held, base in ((copies[1], bk, q_cols), (copies[2], bv, q_cols + kv_cols)):
        copy.wait()
        out[:, base : base + kv_cols] = jnp.dot(
            norm[...], held[...], preferred_element_type=f32
        ).astype(out.dtype)
    for c in range(chunks):
        copies[3 + c].wait()
        for start, size in blocks_of(q_cols, 512):
            cols = slice(start, start + size)
            term = jnp.dot(
                norm[:, c * step : (c + 1) * step],
                bq[c * step : (c + 1) * step, cols],
                preferred_element_type=f32,
            )
            if c:
                term = acc[:, cols] + term
            if c < chunks - 1:
                acc[:, cols] = term
            else:
                out[:, cols] = term.astype(out.dtype)


def project(at, tokens, gain, wq, wk, wv):
    rows, model = tokens.shape
    depth, q_cols = wq.shape
    kv_cols = wk.shape[1]
    chunks = max(1, min(8, depth // 256))
    return pl.pallas_call(
        lambda *refs: project_kernel(chunks, *refs),
        in_specs=[SMEM] + [HBM] * 5,
        out_specs=[VMEM, VMEM],
        out_shape=[
            jax.ShapeDtypeStruct((rows, q_cols + 2 * kv_cols), bf16),
            jax.ShapeDtypeStruct((rows, depth), bf16),
        ],
        scratch_shapes=[
            pltpu.VMEM((rows, model), bf16),
            pltpu.VMEM((model // LANES, LANES), f32),
            pltpu.VMEM((rows, depth), bf16),
            pltpu.VMEM(wq.shape, bf16),
            pltpu.VMEM(wk.shape, bf16),
            pltpu.VMEM(wv.shape, bf16),
            pltpu.VMEM((rows, q_cols), f32),
            pltpu.VMEM((model // LANES, LANES), bf16),
            pltpu.SemaphoreType.DMA((4 + chunks,)),
        ],
        compiler_params=params(16),
        cost_estimate=cost(rows, wq, wk, wv),
        name="project",
    )(at, in_hbm(tokens), in_hbm(gain.reshape(model // LANES, LANES)), in_hbm(wq), in_hbm(wk), in_hbm(wv))


def attend_kernel(n, part, at, cos, sin, cache, source, *rest):
    parts, (out, held, queries, total, stats_f, sems) = rest[:n], rest[n:]
    beside(
        part.copies(at, source, held, sems),
        at,
        lambda: attention(at, cos, sin, cache, parts, out, queries, total, stats_f),
    )


def attention(at, cos, sin, cache, parts, out, queries, total, stats_f):
    rows, q_cols = queries.shape
    context, kv_cols = cache.shape[2:]
    kv_heads = kv_cols // HEAD_WIDTH
    heads = q_cols // HEAD_WIDTH
    group = heads // kv_heads
    tile = 2 * DRAFT_TOKENS
    requests = rows // DRAFT_TOKENS

    def length(r):
        return at[4 + r]

    def slot(r):
        return at[4 + requests + r]

    last = at[1]
    base = at[0] * context

    def column(c):
        return sum(p[:, lanes(c)].astype(f32) for p in parts)

    def rotated(x):
        return x * cos[...] + pltpu.roll(x, HEAD_WIDTH // 2, 1) * sin[...]

    for h in range(heads):
        queries[:, lanes(h)] = (rotated(column(h)) * HEAD_WIDTH ** (-0.5)).astype(bf16).astype(f32)
    new_keys = [rotated(column(heads + k)).astype(bf16) for k in range(kv_heads)]
    new_values = [column(heads + kv_heads + k).astype(bf16) for k in range(kv_heads)]

    high = group * tile
    row = lax.broadcasted_iota(jnp.int32, (high, 1), 0) % tile
    first = row < DRAFT_TOKENS
    position = lax.broadcasted_iota(jnp.int32, (high, context), 1) + base
    draft_col = lax.broadcasted_iota(jnp.int32, (high, rows), 1)
    lane = lax.broadcasted_iota(jnp.int32, (tile, LANES), 1)
    nt = (((1,), (1,)), ((), ()))
    for i in range(rows // tile):
        request = 2 * i
        limit = jnp.where(first, length(request), length(request + 1))
        live = position < limit
        own_at = tile * i + jnp.where(first, 0, DRAFT_TOKENS)
        seen = (draft_col >= own_at) & (draft_col <= tile * i + row) & (last > 0)
        stats = jnp.zeros((tile, LANES), f32)
        for k in range(kv_heads):
            q = jnp.concatenate(
                [queries[tile * i : tile * (i + 1), lanes(k * group + g)] for g in range(group)], axis=0
            ).astype(bf16)
            scores = [
                lax.dot_general(q, cache[0, slot(request + s), :, lanes(k)], nt, preferred_element_type=f32)
                for s in range(2)
            ]
            score = jnp.where(live, jnp.where(first, scores[0], scores[1]), neg_large)
            draft = lax.dot_general(q, new_keys[k], nt, preferred_element_type=f32)
            draft = jnp.where(seen, draft, neg_large)
            top = jnp.maximum(
                jnp.max(score, axis=1, keepdims=True), jnp.max(draft, axis=1, keepdims=True)
            )
            weight = jnp.where(live, jnp.exp(score - top), 0.0)
            draft_weight = jnp.where(seen, jnp.exp(draft - top), 0.0)
            mass = jnp.sum(weight, axis=1, keepdims=True) + jnp.sum(draft_weight, axis=1, keepdims=True)
            weight = weight.astype(bf16)
            sums = [
                jnp.dot(weight, cache[1, slot(request + s), :, lanes(k)], preferred_element_type=f32)
                for s in range(2)
            ]
            value = jnp.where(first, sums[0], sums[1]) + jnp.dot(
                draft_weight.astype(bf16), new_values[k], preferred_element_type=f32
            )
            some = mass > 0.0
            safe = jnp.where(some, mass, 1.0)
            value = value / safe
            lse = jnp.where(some, top + jnp.log(safe), neg_large)
            for g in range(group):
                at_rows = slice(tile * g, tile * (g + 1))
                total[tile * i : tile * (i + 1), lanes(k * group + g)] = value[at_rows]
                stats = jnp.where(lane == k * group + g, lse[at_rows], stats)
        stats_f[tile * i : tile * (i + 1), :] = stats
    out[:, :q_cols] = total[...].astype(bf16)
    for p, term in enumerate(thirds(stats_f[...])):
        out[:, q_cols + p * LANES : q_cols + (p + 1) * LANES] = term


def attend(at, cos, sin, cache, parts, part):
    rows, width = parts[0].shape
    q_cols = width - 2 * cache.shape[3]
    return pl.pallas_call(
        lambda *refs: attend_kernel(len(parts), part, *refs),
        in_specs=[SMEM] + [VMEM] * 3 + [HBM] + [VMEM] * len(parts),
        out_specs=[VMEM, VMEM],
        out_shape=[jax.ShapeDtypeStruct((rows, q_cols + 3 * LANES), bf16), part.out],
        scratch_shapes=[
            pltpu.VMEM((rows, q_cols), f32),
            pltpu.VMEM((rows, q_cols), f32),
            pltpu.VMEM((rows, LANES), f32),
            pltpu.SemaphoreType.DMA((2 * PIECES,)),
        ],
        compiler_params=params(6),
        cost_estimate=cost(rows, cache),
        name="attend",
    )(at, cos, sin, cache, in_hbm(part.array), *parts)


def joined(ref, start):
    return sum(ref[:, start + p * LANES : start + (p + 1) * LANES].astype(f32) for p in range(3))


def product(x, w, out, base, width):
    for start, size in blocks_of(width, 512):
        out[:, start : start + size] = jnp.dot(
            x[...], w[:, base + start : base + start + size], preferred_element_type=f32
        ).astype(out.dtype)


def output_first_kernel(n, w, *rest):
    values, (out, attended) = rest[:n], rest[n:]
    heads = attended.shape[1] // HEAD_WIDTH
    stats = [joined(v, attended.shape[1]) for v in values]
    top = stats[0]
    for s in stats[1:]:
        top = jnp.maximum(top, s)
    shares = [jnp.exp(s - top) for s in stats]
    whole = sum(shares)
    shares = [s / whole for s in shares]
    for h in range(heads):
        attended[:, lanes(h)] = sum(
            v[:, lanes(h)].astype(f32) * s[:, h : h + 1] for v, s in zip(values, shares)
        ).astype(bf16)
    product(attended, w, out, 0, out.shape[1])


def output_first(values, w):
    rows, half = values[0].shape[0], w.shape[1] // 2
    return pl.pallas_call(
        lambda *refs: output_first_kernel(len(values), *refs),
        in_specs=[VMEM] * (1 + len(values)),
        out_specs=[VMEM] * 2,
        out_shape=[
            jax.ShapeDtypeStruct((rows, half), bf16),
            jax.ShapeDtypeStruct((rows, w.shape[0]), bf16),
        ],
        compiler_params=params(4),
        cost_estimate=cost(rows, w),
        name="output_first",
    )(w, *values)


def output_second(attended, w):
    rows, half = attended.shape[0], w.shape[1] // 2
    return pl.pallas_call(
        lambda x, w, out: product(x, w, out, half, half),
        in_specs=[VMEM] * 2,
        out_specs=VMEM,
        out_shape=jax.ShapeDtypeStruct((rows, half), bf16),
        compiler_params=params(4),
        cost_estimate=cost(rows, w),
        name="output_second",
    )(attended, w)


def half_of(side, x, wg, wu, out, before=None):
    half = wg[0].shape[1] // 2
    for base, pieces in ((0, wg), (half, wu)):
        for start, size in blocks_of(half, 512):
            cols = pl.ds(pl.multiple_of(side * half + start, LANES), size)
            to = slice(base + start, base + start + size)
            term = None if before is None else before[:, to]
            row = 0
            for w in pieces:
                more = jnp.dot(x[:, row : row + w.shape[0]], w[:, cols], preferred_element_type=f32)
                term = more if term is None else term + more
                row += w.shape[0]
            out[:, to] = term.astype(out.dtype)


def residual(which, own, gain, parts, resid, x, gain_f):
    gain_f[...] = gain[...].astype(f32)
    count = resid.shape[1] // LANES
    square = jnp.zeros((own.shape[0], LANES), f32)
    for c in range(count):
        at = which * count + c
        value = own[:, lanes(at)].astype(f32) + sum(p[:, lanes(c)].astype(f32) for p in parts)
        value = value.astype(bf16).astype(f32)
        resid[:, lanes(c)] = value
        square = square + value * value
        x[:, lanes(c)] = (value * gain_f[at : at + 1, :]).astype(bf16)
    return square


def expand_first_kernel(n, part, at, own, gain, wg, wu, source, *rest):
    parts, (send, keep, resid, squares, held, x, gain_f, sems) = rest[:n], rest[n:]

    def compute():
        squares[...] = residual(0, own, gain, parts, resid, x, gain_f)
        half_of(1 - at[2], x, [wg], [wu], send)
        half_of(at[2], x, [wg], [wu], keep)

    beside(part.copies(at, source, held, sems), at, compute)


def expand_first(at, own, gain, parts, wg, wu, part):
    rows, depth = own.shape
    width = wg.shape[1]
    return pl.pallas_call(
        lambda *refs: expand_first_kernel(len(parts), part, *refs),
        in_specs=[SMEM] + [VMEM] * 4 + [HBM] + [VMEM] * len(parts),
        out_specs=[VMEM] * 5,
        out_shape=[
            jax.ShapeDtypeStruct((rows, width), f32),
            jax.ShapeDtypeStruct((rows, width), f32),
            jax.ShapeDtypeStruct((rows, depth // 2), f32),
            jax.ShapeDtypeStruct((rows, LANES), f32),
            part.out,
        ],
        scratch_shapes=[
            pltpu.VMEM((rows, depth // 2), bf16),
            pltpu.VMEM((depth // LANES, LANES), f32),
            pltpu.SemaphoreType.DMA((2 * PIECES,)),
        ],
        compiler_params=params(4),
        cost_estimate=cost(rows, wg, wu),
        name="expand_first",
    )(at, own, gain, wg, wu, in_hbm(part.array), *parts)


def expand_send_kernel(n, g, at, own, gain, before, squares, *rest):
    wg, wu, parts, (out, resid, x, gain_f) = rest[:g], rest[g : g + 1], rest[g + 1 : g + 1 + n], rest[g + 1 + n :]
    square = squares[...] + residual(1, own, gain, parts, resid, x, gain_f)
    square = jnp.broadcast_to(jnp.sum(square, axis=1, keepdims=True), square.shape)
    width = wu[0].shape[1]
    for p, term in enumerate(thirds(square)):
        out[:, width + p * LANES : width + (p + 1) * LANES] = term
    half_of(1 - at[2], x, wg, wu, out, before)


def expand_send(at, own, gain, parts, wg, wu, before, squares):
    rows, depth = own.shape
    return pl.pallas_call(
        lambda *refs: expand_send_kernel(len(parts), len(wg), *refs),
        in_specs=[SMEM] + [VMEM] * (5 + len(wg) + len(parts)),
        out_specs=[VMEM] * 3,
        out_shape=[
            jax.ShapeDtypeStruct((rows, wu.shape[1] + 3 * LANES), bf16),
            jax.ShapeDtypeStruct((rows, depth // 2), f32),
            jax.ShapeDtypeStruct((rows, depth // 2), bf16),
        ],
        scratch_shapes=[pltpu.VMEM((depth // LANES, LANES), f32)],
        compiler_params=params(4),
        cost_estimate=cost(rows, wu),
        name="expand_send",
    )(at, own, gain, before, squares, *wg, wu, *parts)


def expand_keep(at, x, wg, wu, before):
    rows = x.shape[0]
    return pl.pallas_call(
        lambda at, x, before, *refs: half_of(at[2], x, refs[:-2], refs[-2:-1], refs[-1], before),
        in_specs=[SMEM] + [VMEM] * (3 + len(wg)),
        out_specs=VMEM,
        out_shape=jax.ShapeDtypeStruct((rows, wu.shape[1]), bf16),
        compiler_params=params(4),
        cost_estimate=cost(rows, wu),
        name="expand_keep",
    )(at, x, before, *wg, wu)


def pair_kernel(keep, received, stats, out):
    width = out.shape[1] - 3 * LANES
    for start, size in blocks_of(width, 512):
        cols = slice(start, start + size)
        out[:, cols] = (keep[:, cols].astype(f32) + received[:, cols].astype(f32)).astype(bf16)
    for p, term in enumerate(thirds(joined(stats, width) + joined(received, width))):
        out[:, width + p * LANES : width + (p + 1) * LANES] = term


def pair(keep, received, stats):
    return pl.pallas_call(
        pair_kernel,
        in_specs=[VMEM] * 3,
        out_specs=VMEM,
        out_shape=jax.ShapeDtypeStruct(received.shape, bf16),
        compiler_params=params(4),
        name="pair",
    )(keep, received, stats)


def gated_kernel(model, one, two, out):
    half = out.shape[1]
    scale = lax.rsqrt((joined(one, 2 * half) + joined(two, 2 * half)) / model + epsilon)
    for c in range(half // LANES):
        gate, up = (
            scale * (one[:, lanes(at)].astype(f32) + two[:, lanes(at)].astype(f32))
            for at in (c, half // LANES + c)
        )
        out[:, lanes(c)] = (gate / (1.0 + jnp.exp(-gate)) * up).astype(bf16)


def gated(model, one, two, after):
    rows, width = one.shape
    return pl.pallas_call(
        lambda _, *refs: gated_kernel(model, *refs),
        in_specs=[ANY] + [VMEM] * 2,
        out_specs=VMEM,
        out_shape=jax.ShapeDtypeStruct((rows, (width - 3 * LANES) // 2), bf16),
        compiler_params=params(4),
        name="gated",
    )(after, one, two)


def contract_kernel(hidden, w, out):
    for start, size in blocks_of(w.shape[1], 512):
        cols = slice(start, start + size)
        out[:, cols] = jnp.dot(hidden[...], w[:, cols], preferred_element_type=f32)


def contract(hidden, w):
    rows = hidden.shape[0]
    return pl.pallas_call(
        contract_kernel,
        in_specs=[VMEM] * 2,
        out_specs=VMEM,
        out_shape=jax.ShapeDtypeStruct((rows, w.shape[1]), f32),
        compiler_params=params(4),
        cost_estimate=cost(rows, w),
        name="contract",
    )(hidden, w)


def contract_last_kernel(n, at, hidden, w, before, resid_0, resid_1, own, *rest):
    sends, acc = rest[:-1], rest[-1]
    share = own.shape[0]
    for start, size in blocks_of(w.shape[1], 512):
        cols = slice(start, start + size)
        acc[:, cols] = before[:, cols] + jnp.dot(hidden[...], w[:, cols], preferred_element_type=f32)

    def block(ref, index):
        if share % 8 == 0:
            return ref[pl.ds(pl.multiple_of(index * share, share), share), :]
        chosen = ref[:share, :]
        for b in range(1, n):
            chosen = jnp.where(index == b, ref[b * share : (b + 1) * share, :], chosen)
        return chosen

    half = resid_0.shape[1]
    mine = block(acc, at[3])
    own[:, :half] = mine[:, :half] + block(resid_0, at[3])
    own[:, half:] = mine[:, half:] + block(resid_1, at[3])
    for s in range(1, n):
        sends[s - 1][...] = block(acc, at[3] ^ s).astype(bf16)


def contract_last(n, at, hidden, w, before, *resid):
    rows, cols = before.shape
    share = rows // n
    return pl.pallas_call(
        lambda *refs: contract_last_kernel(n, *refs),
        in_specs=[SMEM] + [VMEM] * 5,
        out_specs=[VMEM] * n,
        out_shape=[jax.ShapeDtypeStruct((share, cols), f32)]
        + [jax.ShapeDtypeStruct((share, cols), bf16)] * (n - 1),
        scratch_shapes=[pltpu.VMEM((rows, cols), f32)],
        compiler_params=params(4),
        cost_estimate=cost(rows, w),
        name="contract_last",
    )(at, hidden, w, before, *resid)


def add_kernel(one, two, *rest):
    out = rest[-1]
    for start, size in blocks_of(out.shape[1], 512):
        cols = slice(start, start + size)
        out[:, cols] = (one[:, cols].astype(f32) + two[:, cols].astype(f32)).astype(bf16)


def add(one, two, *tokens):
    return pl.pallas_call(
        add_kernel,
        in_specs=[VMEM] * 2 + [ANY] * len(tokens),
        out_specs=VMEM,
        out_shape=jax.ShapeDtypeStruct(one.shape, bf16),
        compiler_params=params(4),
        name="add",
    )(one, two, *tokens)


def swap(x, axis, bit):
    n = lax.axis_size(axis)
    return lax.ppermute(x, axis, [(i, i ^ bit) for i in range(n)])


def bits_of(axis):
    n = lax.axis_size(axis)
    return [1 << b for b in range(n.bit_length() - 1)]


def gathered(x, axis, token):
    parts = [x]
    for bit in reversed(bits_of(axis)):
        parts = parts + [swap(p, axis, bit) for p in parts]
        if bit > 1:
            parts = parts[:-1] + [hold(parts[-1], token)]
    return parts


def summed(x, axis, order, *tokens):
    *bits, last = bits_of(axis)[::order]
    for bit in bits:
        x = add(x, swap(x, axis, bit), *(tokens if bit == bits[-1] else ()))
    return x, swap(x, axis, last)


def per_device(tokens, attn_gain, ffn_gain, w_query, key_matrix, value_matrix, w_out, w_gate, w_up, w_down, kv_cache, lengths, slots):
    rows, model = tokens.shape
    wide_at, head_at = lax.axis_index("wide"), lax.axis_index("head")
    wide_size, head_size = lax.axis_size("wide"), lax.axis_size("head")
    places = jnp.stack([wide_at, (wide_at == wide_size - 1).astype(jnp.int32), wide_at & 1, head_at])
    at = places.astype(jnp.int32)

    half = HEAD_WIDTH // 2
    positions = (
        jnp.broadcast_to(lengths[:, None], (lengths.shape[0], DRAFT_TOKENS))
        + jnp.arange(DRAFT_TOKENS, dtype=jnp.int32)[None, :]
    ).reshape(rows).astype(f32)
    exponent = jnp.arange(half, dtype=f32) * (2.0 / HEAD_WIDTH)
    angles = positions[:, None] * (theta_base ** (-exponent))[None, :]
    cos, sin = jnp.cos(angles), jnp.sin(angles)
    cos = jnp.concatenate([cos, cos], axis=1)
    sin = jnp.concatenate([-sin, sin], axis=1)

    qkv, own = project(at, tokens, attn_gain, w_query, key_matrix, value_matrix)
    depth = own.shape[1]
    half = depth // 2
    gain = ffn_gain.reshape(depth // LANES, LANES)

    flat_cache = kv_cache.reshape((-1,) + kv_cache.shape[2:])
    meta = jnp.concatenate([at, lengths, slots])
    cache, gate_0, token = fetch(at, (qkv, meta, cos, sin), Part(flat_cache), Part(w_gate, 0, half))
    cache = cache.reshape(kv_cache.shape)
    value, w_out = attend(meta, cos, sin, cache, gathered(qkv, "wide", token), Part(w_out))

    quarter = half // 2
    up_0, gate_1, token = fetch(at, value, Part(w_up, 0, half), Part(w_gate, half, quarter))
    out_0, attended = output_first(gathered(value, "wide", token), w_out)
    out_1 = output_second(attended, w_out)
    parts_0 = summed(out_0, "head", -1)
    gate_2, token = fetch(at, parts_0[0], Part(w_gate, half + quarter, quarter))
    parts_1 = summed(out_1, "head", 1, token)
    send, keep, resid_0, squares, up_1 = expand_first(
        at, own, gain, parts_0, gate_0, up_0, Part(w_up, half, half)
    )
    gate_1 = (gate_1, gate_2)
    send, resid_1, x = expand_send(at, own, gain, parts_1, gate_1, up_1, send, squares)
    received = swap(send, "wide", 1)
    total = pair(expand_keep(at, x, gate_1, up_1, keep), received, send)
    down_own, down_other, token = fetch(at, total, Part(w_down, side=0), Part(w_down, side=1))
    for bit in bits_of("wide")[1:-1]:
        there = swap(total, "wide", bit)
        total = pair(total, there, total)
    hidden = gated(model, total, swap(total, "wide", bits_of("wide")[-1]), token)
    other = swap(hidden, "wide", 1)
    total, *sends = contract_last(
        head_size, at, other, down_other, contract(hidden, down_own), resid_0, resid_1
    )
    for s, send in reversed(list(enumerate(sends, 1))):
        total = total + swap(send, "head", s).astype(f32)
    return total.astype(bf16)


def solution(mesh):
    in_specs = (
        P("grp", None),
        P(),
        P("wide"),
        P("wide", "head"),
        P("wide", "head"),
        P("wide", "head"),
        P("head", "wide"),
        P("wide", "head"),
        P("wide", "head"),
        P("head", "wide"),
        P(None, "grp", "wide", "head"),
        P("grp"),
        P("grp"),
    )
    out_specs = P(("grp", "head"), "wide")
    return jax.shard_map(
        per_device, mesh=mesh, in_specs=in_specs, out_specs=out_specs, check_vma=False
    )
```

```python
import math

import jax
import jax.numpy as jnp
from jax import lax
from jax.experimental import pallas as pl
from jax.experimental.pallas import tpu as pltpu
from jax.sharding import PartitionSpec as P

HEAD_WIDTH = 128
DRAFT_TOKENS = 4
LANES = 128
GAP = 32
MIB = 1 << 20

epsilon = 1e-05
theta_base = 500000.0
neg_large = -1e30

f32 = jnp.float32
bf16 = jnp.bfloat16
ANY = pl.BlockSpec(memory_space=pl.ANY)
VMEM = pl.BlockSpec(memory_space=pltpu.VMEM)
SMEM = pl.BlockSpec(memory_space=pltpu.SMEM)
HBM = pl.BlockSpec(memory_space=pltpu.HBM)


def in_hbm(x):
    return pltpu.with_memory_space_constraint(x, pltpu.HBM)


def cost(rows, *weights):
    size = sum(w.size for w in weights)
    return pl.CostEstimate(flops=2 * rows * size, bytes_accessed=2 * size, transcendentals=0)


def params(mib):
    return pltpu.CompilerParams(vmem_limit_bytes=mib * MIB)


def blocks_of(width, most):
    step = max(b for b in range(LANES, most + 1, LANES) if width % b == 0)
    return [(at, step) for at in range(0, width, step)]


def thirds(x):
    high = x.astype(bf16)
    rest = x - high.astype(f32)
    middle = rest.astype(bf16)
    return high, middle, (rest - middle.astype(f32)).astype(bf16)


def packed(x, gap):
    high, middle, low = (term.astype(f32) for term in thirds(x))
    lane = lax.broadcasted_iota(jnp.int32, x.shape, 1)
    if gap > 1:
        middle, low = pltpu.roll(middle, gap, 1), pltpu.roll(low, 2 * gap, 1)
    return jnp.where(lane < gap, high, jnp.where(lane < 2 * gap, middle, low)).astype(bf16)


def joined(ref, start, gap):
    tile = ref[:, start : start + LANES].astype(f32)
    if gap == 1:
        return tile[:, 0:1] + tile[:, 1:2] + tile[:, 2:3]
    return tile + pltpu.roll(tile, LANES - gap, 1) + pltpu.roll(tile, LANES - 2 * gap, 1)


def lanes(at):
    return slice(at * LANES, (at + 1) * LANES)


PIECES = 8


class Part:
    def __init__(self, array, first=0, count=None, side=None):
        rows = array.shape[0]
        self.array, self.first, self.side = array, first, side
        self.count = rows // 2 if side is not None else rows if count is None else count
        self.shape = (self.count,) + array.shape[1:]
        self.out = pltpu.VMEM(self.shape, array.dtype)

    def copies(self, at, source, held, sems):
        step = max(1, self.count // PIECES)
        base = self.first
        if self.side is not None:
            base = pl.multiple_of((at[2] if self.side == 0 else 1 - at[2]) * self.count, LANES)
        return [
            pltpu.make_async_copy(
                source.at[pl.ds(base + p * step, step)], held.at[pl.ds(p * step, step)], sems.at[p]
            )
            for p in range(self.count // step)
        ]


def beside(copies, at, compute):
    for copy in copies:
        copy.start()
    pl.when(at[2] >= 0)(compute)
    for copy in copies:
        copy.wait()


def fetch_kernel(wanted, skip, at, *refs):
    n, refs = len(wanted), refs[skip:]
    sources, held, token, sems = refs[:n], refs[n : 2 * n], refs[2 * n], refs[2 * n + 1 :]
    copies = sum([w.copies(at, *refs) for w, *refs in zip(wanted, sources, held, sems)], [])
    for copy in copies:
        copy.start()
    token[...] = jnp.zeros_like(token)
    for copy in copies:
        copy.wait()


def fetch(at, after, *wanted):
    after = after if isinstance(after, (list, tuple)) else [after]
    size = sum(math.prod(w.shape) for w in wanted)
    return pl.pallas_call(
        lambda *refs: fetch_kernel(wanted, len(after), *refs),
        in_specs=[SMEM] + [ANY] * len(after) + [HBM] * len(wanted),
        out_specs=[VMEM] * (len(wanted) + 1),
        out_shape=[w.out for w in wanted] + [pltpu.VMEM((8, LANES), f32)],
        scratch_shapes=[pltpu.SemaphoreType.DMA((2 * PIECES,))] * len(wanted),
        compiler_params=params(2),
        cost_estimate=pl.CostEstimate(flops=0, bytes_accessed=4 * size, transcendentals=0),
        name="fetch",
    )(at, *after, *[in_hbm(w.array) for w in wanted])


def hold(x, token):
    return pl.pallas_call(
        lambda *_: None,
        in_specs=[VMEM, ANY],
        out_specs=VMEM,
        out_shape=jax.ShapeDtypeStruct(x.shape, x.dtype),
        input_output_aliases={0: 0},
        compiler_params=params(1),
        name="hold",
    )(x, token)


def project_kernel(chunks, at, tokens, gain, wq, wk, wv, out, own, tok, gain_f, norm, bq, bk, bv, acc, gain_b, sems):
    rows, model = tok.shape
    depth, q_cols = bq.shape
    kv_cols = bk.shape[1]
    step = depth // chunks
    gain_copy = pltpu.make_async_copy(gain, gain_b, sems.at[3 + chunks])
    gain_copy.start()
    copies = [
        pltpu.make_async_copy(tokens, tok, sems.at[0]),
        pltpu.make_async_copy(wk, bk, sems.at[1]),
        pltpu.make_async_copy(wv, bv, sems.at[2]),
    ] + [
        pltpu.make_async_copy(
            wq.at[pl.ds(c * step, step)], bq.at[pl.ds(c * step, step)], sems.at[3 + c]
        )
        for c in range(chunks)
    ]
    for copy in copies:
        copy.start()
    gain_copy.wait()
    gain_f[...] = gain_b[...].astype(f32)
    copies[0].wait()
    squares = jnp.zeros((rows, LANES), f32)
    for c in range(model // LANES):
        part = tok[:, lanes(c)].astype(f32)
        squares = squares + part * part
    scale = lax.rsqrt(jnp.sum(squares, axis=1, keepdims=True) / model + epsilon)
    count = depth // LANES
    for c in range(count):
        index = at[0] * count + c
        part = tok[:, pl.ds(pl.multiple_of(index * LANES, LANES), LANES)]
        own[:, lanes(c)] = part
        norm[:, lanes(c)] = (part.astype(f32) * scale * gain_f[pl.ds(index, 1), :]).astype(bf16)
    for copy, held, base in ((copies[1], bk, q_cols), (copies[2], bv, q_cols + kv_cols)):
        copy.wait()
        out[:, base : base + kv_cols] = jnp.dot(
            norm[...], held[...], preferred_element_type=f32
        ).astype(out.dtype)
    for c in range(chunks):
        copies[3 + c].wait()
        for start, size in blocks_of(q_cols, 512):
            cols = slice(start, start + size)
            term = jnp.dot(
                norm[:, c * step : (c + 1) * step],
                bq[c * step : (c + 1) * step, cols],
                preferred_element_type=f32,
            )
            if c:
                term = acc[:, cols] + term
            if c < chunks - 1:
                acc[:, cols] = term
            else:
                out[:, cols] = term.astype(out.dtype)


def project(at, tokens, gain, wq, wk, wv):
    rows, model = tokens.shape
    depth, q_cols = wq.shape
    kv_cols = wk.shape[1]
    chunks = max(1, min(8, depth // 256))
    return pl.pallas_call(
        lambda *refs: project_kernel(chunks, *refs),
        in_specs=[SMEM] + [HBM] * 5,
        out_specs=[VMEM, VMEM],
        out_shape=[
            jax.ShapeDtypeStruct((rows, q_cols + 2 * kv_cols), bf16),
            jax.ShapeDtypeStruct((rows, depth), bf16),
        ],
        scratch_shapes=[
            pltpu.VMEM((rows, model), bf16),
            pltpu.VMEM((model // LANES, LANES), f32),
            pltpu.VMEM((rows, depth), bf16),
            pltpu.VMEM(wq.shape, bf16),
            pltpu.VMEM(wk.shape, bf16),
            pltpu.VMEM(wv.shape, bf16),
            pltpu.VMEM((rows, q_cols), f32),
            pltpu.VMEM((model // LANES, LANES), bf16),
            pltpu.SemaphoreType.DMA((4 + chunks,)),
        ],
        compiler_params=params(16),
        cost_estimate=cost(rows, wq, wk, wv),
        name="project",
    )(at, in_hbm(tokens), in_hbm(gain.reshape(model // LANES, LANES)), in_hbm(wq), in_hbm(wk), in_hbm(wv))


def attend_kernel(n, part, at, cos, sin, cache, source, *rest):
    parts, (out, held, queries, total, stats_f, sems) = rest[:n], rest[n:]
    beside(
        part.copies(at, source, held, sems),
        at,
        lambda: attention(at, cos, sin, cache, parts, out, queries, total, stats_f),
    )


def attention(at, cos, sin, cache, parts, out, queries, total, stats_f):
    rows, q_cols = queries.shape
    context, kv_cols = cache.shape[2:]
    kv_heads = kv_cols // HEAD_WIDTH
    heads = q_cols // HEAD_WIDTH
    group = heads // kv_heads
    tile = 2 * DRAFT_TOKENS
    requests = rows // DRAFT_TOKENS

    def length(r):
        return at[4 + r]

    def slot(r):
        return at[4 + requests + r]

    last = at[1]
    base = at[0] * context

    def column(c):
        return sum(p[:, lanes(c)].astype(f32) for p in parts)

    def rotated(x):
        return x * cos[...] + pltpu.roll(x, HEAD_WIDTH // 2, 1) * sin[...]

    for h in range(heads):
        queries[:, lanes(h)] = (rotated(column(h)) * HEAD_WIDTH ** (-0.5)).astype(bf16).astype(f32)
    new_keys = [rotated(column(heads + k)).astype(bf16) for k in range(kv_heads)]
    new_values = [column(heads + kv_heads + k).astype(bf16) for k in range(kv_heads)]

    high = group * tile
    row = lax.broadcasted_iota(jnp.int32, (high, 1), 0) % tile
    first = row < DRAFT_TOKENS
    position = lax.broadcasted_iota(jnp.int32, (high, context), 1) + base
    draft_col = lax.broadcasted_iota(jnp.int32, (high, rows), 1)
    lane = lax.broadcasted_iota(jnp.int32, (tile, LANES), 1)
    nt = (((1,), (1,)), ((), ()))
    for i in range(rows // tile):
        request = 2 * i
        limit = jnp.where(first, length(request), length(request + 1))
        live = position < limit
        own_at = tile * i + jnp.where(first, 0, DRAFT_TOKENS)
        seen = (draft_col >= own_at) & (draft_col <= tile * i + row) & (last > 0)
        stats = jnp.zeros((tile, LANES), f32)
        for k in range(kv_heads):
            q = jnp.concatenate(
                [queries[tile * i : tile * (i + 1), lanes(k * group + g)] for g in range(group)], axis=0
            ).astype(bf16)
            scores = [
                lax.dot_general(q, cache[0, slot(request + s), :, lanes(k)], nt, preferred_element_type=f32)
                for s in range(2)
            ]
            score = jnp.where(live, jnp.where(first, scores[0], scores[1]), neg_large)
            draft = lax.dot_general(q, new_keys[k], nt, preferred_element_type=f32)
            draft = jnp.where(seen, draft, neg_large)
            top = jnp.maximum(
                jnp.max(score, axis=1, keepdims=True), jnp.max(draft, axis=1, keepdims=True)
            )
            weight = jnp.where(live, jnp.exp(score - top), 0.0)
            draft_weight = jnp.where(seen, jnp.exp(draft - top), 0.0)
            mass = jnp.sum(weight, axis=1, keepdims=True) + jnp.sum(draft_weight, axis=1, keepdims=True)
            weight = weight.astype(bf16)
            sums = [
                jnp.dot(weight, cache[1, slot(request + s), :, lanes(k)], preferred_element_type=f32)
                for s in range(2)
            ]
            value = jnp.where(first, sums[0], sums[1]) + jnp.dot(
                draft_weight.astype(bf16), new_values[k], preferred_element_type=f32
            )
            some = mass > 0.0
            safe = jnp.where(some, mass, 1.0)
            value = value / safe
            lse = jnp.where(some, top + jnp.log(safe), neg_large)
            for g in range(group):
                at_rows = slice(tile * g, tile * (g + 1))
                total[tile * i : tile * (i + 1), lanes(k * group + g)] = value[at_rows]
                stats = jnp.where(lane == k * group + g, lse[at_rows], stats)
        stats_f[tile * i : tile * (i + 1), :] = stats
    out[:, :q_cols] = total[...].astype(bf16)
    out[:, q_cols : q_cols + LANES] = packed(stats_f[...], GAP)


def attend(at, cos, sin, cache, parts, part):
    rows, width = parts[0].shape
    q_cols = width - 2 * cache.shape[3]
    return pl.pallas_call(
        lambda *refs: attend_kernel(len(parts), part, *refs),
        in_specs=[SMEM] + [VMEM] * 3 + [HBM] + [VMEM] * len(parts),
        out_specs=[VMEM, VMEM],
        out_shape=[jax.ShapeDtypeStruct((rows, q_cols + LANES), bf16), part.out],
        scratch_shapes=[
            pltpu.VMEM((rows, q_cols), f32),
            pltpu.VMEM((rows, q_cols), f32),
            pltpu.VMEM((rows, LANES), f32),
            pltpu.SemaphoreType.DMA((2 * PIECES,)),
        ],
        compiler_params=params(6),
        cost_estimate=cost(rows, cache),
        name="attend",
    )(at, cos, sin, cache, in_hbm(part.array), *parts)


def product(x, w, out, base, width):
    for start, size in blocks_of(width, 512):
        out[:, start : start + size] = jnp.dot(
            x[...], w[:, base + start : base + start + size], preferred_element_type=f32
        ).astype(out.dtype)


def output_first_kernel(n, w, *rest):
    values, (out, attended) = rest[:n], rest[n:]
    heads = attended.shape[1] // HEAD_WIDTH
    stats = [joined(v, attended.shape[1], GAP) for v in values]
    top = stats[0]
    for s in stats[1:]:
        top = jnp.maximum(top, s)
    shares = [jnp.exp(s - top) for s in stats]
    whole = sum(shares)
    shares = [s / whole for s in shares]
    for h in range(heads):
        attended[:, lanes(h)] = sum(
            v[:, lanes(h)].astype(f32) * s[:, h : h + 1] for v, s in zip(values, shares)
        ).astype(bf16)
    product(attended, w, out, 0, out.shape[1])


def output_first(values, w):
    rows, half = values[0].shape[0], w.shape[1] // 2
    return pl.pallas_call(
        lambda *refs: output_first_kernel(len(values), *refs),
        in_specs=[VMEM] * (1 + len(values)),
        out_specs=[VMEM] * 2,
        out_shape=[
            jax.ShapeDtypeStruct((rows, half), bf16),
            jax.ShapeDtypeStruct((rows, w.shape[0]), bf16),
        ],
        compiler_params=params(4),
        cost_estimate=cost(rows, w),
        name="output_first",
    )(w, *values)


def output_second(attended, w):
    rows, half = attended.shape[0], w.shape[1] // 2
    return pl.pallas_call(
        lambda x, w, out: product(x, w, out, half, half),
        in_specs=[VMEM] * 2,
        out_specs=VMEM,
        out_shape=jax.ShapeDtypeStruct((rows, half), bf16),
        compiler_params=params(4),
        cost_estimate=cost(rows, w),
        name="output_second",
    )(attended, w)


def half_of(side, x, wg, wu, out, before=None):
    half = wg[0].shape[1] // 2
    for base, pieces in ((0, wg), (half, wu)):
        for start, size in blocks_of(half, 512):
            cols = pl.ds(pl.multiple_of(side * half + start, LANES), size)
            to = slice(base + start, base + start + size)
            term = None if before is None else before[:, to]
            row = 0
            for w in pieces:
                more = jnp.dot(x[:, row : row + w.shape[0]], w[:, cols], preferred_element_type=f32)
                term = more if term is None else term + more
                row += w.shape[0]
            out[:, to] = term.astype(out.dtype)


def residual(which, own, gain, parts, resid, x, gain_f):
    gain_f[...] = gain[...].astype(f32)
    count = resid.shape[1] // LANES
    square = jnp.zeros((own.shape[0], LANES), f32)
    for c in range(count):
        at = which * count + c
        value = own[:, lanes(at)].astype(f32) + sum(p[:, lanes(c)].astype(f32) for p in parts)
        value = value.astype(bf16).astype(f32)
        resid[:, lanes(c)] = value
        square = square + value * value
        x[:, lanes(c)] = (value * gain_f[at : at + 1, :]).astype(bf16)
    return square


def expand_first_kernel(n, part, at, own, gain, wg, wu, source, *rest):
    parts, (send, keep, resid, squares, held, x, gain_f, sems) = rest[:n], rest[n:]

    def compute():
        squares[...] = residual(0, own, gain, parts, resid, x, gain_f)
        half_of(1 - at[2], x, [wg], [wu], send)
        half_of(at[2], x, [wg], [wu], keep)

    beside(part.copies(at, source, held, sems), at, compute)


def expand_first(at, own, gain, parts, wg, wu, part):
    rows, depth = own.shape
    width = wg.shape[1]
    return pl.pallas_call(
        lambda *refs: expand_first_kernel(len(parts), part, *refs),
        in_specs=[SMEM] + [VMEM] * 4 + [HBM] + [VMEM] * len(parts),
        out_specs=[VMEM] * 5,
        out_shape=[
            jax.ShapeDtypeStruct((rows, width), f32),
            jax.ShapeDtypeStruct((rows, width), f32),
            jax.ShapeDtypeStruct((rows, depth // 2), f32),
            jax.ShapeDtypeStruct((rows, LANES), f32),
            part.out,
        ],
        scratch_shapes=[
            pltpu.VMEM((rows, depth // 2), bf16),
            pltpu.VMEM((depth // LANES, LANES), f32),
            pltpu.SemaphoreType.DMA((2 * PIECES,)),
        ],
        compiler_params=params(4),
        cost_estimate=cost(rows, wg, wu),
        name="expand_first",
    )(at, own, gain, wg, wu, in_hbm(part.array), *parts)


def expand_send_kernel(n, g, at, own, gain, before, squares, *rest):
    wg, wu, parts, (out, resid, x, gain_f) = rest[:g], rest[g : g + 1], rest[g + 1 : g + 1 + n], rest[g + 1 + n :]
    square = squares[...] + residual(1, own, gain, parts, resid, x, gain_f)
    square = jnp.broadcast_to(jnp.sum(square, axis=1, keepdims=True), square.shape)
    width = wu[0].shape[1]
    out[:, width : width + LANES] = packed(square, 1)
    half_of(1 - at[2], x, wg, wu, out, before)


def expand_send(at, own, gain, parts, wg, wu, before, squares):
    rows, depth = own.shape
    return pl.pallas_call(
        lambda *refs: expand_send_kernel(len(parts), len(wg), *refs),
        in_specs=[SMEM] + [VMEM] * (5 + len(wg) + len(parts)),
        out_specs=[VMEM] * 3,
        out_shape=[
            jax.ShapeDtypeStruct((rows, wu.shape[1] + LANES), bf16),
            jax.ShapeDtypeStruct((rows, depth // 2), f32),
            jax.ShapeDtypeStruct((rows, depth // 2), bf16),
        ],
        scratch_shapes=[pltpu.VMEM((depth // LANES, LANES), f32)],
        compiler_params=params(4),
        cost_estimate=cost(rows, wu),
        name="expand_send",
    )(at, own, gain, before, squares, *wg, wu, *parts)


def expand_keep(at, x, wg, wu, before):
    rows = x.shape[0]
    return pl.pallas_call(
        lambda at, x, before, *refs: half_of(at[2], x, refs[:-2], refs[-2:-1], refs[-1], before),
        in_specs=[SMEM] + [VMEM] * (3 + len(wg)),
        out_specs=VMEM,
        out_shape=jax.ShapeDtypeStruct((rows, wu.shape[1]), bf16),
        compiler_params=params(4),
        cost_estimate=cost(rows, wu),
        name="expand_keep",
    )(at, x, before, *wg, wu)


def pair_kernel(keep, received, stats, out):
    width = out.shape[1] - LANES
    for start, size in blocks_of(width, 512):
        cols = slice(start, start + size)
        out[:, cols] = (keep[:, cols].astype(f32) + received[:, cols].astype(f32)).astype(bf16)
    square = joined(stats, width, 1) + joined(received, width, 1)
    out[:, width : width + LANES] = packed(jnp.broadcast_to(square, (square.shape[0], LANES)), 1)


def pair(keep, received, stats):
    return pl.pallas_call(
        pair_kernel,
        in_specs=[VMEM] * 3,
        out_specs=VMEM,
        out_shape=jax.ShapeDtypeStruct(received.shape, bf16),
        compiler_params=params(4),
        name="pair",
    )(keep, received, stats)


def gated_kernel(model, one, two, out):
    half = out.shape[1]
    scale = lax.rsqrt((joined(one, 2 * half, 1) + joined(two, 2 * half, 1)) / model + epsilon)
    for c in range(half // LANES):
        gate, up = (
            scale * (one[:, lanes(at)].astype(f32) + two[:, lanes(at)].astype(f32))
            for at in (c, half // LANES + c)
        )
        out[:, lanes(c)] = (gate / (1.0 + jnp.exp(-gate)) * up).astype(bf16)


def gated(model, one, two, after):
    rows, width = one.shape
    return pl.pallas_call(
        lambda _, *refs: gated_kernel(model, *refs),
        in_specs=[ANY] + [VMEM] * 2,
        out_specs=VMEM,
        out_shape=jax.ShapeDtypeStruct((rows, (width - LANES) // 2), bf16),
        compiler_params=params(4),
        name="gated",
    )(after, one, two)


def contract_kernel(hidden, w, out):
    for start, size in blocks_of(w.shape[1], 512):
        cols = slice(start, start + size)
        out[:, cols] = jnp.dot(hidden[...], w[:, cols], preferred_element_type=f32)


def contract(hidden, w):
    rows = hidden.shape[0]
    return pl.pallas_call(
        contract_kernel,
        in_specs=[VMEM] * 2,
        out_specs=VMEM,
        out_shape=jax.ShapeDtypeStruct((rows, w.shape[1]), f32),
        compiler_params=params(4),
        cost_estimate=cost(rows, w),
        name="contract",
    )(hidden, w)


def contract_last_kernel(n, at, hidden, w, before, resid_0, resid_1, own, *rest):
    sends, acc = rest[:-1], rest[-1]
    share = own.shape[0]
    for start, size in blocks_of(w.shape[1], 512):
        cols = slice(start, start + size)
        acc[:, cols] = before[:, cols] + jnp.dot(hidden[...], w[:, cols], preferred_element_type=f32)

    def block(ref, index):
        if share % 8 == 0:
            return ref[pl.ds(pl.multiple_of(index * share, share), share), :]
        chosen = ref[:share, :]
        for b in range(1, n):
            chosen = jnp.where(index == b, ref[b * share : (b + 1) * share, :], chosen)
        return chosen

    half = resid_0.shape[1]
    mine = block(acc, at[3])
    own[:, :half] = mine[:, :half] + block(resid_0, at[3])
    own[:, half:] = mine[:, half:] + block(resid_1, at[3])
    for s in range(1, n):
        sends[s - 1][...] = block(acc, at[3] ^ s).astype(bf16)


def contract_last(n, at, hidden, w, before, *resid):
    rows, cols = before.shape
    share = rows // n
    return pl.pallas_call(
        lambda *refs: contract_last_kernel(n, *refs),
        in_specs=[SMEM] + [VMEM] * 5,
        out_specs=[VMEM] * n,
        out_shape=[jax.ShapeDtypeStruct((share, cols), f32)]
        + [jax.ShapeDtypeStruct((share, cols), bf16)] * (n - 1),
        scratch_shapes=[pltpu.VMEM((rows, cols), f32)],
        compiler_params=params(4),
        cost_estimate=cost(rows, w),
        name="contract_last",
    )(at, hidden, w, before, *resid)


def add_kernel(one, two, *rest):
    out = rest[-1]
    for start, size in blocks_of(out.shape[1], 512):
        cols = slice(start, start + size)
        out[:, cols] = (one[:, cols].astype(f32) + two[:, cols].astype(f32)).astype(bf16)


def add(one, two, *tokens):
    return pl.pallas_call(
        add_kernel,
        in_specs=[VMEM] * 2 + [ANY] * len(tokens),
        out_specs=VMEM,
        out_shape=jax.ShapeDtypeStruct(one.shape, bf16),
        compiler_params=params(4),
        name="add",
    )(one, two, *tokens)


def swap(x, axis, bit):
    n = lax.axis_size(axis)
    return lax.ppermute(x, axis, [(i, i ^ bit) for i in range(n)])


def bits_of(axis):
    n = lax.axis_size(axis)
    return [1 << b for b in range(n.bit_length() - 1)]


def gathered(x, axis, token):
    parts = [x]
    for bit in reversed(bits_of(axis)):
        parts = parts + [swap(p, axis, bit) for p in parts]
        if bit > 1:
            parts = parts[:-1] + [hold(parts[-1], token)]
    return parts


def summed(x, axis, order, *tokens):
    *bits, last = bits_of(axis)[::order]
    for bit in bits:
        x = add(x, swap(x, axis, bit), *(tokens if bit == bits[-1] else ()))
    return x, swap(x, axis, last)


def per_device(tokens, attn_gain, ffn_gain, w_query, key_matrix, value_matrix, w_out, w_gate, w_up, w_down, kv_cache, lengths, slots):
    rows, model = tokens.shape
    wide_at, head_at = lax.axis_index("wide"), lax.axis_index("head")
    wide_size, head_size = lax.axis_size("wide"), lax.axis_size("head")
    places = jnp.stack([wide_at, (wide_at == wide_size - 1).astype(jnp.int32), wide_at & 1, head_at])
    at = places.astype(jnp.int32)

    half = HEAD_WIDTH // 2
    positions = (
        jnp.broadcast_to(lengths[:, None], (lengths.shape[0], DRAFT_TOKENS))
        + jnp.arange(DRAFT_TOKENS, dtype=jnp.int32)[None, :]
    ).reshape(rows).astype(f32)
    exponent = jnp.arange(half, dtype=f32) * (2.0 / HEAD_WIDTH)
    angles = positions[:, None] * (theta_base ** (-exponent))[None, :]
    cos, sin = jnp.cos(angles), jnp.sin(angles)
    cos = jnp.concatenate([cos, cos], axis=1)
    sin = jnp.concatenate([-sin, sin], axis=1)

    qkv, own = project(at, tokens, attn_gain, w_query, key_matrix, value_matrix)
    depth = own.shape[1]
    half = depth // 2
    gain = ffn_gain.reshape(depth // LANES, LANES)

    flat_cache = kv_cache.reshape((-1,) + kv_cache.shape[2:])
    meta = jnp.concatenate([at, lengths, slots])
    cache, gate_0, token = fetch(at, (qkv, meta, cos, sin), Part(flat_cache), Part(w_gate, 0, half))
    cache = cache.reshape(kv_cache.shape)
    value, w_out = attend(meta, cos, sin, cache, gathered(qkv, "wide", token), Part(w_out))

    quarter = half // 2
    up_0, gate_1, token = fetch(at, value, Part(w_up, 0, half), Part(w_gate, half, quarter))
    out_0, attended = output_first(gathered(value, "wide", token), w_out)
    out_1 = output_second(attended, w_out)
    parts_0 = summed(out_0, "head", 1)
    gate_2, token = fetch(at, parts_0[0], Part(w_gate, half + quarter, quarter))
    parts_1 = summed(out_1, "head", -1, token)
    send, keep, resid_0, squares, up_1 = expand_first(
        at, own, gain, parts_0, gate_0, up_0, Part(w_up, half, half)
    )
    gate_1 = (gate_1, gate_2)
    send, resid_1, x = expand_send(at, own, gain, parts_1, gate_1, up_1, send, squares)
    received = swap(send, "wide", 1)
    total = pair(expand_keep(at, x, gate_1, up_1, keep), received, send)
    down_own, down_other, token = fetch(at, total, Part(w_down, side=0), Part(w_down, side=1))
    for bit in bits_of("wide")[1:-1]:
        there = swap(total, "wide", bit)
        total = pair(total, there, total)
    hidden = gated(model, total, swap(total, "wide", bits_of("wide")[-1]), token)
    other = swap(hidden, "wide", 1)
    total, *sends = contract_last(
        head_size, at, other, down_other, contract(hidden, down_own), resid_0, resid_1
    )
    for s, send in reversed(list(enumerate(sends, 1))):
        total = total + swap(send, "head", s).astype(f32)
    return total.astype(bf16)


def solution(mesh):
    in_specs = (
        P("grp", None),
        P(),
        P("wide"),
        P("wide", "head"),
        P("wide", "head"),
        P("wide", "head"),
        P("head", "wide"),
        P("wide", "head"),
        P("wide", "head"),
        P("head", "wide"),
        P(None, "grp", "wide", "head"),
        P("grp"),
        P("grp"),
    )
    out_specs = P(("grp", "head"), "wide")
    return jax.shard_map(
        per_device, mesh=mesh, in_specs=in_specs, out_specs=out_specs, check_vma=False
    )
```

```python
import math

import jax
import jax.numpy as jnp
from jax import lax
from jax.experimental import pallas as pl
from jax.experimental.pallas import tpu as pltpu
from jax.sharding import PartitionSpec as P

HEAD_WIDTH = 128
DRAFT_TOKENS = 4
LANES = 128
GAP = 32
MIB = 1 << 20

epsilon = 1e-05
theta_base = 500000.0
neg_large = -1e30

f32 = jnp.float32
bf16 = jnp.bfloat16
ANY = pl.BlockSpec(memory_space=pl.ANY)
VMEM = pl.BlockSpec(memory_space=pltpu.VMEM)
SMEM = pl.BlockSpec(memory_space=pltpu.SMEM)
HBM = pl.BlockSpec(memory_space=pltpu.HBM)


def in_hbm(x):
    return pltpu.with_memory_space_constraint(x, pltpu.HBM)


def cost(rows, *weights):
    size = sum(w.size for w in weights)
    return pl.CostEstimate(flops=2 * rows * size, bytes_accessed=2 * size, transcendentals=0)


def params(mib):
    return pltpu.CompilerParams(vmem_limit_bytes=mib * MIB)


def blocks_of(width, most):
    step = max(b for b in range(LANES, most + 1, LANES) if width % b == 0)
    return [(at, step) for at in range(0, width, step)]


def thirds(x):
    high = x.astype(bf16)
    rest = x - high.astype(f32)
    middle = rest.astype(bf16)
    return high, middle, (rest - middle.astype(f32)).astype(bf16)


def packed(x, gap):
    high, middle, low = (term.astype(f32) for term in thirds(x))
    lane = lax.broadcasted_iota(jnp.int32, x.shape, 1)
    if gap > 1:
        middle, low = pltpu.roll(middle, gap, 1), pltpu.roll(low, 2 * gap, 1)
    return jnp.where(lane < gap, high, jnp.where(lane < 2 * gap, middle, low)).astype(bf16)


def joined(ref, start, gap):
    tile = ref[:, start : start + LANES].astype(f32)
    if gap == 1:
        return tile[:, 0:1] + tile[:, 1:2] + tile[:, 2:3]
    return tile + pltpu.roll(tile, LANES - gap, 1) + pltpu.roll(tile, LANES - 2 * gap, 1)


def lanes(at):
    return slice(at * LANES, (at + 1) * LANES)


PIECES = 4


class Part:
    def __init__(self, array, first=0, count=None, side=None):
        rows = array.shape[0]
        self.array, self.first, self.side = array, first, side
        self.count = rows // 2 if side is not None else rows if count is None else count
        self.shape = (self.count,) + array.shape[1:]
        self.out = pltpu.VMEM(self.shape, array.dtype)

    def copies(self, at, source, held, sems):
        step = max(1, self.count // PIECES)
        base = self.first
        if self.side is not None:
            base = pl.multiple_of((at[2] if self.side == 0 else 1 - at[2]) * self.count, LANES)
        return [
            pltpu.make_async_copy(
                source.at[pl.ds(base + p * step, step)], held.at[pl.ds(p * step, step)], sems.at[p]
            )
            for p in range(self.count // step)
        ]


def beside(copies, at, compute):
    for copy in copies:
        copy.start()
    pl.when(at[2] >= 0)(compute)
    for copy in copies:
        copy.wait()


def fetch_kernel(wanted, skip, at, *refs):
    n, refs = len(wanted), refs[skip:]
    sources, held, token, sems = refs[:n], refs[n : 2 * n], refs[2 * n], refs[2 * n + 1 :]
    copies = sum([w.copies(at, *refs) for w, *refs in zip(wanted, sources, held, sems)], [])
    for copy in copies:
        copy.start()
    token[...] = jnp.zeros_like(token)
    for copy in copies:
        copy.wait()


def fetch(at, after, *wanted):
    after = after if isinstance(after, (list, tuple)) else [after]
    size = sum(math.prod(w.shape) for w in wanted)
    return pl.pallas_call(
        lambda *refs: fetch_kernel(wanted, len(after), *refs),
        in_specs=[SMEM] + [ANY] * len(after) + [HBM] * len(wanted),
        out_specs=[VMEM] * (len(wanted) + 1),
        out_shape=[w.out for w in wanted] + [pltpu.VMEM((8, LANES), f32)],
        scratch_shapes=[pltpu.SemaphoreType.DMA((2 * PIECES,))] * len(wanted),
        compiler_params=params(2),
        cost_estimate=pl.CostEstimate(flops=0, bytes_accessed=4 * size, transcendentals=0),
        name="fetch",
    )(at, *after, *[in_hbm(w.array) for w in wanted])


def hold(x, token):
    return pl.pallas_call(
        lambda *_: None,
        in_specs=[VMEM, ANY],
        out_specs=VMEM,
        out_shape=jax.ShapeDtypeStruct(x.shape, x.dtype),
        input_output_aliases={0: 0},
        compiler_params=params(1),
        name="hold",
    )(x, token)


def project_kernel(chunks, at, tokens, gain, wq, wk, wv, out, own, tok, gain_f, norm, bq, bk, bv, acc, gain_b, sems):
    rows, model = tok.shape
    depth, q_cols = bq.shape
    kv_cols = bk.shape[1]
    step = depth // chunks
    gain_copy = pltpu.make_async_copy(gain, gain_b, sems.at[3 + chunks])
    gain_copy.start()
    copies = [
        pltpu.make_async_copy(tokens, tok, sems.at[0]),
        pltpu.make_async_copy(wk, bk, sems.at[1]),
        pltpu.make_async_copy(wv, bv, sems.at[2]),
    ] + [
        pltpu.make_async_copy(
            wq.at[pl.ds(c * step, step)], bq.at[pl.ds(c * step, step)], sems.at[3 + c]
        )
        for c in range(chunks)
    ]
    for copy in copies:
        copy.start()
    gain_copy.wait()
    gain_f[...] = gain_b[...].astype(f32)
    copies[0].wait()
    squares = jnp.zeros((rows, LANES), f32)
    for c in range(model // LANES):
        part = tok[:, lanes(c)].astype(f32)
        squares = squares + part * part
    scale = lax.rsqrt(jnp.sum(squares, axis=1, keepdims=True) / model + epsilon)
    count = depth // LANES
    for c in range(count):
        index = at[0] * count + c
        part = tok[:, pl.ds(pl.multiple_of(index * LANES, LANES), LANES)]
        own[:, lanes(c)] = part
        norm[:, lanes(c)] = (part.astype(f32) * scale * gain_f[pl.ds(index, 1), :]).astype(bf16)
    for copy, held, base in ((copies[1], bk, q_cols), (copies[2], bv, q_cols + kv_cols)):
        copy.wait()
        out[:, base : base + kv_cols] = jnp.dot(
            norm[...], held[...], preferred_element_type=f32
        ).astype(out.dtype)
    for c in range(chunks):
        copies[3 + c].wait()
        for start, size in blocks_of(q_cols, 512):
            cols = slice(start, start + size)
            term = jnp.dot(
                norm[:, c * step : (c + 1) * step],
                bq[c * step : (c + 1) * step, cols],
                preferred_element_type=f32,
            )
            if c:
                term = acc[:, cols] + term
            if c < chunks - 1:
                acc[:, cols] = term
            else:
                out[:, cols] = term.astype(out.dtype)


def project(at, tokens, gain, wq, wk, wv):
    rows, model = tokens.shape
    depth, q_cols = wq.shape
    kv_cols = wk.shape[1]
    chunks = max(1, min(8, depth // 256))
    return pl.pallas_call(
        lambda *refs: project_kernel(chunks, *refs),
        in_specs=[SMEM] + [HBM] * 5,
        out_specs=[VMEM, VMEM],
        out_shape=[
            jax.ShapeDtypeStruct((rows, q_cols + 2 * kv_cols), bf16),
            jax.ShapeDtypeStruct((rows, depth), bf16),
        ],
        scratch_shapes=[
            pltpu.VMEM((rows, model), bf16),
            pltpu.VMEM((model // LANES, LANES), f32),
            pltpu.VMEM((rows, depth), bf16),
            pltpu.VMEM(wq.shape, bf16),
            pltpu.VMEM(wk.shape, bf16),
            pltpu.VMEM(wv.shape, bf16),
            pltpu.VMEM((rows, q_cols), f32),
            pltpu.VMEM((model // LANES, LANES), bf16),
            pltpu.SemaphoreType.DMA((4 + chunks,)),
        ],
        compiler_params=params(16),
        cost_estimate=cost(rows, wq, wk, wv),
        name="project",
    )(at, in_hbm(tokens), in_hbm(gain.reshape(model // LANES, LANES)), in_hbm(wq), in_hbm(wk), in_hbm(wv))


def attend_kernel(n, part, at, cos, sin, cache, source, *rest):
    parts, (out, held, queries, total, stats_f, sems) = rest[:n], rest[n:]
    beside(
        part.copies(at, source, held, sems),
        at,
        lambda: attention(at, cos, sin, cache, parts, out, queries, total, stats_f),
    )


def attention(at, cos, sin, cache, parts, out, queries, total, stats_f):
    rows, q_cols = queries.shape
    context, kv_cols = cache.shape[2:]
    kv_heads = kv_cols // HEAD_WIDTH
    heads = q_cols // HEAD_WIDTH
    group = heads // kv_heads
    tile = 2 * DRAFT_TOKENS
    requests = rows // DRAFT_TOKENS

    def length(r):
        return at[4 + r]

    def slot(r):
        return at[4 + requests + r]

    last = at[1]
    base = at[0] * context

    def column(c):
        return sum(p[:, lanes(c)].astype(f32) for p in parts)

    def rotated(x):
        return x * cos[...] + pltpu.roll(x, HEAD_WIDTH // 2, 1) * sin[...]

    for h in range(heads):
        queries[:, lanes(h)] = (rotated(column(h)) * HEAD_WIDTH ** (-0.5)).astype(bf16).astype(f32)
    new_keys = [rotated(column(heads + k)).astype(bf16) for k in range(kv_heads)]
    new_values = [column(heads + kv_heads + k).astype(bf16) for k in range(kv_heads)]

    high = group * tile
    row = lax.broadcasted_iota(jnp.int32, (high, 1), 0) % tile
    first = row < DRAFT_TOKENS
    position = lax.broadcasted_iota(jnp.int32, (high, context), 1) + base
    draft_col = lax.broadcasted_iota(jnp.int32, (high, rows), 1)
    lane = lax.broadcasted_iota(jnp.int32, (tile, LANES), 1)
    nt = (((1,), (1,)), ((), ()))
    for i in range(rows // tile):
        request = 2 * i
        limit = jnp.where(first, length(request), length(request + 1))
        live = position < limit
        own_at = tile * i + jnp.where(first, 0, DRAFT_TOKENS)
        seen = (draft_col >= own_at) & (draft_col <= tile * i + row) & (last > 0)
        stats = jnp.zeros((tile, LANES), f32)
        for k in range(kv_heads):
            q = jnp.concatenate(
                [queries[tile * i : tile * (i + 1), lanes(k * group + g)] for g in range(group)], axis=0
            ).astype(bf16)
            scores = [
                lax.dot_general(q, cache[0, slot(request + s), :, lanes(k)], nt, preferred_element_type=f32)
                for s in range(2)
            ]
            score = jnp.where(live, jnp.where(first, scores[0], scores[1]), neg_large)
            draft = lax.dot_general(q, new_keys[k], nt, preferred_element_type=f32)
            draft = jnp.where(seen, draft, neg_large)
            top = jnp.maximum(
                jnp.max(score, axis=1, keepdims=True), jnp.max(draft, axis=1, keepdims=True)
            )
            weight = jnp.where(live, jnp.exp(score - top), 0.0)
            draft_weight = jnp.where(seen, jnp.exp(draft - top), 0.0)
            mass = jnp.sum(weight, axis=1, keepdims=True) + jnp.sum(draft_weight, axis=1, keepdims=True)
            weight = weight.astype(bf16)
            sums = [
                jnp.dot(weight, cache[1, slot(request + s), :, lanes(k)], preferred_element_type=f32)
                for s in range(2)
            ]
            value = jnp.where(first, sums[0], sums[1]) + jnp.dot(
                draft_weight.astype(bf16), new_values[k], preferred_element_type=f32
            )
            some = mass > 0.0
            safe = jnp.where(some, mass, 1.0)
            value = value / safe
            lse = jnp.where(some, top + jnp.log(safe), neg_large)
            for g in range(group):
                at_rows = slice(tile * g, tile * (g + 1))
                total[tile * i : tile * (i + 1), lanes(k * group + g)] = value[at_rows]
                stats = jnp.where(lane == k * group + g, lse[at_rows], stats)
        stats_f[tile * i : tile * (i + 1), :] = stats
    out[:, :q_cols] = total[...].astype(bf16)
    out[:, q_cols : q_cols + LANES] = packed(stats_f[...], GAP)


def attend(at, cos, sin, cache, parts, part):
    rows, width = parts[0].shape
    q_cols = width - 2 * cache.shape[3]
    return pl.pallas_call(
        lambda *refs: attend_kernel(len(parts), part, *refs),
        in_specs=[SMEM] + [VMEM] * 3 + [HBM] + [VMEM] * len(parts),
        out_specs=[VMEM, VMEM],
        out_shape=[jax.ShapeDtypeStruct((rows, q_cols + LANES), bf16), part.out],
        scratch_shapes=[
            pltpu.VMEM((rows, q_cols), f32),
            pltpu.VMEM((rows, q_cols), f32),
            pltpu.VMEM((rows, LANES), f32),
            pltpu.SemaphoreType.DMA((2 * PIECES,)),
        ],
        compiler_params=params(6),
        cost_estimate=cost(rows, cache),
        name="attend",
    )(at, cos, sin, cache, in_hbm(part.array), *parts)


def product(x, w, out, base, width):
    for start, size in blocks_of(width, 512):
        out[:, start : start + size] = jnp.dot(
            x[...], w[:, base + start : base + start + size], preferred_element_type=f32
        ).astype(out.dtype)


def output_first_kernel(n, w, *rest):
    values, (out, attended) = rest[:n], rest[n:]
    heads = attended.shape[1] // HEAD_WIDTH
    stats = [joined(v, attended.shape[1], GAP) for v in values]
    top = stats[0]
    for s in stats[1:]:
        top = jnp.maximum(top, s)
    shares = [jnp.exp(s - top) for s in stats]
    whole = sum(shares)
    shares = [s / whole for s in shares]
    for h in range(heads):
        attended[:, lanes(h)] = sum(
            v[:, lanes(h)].astype(f32) * s[:, h : h + 1] for v, s in zip(values, shares)
        ).astype(bf16)
    product(attended, w, out, 0, out.shape[1])


def output_first(values, w):
    rows, half = values[0].shape[0], w.shape[1] // 2
    return pl.pallas_call(
        lambda *refs: output_first_kernel(len(values), *refs),
        in_specs=[VMEM] * (1 + len(values)),
        out_specs=[VMEM] * 2,
        out_shape=[
            jax.ShapeDtypeStruct((rows, half), bf16),
            jax.ShapeDtypeStruct((rows, w.shape[0]), bf16),
        ],
        compiler_params=params(4),
        cost_estimate=cost(rows, w),
        name="output_first",
    )(w, *values)


def output_second(attended, w):
    rows, half = attended.shape[0], w.shape[1] // 2
    return pl.pallas_call(
        lambda x, w, out: product(x, w, out, half, half),
        in_specs=[VMEM] * 2,
        out_specs=VMEM,
        out_shape=jax.ShapeDtypeStruct((rows, half), bf16),
        compiler_params=params(4),
        cost_estimate=cost(rows, w),
        name="output_second",
    )(attended, w)


def half_of(side, x, wg, wu, out, before=None):
    half = wg[0].shape[1] // 2
    for base, pieces in ((0, wg), (half, wu)):
        for start, size in blocks_of(half, 512):
            cols = pl.ds(pl.multiple_of(side * half + start, LANES), size)
            to = slice(base + start, base + start + size)
            term = None if before is None else before[:, to]
            row = 0
            for w in pieces:
                more = jnp.dot(x[:, row : row + w.shape[0]], w[:, cols], preferred_element_type=f32)
                term = more if term is None else term + more
                row += w.shape[0]
            out[:, to] = term.astype(out.dtype)


def residual(which, own, gain, parts, resid, x, gain_f):
    gain_f[...] = gain[...].astype(f32)
    count = resid.shape[1] // LANES
    square = jnp.zeros((own.shape[0], LANES), f32)
    for c in range(count):
        at = which * count + c
        value = own[:, lanes(at)].astype(f32) + sum(p[:, lanes(c)].astype(f32) for p in parts)
        value = value.astype(bf16).astype(f32)
        resid[:, lanes(c)] = value
        square = square + value * value
        x[:, lanes(c)] = (value * gain_f[at : at + 1, :]).astype(bf16)
    return square


def expand_first_kernel(n, part, at, own, gain, wg, wu, source, *rest):
    parts, (send, keep, resid, squares, held, x, gain_f, sems) = rest[:n], rest[n:]

    def compute():
        squares[...] = residual(0, own, gain, parts, resid, x, gain_f)
        half_of(1 - at[2], x, [wg], [wu], send)
        half_of(at[2], x, [wg], [wu], keep)

    beside(part.copies(at, source, held, sems), at, compute)


def expand_first(at, own, gain, parts, wg, wu, part):
    rows, depth = own.shape
    width = wg.shape[1]
    return pl.pallas_call(
        lambda *refs: expand_first_kernel(len(parts), part, *refs),
        in_specs=[SMEM] + [VMEM] * 4 + [HBM] + [VMEM] * len(parts),
        out_specs=[VMEM] * 5,
        out_shape=[
            jax.ShapeDtypeStruct((rows, width), f32),
            jax.ShapeDtypeStruct((rows, width), f32),
            jax.ShapeDtypeStruct((rows, depth // 2), f32),
            jax.ShapeDtypeStruct((rows, LANES), f32),
            part.out,
        ],
        scratch_shapes=[
            pltpu.VMEM((rows, depth // 2), bf16),
            pltpu.VMEM((depth // LANES, LANES), f32),
            pltpu.SemaphoreType.DMA((2 * PIECES,)),
        ],
        compiler_params=params(4),
        cost_estimate=cost(rows, wg, wu),
        name="expand_first",
    )(at, own, gain, wg, wu, in_hbm(part.array), *parts)


def expand_send_kernel(n, g, at, own, gain, before, squares, *rest):
    wg, wu, parts, (out, resid, x, gain_f) = rest[:g], rest[g : g + 1], rest[g + 1 : g + 1 + n], rest[g + 1 + n :]
    square = squares[...] + residual(1, own, gain, parts, resid, x, gain_f)
    square = jnp.broadcast_to(jnp.sum(square, axis=1, keepdims=True), square.shape)
    width = wu[0].shape[1]
    out[:, width : width + LANES] = packed(square, 1)
    half_of(1 - at[2], x, wg, wu, out, before)


def expand_send(at, own, gain, parts, wg, wu, before, squares):
    rows, depth = own.shape
    return pl.pallas_call(
        lambda *refs: expand_send_kernel(len(parts), len(wg), *refs),
        in_specs=[SMEM] + [VMEM] * (5 + len(wg) + len(parts)),
        out_specs=[VMEM] * 3,
        out_shape=[
            jax.ShapeDtypeStruct((rows, wu.shape[1] + LANES), bf16),
            jax.ShapeDtypeStruct((rows, depth // 2), f32),
            jax.ShapeDtypeStruct((rows, depth // 2), bf16),
        ],
        scratch_shapes=[pltpu.VMEM((depth // LANES, LANES), f32)],
        compiler_params=params(4),
        cost_estimate=cost(rows, wu),
        name="expand_send",
    )(at, own, gain, before, squares, *wg, wu, *parts)


def expand_keep(at, x, wg, wu, before):
    rows = x.shape[0]
    return pl.pallas_call(
        lambda at, x, before, *refs: half_of(at[2], x, refs[:-2], refs[-2:-1], refs[-1], before),
        in_specs=[SMEM] + [VMEM] * (3 + len(wg)),
        out_specs=VMEM,
        out_shape=jax.ShapeDtypeStruct((rows, wu.shape[1]), bf16),
        compiler_params=params(4),
        cost_estimate=cost(rows, wu),
        name="expand_keep",
    )(at, x, before, *wg, wu)


def pair_kernel(keep, received, stats, out):
    width = out.shape[1] - LANES
    for start, size in blocks_of(width, 512):
        cols = slice(start, start + size)
        out[:, cols] = (keep[:, cols].astype(f32) + received[:, cols].astype(f32)).astype(bf16)
    square = joined(stats, width, 1) + joined(received, width, 1)
    out[:, width : width + LANES] = packed(jnp.broadcast_to(square, (square.shape[0], LANES)), 1)


def pair(keep, received, stats):
    return pl.pallas_call(
        pair_kernel,
        in_specs=[VMEM] * 3,
        out_specs=VMEM,
        out_shape=jax.ShapeDtypeStruct(received.shape, bf16),
        compiler_params=params(4),
        name="pair",
    )(keep, received, stats)


def gated_kernel(model, one, two, out):
    half = out.shape[1]
    scale = lax.rsqrt((joined(one, 2 * half, 1) + joined(two, 2 * half, 1)) / model + epsilon)
    for c in range(half // LANES):
        gate, up = (
            scale * (one[:, lanes(at)].astype(f32) + two[:, lanes(at)].astype(f32))
            for at in (c, half // LANES + c)
        )
        out[:, lanes(c)] = (gate / (1.0 + jnp.exp(-gate)) * up).astype(bf16)


def gated(model, one, two, after):
    rows, width = one.shape
    return pl.pallas_call(
        lambda _, *refs: gated_kernel(model, *refs),
        in_specs=[ANY] + [VMEM] * 2,
        out_specs=VMEM,
        out_shape=jax.ShapeDtypeStruct((rows, (width - LANES) // 2), bf16),
        compiler_params=params(4),
        name="gated",
    )(after, one, two)


def contract_kernel(hidden, w, out):
    for start, size in blocks_of(w.shape[1], 512):
        cols = slice(start, start + size)
        out[:, cols] = jnp.dot(hidden[...], w[:, cols], preferred_element_type=f32)


def contract(hidden, w):
    rows = hidden.shape[0]
    return pl.pallas_call(
        contract_kernel,
        in_specs=[VMEM] * 2,
        out_specs=VMEM,
        out_shape=jax.ShapeDtypeStruct((rows, w.shape[1]), f32),
        compiler_params=params(4),
        cost_estimate=cost(rows, w),
        name="contract",
    )(hidden, w)


def contract_last_kernel(n, at, hidden, w, before, resid_0, resid_1, own, *rest):
    sends, acc = rest[:-1], rest[-1]
    share = own.shape[0]
    for start, size in blocks_of(w.shape[1], 512):
        cols = slice(start, start + size)
        acc[:, cols] = before[:, cols] + jnp.dot(hidden[...], w[:, cols], preferred_element_type=f32)

    def block(ref, index):
        if share % 8 == 0:
            return ref[pl.ds(pl.multiple_of(index * share, share), share), :]
        chosen = ref[:share, :]
        for b in range(1, n):
            chosen = jnp.where(index == b, ref[b * share : (b + 1) * share, :], chosen)
        return chosen

    half = resid_0.shape[1]
    mine = block(acc, at[3])
    own[:, :half] = mine[:, :half] + block(resid_0, at[3])
    own[:, half:] = mine[:, half:] + block(resid_1, at[3])
    for s in range(1, n):
        sends[s - 1][...] = block(acc, at[3] ^ s).astype(bf16)


def contract_last(n, at, hidden, w, before, *resid):
    rows, cols = before.shape
    share = rows // n
    return pl.pallas_call(
        lambda *refs: contract_last_kernel(n, *refs),
        in_specs=[SMEM] + [VMEM] * 5,
        out_specs=[VMEM] * n,
        out_shape=[jax.ShapeDtypeStruct((share, cols), f32)]
        + [jax.ShapeDtypeStruct((share, cols), bf16)] * (n - 1),
        scratch_shapes=[pltpu.VMEM((rows, cols), f32)],
        compiler_params=params(4),
        cost_estimate=cost(rows, w),
        name="contract_last",
    )(at, hidden, w, before, *resid)


def add_kernel(one, two, *rest):
    out = rest[-1]
    for start, size in blocks_of(out.shape[1], 512):
        cols = slice(start, start + size)
        out[:, cols] = (one[:, cols].astype(f32) + two[:, cols].astype(f32)).astype(bf16)


def add(one, two, *tokens):
    return pl.pallas_call(
        add_kernel,
        in_specs=[VMEM] * 2 + [ANY] * len(tokens),
        out_specs=VMEM,
        out_shape=jax.ShapeDtypeStruct(one.shape, bf16),
        compiler_params=params(4),
        name="add",
    )(one, two, *tokens)


def swap(x, axis, bit):
    n = lax.axis_size(axis)
    return lax.ppermute(x, axis, [(i, i ^ bit) for i in range(n)])


def bits_of(axis):
    n = lax.axis_size(axis)
    return [1 << b for b in range(n.bit_length() - 1)]


def gathered(x, axis, token):
    parts = [x]
    for bit in reversed(bits_of(axis)):
        parts = parts + [swap(p, axis, bit) for p in parts]
        if bit > 1:
            parts = parts[:-1] + [hold(parts[-1], token)]
    return parts


def summed(x, axis, order, *tokens):
    *bits, last = bits_of(axis)[::order]
    for bit in bits:
        x = add(x, swap(x, axis, bit), *(tokens if bit == bits[-1] else ()))
    return x, swap(x, axis, last)


def per_device(tokens, attn_gain, ffn_gain, w_query, key_matrix, value_matrix, w_out, w_gate, w_up, w_down, kv_cache, lengths, slots):
    rows, model = tokens.shape
    wide_at, head_at = lax.axis_index("wide"), lax.axis_index("head")
    wide_size, head_size = lax.axis_size("wide"), lax.axis_size("head")
    places = jnp.stack([wide_at, (wide_at == wide_size - 1).astype(jnp.int32), wide_at & 1, head_at])
    at = places.astype(jnp.int32)

    half = HEAD_WIDTH // 2
    positions = (
        jnp.broadcast_to(lengths[:, None], (lengths.shape[0], DRAFT_TOKENS))
        + jnp.arange(DRAFT_TOKENS, dtype=jnp.int32)[None, :]
    ).reshape(rows).astype(f32)
    exponent = jnp.arange(half, dtype=f32) * (2.0 / HEAD_WIDTH)
    angles = positions[:, None] * (theta_base ** (-exponent))[None, :]
    cos, sin = jnp.cos(angles), jnp.sin(angles)
    cos = jnp.concatenate([cos, cos], axis=1)
    sin = jnp.concatenate([-sin, sin], axis=1)

    qkv, own = project(at, tokens, attn_gain, w_query, key_matrix, value_matrix)
    depth = own.shape[1]
    half = depth // 2
    gain = ffn_gain.reshape(depth // LANES, LANES)

    flat_cache = kv_cache.reshape((-1,) + kv_cache.shape[2:])
    meta = jnp.concatenate([at, lengths, slots])
    cache, gate_0, token = fetch(at, (qkv, meta, cos, sin), Part(flat_cache), Part(w_gate, 0, half))
    cache = cache.reshape(kv_cache.shape)
    value, w_out = attend(meta, cos, sin, cache, gathered(qkv, "wide", token), Part(w_out))

    quarter = half // 2
    up_0, gate_1, token = fetch(at, value, Part(w_up, 0, half), Part(w_gate, half, quarter))
    out_0, attended = output_first(gathered(value, "wide", token), w_out)
    out_1 = output_second(attended, w_out)
    parts_0 = summed(out_0, "head", 1)
    gate_2, token = fetch(at, parts_0[0], Part(w_gate, half + quarter, quarter))
    parts_1 = summed(out_1, "head", -1, token)
    send, keep, resid_0, squares, up_1 = expand_first(
        at, own, gain, parts_0, gate_0, up_0, Part(w_up, half, half)
    )
    gate_1 = (gate_1, gate_2)
    send, resid_1, x = expand_send(at, own, gain, parts_1, gate_1, up_1, send, squares)
    received = swap(send, "wide", 1)
    total = pair(expand_keep(at, x, gate_1, up_1, keep), received, send)
    down_own, down_other, token = fetch(at, total, Part(w_down, side=0), Part(w_down, side=1))
    for bit in bits_of("wide")[1:-1]:
        there = swap(total, "wide", bit)
        total = pair(total, there, total)
    hidden = gated(model, total, swap(total, "wide", bits_of("wide")[-1]), token)
    other = swap(hidden, "wide", 1)
    total, *sends = contract_last(
        head_size, at, other, down_other, contract(hidden, down_own), resid_0, resid_1
    )
    for s, send in reversed(list(enumerate(sends, 1))):
        total = total + swap(send, "head", s).astype(f32)
    return total.astype(bf16)


def solution(mesh):
    in_specs = (
        P("grp", None),
        P(),
        P("wide"),
        P("wide", "head"),
        P("wide", "head"),
        P("wide", "head"),
        P("head", "wide"),
        P("wide", "head"),
        P("wide", "head"),
        P("head", "wide"),
        P(None, "grp", "wide", "head"),
        P("grp"),
        P("grp"),
    )
    out_specs = P(("grp", "head"), "wide")
    return jax.shard_map(
        per_device, mesh=mesh, in_specs=in_specs, out_specs=out_specs, check_vma=False
    )
```
